32 devices in a mesh: section: 4 (over y, x), dp: 8 (over z, core).
Axes of the slice: x: 2, y: 2, z: 4, core: 2. Of those that a mesh axis runs over, the one named last changes fastest.
Arguments:
- text_rows: bfloat16 [32, 2, 300, 768], P(('section', 'dp')), may hold values from -6 to 6
- memory_init: bfloat16 [10, 768], replicated, may hold values from -6 to 6
- cotangent: bfloat16 [32, 2, 320, 768], P(('section', 'dp')), may hold values from -6 to 6
- w_qkv: bfloat16 [4, 384, 2304], P('section'), may hold values from -0.21875 to 0.21875
- w_out: bfloat16 [4, 384, 768], P('section'), may hold values from -0.875 to 0.875
- w_in: bfloat16 [4, 384, 3072], P('section'), may hold values from -0.21875 to 0.21875
- w_hid: bfloat16 [4, 1536, 768], P('section'), may hold values from -0.109375 to 0.109375
- biases: bfloat16 [4, 3840], P('section'), may hold values from -1.5 to 1.5
- norm_gains: bfloat16 [4, 768], P('section'), may hold values from 0.25 to 1.75
- boundaries: int32 [32, 2, 300], P(('section', 'dp')), may hold values 0 or 1
- mem_resets: int32 [32, 2], P(('section', 'dp')), may hold values 0 or 1
- seg_counts: int32 [32], P(('section', 'dp')), may hold values from 1 to 2, as said below
Outputs:
- activations: bfloat16 [32, 2, 320, 768], P(('section', 'dp'))
- input_grads: bfloat16 [32, 2, 320, 768], P(('section', 'dp'))
- memory_grad: float32 [10, 768], replicated
- qkv_grad: float32 [4, 384, 2304], P('section', None, 'dp')
- proj_grad: float32 [4, 384, 768], P('section', None, 'dp')
- up_grad: float32 [4, 384, 3072], P('section', None, 'dp')
- down_grad: float32 [4, 1536, 768], P('section', None, 'dp')
- bias_grad: float32 [4, 3840], P('section', 'dp')
- gain_grad: float32 [4, 768], P('section', 'dp')
The draws below stay inside these ranges and needn't reach their ends.
Inputs may be any that keep to these rules, and one draw needn't show every extreme that they name: `seg_counts`: every item has at least one segment, and some item has 2.
All inputs are finite; a program needn't handle non-finite values. No bound on the sum of `boundaries` or of `mem_resets` on one device may be relied on, other than what follows from the above.
Results may differ from the reference program's by a relative error of at most 0.02.
Values may be sent and summed in bfloat16 or wider, within the bound.
A program may use at most 512 MiB of HBM per device.

```python
import jax
import jax.numpy as jnp
from jax import lax

D = 768
HEADS = 12
HEAD_DIM = 64
FF = 3072
MEM = 10
TEXT = 300
SEGS = 2
SEG = 320
ITEMS = 32


def draw_seg_counts(key, part):
    key = jax.random.fold_in(key, 11)
    first_key, second_key = jax.random.split(key)
    values = jax.random.randint(first_key, (ITEMS,), 1, SEGS + 1)
    chosen = jax.random.randint(second_key, (), 0, ITEMS)
    return jnp.where(jnp.arange(ITEMS) == chosen, SEGS, values).astype(jnp.int32)


def place_ends(result, key, least, high):
    place = [jax.random.randint(jax.random.fold_in(key, axis), (), 0, length) for axis, length in enumerate(result.shape)]
    main_axis = result.shape.index(max(result.shape))
    next_to = place[:main_axis] + [(place[main_axis] + 1) % result.shape[main_axis]] + place[main_axis + 1:]
    return result.at[tuple(place)].set(least).at[tuple(next_to)].set(high)


def levels(rng, extent, cuts, low, high):
    def one(axis_at, shards_of):
        steps = jax.random.uniform(jax.random.fold_in(jax.random.fold_in(rng, 6), axis_at), (shards_of,), jnp.float32, low / len(cuts), high / len(cuts))
        return jnp.repeat(jnp.exp(steps), extent[axis_at] // shards_of).reshape((-1,) + (1,) * (len(extent) - axis_at - 1))

    gain = one(*cuts[0])
    for cut in cuts[1:]:
        gain = gain * one(*cut)
    return gain


def scatter_about(key, dims, scale, bound, pieces=(), kind=jnp.bfloat16):
    gain = levels(key, dims, pieces, -0.22, 0.18) if pieces else 1.0
    entries = jax.random.normal(key, dims, jnp.float32) * scale * gain
    return jnp.minimum(jnp.maximum(entries, -bound), bound).astype(kind)


def setup_inputs(seed: int = 0) -> dict:
    keys = jax.random.split(jax.random.key(seed), 13)
    text_rows = scatter_about(keys[0], (ITEMS, SEGS, TEXT, D), 1.0, 6.0, ((0, 32),))
    memory_init = scatter_about(keys[1], (MEM, D), 1.0, 6.0)
    cotangent = scatter_about(keys[2], (ITEMS, SEGS, SEG, D), 1.0, 6.0, ((0, 32),))
    w_qkv = scatter_about(keys[3], (4, D // 2, 3 * D), D ** -0.5, 0.21875, ((0, 4),))
    w_out = scatter_about(keys[4], (4, D // 2, D), (D // 16) ** -0.5, 0.875, ((0, 4),))
    w_in = scatter_about(keys[5], (4, D // 2, FF), D ** -0.5, 0.21875, ((0, 4),))
    w_hid = scatter_about(keys[6], (4, FF // 2, D), FF ** -0.5, 0.109375, ((0, 4),))
    biases = scatter_about(keys[7], (4, (6 * D + FF) // 2), 0.3, 1.5, ((0, 4),))
    norm_gains = jnp.clip(1.0 + 0.15 * jax.random.normal(keys[8], (4, D), jnp.float32), 0.25, 1.75).astype(jnp.bfloat16)
    boundaries = place_ends((jax.random.randint(keys[9], (ITEMS, SEGS, TEXT), 0, max(4, TEXT // 5)) < 1).astype(jnp.int32), jax.random.fold_in(keys[9], 1), 0, 1)
    mem_resets = place_ends((jax.random.randint(keys[10], (ITEMS, SEGS), 0, 3) < 1).astype(jnp.int32), jax.random.fold_in(keys[10], 1), 0, 1)
    seg_counts = draw_seg_counts(jax.random.fold_in(keys[12], 71), 0)
    return dict(text_rows=text_rows, memory_init=memory_init, cotangent=cotangent, w_qkv=w_qkv, w_out=w_out, w_in=w_in, w_hid=w_hid, biases=biases, norm_gains=norm_gains, boundaries=boundaries, mem_resets=mem_resets, seg_counts=seg_counts)


@jax.custom_vjp
def low(v):
    return lax.optimization_barrier(v.astype(jnp.bfloat16)).astype(jnp.float32)

@jax.custom_vjp
def low_back(v):
    return v

def low_keep(v):
    return (low(v), None)

def low_pass(kept, grad):
    return (grad,)

def back_keep(v):
    return (v, None)

def back_low(kept, grad):
    return (low(grad),)
low.defvjp(low_keep, low_pass)
low_back.defvjp(back_keep, back_low)
MASKED = -1e+30

def rounded(values):
    return low_back(low(values))

def stacked(blocks, layer_index):
    return jnp.concatenate([blocks[layer_index], blocks[2 + layer_index]], axis=0)

def norm_rows(values, scale_vec, shift_vec):
    centre = lax.optimization_barrier(jnp.mean(values, axis=-1, keepdims=True))
    offset = values - centre
    spread = lax.optimization_barrier(jnp.mean(offset * offset, axis=-1, keepdims=True))
    return offset * lax.rsqrt(spread + 1e-05) * scale_vec + shift_vec

def doc_allowed(bounds):
    numbers = jnp.cumsum(bounds, axis=-1).astype(jnp.int32)
    filler = jnp.full(bounds.shape[:-1] + (MEM,), -1, jnp.int32)
    labels = jnp.concatenate([filler, numbers, filler], axis=-1)
    row_side = labels[..., :, None]
    col_side = labels[..., None, :]
    return (row_side == col_side) | (row_side < 0) | (col_side < 0)

def layer_apply(inputs, params, layer_index, allowed):
    highest = lax.Precision.HIGHEST
    w_mix, w_proj, w_up, w_down, vector, gain_pair = [stacked(blocks, layer_index) for blocks in params]
    rows = inputs.shape[0]
    width = inputs.shape[1]
    hidden = w_up.shape[1]
    bias_q = vector[:width]
    bias_v = vector[width:2 * width]
    bias_o = vector[2 * width:3 * width]
    shift_one = vector[3 * width:4 * width]
    bias_in = vector[4 * width:4 * width + hidden]
    bias_hid = vector[4 * width + hidden:5 * width + hidden]
    shift_two = vector[5 * width + hidden:6 * width + hidden]
    mixed = rounded(jnp.dot(inputs, w_mix, precision=highest) + jnp.concatenate([bias_q, jnp.zeros_like(bias_q), bias_v]))
    queries = mixed[:, :width].reshape(rows, HEADS, HEAD_DIM)
    keys_f = mixed[:, width:2 * width].reshape(rows, HEADS, HEAD_DIM)
    values_f = mixed[:, 2 * width:].reshape(rows, HEADS, HEAD_DIM)
    scores = jnp.einsum('qhd,khd->hqk', queries, keys_f, precision=highest) * HEAD_DIM ** (-0.5)
    scores = low_back(jnp.where(allowed[None], scores, MASKED))
    probs = low(jax.nn.softmax(scores, axis=-1))
    heads_out = rounded(jnp.einsum('hqk,khd->qhd', probs, values_f, precision=highest).reshape(rows, width))
    attn = low_back(jnp.dot(heads_out, w_proj, precision=highest) + bias_o)
    first = norm_rows(inputs + attn, gain_pair[:width], shift_one)
    inner = low_back(jnp.dot(low(first), w_up, precision=highest) + bias_in)
    active = low(jax.nn.gelu(inner, approximate=False))
    branch = low_back(jnp.dot(active, w_down, precision=highest) + bias_hid)
    return norm_rows(first + branch, gain_pair[width:], shift_two)

def run_item(params, init, probe, text_item, allowed, fresh, live):
    memory = init
    outputs = []
    for seg_index in range(SEGS):
        mem_now = low_back(jnp.where(fresh[seg_index], init, memory))
        layer_in = rounded(jnp.concatenate([mem_now, text_item[seg_index], mem_now], axis=0) + probe[seg_index])
        middle = rounded(layer_apply(layer_in, params, 0, allowed[seg_index]))
        top_rows = rounded(layer_apply(middle, params, 1, allowed[seg_index]))
        outputs.append(top_rows * live[seg_index])
        memory = top_rows[SEG - MEM:]
    return jnp.stack(outputs)

def reference(text_rows, memory_init, cotangent, w_qkv, w_out, w_in, w_hid, biases, norm_gains, boundaries, mem_resets, seg_counts):
    params = tuple((blocks.astype(jnp.float32) for blocks in (w_qkv, w_out, w_in, w_hid, biases, norm_gains)))
    init = memory_init.astype(jnp.float32)
    probe = jnp.zeros((SEGS, SEG, D), jnp.float32)
    seg_ids = jnp.arange(SEGS)

    def one_item(carry, item):
        text_item, cot_item, bounds, flags, count = item
        allowed = doc_allowed(bounds)
        fresh = (seg_ids == 0) | (flags > 0)
        live = (seg_ids < count).astype(jnp.float32)

        def forward(params_in, init_in, probe_in):
            return run_item(params_in, init_in, probe_in, text_item.astype(jnp.float32), allowed, fresh, live)
        outputs, pull = jax.vjp(forward, params, init, probe)
        grad_params, grad_init, grad_probe = pull(cot_item.astype(jnp.float32))
        new_carry = (jax.tree.map(jnp.add, carry[0], grad_params), carry[1] + grad_init)
        return (new_carry, (outputs.astype(jnp.bfloat16), grad_probe.astype(jnp.bfloat16)))
    start = (jax.tree.map(jnp.zeros_like, params), jnp.zeros_like(init))
    totals, stacks = lax.scan(one_item, start, (text_rows, cotangent, boundaries, mem_resets, seg_counts))
    grad_params, grad_init = totals
    activations, input_grads = stacks
    return (activations, input_grads, grad_init, grad_params[0], grad_params[1], grad_params[2], grad_params[3], grad_params[4], grad_params[5])
```

```python
from functools import partial

import jax
import jax.numpy as jnp
from jax import lax
from jax.sharding import PartitionSpec as P

HEADS = 12
HEAD_DIM = 64


EPS = 1e-05
MASKED = -1e30


def norm_rows(values, scale_vec, shift_vec):
    centre = jnp.mean(values, axis=-1, keepdims=True)
    offset = values - centre
    spread = jnp.mean(offset * offset, axis=-1, keepdims=True)
    return offset * lax.rsqrt(spread + EPS) * scale_vec + shift_vec


def exact_gelu(values):
    return jax.nn.gelu(values, approximate=False)


def split_vector(vector, width, hidden):
    vector = vector.astype(jnp.float32)
    bounds_list = [
        0,
        width,
        2 * width,
        3 * width,
        4 * width,
        4 * width + hidden,
        5 * width + hidden,
        6 * width + hidden,
    ]
    return [vector[bounds_list[number] : bounds_list[number + 1]] for number in range(7)]


def doc_allowed(bounds, mem_rows):
    numbers = jnp.cumsum(bounds, axis=-1)
    filler = jnp.full(bounds.shape[:-1] + (mem_rows,), -1, jnp.int32)
    labels = jnp.concatenate([filler, numbers, filler], axis=-1)
    row_side = labels[..., :, None]
    col_side = labels[..., None, :]
    return (row_side == col_side) | (row_side < 0) | (col_side < 0)


def split_heads(mixed_b, width):
    rows = mixed_b.shape[0]
    queries = mixed_b[:, :width].reshape(rows, HEADS, HEAD_DIM)
    keys_b = mixed_b[:, width : 2 * width].reshape(rows, HEADS, HEAD_DIM)
    values_b = mixed_b[:, 2 * width :].reshape(rows, HEADS, HEAD_DIM)
    return (queries, keys_b, values_b)


def masked_scores(queries, keys_b, allowed):
    scores = jnp.einsum(
        "qhd,khd->hqk", queries, keys_b, preferred_element_type=jnp.float32
    ) * HEAD_DIM ** (-0.5)
    return jnp.where(allowed[None], scores, MASKED)


def layer_forward(inputs, weights, allowed):
    w_mix, w_proj, w_up, w_down, vector, gain_pair = weights
    rows, width = inputs.shape
    hidden = w_up.shape[1]
    bias_q, bias_v, bias_o, shift_one, bias_in, bias_hid, shift_two = split_vector(
        vector, width, hidden
    )
    gain_pair = gain_pair.astype(jnp.float32)
    mixed = jnp.dot(inputs, w_mix, preferred_element_type=jnp.float32)
    mixed = mixed + jnp.concatenate([bias_q, jnp.zeros_like(bias_q), bias_v])
    mixed_b = mixed.astype(jnp.bfloat16)
    queries, keys_b, values_b = split_heads(mixed_b, width)
    scores = masked_scores(queries, keys_b, allowed)
    peak = jnp.max(scores, axis=-1, keepdims=True)
    expo = jnp.exp(scores - peak)
    totals = jnp.sum(expo, axis=-1, keepdims=True)
    probs_b = (expo / totals).astype(jnp.bfloat16)
    log_total = peak + jnp.log(totals)
    heads_b = (
        jnp.einsum("hqk,khd->qhd", probs_b, values_b, preferred_element_type=jnp.float32)
        .reshape(rows, width)
        .astype(jnp.bfloat16)
    )
    attn = jnp.dot(heads_b, w_proj, preferred_element_type=jnp.float32) + bias_o
    resid = inputs.astype(jnp.float32) + attn
    first = norm_rows(resid, gain_pair[:width], shift_one)
    first_b = first.astype(jnp.bfloat16)
    inner = jnp.dot(first_b, w_up, preferred_element_type=jnp.float32) + bias_in
    active_b = exact_gelu(inner).astype(jnp.bfloat16)
    branch = jnp.dot(active_b, w_down, preferred_element_type=jnp.float32) + bias_hid
    second = first + branch
    output = norm_rows(second, gain_pair[width:], shift_two)
    return (
        output,
        (inputs, mixed_b, log_total, heads_b, resid, first, first_b, inner, active_b, second),
    )


def layer_backward(grad_out, stored, weights, allowed):
    w_mix, w_proj, w_up, w_down, vector, gain_pair = weights
    inputs, mixed_b, log_total, heads_b, resid, first, first_b, inner, active_b, second = stored
    rows, width = inputs.shape
    hidden = w_up.shape[1]
    shift_one, shift_two = [split_vector(vector, width, hidden)[at] for at in (3, 6)]
    gain_pair = gain_pair.astype(jnp.float32)
    gain_one = gain_pair[:width]
    gain_two = gain_pair[width:]
    fl_type = jnp.float32
    bf_type = jnp.bfloat16
    _, pull_two = jax.vjp(norm_rows, second, gain_two, shift_two)
    grad_second, grad_gain_two, grad_shift_two = pull_two(grad_out)
    grad_branch = grad_second.astype(bf_type)
    grad_active = jnp.einsum("rd,fd->rf", grad_branch, w_down, preferred_element_type=fl_type)
    _, pull_gelu = jax.vjp(exact_gelu, inner)
    grad_inner = pull_gelu(grad_active)[0].astype(bf_type)
    grad_first = grad_second + jnp.einsum(
        "rf,df->rd", grad_inner, w_up, preferred_element_type=fl_type
    )
    _, pull_one = jax.vjp(norm_rows, resid, gain_one, shift_one)
    grad_resid, grad_gain_one, grad_shift_one = pull_one(grad_first)
    grad_attn = grad_resid.astype(bf_type)
    grad_heads = jnp.einsum("re,de->rd", grad_attn, w_proj, preferred_element_type=fl_type).astype(
        bf_type
    )
    grad_heads = grad_heads.reshape(rows, HEADS, HEAD_DIM)
    queries, keys_b, values_b = split_heads(mixed_b, width)
    scores = masked_scores(queries, keys_b, allowed)
    probs = jnp.exp(scores - log_total)
    probs_b = probs.astype(bf_type)
    grad_value = jnp.einsum("hqk,qhd->khd", probs_b, grad_heads, preferred_element_type=fl_type)
    grad_probs = jnp.einsum("qhd,khd->hqk", grad_heads, values_b, preferred_element_type=fl_type)
    centre = jnp.sum(probs * grad_probs, axis=-1, keepdims=True)
    grad_scores = (probs * (grad_probs - centre)).astype(bf_type)
    grad_query = jnp.einsum(
        "hqk,khd->qhd", grad_scores, keys_b, preferred_element_type=fl_type
    ) * HEAD_DIM ** (-0.5)
    grad_key = jnp.einsum(
        "hqk,qhd->khd", grad_scores, queries, preferred_element_type=fl_type
    ) * HEAD_DIM ** (-0.5)
    grad_mixed = jnp.concatenate(
        [
            grad_query.reshape(rows, width),
            grad_key.reshape(rows, width),
            grad_value.reshape(rows, width),
        ],
        axis=1,
    ).astype(bf_type)
    grad_inputs = (
        grad_resid + jnp.einsum("re,de->rd", grad_mixed, w_mix, preferred_element_type=fl_type)
    ).astype(bf_type)
    pairs = (
        (inputs, grad_mixed),
        (heads_b, grad_attn),
        (first_b, grad_inner),
        (active_b, grad_branch),
    )
    sums = (grad_gain_one, grad_gain_two, grad_shift_one, grad_shift_two)
    return (grad_inputs, pairs, sums)


def weight_grads(records):
    fl_type = jnp.float32
    mats = []
    cols = []
    for number in range(4):
        left = jnp.concatenate([pairs[number][0] for pairs, _ in records], axis=0)
        right = jnp.concatenate([pairs[number][1] for pairs, _ in records], axis=0)
        mats.append(jnp.einsum("rd,re->de", left, right, preferred_element_type=fl_type))
        cols.append(jnp.sum(right.astype(fl_type), axis=0))
    gain_one, gain_two, shift_one, shift_two = [
        sum(sums[number] for _, sums in records) for number in range(4)
    ]
    width = cols[1].shape[0]
    vector = jnp.concatenate(
        [
            cols[0][:width],
            cols[0][2 * width :],
            cols[1],
            shift_one,
            cols[2],
            cols[3],
            shift_two,
        ]
    )
    return (*mats, vector, jnp.concatenate([gain_one, gain_two]))


def per_device(
    text_rows,
    memory_init,
    cotangent,
    w_qkv,
    w_out,
    w_in,
    w_hid,
    biases,
    norm_gains,
    boundaries,
    mem_resets,
    seg_counts,
):
    fl_type = jnp.float32
    bf_type = jnp.bfloat16
    items, segs, text_len, width = text_rows.shape
    mem_rows = memory_init.shape[0]
    seg_rows = text_len + 2 * mem_rows
    blocks = [
        lax.all_gather(block[0], "section")
        for block in (w_qkv, w_out, w_in, w_hid, biases, norm_gains)
    ]
    layers = [
        tuple(jnp.concatenate([block[at], block[2 + at]], axis=0) for block in blocks)
        for at in range(2)
    ]
    allowed = doc_allowed(boundaries, mem_rows)
    live = jnp.arange(segs)[None] < seg_counts[:, None]
    fresh = (jnp.arange(segs)[None] == 0) | (mem_resets > 0)
    stored = {}
    tops = {}
    for item in range(items):
        memory = memory_init
        for seg in range(segs):
            mem_now = jnp.where(fresh[item, seg], memory_init, memory)
            rows_now = jnp.concatenate([mem_now, text_rows[item, seg], mem_now], axis=0)
            for at in range(2):
                result, stored[item, seg, at] = layer_forward(
                    rows_now, layers[at], allowed[item, seg]
                )
                rows_now = result.astype(bf_type)
            tops[item, seg] = jnp.where(live[item, seg], rows_now, 0)
            memory = rows_now[seg_rows - mem_rows :]
    records = {0: [], 1: []}
    input_grads = {}
    memory_grad = jnp.zeros((mem_rows, width), fl_type)
    for item in range(items):
        carried = jnp.zeros((mem_rows, width), fl_type)
        for seg in reversed(range(segs)):
            grad_now = jnp.where(live[item, seg], cotangent[item, seg].astype(fl_type), 0.0)
            grad_now = jnp.concatenate(
                [grad_now[: seg_rows - mem_rows], grad_now[seg_rows - mem_rows :] + carried],
                axis=0,
            ).astype(bf_type)
            for at in (1, 0):
                grad_now, pairs, sums = layer_backward(
                    grad_now.astype(fl_type), stored[item, seg, at], layers[at], allowed[item, seg]
                )
                records[at].append((pairs, sums))
            input_grads[item, seg] = grad_now
            folded = grad_now[:mem_rows].astype(fl_type) + grad_now[
                seg_rows - mem_rows :
            ].astype(fl_type)
            folded = folded.astype(bf_type).astype(fl_type)
            memory_grad = memory_grad + jnp.where(fresh[item, seg], folded, 0.0)
            carried = jnp.where(fresh[item, seg], 0.0, folded)

    def stacked(table):
        return jnp.stack(
            [jnp.stack([table[item, seg] for seg in range(segs)]) for item in range(items)]
        )

    totals = [weight_grads(records[at]) for at in range(2)]

    def reduce_blocks(one, two):
        halves = jnp.stack([one, two])
        halves = halves.reshape(2, 2, -1, halves.shape[-1])
        ordered = halves.transpose(1, 0, 2, 3).reshape(4, -1, halves.shape[-1]).astype(bf_type)
        mine = lax.psum_scatter(ordered, "section", scatter_dimension=0, tiled=True)
        return lax.psum_scatter(mine, "dp", scatter_dimension=2, tiled=True).astype(fl_type)

    reduced = [reduce_blocks(totals[0][number], totals[1][number]) for number in range(4)]
    vector = [totals[at][4].reshape(2, -1) for at in range(2)]
    gain = [totals[at][5].reshape(2, -1) for at in range(2)]
    small = [reduce_blocks(*vector)[:, 0], reduce_blocks(*gain)[:, 0]]
    return (
        stacked(tops),
        stacked(input_grads),
        lax.psum(memory_grad, ("section", "dp")),
        *reduced,
        *small,
    )


def solution(mesh):
    in_specs = (
        P(("section", "dp"), None, None, None),
        P(),
        P(("section", "dp"), None, None, None),
        P("section", None, None),
        P("section", None, None),
        P("section", None, None),
        P("section", None, None),
        P("section", None),
        P("section", None),
        P(("section", "dp"), None, None),
        P(("section", "dp"), None),
        P(("section", "dp")),
    )
    out_specs = (
        P(("section", "dp"), None, None, None),
        P(("section", "dp"), None, None, None),
        P(),
        P("section", None, "dp"),
        P("section", None, "dp"),
        P("section", None, "dp"),
        P("section", None, "dp"),
        P("section", "dp"),
        P("section", "dp"),
    )
    return jax.shard_map(
        per_device, mesh=mesh, in_specs=in_specs, out_specs=out_specs, check_vma=False
    )
```

```python
import functools

import jax
import jax.numpy as jnp
from jax import lax
from jax.experimental import pallas as pl
from jax.experimental.pallas import tpu as pltpu
from jax.sharding import PartitionSpec as P

HEADS = 12
HEAD_DIM = 64
EPS = 1e-05
MASKED = -1e30
VMEM_BYTES = 63 * 2**20
F32 = jnp.float32
BF16 = jnp.bfloat16


def dot_nn(one, two):
    return jnp.dot(one, two, preferred_element_type=F32)


def dot_nt(one, two):
    return lax.dot_general(one, two, (((1,), (1,)), ((), ())), preferred_element_type=F32)


def dot_tn(one, two):
    return lax.dot_general(one, two, (((0,), (0,)), ((), ())), preferred_element_type=F32)


def weight_tile(pack_ref, kind, tile, width):
    part = width // 4
    if kind == "hid":
        return pack_ref[tile % 2, tile // 2, 0, 8 * part : 8 * part + width, :]
    start = {"qkv": 0, "out": 3, "in": 4}[kind] * part
    at = start + tile * part
    pieces = [pack_ref[core, half, 0, pl.ds(at, part), :] for half in range(2) for core in range(2)]
    return jnp.concatenate(pieces, axis=0)


def head_lanes(shape, head):
    lanes = lax.broadcasted_iota(jnp.int32, shape, 1)
    return (lanes // HEAD_DIM) == head


def erf_parts(values):
    density = jnp.exp(-0.5 * values * values) * 0.3989422804014327
    phi = 0.5 * (1.0 + lax.erf(values * 0.7071067811865476))
    return phi, density


def forward_body(
    first_step, segs, fresh_ref, live_ref, text_ref, init_ref, prev_ref, labels_row_ref,
    labels_col_ref, pack_ref, vector_ref, gain_ref,
    x_ref, mixed_ref, heads_ref, hat_one_ref, first_ref, active_ref, slope_ref, hat_two_ref,
    stats_ref, out_ref, acts_ref,
    y_scr, bias_scr, sum_scr,
):
    step = pl.program_id(0) + first_step
    layer = step % 2
    seg = (step // 2) % segs
    item = step // (2 * segs)
    rows, width = y_scr.shape
    hidden = 4 * width

    @pl.when(pl.program_id(0) == 0)
    def _():
        y_scr[...] = prev_ref[...]

    @pl.when(layer == 0)
    def _():
        fresh = fresh_ref[item * segs + seg] > 0
        text = text_ref[0, 0]
        last = y_scr[rows - 16 : rows, :].astype(F32)
        head_rows = pltpu.roll(last, 10, 0)
        number = lax.broadcasted_iota(jnp.int32, (16, width), 0)
        top = jnp.where(fresh, init_ref[0], head_rows)
        low = jnp.where(fresh, init_ref[1], last)
        x_ref[0] = text
        x_ref[0, 0:16, :] = jnp.where(number < 10, top, text[0:16].astype(F32)).astype(BF16)
        x_ref[0, rows - 16 : rows, :] = jnp.where(
            number >= 6, low, text[rows - 16 : rows].astype(F32)
        ).astype(BF16)

    @pl.when(layer == 1)
    def _():
        x_ref[0] = y_scr[...]

    row_side = labels_row_ref[0, 0]
    col_side = labels_col_ref[0, 0]
    allowed = (row_side == col_side) | (row_side < 0) | (col_side < 0)
    bias_scr[...] = jnp.where(allowed, 0.0, MASKED)

    vector = lambda at, size: vector_ref[0, :, at : at + size]
    inputs = x_ref[0]
    for tile in range(3):
        mixed = dot_nn(inputs, weight_tile(pack_ref, "qkv", tile, width))
        if tile == 0:
            mixed = mixed + vector(0, width)
        if tile == 2:
            mixed = mixed + vector(width, width)
        mixed_ref[0, :, tile * width : (tile + 1) * width] = mixed.astype(BF16)

    group = 4 * HEAD_DIM
    stat_lane = lax.broadcasted_iota(jnp.int32, (rows, 128), 1)
    stats = jnp.zeros((rows, 128), F32)
    for number in range(width // group):
        at = number * group
        queries = mixed_ref[0, :, at : at + group] * BF16(HEAD_DIM**-0.5)
        keys = mixed_ref[0, :, width + at : width + at + group]
        values = mixed_ref[0, :, 2 * width + at : 2 * width + at + group]
        total = jnp.zeros((rows, group), F32)
        for head in range(4):
            mine = head_lanes((rows, group), head)
            scores = dot_nt(jnp.where(mine, queries, 0), keys) + bias_scr[...]
            peak = jnp.max(scores, axis=-1, keepdims=True)
            expo = jnp.exp(scores - peak)
            norm = jnp.sum(expo, axis=-1, keepdims=True)
            probs = (expo * (1.0 / norm)).astype(BF16)
            total = total + dot_nn(probs, jnp.where(mine, values, 0))
            stats = jnp.where(stat_lane == number * 4 + head, peak + jnp.log(norm), stats)
        heads_ref[0, :, at : at + group] = total.astype(BF16)

    attn = dot_nn(heads_ref[0], weight_tile(pack_ref, "out", 0, width)) + vector(2 * width, width)
    resid = inputs.astype(F32) + attn
    offset = resid - jnp.mean(resid, axis=-1, keepdims=True)
    scale = lax.rsqrt(jnp.mean(offset * offset, axis=-1, keepdims=True) + EPS)
    hat = offset * scale
    hat_one_ref[0] = hat.astype(BF16)
    stats = jnp.where(stat_lane == HEADS, scale, stats)
    first = hat * gain_ref[0, :, 0:width] + vector(3 * width, width)
    first_b = first.astype(BF16)
    first_ref[0] = first_b
    sum_scr[...] = first + vector(4 * width + hidden, width)

    def ff_tile(tile, _):
        at = pl.multiple_of(tile * width, width)
        inner = dot_nn(first_b, weight_tile(pack_ref, "in", tile, width))
        inner = inner + vector_ref[0, :, pl.ds(4 * width + at, width)]
        phi, density = erf_parts(inner)
        active = (inner * phi).astype(BF16)
        active_ref[0, :, pl.ds(at, width)] = active
        slope_ref[0, :, pl.ds(at, width)] = (phi + inner * density).astype(BF16)
        sum_scr[...] += dot_nn(active, weight_tile(pack_ref, "hid", tile, width))
        return _

    lax.fori_loop(0, 4, ff_tile, 0)
    second = sum_scr[...]
    offset = second - jnp.mean(second, axis=-1, keepdims=True)
    scale = lax.rsqrt(jnp.mean(offset * offset, axis=-1, keepdims=True) + EPS)
    hat = offset * scale
    hat_two_ref[0] = hat.astype(BF16)
    stats_ref[0] = jnp.where(stat_lane == HEADS + 1, scale, stats)
    result = (hat * gain_ref[0, :, width : 2 * width] + vector(5 * width + hidden, width)).astype(BF16)
    y_scr[...] = result
    out_ref[0] = result

    @pl.when(layer == 1)
    def _():
        live = live_ref[item * segs + seg] > 0
        acts_ref[0, 0] = jnp.where(live, result, 0)


def forward_steps(first_step, count, fresh, live, text, init, prev, labels, pack, vectors, gains):
    items, segs, rows, width = text.shape
    hidden = 4 * width
    at = lambda t: t + first_step
    by_seg = lambda t, *_: (at(t) // (2 * segs), (at(t) // 2) % segs, 0, 0)
    by_layer3 = lambda t, *_: (at(t) % 2, 0, 0)
    by_step = lambda t, *_: (t, 0, 0)
    whole = lambda shape: pl.BlockSpec(shape, lambda t, *_: (0,) * len(shape))
    saved = [
        ((rows, width), BF16),
        ((rows, 3 * width), BF16),
        ((rows, width), BF16),
        ((rows, width), BF16),
        ((rows, width), BF16),
        ((rows, hidden), BF16),
        ((rows, hidden), BF16),
        ((rows, width), BF16),
        ((rows, 128), F32),
        ((rows, width), BF16),
    ]
    labels_row = labels[:, :, :, None]
    labels_col = labels[:, :, None, :]
    grid_spec = pltpu.PrefetchScalarGridSpec(
        num_scalar_prefetch=2,
        grid=(count,),
        in_specs=[
            pl.BlockSpec((1, 1, rows, width), by_seg),
            whole(init.shape),
            whole(prev.shape),
            pl.BlockSpec((1, 1, rows, 1), by_seg),
            pl.BlockSpec((1, 1, 1, rows), by_seg),
            pl.BlockSpec((2, 2, 1) + pack.shape[3:], lambda t, *_: (0, 0, at(t) % 2, 0, 0)),
            pl.BlockSpec((1, 1, vectors.shape[2]), by_layer3),
            pl.BlockSpec((1, 1, gains.shape[2]), by_layer3),
        ],
        out_specs=[pl.BlockSpec((1,) + shape, by_step) for shape, _ in saved]
        + [pl.BlockSpec((1, 1, rows, width), by_seg)],
        scratch_shapes=[
            pltpu.VMEM((rows, width), BF16),
            pltpu.VMEM((rows, rows), F32),
            pltpu.VMEM((rows, width), F32),
        ],
    )
    return pl.pallas_call(
        functools.partial(forward_body, first_step, segs),
        grid_spec=grid_spec,
        out_shape=[jax.ShapeDtypeStruct((count,) + shape, kind) for shape, kind in saved]
        + [jax.ShapeDtypeStruct(text.shape, BF16)],
        compiler_params=pltpu.CompilerParams(vmem_limit_bytes=VMEM_BYTES),
        name="forward_steps",
    )(fresh, live, text, init, prev, labels_row, labels_col, pack, vectors, gains)


def norm_backward(grad, hat, scale, gain):
    scaled = grad * gain
    mean_one = jnp.mean(scaled, axis=-1, keepdims=True)
    mean_two = jnp.mean(scaled * hat, axis=-1, keepdims=True)
    return (scaled - mean_one - hat * mean_two) * scale


def column_sum(values):
    return jnp.sum(values, axis=0, keepdims=True)


def backward_body(
    top_step, segs, fresh_ref, live_ref, cot_ref, prev_ref, carry_in_ref, labels_row_ref,
    labels_col_ref, pack_ref, gain_ref, mixed_ref, heads_ref, hat_one_ref, slope_ref, hat_two_ref,
    stats_ref,
    branch_ref, inner_ref, attn_ref, mix_ref, grad_ref, sums_ref, inputs_ref, init_ref, carry_out_ref,
    g_scr, carry_scr, bias_scr, sum_scr, go_scr,
):
    step = top_step - pl.program_id(0)
    layer = step % 2
    seg = (step // 2) % segs
    item = step // (2 * segs)
    rows, width = g_scr.shape
    hidden = 4 * width

    @pl.when(pl.program_id(0) == 0)
    def _():
        g_scr[...] = prev_ref[...]
        carry_scr[...] = carry_in_ref[...]
        init_ref[...] = jnp.zeros_like(init_ref)

    @pl.when(layer == 1)
    def _():
        live = live_ref[item * segs + seg] > 0
        cot = jnp.where(live, cot_ref[0, 0], 0)
        g_scr[...] = cot
        carried = jnp.where(seg == segs - 1, 0.0, carry_scr[...])
        g_scr[rows - 16 : rows, :] = (cot[rows - 16 : rows].astype(F32) + carried).astype(BF16)

    row_side = labels_row_ref[0, 0]
    col_side = labels_col_ref[0, 0]
    allowed = (row_side == col_side) | (row_side < 0) | (col_side < 0)
    bias_scr[...] = jnp.where(allowed, 0.0, MASKED)

    stats = stats_ref[0]
    scale_one = stats[:, HEADS : HEADS + 1]
    scale_two = stats[:, HEADS + 1 : HEADS + 2]
    grad = g_scr[...].astype(F32)
    hat = hat_two_ref[0].astype(F32)
    gain = gain_ref[0]
    sums_ref[0, :, 0:width] = column_sum(grad * hat)
    sums_ref[0, :, width : 2 * width] = column_sum(grad)
    grad_second = norm_backward(grad, hat, scale_two, gain[:, width : 2 * width])
    branch = grad_second.astype(BF16)
    branch_ref[0] = branch
    sums_ref[0, :, 2 * width : 3 * width] = column_sum(branch.astype(F32))
    sum_scr[...] = grad_second

    def ff_tile(tile, _):
        at = pl.multiple_of(tile * width, width)
        active = dot_nt(branch, weight_tile(pack_ref, "hid", tile, width))
        inner = (active * slope_ref[0, :, pl.ds(at, width)].astype(F32)).astype(BF16)
        inner_ref[0, :, pl.ds(at, width)] = inner
        sums_ref[0, :, pl.ds(8 * width + at, width)] = column_sum(inner.astype(F32))
        sum_scr[...] += dot_nt(inner, weight_tile(pack_ref, "in", tile, width))
        return _

    lax.fori_loop(0, 4, ff_tile, 0)
    grad = sum_scr[...]
    hat = hat_one_ref[0].astype(F32)
    sums_ref[0, :, 3 * width : 4 * width] = column_sum(grad * hat)
    sums_ref[0, :, 4 * width : 5 * width] = column_sum(grad)
    resid = norm_backward(grad, hat, scale_one, gain[:, 0:width])
    sum_scr[...] = resid
    attn = resid.astype(BF16)
    attn_ref[0] = attn
    sums_ref[0, :, 5 * width : 6 * width] = column_sum(attn.astype(F32))
    go = dot_nt(attn, weight_tile(pack_ref, "out", 0, width)).astype(BF16)
    go_scr[...] = go
    product = go.astype(F32) * heads_ref[0].astype(F32)
    high = product.astype(BF16)
    low = (product - high.astype(F32)).astype(BF16)
    picks = (
        lax.broadcasted_iota(jnp.int32, (16, width), 1) // HEAD_DIM
        == lax.broadcasted_iota(jnp.int32, (16, width), 0)
    ).astype(BF16)
    centres = dot_nt(picks, high) + dot_nt(picks, low)
    logs = jnp.transpose(stats)

    group = 4 * HEAD_DIM
    for number in range(width // group):
        at = number * group
        queries = mixed_ref[0, :, at : at + group] * BF16(HEAD_DIM**-0.5)
        keys = mixed_ref[0, :, width + at : width + at + group]
        values = mixed_ref[0, :, 2 * width + at : 2 * width + at + group]
        outs = go_scr[:, at : at + group]
        grad_q = jnp.zeros((rows, group), F32)
        grad_k = jnp.zeros((rows, group), F32)
        grad_v = jnp.zeros((rows, group), F32)
        for head in range(4):
            mine = head_lanes((rows, group), head)
            row = number * 4 + head
            keys_h = jnp.where(mine, keys, 0)
            scores = dot_nt(keys_h, queries) + bias_scr[...]
            probs = jnp.exp(scores - logs[row : row + 1, :])
            grad_p = dot_nt(jnp.where(mine, values, 0), outs)
            grad_s = (probs * (grad_p - centres[row : row + 1, :])).astype(BF16)
            grad_v = grad_v + dot_nn(probs.astype(BF16), jnp.where(mine, outs, 0))
            grad_k = grad_k + dot_nn(grad_s, jnp.where(mine, queries, 0))
            grad_q = grad_q + dot_tn(grad_s, keys_h)
        mix_ref[0, :, at : at + group] = (grad_q * HEAD_DIM**-0.5).astype(BF16)
        mix_ref[0, :, width + at : width + at + group] = grad_k.astype(BF16)
        mix_ref[0, :, 2 * width + at : 2 * width + at + group] = grad_v.astype(BF16)

    sums_ref[0, :, 6 * width : 7 * width] = column_sum(mix_ref[0, :, 0:width].astype(F32))
    sums_ref[0, :, 7 * width : 8 * width] = column_sum(mix_ref[0, :, 2 * width : 3 * width].astype(F32))
    total = sum_scr[...]
    for tile in range(3):
        total = total + dot_nt(
            mix_ref[0, :, tile * width : (tile + 1) * width], weight_tile(pack_ref, "qkv", tile, width)
        )
    result = total.astype(BF16)
    g_scr[...] = result
    grad_ref[...] = result

    @pl.when(layer == 0)
    def _():
        inputs_ref[0, 0] = result
        fresh = fresh_ref[item * segs + seg] > 0
        number = lax.broadcasted_iota(jnp.int32, (16, width), 0)
        folded = result[rows - 16 : rows].astype(F32) + pltpu.roll(result[0:16].astype(F32), 6, 0)
        folded = jnp.where(number >= 6, folded, 0.0).astype(BF16).astype(F32)
        init_ref[...] += jnp.where(fresh, folded, 0.0)
        carry_scr[...] = jnp.where(fresh, 0.0, folded)

    carry_out_ref[...] = carry_scr[...]


def backward_steps(
    top_step, count, fresh, live, cot, prev, carry, labels, pack, gains, saved, inputs_so_far=None
):
    items, segs, rows, width = cot.shape
    hidden = 4 * width
    at = lambda t: top_step - t
    by_seg = lambda t, *_: (at(t) // (2 * segs), (at(t) // 2) % segs, 0, 0)
    by_layer3 = lambda t, *_: (at(t) % 2, 0, 0)
    by_step = lambda t, *_: (count - 1 - t, 0, 0)
    whole = lambda shape: pl.BlockSpec(shape, lambda t, *_: (0,) * len(shape))
    names = ("mixed", "heads", "hat_one", "slope", "hat_two", "stats")
    outs = [
        ((rows, width), BF16),
        ((rows, hidden), BF16),
        ((rows, width), BF16),
        ((rows, 3 * width), BF16),
    ]
    labels_row = labels[:, :, :, None]
    labels_col = labels[:, :, None, :]
    operands = [fresh, live, cot, prev, carry, labels_row, labels_col, pack, gains]
    operands += [saved[name] for name in names]
    in_specs = [
        pl.BlockSpec((1, 1, rows, width), by_seg),
        whole(prev.shape),
        whole(carry.shape),
        pl.BlockSpec((1, 1, rows, 1), by_seg),
        pl.BlockSpec((1, 1, 1, rows), by_seg),
        pl.BlockSpec((2, 2, 1) + pack.shape[3:], lambda t, *_: (0, 0, at(t) % 2, 0, 0)),
        pl.BlockSpec((1, 1, gains.shape[2]), by_layer3),
    ] + [pl.BlockSpec((1,) + saved[name].shape[1:], by_step) for name in names]
    body = functools.partial(backward_body, top_step, segs)
    aliases = {}
    if inputs_so_far is not None:
        operands.append(inputs_so_far)
        in_specs.append(pl.BlockSpec(memory_space=pl.ANY))
        aliases = {len(operands) - 1: len(outs) + 2}
        inner_body = body

        def body(*refs):
            cut = 2 + len(in_specs)
            return inner_body(*refs[: cut - 1], *refs[cut:])

    grid_spec = pltpu.PrefetchScalarGridSpec(
        num_scalar_prefetch=2,
        grid=(count,),
        in_specs=in_specs,
        out_specs=[pl.BlockSpec((1,) + shape, by_step) for shape, _ in outs]
        + [
            whole((rows, width)),
            pl.BlockSpec((1, 1, 12 * width), by_step),
            pl.BlockSpec((1, 1, rows, width), by_seg),
            whole((16, width)),
            whole((16, width)),
        ],
        scratch_shapes=[
            pltpu.VMEM((rows, width), BF16),
            pltpu.VMEM((16, width), F32),
            pltpu.VMEM((rows, rows), F32),
            pltpu.VMEM((rows, width), F32),
            pltpu.VMEM((rows, width), BF16),
        ],
    )
    return pl.pallas_call(
        body,
        grid_spec=grid_spec,
        out_shape=[jax.ShapeDtypeStruct((count,) + shape, kind) for shape, kind in outs]
        + [
            jax.ShapeDtypeStruct((rows, width), BF16),
            jax.ShapeDtypeStruct((count, 1, 12 * width), F32),
            jax.ShapeDtypeStruct(cot.shape, BF16),
            jax.ShapeDtypeStruct((16, width), F32),
            jax.ShapeDtypeStruct((16, width), F32),
        ],
        input_output_aliases=aliases,
        compiler_params=pltpu.CompilerParams(vmem_limit_bytes=VMEM_BYTES),
        name="backward_steps",
    )(*operands)


GRAD_NAMES = ("first", "inner", "active", "branch", "x", "mix", "heads", "attn")


def weight_grad_body(
    layer, segs_all, dp, *refs,
):
    sources = refs[:8]
    extra_ref, mine_ref, theirs_ref = refs[8:11]
    held = refs[11:19]
    wire, in_sems, extra_sem, out_sems = refs[19:23]
    core = lax.axis_index("dp") % 2
    rows = sources[0].shape[1]
    width = sources[0].shape[2]
    half = width // 2
    lanes = wire.shape[-1]
    thin = width // dp
    wide = 3 * thin

    def loads(number):
        return [
            pltpu.make_async_copy(
                sources[number].at[2 * at + layer],
                held[number].at[pl.ds(at * rows, rows)],
                in_sems.at[number, at],
            )
            for at in range(segs_all)
        ]

    for number in range(8):
        for copy in loads(number):
            copy.start()
    extra = pltpu.make_async_copy(extra_ref, wire.at[:, :, :, :, pl.ds(half, extra_ref.shape[4])], extra_sem)
    extra.start()

    def ready(*numbers):
        for number in numbers:
            for copy in loads(number):
                copy.wait()

    def stores(kind):
        return [
            pltpu.make_async_copy(wire.at[kind, core], mine_ref.at[kind], out_sems.at[kind, 0]),
            pltpu.make_async_copy(wire.at[kind, 1 - core], theirs_ref.at[kind], out_sems.at[kind, 1]),
        ]

    first, inner, active, branch, inputs, mix, heads, attn = held
    extra.wait()

    ready(0, 1)
    per_tile = width // lanes

    def in_tile(tile, _):
        right = inner[:, pl.ds(pl.multiple_of(tile * width, width), width)]
        for side in range(2):
            result = dot_tn(first[:, side * half : (side + 1) * half], right).astype(BF16)
            for at in range(per_tile):
                wire[1, at % 2, tile * (per_tile // 2) + at // 2, side, 0:half, :] = result[
                    :, at * lanes : (at + 1) * lanes
                ]
        return _

    lax.fori_loop(0, 4, in_tile, 0)
    for copy in stores(1):
        copy.start()

    ready(2, 3)
    def hid_tile(side, _):
        for part in range(4):
            left = active[:, pl.ds(pl.multiple_of(side * 4 * half + part * half, half), half)]
            result = dot_tn(left, branch[...]).astype(BF16)
            for at in range(dp):
                wire[2, at % 2, at // 2, side, 0:half, part * thin : (part + 1) * thin] = result[
                    :, at * thin : (at + 1) * thin
                ]
        return _
    lax.fori_loop(0, 2, hid_tile, 0)
    for copy in stores(2):
        copy.start()

    ready(4, 5, 6, 7)
    for side in range(2):
        left = inputs[:, side * half : (side + 1) * half]
        for tile in range(2):
            result = dot_tn(left, mix[:, tile * 3 * half : (tile + 1) * 3 * half]).astype(BF16)
            for at in range(dp // 2):
                place = tile * (dp // 2) + at
                wire[0, place % 2, place // 2, side, 0:half, 0:wide] = result[
                    :, at * wide : (at + 1) * wide
                ]
        result = dot_tn(heads[:, side * half : (side + 1) * half], attn[...]).astype(BF16)
        for at in range(dp):
            wire[0, at % 2, at // 2, side, 0:half, wide:lanes] = result[:, at * thin : (at + 1) * thin]
    for copy in stores(0):
        copy.start()
    for kind in range(3):
        for copy in stores(kind):
            copy.wait()


def weight_grads(layer, dp, saved, extras):
    sources = [saved[name] for name in GRAD_NAMES]
    steps, rows, width = sources[0].shape
    segs_all = steps // 2
    half = width // 2
    lanes = 4 * width // dp
    extra_rows = extras.shape[4]
    kind = jax.ShapeDtypeStruct((3, dp // 2, 2, half + extra_rows, lanes), BF16)
    any_spec = pl.BlockSpec(memory_space=pl.ANY)
    return pl.pallas_call(
        functools.partial(weight_grad_body, layer, segs_all, dp),
        in_specs=[any_spec] * 9,
        out_specs=[any_spec] * 2,
        out_shape=[kind, kind],
        scratch_shapes=[pltpu.VMEM((segs_all * rows, source.shape[2]), BF16) for source in sources]
        + [
            pltpu.VMEM((3, 2, dp // 2, 2, half + extra_rows, lanes), BF16),
            pltpu.SemaphoreType.DMA((8, segs_all)),
            pltpu.SemaphoreType.DMA,
            pltpu.SemaphoreType.DMA((3, 2)),
        ],
        compiler_params=pltpu.CompilerParams(vmem_limit_bytes=VMEM_BYTES),
        name="weight_grads",
    )(*sources, extras)


SAVED_NAMES = (
    "x", "mixed", "heads", "hat_one", "first", "active", "slope", "hat_two", "stats", "out",
)


def core_groups(dp):
    return [[2 * at, 2 * at + 1] for at in range(dp // 2)]


def other_core(block, dp):
    return lax.ppermute(block, "dp", [(at, at ^ 1) for at in range(dp)])


def pack_blocks(core, w_qkv, w_out, w_in, w_hid, biases, norm_gains):
    half, width = w_out.shape
    part = half // 2

    def own(block):
        size = block.shape[0] // 2
        return lax.dynamic_slice_in_dim(block, core * size, size, 0)

    tiles = []
    for block in (w_qkv, w_out, w_in):
        block = own(block)
        tiles += [block[:, at : at + width] for at in range(0, block.shape[1], width)]
    tiles.append(own(w_hid))
    vector = jnp.concatenate([biases, norm_gains])
    vector = jnp.pad(vector, (0, 16 * width - vector.shape[0])).reshape(16, width)
    return jnp.concatenate(tiles + [vector], axis=0)


def per_device(
    text_rows,
    memory_init,
    cotangent,
    w_qkv,
    w_out,
    w_in,
    w_hid,
    biases,
    norm_gains,
    boundaries,
    mem_resets,
    seg_counts,
):
    items, segs, text_len, width = text_rows.shape
    mem_rows = memory_init.shape[0]
    rows = text_len + 2 * mem_rows
    half = width // 2
    dp = lax.axis_size("dp")
    core = lax.axis_index("dp") % 2
    vector_len = biases.shape[1]

    packed = pack_blocks(core, w_qkv[0], w_out[0], w_in[0], w_hid[0], biases[0], norm_gains[0])
    gathered = lax.all_gather(packed, "section")
    small = gathered[:, -16:].reshape(4, 16 * width).astype(F32)
    pack = lax.all_gather(gathered, "dp", axis_index_groups=core_groups(dp))
    pack = pack.reshape(2, 2, 2, *pack.shape[2:])
    vectors = jnp.concatenate([small[:2, :vector_len], small[2:, :vector_len]], axis=1)[:, None]
    gains = small[:, vector_len : vector_len + width]
    gains = jnp.concatenate([gains[:2], gains[2:]], axis=1)[:, None]

    filler = jnp.full((items, segs, mem_rows), -1, jnp.int32)
    labels = jnp.concatenate([filler, jnp.cumsum(boundaries, axis=-1), filler], axis=-1)
    live = (jnp.arange(segs)[None] < seg_counts[:, None]).astype(jnp.int32).reshape(-1)
    fresh = ((jnp.arange(segs)[None] == 0) | (mem_resets > 0)).astype(jnp.int32).reshape(-1)
    text = jnp.pad(text_rows, ((0, 0), (0, 0), (mem_rows, mem_rows), (0, 0)))
    start = memory_init.astype(F32)
    init = jnp.stack(
        [jnp.pad(start, ((0, 16 - mem_rows), (0, 0))), jnp.pad(start, ((16 - mem_rows, 0), (0, 0)))]
    )

    steps = 2 * items * segs
    blank = jnp.zeros((rows, width), BF16)
    *saved, activations = forward_steps(
        0, steps, fresh, live, text, init, blank, labels, pack, vectors, gains
    )
    saved = dict(zip(SAVED_NAMES, saved))
    branch, inner, attn, mix, _, sums, input_grads, memory_grad, _ = backward_steps(
        steps - 1, steps, fresh, live, cotangent, blank, jnp.zeros((16, width), F32), labels, pack,
        gains, saved,
    )
    saved.update(branch=branch, inner=inner, attn=attn, mix=mix)

    lanes = 4 * width // dp
    memory_part = memory_grad[16 - mem_rows :].reshape(-1)
    memory_len = -(-memory_part.shape[0] // lanes) * lanes
    memory_part = jnp.pad(memory_part, (0, memory_len - memory_part.shape[0]))
    vector_part = vector_len // dp
    gain_part = width // dp
    used = memory_len + vector_part + gain_part
    extra_rows = -(-used // (3 * 16 * lanes)) * 16
    wires = []
    for layer in range(2):
        total = sums.reshape(steps // 2, 2, 12 * width)[:, layer].sum(axis=0)
        gain_two, shift_two, bias_hid, gain_one, shift_one, bias_o, bias_q, bias_v = [
            total[at * width : (at + 1) * width] for at in range(8)
        ]
        vector = jnp.concatenate(
            [bias_q, bias_v, bias_o, shift_one, total[8 * width :], bias_hid, shift_two]
        ).reshape(2, dp, vector_part)
        gain = jnp.stack([gain_one, gain_two]).reshape(2, dp, gain_part)
        extra = jnp.concatenate(
            [jnp.broadcast_to(memory_part, (2, dp, memory_len)), vector, gain], axis=-1
        )
        extra = jnp.pad(extra, ((0, 0), (0, 0), (0, 3 * extra_rows * lanes - used)))
        extra = extra.reshape(2, dp // 2, 2, 3, extra_rows, lanes).transpose(3, 2, 1, 0, 4, 5)
        wires.append(weight_grads(layer, dp, saved, extra.astype(BF16)))
    mine = jnp.stack([wires[0][0], wires[1][0]])
    theirs = other_core(jnp.stack([wires[0][1], wires[1][1]]), dp)
    both = mine.astype(F32) + theirs.astype(F32)
    both = both.transpose(3, 0, 2, 1, 4, 5).astype(BF16)
    both = both.reshape(4, dp // 2, 3, half + extra_rows, lanes)
    own = lax.psum_scatter(both, "section", scatter_dimension=0, tiled=True)[0]
    groups = [[2 * at + side for at in range(dp // 2)] for side in range(2)]
    own = lax.psum_scatter(
        own, "dp", scatter_dimension=0, axis_index_groups=groups, tiled=True
    )[0].astype(F32)

    thin = width // dp
    wide = 3 * thin
    body = own[:, :half]
    hid = body[2].reshape(half, 4, thin).transpose(1, 0, 2).reshape(4 * half, thin)
    flat = own[:, half:].reshape(-1)
    return (
        activations,
        input_grads,
        flat[: mem_rows * width].reshape(mem_rows, width),
        body[0, :, :wide][None],
        body[0, :, wide:][None],
        body[1][None],
        hid[None],
        flat[memory_len : memory_len + vector_part][None],
        flat[memory_len + vector_part : used][None],
    )


def solution(mesh):
    in_specs = (
        P(("section", "dp"), None, None, None),
        P(),
        P(("section", "dp"), None, None, None),
        P("section", None, None),
        P("section", None, None),
        P("section", None, None),
        P("section", None, None),
        P("section", None),
        P("section", None),
        P(("section", "dp"), None, None),
        P(("section", "dp"), None),
        P(("section", "dp")),
    )
    out_specs = (
        P(("section", "dp"), None, None, None),
        P(("section", "dp"), None, None, None),
        P(),
        P("section", None, "dp"),
        P("section", None, "dp"),
        P("section", None, "dp"),
        P("section", None, "dp"),
        P("section", "dp"),
        P("section", "dp"),
    )
    return jax.shard_map(
        per_device, mesh=mesh, in_specs=in_specs, out_specs=out_specs, check_vma=False
    )
```

```python
import functools

import jax
import jax.numpy as jnp
from jax import lax
from jax.experimental import pallas as pl
from jax.experimental.pallas import tpu as pltpu
from jax.sharding import PartitionSpec as P

HEADS = 12
HEAD_DIM = 64
EPS = 1e-05
MASKED = -1e30
VMEM_BYTES = 63 * 2**20
F32 = jnp.float32
BF16 = jnp.bfloat16


def dot_nn(one, two):
    return jnp.dot(one, two, preferred_element_type=F32)


def dot_nt(one, two):
    return lax.dot_general(one, two, (((1,), (1,)), ((), ())), preferred_element_type=F32)


def dot_tn(one, two):
    return lax.dot_general(one, two, (((0,), (0,)), ((), ())), preferred_element_type=F32)


def weight_tile(pack_ref, kind, tile, width):
    part = width // 4
    if kind == "hid":
        return pack_ref[tile % 2, tile // 2, 0, 8 * part : 8 * part + width, :]
    start = {"qkv": 0, "out": 3, "in": 4}[kind] * part
    at = start + tile * part
    pieces = [pack_ref[core, half, 0, pl.ds(at, part), :] for half in range(2) for core in range(2)]
    return jnp.concatenate(pieces, axis=0)


def head_lanes(shape, head):
    lanes = lax.broadcasted_iota(jnp.int32, shape, 1)
    return (lanes // HEAD_DIM) == head


def erf_parts(values):
    density = jnp.exp(-0.5 * values * values) * 0.3989422804014327
    phi = 0.5 * (1.0 + lax.erf(values * 0.7071067811865476))
    return phi, density


def forward_body(
    first_step, segs, fresh_ref, live_ref, text_ref, init_ref, prev_ref, labels_row_ref,
    labels_col_ref, pack_ref, vector_ref, gain_ref,
    x_ref, mixed_ref, heads_ref, hat_one_ref, first_ref, active_ref, slope_ref, hat_two_ref,
    stats_ref, out_ref, acts_ref,
    y_scr, bias_scr, sum_scr,
):
    step = pl.program_id(0) + first_step
    layer = step % 2
    seg = (step // 2) % segs
    item = step // (2 * segs)
    rows, width = y_scr.shape
    hidden = 4 * width

    @pl.when(pl.program_id(0) == 0)
    def _():
        y_scr[...] = prev_ref[...]

    @pl.when(layer == 0)
    def _():
        fresh = fresh_ref[item * segs + seg] > 0
        text = text_ref[0, 0]
        last = y_scr[rows - 16 : rows, :].astype(F32)
        head_rows = pltpu.roll(last, 10, 0)
        number = lax.broadcasted_iota(jnp.int32, (16, width), 0)
        top = jnp.where(fresh, init_ref[0], head_rows)
        low = jnp.where(fresh, init_ref[1], last)
        x_ref[0] = text
        x_ref[0, 0:16, :] = jnp.where(number < 10, top, text[0:16].astype(F32)).astype(BF16)
        x_ref[0, rows - 16 : rows, :] = jnp.where(
            number >= 6, low, text[rows - 16 : rows].astype(F32)
        ).astype(BF16)

    @pl.when(layer == 1)
    def _():
        x_ref[0] = y_scr[...]

    row_side = labels_row_ref[0, 0]
    col_side = labels_col_ref[0, 0]
    allowed = (row_side == col_side) | (row_side < 0) | (col_side < 0)
    bias_scr[...] = jnp.where(allowed, 0.0, MASKED)

    vector = lambda at, size: vector_ref[0, :, at : at + size]
    inputs = x_ref[0]
    for tile in range(3):
        mixed = dot_nn(inputs, weight_tile(pack_ref, "qkv", tile, width))
        if tile == 0:
            mixed = mixed + vector(0, width)
        if tile == 2:
            mixed = mixed + vector(width, width)
        mixed_ref[0, :, tile * width : (tile + 1) * width] = mixed.astype(BF16)

    group = 4 * HEAD_DIM
    stat_lane = lax.broadcasted_iota(jnp.int32, (rows, 128), 1)
    stats = jnp.zeros((rows, 128), F32)
    for number in range(width // group):
        at = number * group
        queries = mixed_ref[0, :, at : at + group] * BF16(HEAD_DIM**-0.5)
        keys = mixed_ref[0, :, width + at : width + at + group]
        values = mixed_ref[0, :, 2 * width + at : 2 * width + at + group]
        total = jnp.zeros((rows, group), F32)
        for head in range(4):
            mine = head_lanes((rows, group), head)
            scores = dot_nt(jnp.where(mine, queries, 0), keys) + bias_scr[...]
            peak = jnp.max(scores, axis=-1, keepdims=True)
            expo = jnp.exp(scores - peak)
            norm = jnp.sum(expo, axis=-1, keepdims=True)
            probs = (expo * (1.0 / norm)).astype(BF16)
            total = total + dot_nn(probs, jnp.where(mine, values, 0))
            stats = jnp.where(stat_lane == number * 4 + head, peak + jnp.log(norm), stats)
        heads_ref[0, :, at : at + group] = total.astype(BF16)

    attn = dot_nn(heads_ref[0], weight_tile(pack_ref, "out", 0, width)) + vector(2 * width, width)
    resid = inputs.astype(F32) + attn
    offset = resid - jnp.mean(resid, axis=-1, keepdims=True)
    scale = lax.rsqrt(jnp.mean(offset * offset, axis=-1, keepdims=True) + EPS)
    hat = offset * scale
    hat_one_ref[0] = hat.astype(BF16)
    stats = jnp.where(stat_lane == HEADS, scale, stats)
    first = hat * gain_ref[0, :, 0:width] + vector(3 * width, width)
    first_b = first.astype(BF16)
    first_ref[0] = first_b
    sum_scr[...] = first + vector(4 * width + hidden, width)

    def ff_tile(tile, _):
        at = pl.multiple_of(tile * width, width)
        inner = dot_nn(first_b, weight_tile(pack_ref, "in", tile, width))
        inner = inner + vector_ref[0, :, pl.ds(4 * width + at, width)]
        phi, density = erf_parts(inner)
        active = (inner * phi).astype(BF16)
        active_ref[0, :, pl.ds(at, width)] = active
        slope_ref[0, :, pl.ds(at, width)] = (phi + inner * density).astype(BF16)
        sum_scr[...] += dot_nn(active, weight_tile(pack_ref, "hid", tile, width))
        return _

    lax.fori_loop(0, 4, ff_tile, 0)
    second = sum_scr[...]
    offset = second - jnp.mean(second, axis=-1, keepdims=True)
    scale = lax.rsqrt(jnp.mean(offset * offset, axis=-1, keepdims=True) + EPS)
    hat = offset * scale
    hat_two_ref[0] = hat.astype(BF16)
    stats_ref[0] = jnp.where(stat_lane == HEADS + 1, scale, stats)
    result = (hat * gain_ref[0, :, width : 2 * width] + vector(5 * width + hidden, width)).astype(BF16)
    y_scr[...] = result
    out_ref[0] = result

    @pl.when(layer == 1)
    def _():
        live = live_ref[item * segs + seg] > 0
        acts_ref[0, 0] = jnp.where(live, result, 0)


def forward_steps(first_step, count, fresh, live, text, init, prev, labels, pack, vectors, gains):
    items, segs, rows, width = text.shape
    hidden = 4 * width
    at = lambda t: t + first_step
    by_seg = lambda t, *_: (at(t) // (2 * segs), (at(t) // 2) % segs, 0, 0)
    by_layer3 = lambda t, *_: (at(t) % 2, 0, 0)
    by_step = lambda t, *_: (t, 0, 0)
    whole = lambda shape: pl.BlockSpec(shape, lambda t, *_: (0,) * len(shape))
    saved = [
        ((rows, width), BF16),
        ((rows, 3 * width), BF16),
        ((rows, width), BF16),
        ((rows, width), BF16),
        ((rows, width), BF16),
        ((rows, hidden), BF16),
        ((rows, hidden), BF16),
        ((rows, width), BF16),
        ((rows, 128), F32),
        ((rows, width), BF16),
    ]
    labels_row = labels[:, :, :, None]
    labels_col = labels[:, :, None, :]
    grid_spec = pltpu.PrefetchScalarGridSpec(
        num_scalar_prefetch=2,
        grid=(count,),
        in_specs=[
            pl.BlockSpec((1, 1, rows, width), by_seg),
            whole(init.shape),
            whole(prev.shape),
            pl.BlockSpec((1, 1, rows, 1), by_seg),
            pl.BlockSpec((1, 1, 1, rows), by_seg),
            pl.BlockSpec((2, 2, 1) + pack.shape[3:], lambda t, *_: (0, 0, at(t) % 2, 0, 0)),
            pl.BlockSpec((1, 1, vectors.shape[2]), by_layer3),
            pl.BlockSpec((1, 1, gains.shape[2]), by_layer3),
        ],
        out_specs=[pl.BlockSpec((1,) + shape, by_step) for shape, _ in saved]
        + [pl.BlockSpec((1, 1, rows, width), by_seg)],
        scratch_shapes=[
            pltpu.VMEM((rows, width), BF16),
            pltpu.VMEM((rows, rows), F32),
            pltpu.VMEM((rows, width), F32),
        ],
    )
    return pl.pallas_call(
        functools.partial(forward_body, first_step, segs),
        grid_spec=grid_spec,
        out_shape=[jax.ShapeDtypeStruct((count,) + shape, kind) for shape, kind in saved]
        + [jax.ShapeDtypeStruct(text.shape, BF16)],
        compiler_params=pltpu.CompilerParams(vmem_limit_bytes=VMEM_BYTES),
        name="forward_steps",
    )(fresh, live, text, init, prev, labels_row, labels_col, pack, vectors, gains)


def norm_backward(grad, hat, scale, gain):
    scaled = grad * gain
    mean_one = jnp.mean(scaled, axis=-1, keepdims=True)
    mean_two = jnp.mean(scaled * hat, axis=-1, keepdims=True)
    return (scaled - mean_one - hat * mean_two) * scale


def column_sum(values):
    return jnp.sum(values, axis=0, keepdims=True)


def backward_body(
    top_step, segs, fresh_ref, live_ref, cot_ref, prev_ref, carry_in_ref, labels_row_ref,
    labels_col_ref, pack_ref, gain_ref, mixed_ref, heads_ref, hat_one_ref, slope_ref, hat_two_ref,
    stats_ref,
    branch_ref, inner_ref, attn_ref, mix_ref, grad_ref, sums_ref, inputs_ref, init_ref, carry_out_ref,
    g_scr, carry_scr, bias_scr, sum_scr, go_scr,
):
    step = top_step - pl.program_id(0)
    layer = step % 2
    seg = (step // 2) % segs
    item = step // (2 * segs)
    rows, width = g_scr.shape
    hidden = 4 * width

    @pl.when(pl.program_id(0) == 0)
    def _():
        g_scr[...] = prev_ref[...]
        carry_scr[...] = carry_in_ref[...]
        init_ref[...] = jnp.zeros_like(init_ref)

    @pl.when(layer == 1)
    def _():
        live = live_ref[item * segs + seg] > 0
        cot = jnp.where(live, cot_ref[0, 0], 0)
        g_scr[...] = cot
        carried = jnp.where(seg == segs - 1, 0.0, carry_scr[...])
        g_scr[rows - 16 : rows, :] = (cot[rows - 16 : rows].astype(F32) + carried).astype(BF16)

    row_side = labels_row_ref[0, 0]
    col_side = labels_col_ref[0, 0]
    allowed = (row_side == col_side) | (row_side < 0) | (col_side < 0)
    bias_scr[...] = jnp.where(allowed, 0.0, MASKED)

    stats = stats_ref[0]
    scale_one = stats[:, HEADS : HEADS + 1]
    scale_two = stats[:, HEADS + 1 : HEADS + 2]
    grad = g_scr[...].astype(F32)
    hat = hat_two_ref[0].astype(F32)
    gain = gain_ref[0]
    sums_ref[0, :, 0:width] = column_sum(grad * hat)
    sums_ref[0, :, width : 2 * width] = column_sum(grad)
    grad_second = norm_backward(grad, hat, scale_two, gain[:, width : 2 * width])
    branch = grad_second.astype(BF16)
    branch_ref[0] = branch
    sums_ref[0, :, 2 * width : 3 * width] = column_sum(branch.astype(F32))
    sum_scr[...] = grad_second

    def ff_tile(tile, _):
        at = pl.multiple_of(tile * width, width)
        active = dot_nt(branch, weight_tile(pack_ref, "hid", tile, width))
        inner = (active * slope_ref[0, :, pl.ds(at, width)].astype(F32)).astype(BF16)
        inner_ref[0, :, pl.ds(at, width)] = inner
        sums_ref[0, :, pl.ds(8 * width + at, width)] = column_sum(inner.astype(F32))
        sum_scr[...] += dot_nt(inner, weight_tile(pack_ref, "in", tile, width))
        return _

    lax.fori_loop(0, 4, ff_tile, 0)
    grad = sum_scr[...]
    hat = hat_one_ref[0].astype(F32)
    sums_ref[0, :, 3 * width : 4 * width] = column_sum(grad * hat)
    sums_ref[0, :, 4 * width : 5 * width] = column_sum(grad)
    resid = norm_backward(grad, hat, scale_one, gain[:, 0:width])
    sum_scr[...] = resid
    attn = resid.astype(BF16)
    attn_ref[0] = attn
    sums_ref[0, :, 5 * width : 6 * width] = column_sum(attn.astype(F32))
    go = dot_nt(attn, weight_tile(pack_ref, "out", 0, width)).astype(BF16)
    go_scr[...] = go
    product = go.astype(F32) * heads_ref[0].astype(F32)
    high = product.astype(BF16)
    low = (product - high.astype(F32)).astype(BF16)
    picks = (
        lax.broadcasted_iota(jnp.int32, (16, width), 1) // HEAD_DIM
        == lax.broadcasted_iota(jnp.int32, (16, width), 0)
    ).astype(BF16)
    centres = dot_nt(picks, high) + dot_nt(picks, low)
    logs = jnp.transpose(stats)

    group = 4 * HEAD_DIM
    for number in range(width // group):
        at = number * group
        queries = mixed_ref[0, :, at : at + group] * BF16(HEAD_DIM**-0.5)
        keys = mixed_ref[0, :, width + at : width + at + group]
        values = mixed_ref[0, :, 2 * width + at : 2 * width + at + group]
        outs = go_scr[:, at : at + group]
        grad_q = jnp.zeros((rows, group), F32)
        grad_k = jnp.zeros((rows, group), F32)
        grad_v = jnp.zeros((rows, group), F32)
        for head in range(4):
            mine = head_lanes((rows, group), head)
            row = number * 4 + head
            keys_h = jnp.where(mine, keys, 0)
            scores = dot_nt(keys_h, queries) + bias_scr[...]
            probs = jnp.exp(scores - logs[row : row + 1, :])
            grad_p = dot_nt(jnp.where(mine, values, 0), outs)
            grad_s = (probs * (grad_p - centres[row : row + 1, :])).astype(BF16)
            grad_v = grad_v + dot_nn(probs.astype(BF16), jnp.where(mine, outs, 0))
            grad_k = grad_k + dot_nn(grad_s, jnp.where(mine, queries, 0))
            grad_q = grad_q + dot_tn(grad_s, keys_h)
        mix_ref[0, :, at : at + group] = (grad_q * HEAD_DIM**-0.5).astype(BF16)
        mix_ref[0, :, width + at : width + at + group] = grad_k.astype(BF16)
        mix_ref[0, :, 2 * width + at : 2 * width + at + group] = grad_v.astype(BF16)

    sums_ref[0, :, 6 * width : 7 * width] = column_sum(mix_ref[0, :, 0:width].astype(F32))
    sums_ref[0, :, 7 * width : 8 * width] = column_sum(mix_ref[0, :, 2 * width : 3 * width].astype(F32))
    total = sum_scr[...]
    for tile in range(3):
        total = total + dot_nt(
            mix_ref[0, :, tile * width : (tile + 1) * width], weight_tile(pack_ref, "qkv", tile, width)
        )
    result = total.astype(BF16)
    g_scr[...] = result
    grad_ref[...] = result

    @pl.when(layer == 0)
    def _():
        inputs_ref[0, 0] = result
        fresh = fresh_ref[item * segs + seg] > 0
        number = lax.broadcasted_iota(jnp.int32, (16, width), 0)
        folded = result[rows - 16 : rows].astype(F32) + pltpu.roll(result[0:16].astype(F32), 6, 0)
        folded = jnp.where(number >= 6, folded, 0.0).astype(BF16).astype(F32)
        init_ref[...] += jnp.where(fresh, folded, 0.0)
        carry_scr[...] = jnp.where(fresh, 0.0, folded)

    carry_out_ref[...] = carry_scr[...]


def backward_steps(
    top_step, count, fresh, live, cot, prev, carry, labels, pack, gains, saved, inputs_so_far=None
):
    items, segs, rows, width = cot.shape
    hidden = 4 * width
    at = lambda t: top_step - t
    by_seg = lambda t, *_: (at(t) // (2 * segs), (at(t) // 2) % segs, 0, 0)
    by_layer3 = lambda t, *_: (at(t) % 2, 0, 0)
    by_step = lambda t, *_: (count - 1 - t, 0, 0)
    whole = lambda shape: pl.BlockSpec(shape, lambda t, *_: (0,) * len(shape))
    names = ("mixed", "heads", "hat_one", "slope", "hat_two", "stats")
    outs = [
        ((rows, width), BF16),
        ((rows, hidden), BF16),
        ((rows, width), BF16),
        ((rows, 3 * width), BF16),
    ]
    labels_row = labels[:, :, :, None]
    labels_col = labels[:, :, None, :]
    operands = [fresh, live, cot, prev, carry, labels_row, labels_col, pack, gains]
    operands += [saved[name] for name in names]
    in_specs = [
        pl.BlockSpec((1, 1, rows, width), by_seg),
        whole(prev.shape),
        whole(carry.shape),
        pl.BlockSpec((1, 1, rows, 1), by_seg),
        pl.BlockSpec((1, 1, 1, rows), by_seg),
        pl.BlockSpec((2, 2, 1) + pack.shape[3:], lambda t, *_: (0, 0, at(t) % 2, 0, 0)),
        pl.BlockSpec((1, 1, gains.shape[2]), by_layer3),
    ] + [pl.BlockSpec((1,) + saved[name].shape[1:], by_step) for name in names]
    body = functools.partial(backward_body, top_step, segs)
    aliases = {}
    if inputs_so_far is not None:
        operands.append(inputs_so_far)
        in_specs.append(pl.BlockSpec(memory_space=pl.ANY))
        aliases = {len(operands) - 1: len(outs) + 2}
        inner_body = body

        def body(*refs):
            cut = 2 + len(in_specs)
            return inner_body(*refs[: cut - 1], *refs[cut:])

    grid_spec = pltpu.PrefetchScalarGridSpec(
        num_scalar_prefetch=2,
        grid=(count,),
        in_specs=in_specs,
        out_specs=[pl.BlockSpec((1,) + shape, by_step) for shape, _ in outs]
        + [
            whole((rows, width)),
            pl.BlockSpec((1, 1, 12 * width), by_step),
            pl.BlockSpec((1, 1, rows, width), by_seg),
            whole((16, width)),
            whole((16, width)),
        ],
        scratch_shapes=[
            pltpu.VMEM((rows, width), BF16),
            pltpu.VMEM((16, width), F32),
            pltpu.VMEM((rows, rows), F32),
            pltpu.VMEM((rows, width), F32),
            pltpu.VMEM((rows, width), BF16),
        ],
    )
    return pl.pallas_call(
        body,
        grid_spec=grid_spec,
        out_shape=[jax.ShapeDtypeStruct((count,) + shape, kind) for shape, kind in outs]
        + [
            jax.ShapeDtypeStruct((rows, width), BF16),
            jax.ShapeDtypeStruct((count, 1, 12 * width), F32),
            jax.ShapeDtypeStruct(cot.shape, BF16),
            jax.ShapeDtypeStruct((16, width), F32),
            jax.ShapeDtypeStruct((16, width), F32),
        ],
        input_output_aliases=aliases,
        compiler_params=pltpu.CompilerParams(vmem_limit_bytes=VMEM_BYTES),
        name="backward_steps",
    )(*operands)


GRAD_NAMES = ("first", "inner", "active", "branch", "x", "mix", "heads", "attn")


def weight_grad_body(
    layer, segs_all, dp, *refs,
):
    sources = refs[:8]
    extra_ref, mine_ref, theirs_ref = refs[8:11]
    held = refs[11:19]
    wire, in_sems, extra_sem, out_sems = refs[19:23]
    core = lax.axis_index("dp") % 2
    rows = sources[0].shape[1]
    width = sources[0].shape[2]
    half = width // 2
    lanes = wire.shape[-1]
    thin = width // dp
    wide = 3 * thin

    def loads(number):
        return [
            pltpu.make_async_copy(
                sources[number].at[2 * at + layer],
                held[number].at[pl.ds(at * rows, rows)],
                in_sems.at[number, at],
            )
            for at in range(segs_all)
        ]

    for number in range(8):
        for copy in loads(number):
            copy.start()
    extra = pltpu.make_async_copy(extra_ref, wire.at[:, :, :, :, pl.ds(half, extra_ref.shape[4])], extra_sem)
    extra.start()

    def ready(*numbers):
        for number in numbers:
            for copy in loads(number):
                copy.wait()

    def stores(kind):
        return [
            pltpu.make_async_copy(wire.at[kind, core], mine_ref.at[kind], out_sems.at[kind, 0]),
            pltpu.make_async_copy(wire.at[kind, 1 - core], theirs_ref.at[kind], out_sems.at[kind, 1]),
        ]

    first, inner, active, branch, inputs, mix, heads, attn = held
    extra.wait()

    ready(0, 1)
    per_tile = width // lanes

    def in_tile(tile, _):
        right = inner[:, pl.ds(pl.multiple_of(tile * width, width), width)]
        for side in range(2):
            result = dot_tn(first[:, side * half : (side + 1) * half], right).astype(BF16)
            for at in range(per_tile):
                wire[1, at % 2, tile * (per_tile // 2) + at // 2, side, 0:half, :] = result[
                    :, at * lanes : (at + 1) * lanes
                ]
        return _

    lax.fori_loop(0, 4, in_tile, 0)
    for copy in stores(1):
        copy.start()

    ready(2, 3)
    def hid_tile(side, _):
        for part in range(4):
            left = active[:, pl.ds(pl.multiple_of(side * 4 * half + part * half, half), half)]
            result = dot_tn(left, branch[...]).astype(BF16)
            for at in range(dp):
                wire[2, at % 2, at // 2, side, 0:half, part * thin : (part + 1) * thin] = result[
                    :, at * thin : (at + 1) * thin
                ]
        return _
    lax.fori_loop(0, 2, hid_tile, 0)
    for copy in stores(2):
        copy.start()

    ready(4, 5, 6, 7)
    for side in range(2):
        left = inputs[:, side * half : (side + 1) * half]
        for tile in range(2):
            result = dot_tn(left, mix[:, tile * 3 * half : (tile + 1) * 3 * half]).astype(BF16)
            for at in range(dp // 2):
                place = tile * (dp // 2) + at
                wire[0, place % 2, place // 2, side, 0:half, 0:wide] = result[
                    :, at * wide : (at + 1) * wide
                ]
        result = dot_tn(heads[:, side * half : (side + 1) * half], attn[...]).astype(BF16)
        for at in range(dp):
            wire[0, at % 2, at // 2, side, 0:half, wide:lanes] = result[:, at * thin : (at + 1) * thin]
    for copy in stores(0):
        copy.start()
    for kind in range(3):
        for copy in stores(kind):
            copy.wait()


def weight_grads(layer, dp, saved, extras):
    sources = [saved[name] for name in GRAD_NAMES]
    steps, rows, width = sources[0].shape
    segs_all = steps // 2
    half = width // 2
    lanes = 4 * width // dp
    extra_rows = extras.shape[4]
    kind = jax.ShapeDtypeStruct((3, dp // 2, 2, half + extra_rows, lanes), BF16)
    any_spec = pl.BlockSpec(memory_space=pl.ANY)
    return pl.pallas_call(
        functools.partial(weight_grad_body, layer, segs_all, dp),
        in_specs=[any_spec] * 9,
        out_specs=[any_spec] * 2,
        out_shape=[kind, kind],
        scratch_shapes=[pltpu.VMEM((segs_all * rows, source.shape[2]), BF16) for source in sources]
        + [
            pltpu.VMEM((3, 2, dp // 2, 2, half + extra_rows, lanes), BF16),
            pltpu.SemaphoreType.DMA((8, segs_all)),
            pltpu.SemaphoreType.DMA,
            pltpu.SemaphoreType.DMA((3, 2)),
        ],
        compiler_params=pltpu.CompilerParams(vmem_limit_bytes=VMEM_BYTES),
        name="weight_grads",
    )(*sources, extras)


MESH = pl.DeviceIdType.MESH


def add_into(ref, other):
    ref[...] = (ref[...].astype(F32) + other[...].astype(F32)).astype(BF16)


def grad_reduce_body(dp, segs_all, *refs):
    sources = refs[:8]
    extra_ref = refs[8]
    qkv_out, out_out, in_out, hid_out, extra_out = refs[9:14]
    held = refs[14:22]
    mine, theirs, landed, xp, xq, yq, yp, from_low, from_high = refs[22:31]
    in_sems, extra_sems, core_sems, free_sem, xp_sems, xq_sems, yq_sems, yp_sems, up_sems, down_sems = refs[31:41]
    section, place = lax.axis_index("section"), lax.axis_index("dp")
    x, y = section % 2, section // 2
    core, z = place % 2, place // 2
    depth = dp // 2
    cut = depth // 2
    rows, width = sources[0].shape[1:]
    half = width // 2
    lanes = mine.shape[-1]
    thin = width // dp
    wide = 3 * thin
    x_dev = (y * 2 + 1 - x, place)
    y_dev = ((1 - y) * 2 + x, place)
    core_dev = (section, z * 2 + 1 - core)
    up_dev = (section, (z + 1) % depth * 2 + core)
    down_dev = (section, (z + depth - 1) % depth * 2 + core)
    kinds = (1, 2, 0)
    used = {1: (0, 1), 2: (2, 3), 0: (4, 5, 6, 7)}
    first, inner, active, branch, inputs, mix, heads, attn = held

    def loads(side, kind):
        layer = (1 - x) if side == 0 else x
        return [
            pltpu.make_async_copy(
                sources[number].at[2 * at + layer],
                held[number].at[pl.ds(at * rows, rows)],
                in_sems.at[number, at],
            )
            for number in used[kind]
            for at in range(segs_all)
        ]

    for kind in kinds:
        for copy in loads(0, kind):
            copy.start()

    barrier = pltpu.get_barrier_semaphore()
    for device in (x_dev, y_dev, core_dev):
        pl.semaphore_signal(barrier, inc=1, device_id=device, device_id_type=MESH)

    @pl.when(z < depth - 1)
    def _():
        pl.semaphore_signal(barrier, inc=1, device_id=up_dev, device_id_type=MESH)

    @pl.when(z > 0)
    def _():
        pl.semaphore_signal(barrier, inc=1, device_id=down_dev, device_id_type=MESH)

    pl.semaphore_wait(barrier, 3 + jnp.where(z > 0, 1, 0) + jnp.where(z < depth - 1, 1, 0))

    def remote(source, target, sems, index, device):
        return pltpu.make_async_remote_copy(
            src_ref=source, dst_ref=target, send_sem=sems.at[(0, *index)], recv_sem=sems.at[(1, *index)],
            device_id=device, device_id_type=MESH,
        )

    def core_copy(unit):
        return remote(theirs.at[unit % 2], landed.at[unit % 2], core_sems, (unit,), core_dev)

    def xp_copy(kind):
        return remote(mine.at[0, kind, pl.ds(0, cut)], xp.at[kind], xp_sems, (kind,), x_dev)

    def yq_copy(side, kind):
        return remote(
            mine.at[side, kind, pl.ds(cut, depth - cut), 1 - y], yq.at[side, kind], yq_sems,
            (side, kind), y_dev,
        )

    def xq_copy(kind):
        return remote(mine.at[0, kind, pl.ds(cut, depth - cut), y], xq.at[kind], xq_sems, (kind,), x_dev)

    def yp_copy(kind):
        return remote(mine.at[1, kind, pl.ds(0, cut), 1 - y], yp.at[kind], yp_sems, (kind,), y_dev)

    def up_copy(kind, at):
        return remote(mine.at[1, kind, at, y], from_low.at[kind, at], up_sems, (kind, at), up_dev)

    def down_copy(kind, at):
        return remote(mine.at[1, kind, at, y], from_high.at[kind, at], down_sems, (kind, at), down_dev)

    def multiply(side, kind, unit):
        slot = unit % 2

        def put(at, block, piece, start, stop):
            if isinstance(at, int):
                chunk_core, chunk_z = at % 2, at // 2
            else:
                chunk_core, chunk_z = at

            @pl.when(core == chunk_core)
            def _():
                mine[side, kind, chunk_z, block, 0:half, start:stop] = piece

            @pl.when(core != chunk_core)
            def _():
                theirs[slot, chunk_z, block, 0:half, start:stop] = piece

        if kind == 1:
            per_tile = width // lanes

            def in_tile(tile, _):
                right = inner[:, pl.ds(pl.multiple_of(tile * width, width), width)]
                for block in range(2):
                    result = dot_tn(first[:, block * half : (block + 1) * half], right).astype(BF16)
                    for at in range(per_tile):
                        put(
                            (at % 2, tile * (per_tile // 2) + at // 2), block,
                            result[:, at * lanes : (at + 1) * lanes], 0, lanes,
                        )
                return _

            lax.fori_loop(0, 4, in_tile, 0)
        elif kind == 2:

            def hid_tile(block, _):
                for part in range(4):
                    left = active[:, pl.ds(pl.multiple_of((block * 4 + part) * half, half), half)]
                    result = dot_tn(left, branch[...]).astype(BF16)
                    for at in range(dp):
                        put(
                            at, block, result[:, at * thin : (at + 1) * thin], part * thin,
                            (part + 1) * thin,
                        )
                return _

            lax.fori_loop(0, 2, hid_tile, 0)
        else:
            for block in range(2):
                left = inputs[:, block * half : (block + 1) * half]
                for tile in range(2):
                    result = dot_tn(left, mix[:, tile * 3 * half : (tile + 1) * 3 * half]).astype(BF16)
                    for at in range(depth):
                        put(
                            tile * depth + at, block, result[:, at * wide : (at + 1) * wide], 0, wide
                        )
                result = dot_tn(heads[:, block * half : (block + 1) * half], attn[...]).astype(BF16)
                for at in range(dp):
                    put(at, block, result[:, at * thin : (at + 1) * thin], wide, lanes)

    def after_core(side, kind, unit):
        core_copy(unit).wait_recv()

        def add(at, _):
            add_into(mine.at[side, kind, at], landed.at[unit % 2, at])
            return _

        lax.fori_loop(0, depth, add, 0)
        if unit + 2 < 6:
            pl.semaphore_signal(free_sem, inc=1, device_id=core_dev, device_id_type=MESH)
        if side == 0:
            xp_copy(kind).start()
        yq_copy(side, kind).start()

    def forward_q(kind):
        yq_copy(0, kind).wait_recv()

        def add(at, _):
            add_into(mine.at[0, kind, cut + at, y], yq.at[0, kind, at])
            return _

        lax.fori_loop(0, depth - cut, add, 0)
        xq_copy(kind).start()

    def forward_p(kind):
        xp_copy(kind).wait_recv()

        def add(at, _):
            add_into(mine.at[1, kind, at], xp.at[kind, at])
            return _

        lax.fori_loop(0, cut, add, 0)
        yp_copy(kind).start()

    def finish_plane(kind):
        yq_copy(1, kind).wait_recv()
        xq_copy(kind).wait_recv()

        def add_two(at, _):
            ref = mine.at[1, kind, cut + at, y]
            total = ref[...].astype(F32) + yq[1, kind, at].astype(F32) + xq[kind, at].astype(F32)
            ref[...] = total.astype(BF16)
            return _

        lax.fori_loop(0, depth - cut, add_two, 0)
        yp_copy(kind).wait_recv()

        def add(at, _):
            add_into(mine.at[1, kind, at, y], yp.at[kind, at])
            return _

        lax.fori_loop(0, cut, add, 0)

    def line(kind):
        def hop(count, _):
            high, low = depth - 1 - count, count

            @pl.when(z < high)
            def _():
                @pl.when(z > 0)
                def _():
                    up_copy(kind, high).wait_recv()
                    add_into(mine.at[1, kind, high, y], from_low.at[kind, high])

                up_copy(kind, high).start()

            @pl.when(z > low)
            def _():
                @pl.when(z < depth - 1)
                def _():
                    down_copy(kind, low).wait_recv()
                    add_into(mine.at[1, kind, low, y], from_high.at[kind, low])

                down_copy(kind, low).start()

            return 0

        lax.fori_loop(0, depth - 1, hop, 0)

    def finish(kind):
        @pl.when(z > 0)
        def _():
            up_copy(kind, z).wait_recv()
            add_into(mine.at[1, kind, z, y], from_low.at[kind, z])

        @pl.when(z < depth - 1)
        def _():
            down_copy(kind, z).wait_recv()
            add_into(mine.at[1, kind, z, y], from_high.at[kind, z])

        total = mine[1, kind, z, y].astype(F32)
        extra_out[kind] = total[half:, :]
        if kind == 0:
            qkv_out[0] = total[:half, 0:wide]
            out_out[0] = total[:half, wide:lanes]
        elif kind == 1:
            in_out[0] = total[:half]
        else:
            for part in range(4):
                hid_out[0, part * half : (part + 1) * half, :] = total[:half, part * thin : (part + 1) * thin]

    units = [(side, kind) for side in range(2) for kind in kinds]
    for unit, (side, kind) in enumerate(units):
        layer = (1 - x) if side == 0 else x
        for copy in loads(side, kind):
            copy.wait()
        if unit >= 2:
            core_copy(unit - 2).wait_send()
        extra_rows = extra_ref.shape[5]
        extras = [
            pltpu.make_async_copy(
                extra_ref.at[layer, kind, core], mine.at[side, kind, :, :, pl.ds(half, extra_rows)],
                extra_sems.at[0],
            ),
            pltpu.make_async_copy(
                extra_ref.at[layer, kind, 1 - core], theirs.at[unit % 2, :, :, pl.ds(half, extra_rows)],
                extra_sems.at[1],
            ),
        ]
        for copy in extras:
            copy.start()
        multiply(side, kind, unit)
        for copy in extras:
            copy.wait()
        if unit >= 2:
            pl.semaphore_wait(free_sem, 1)
        core_copy(unit).start()
        if side == 0:
            for copy in loads(1, kind):
                copy.start()
        if unit >= 1:
            after_core(*units[unit - 1], unit - 1)
        if unit == 4:
            forward_q(kinds[0])
        if unit == 5:
            forward_q(kinds[1])
    after_core(*units[5], 5)
    forward_p(kinds[0])
    forward_q(kinds[2])
    forward_p(kinds[1])
    forward_p(kinds[2])
    finish_plane(kinds[0])
    line(kinds[0])
    finish_plane(kinds[1])
    line(kinds[1])
    finish(kinds[0])
    finish_plane(kinds[2])
    line(kinds[2])
    finish(kinds[1])
    finish(kinds[2])
    core_copy(4).wait_send()
    core_copy(5).wait_send()
    for kind in kinds:
        xp_copy(kind).wait_send()
        xq_copy(kind).wait_send()
        yp_copy(kind).wait_send()
        for side in range(2):
            yq_copy(side, kind).wait_send()

        def sent(at, _):
            @pl.when(at > z)
            def _():
                up_copy(kind, at).wait_send()

            @pl.when(at < z)
            def _():
                down_copy(kind, at).wait_send()

            return 0

        lax.fori_loop(0, depth, sent, 0)


def grad_reduce_shapes(dp, steps, rows, width, extra_rows):
    half = width // 2
    lanes = 4 * width // dp
    depth = dp // 2
    cut = depth // 2
    tall = half + extra_rows
    held = [width, 4 * width, 4 * width, width, width, 3 * width, width, width]
    return [pltpu.VMEM((steps // 2 * rows, columns), BF16) for columns in held] + [
        pltpu.VMEM(shape + (tall, lanes), BF16)
        for shape in (
            (2, 3, depth, 2), (2, depth, 2), (2, depth, 2), (3, cut, 2), (3, depth - cut),
            (2, 3, depth - cut), (3, cut), (3, depth), (3, depth),
        )
    ]


def padded_bytes(shapes):
    total = 0
    for shape in shapes:
        *lead, tall, lanes = shape.shape
        size = 2 * tall * -(-lanes // 128) * 128
        for count in lead:
            size *= count
        total += size
    return total


def grad_reduce(dp, saved, extras):
    sources = [saved[name] for name in GRAD_NAMES]
    steps, rows, width = sources[0].shape
    segs_all = steps // 2
    half = width // 2
    lanes = 4 * width // dp
    thin = width // dp
    extra_rows = extras.shape[5]
    depth = dp // 2
    any_spec = pl.BlockSpec(memory_space=pl.ANY)
    dma = pltpu.SemaphoreType.DMA
    return pl.pallas_call(
        functools.partial(grad_reduce_body, dp, segs_all),
        in_specs=[any_spec] * 9,
        out_specs=[pl.BlockSpec(memory_space=pltpu.VMEM)] * 5,
        out_shape=[
            jax.ShapeDtypeStruct(shape, F32)
            for shape in (
                (1, half, 3 * thin), (1, half, thin), (1, half, lanes), (1, 4 * half, thin),
                (3, extra_rows, lanes),
            )
        ],
        scratch_shapes=grad_reduce_shapes(dp, steps, rows, width, extra_rows)
        + [
            dma((8, segs_all)), dma((2,)), dma((2, 6)), pltpu.SemaphoreType.REGULAR, dma((2, 3)),
            dma((2, 3)), dma((2, 2, 3)), dma((2, 3)), dma((2, 3, depth)), dma((2, 3, depth)),
        ],
        compiler_params=pltpu.CompilerParams(
            vmem_limit_bytes=VMEM_BYTES, collective_id=0, has_side_effects=True
        ),
        name="grad_reduce",
    )(*sources, extras)


SAVED_NAMES = (
    "x", "mixed", "heads", "hat_one", "first", "active", "slope", "hat_two", "stats", "out",
)


def core_groups(dp):
    return [[2 * at, 2 * at + 1] for at in range(dp // 2)]


def other_core(block, dp):
    return lax.ppermute(block, "dp", [(at, at ^ 1) for at in range(dp)])


def pack_blocks(core, w_qkv, w_out, w_in, w_hid, biases, norm_gains):
    half, width = w_out.shape
    part = half // 2

    def own(block):
        size = block.shape[0] // 2
        return lax.dynamic_slice_in_dim(block, core * size, size, 0)

    tiles = []
    for block in (w_qkv, w_out, w_in):
        block = own(block)
        tiles += [block[:, at : at + width] for at in range(0, block.shape[1], width)]
    tiles.append(own(w_hid))
    vector = jnp.concatenate([biases, norm_gains])
    vector = jnp.pad(vector, (0, 16 * width - vector.shape[0])).reshape(16, width)
    return jnp.concatenate(tiles + [vector], axis=0)


def per_device(
    text_rows,
    memory_init,
    cotangent,
    w_qkv,
    w_out,
    w_in,
    w_hid,
    biases,
    norm_gains,
    boundaries,
    mem_resets,
    seg_counts,
):
    items, segs, text_len, width = text_rows.shape
    mem_rows = memory_init.shape[0]
    rows = text_len + 2 * mem_rows
    half = width // 2
    dp = lax.axis_size("dp")
    core = lax.axis_index("dp") % 2
    vector_len = biases.shape[1]

    packed = pack_blocks(core, w_qkv[0], w_out[0], w_in[0], w_hid[0], biases[0], norm_gains[0])
    gathered = lax.all_gather(packed, "section")
    small = gathered[:, -16:].reshape(4, 16 * width).astype(F32)
    pack = lax.all_gather(gathered, "dp", axis_index_groups=core_groups(dp))
    pack = pack.reshape(2, 2, 2, *pack.shape[2:])
    vectors = jnp.concatenate([small[:2, :vector_len], small[2:, :vector_len]], axis=1)[:, None]
    gains = small[:, vector_len : vector_len + width]
    gains = jnp.concatenate([gains[:2], gains[2:]], axis=1)[:, None]

    filler = jnp.full((items, segs, mem_rows), -1, jnp.int32)
    labels = jnp.concatenate([filler, jnp.cumsum(boundaries, axis=-1), filler], axis=-1)
    live = (jnp.arange(segs)[None] < seg_counts[:, None]).astype(jnp.int32).reshape(-1)
    fresh = ((jnp.arange(segs)[None] == 0) | (mem_resets > 0)).astype(jnp.int32).reshape(-1)
    text = jnp.pad(text_rows, ((0, 0), (0, 0), (mem_rows, mem_rows), (0, 0)))
    start = memory_init.astype(F32)
    init = jnp.stack(
        [jnp.pad(start, ((0, 16 - mem_rows), (0, 0))), jnp.pad(start, ((16 - mem_rows, 0), (0, 0)))]
    )

    steps = 2 * items * segs
    blank = jnp.zeros((rows, width), BF16)
    *saved, activations = forward_steps(
        0, steps, fresh, live, text, init, blank, labels, pack, vectors, gains
    )
    saved = dict(zip(SAVED_NAMES, saved))
    branch, inner, attn, mix, _, sums, input_grads, memory_grad, _ = backward_steps(
        steps - 1, steps, fresh, live, cotangent, blank, jnp.zeros((16, width), F32), labels, pack,
        gains, saved,
    )
    saved.update(branch=branch, inner=inner, attn=attn, mix=mix)

    lanes = 4 * width // dp
    memory_part = memory_grad[16 - mem_rows :].reshape(-1)
    memory_len = -(-memory_part.shape[0] // lanes) * lanes
    memory_part = jnp.pad(memory_part, (0, memory_len - memory_part.shape[0]))
    vector_part = vector_len // dp
    gain_part = width // dp
    used = memory_len + vector_part + gain_part
    extra_rows = -(-used // (3 * 16 * lanes)) * 16
    extras = []
    for layer in range(2):
        total = sums.reshape(steps // 2, 2, 12 * width)[:, layer].sum(axis=0)
        gain_two, shift_two, bias_hid, gain_one, shift_one, bias_o, bias_q, bias_v = [
            total[at * width : (at + 1) * width] for at in range(8)
        ]
        vector = jnp.concatenate(
            [bias_q, bias_v, bias_o, shift_one, total[8 * width :], bias_hid, shift_two]
        ).reshape(2, dp, vector_part)
        gain = jnp.stack([gain_one, gain_two]).reshape(2, dp, gain_part)
        extra = jnp.concatenate(
            [jnp.broadcast_to(memory_part, (2, dp, memory_len)), vector, gain], axis=-1
        )
        extra = jnp.pad(extra, ((0, 0), (0, 0), (0, 3 * extra_rows * lanes - used)))
        extra = extra.reshape(2, dp // 2, 2, 3, extra_rows, lanes).transpose(3, 2, 1, 0, 4, 5)
        extras.append(extra.astype(BF16))
    extras = jnp.stack(extras)
    reduce = grad_reduce
    if padded_bytes(grad_reduce_shapes(dp, steps, rows, width, extra_rows)) > 60 * 2**20:
        reduce = grad_reduce_apart
    *grads, flat = reduce(dp, saved, extras)
    flat = flat.reshape(-1)
    return (
        activations,
        input_grads,
        flat[: mem_rows * width].reshape(mem_rows, width),
        *grads,
        flat[memory_len : memory_len + vector_part][None],
        flat[memory_len + vector_part : used][None],
    )


def grad_reduce_apart(dp, saved, extras):
    wires = [weight_grads(layer, dp, saved, extras[layer]) for layer in range(2)]
    mine = jnp.stack([wires[0][0], wires[1][0]])
    theirs = other_core(jnp.stack([wires[0][1], wires[1][1]]), dp)
    both = mine.astype(F32) + theirs.astype(F32)
    both = both.transpose(3, 0, 2, 1, 4, 5).astype(BF16)
    tall, lanes = both.shape[-2:]
    both = both.reshape(4, dp // 2, 3, tall, lanes)
    own = lax.psum_scatter(both, "section", scatter_dimension=0, tiled=True)[0]
    groups = [[2 * at + side for at in range(dp // 2)] for side in range(2)]
    own = lax.psum_scatter(
        own, "dp", scatter_dimension=0, axis_index_groups=groups, tiled=True
    )[0].astype(F32)
    half = tall - extras.shape[5]
    thin = lanes // 4
    body = own[:, :half]
    hid = body[2].reshape(half, 4, thin).transpose(1, 0, 2).reshape(4 * half, thin)
    return (
        body[0, :, : 3 * thin][None],
        body[0, :, 3 * thin :][None],
        body[1][None],
        hid[None],
        own[:, half:],
    )


def solution(mesh):
    in_specs = (
        P(("section", "dp"), None, None, None),
        P(),
        P(("section", "dp"), None, None, None),
        P("section", None, None),
        P("section", None, None),
        P("section", None, None),
        P("section", None, None),
        P("section", None),
        P("section", None),
        P(("section", "dp"), None, None),
        P(("section", "dp"), None),
        P(("section", "dp")),
    )
    out_specs = (
        P(("section", "dp"), None, None, None),
        P(("section", "dp"), None, None, None),
        P(),
        P("section", None, "dp"),
        P("section", None, "dp"),
        P("section", None, "dp"),
        P("section", None, "dp"),
        P("section", "dp"),
        P("section", "dp"),
    )
    return jax.shard_map(
        per_device, mesh=mesh, in_specs=in_specs, out_specs=out_specs, check_vma=False
    )
```

```python
import functools

import jax
import jax.numpy as jnp
from jax import lax
from jax.experimental import pallas as pl
from jax.experimental.pallas import tpu as pltpu
from jax.sharding import PartitionSpec as P

HEADS = 12
HEAD_DIM = 64
EPS = 1e-05
MASKED = -1e30
VMEM_BYTES = 63 * 2**20
F32 = jnp.float32
BF16 = jnp.bfloat16
MESH = pl.DeviceIdType.MESH


def dot_nn(one, two):
    return jnp.dot(one, two, preferred_element_type=F32)


def dot_nt(one, two):
    return lax.dot_general(one, two, (((1,), (1,)), ((), ())), preferred_element_type=F32)


def dot_tn(one, two):
    return lax.dot_general(one, two, (((0,), (0,)), ((), ())), preferred_element_type=F32)


def weight_tile(refs, kind, tile, layer):
    qkv_ref, out_ref, in_ref, hid_ref = refs
    width = out_ref.shape[-1]
    if kind == "hid":
        quarters = hid_ref.shape[0] // 2
        pieces = [
            hid_ref[(tile % 2) * quarters + at, core, tile // 2, layer]
            for at in range(quarters)
            for core in range(2)
        ]
    else:
        ref = {"qkv": qkv_ref, "out": out_ref, "in": in_ref}[kind]
        at = tile * width if isinstance(tile, int) else pl.multiple_of(tile * width, width)
        pieces = [ref[core, half, layer, :, pl.ds(at, width)] for half in range(2) for core in range(2)]
    return jnp.concatenate(pieces, axis=0)


def weight_specs(shapes, layer_of):
    specs = []
    for shape in shapes:
        lead = len(shape) - 3
        block = shape[:lead] + (1,) + shape[lead + 1 :]
        specs.append(
            pl.BlockSpec(block, lambda t, *_, lead=lead: (0,) * lead + (layer_of(t), 0, 0))
        )
    return specs


def head_lanes(shape, head):
    lanes = lax.broadcasted_iota(jnp.int32, shape, 1)
    return (lanes // HEAD_DIM) == head


def erf_parts(values):
    density = jnp.exp(-0.5 * values * values) * 0.3989422804014327
    phi = 0.5 * (1.0 + lax.erf(values * 0.7071067811865476))
    return phi, density


def vector_rows(vec_ref, layer):
    low, high = vec_ref[0, layer].astype(F32), vec_ref[1, layer].astype(F32)
    row = lambda block, at: block[at : at + 1]
    return dict(
        bias_q=row(low, 0), bias_v=row(low, 1), bias_o=row(low, 2), shift_one=row(low, 3),
        bias_hid=row(high, 3), shift_two=row(high, 4), gain_one=row(low, 5), gain_two=row(high, 5),
    )


def norm_forward(values):
    offset = values - jnp.mean(values, axis=-1, keepdims=True)
    scale = lax.rsqrt(jnp.mean(offset * offset, axis=-1, keepdims=True) + EPS)
    return offset * scale, scale


def forward_layer(
    step, layer, at_layer, before_mix, before_out, fresh_ref, live_ref, text_ref, init_ref,
    labels_row_ref, labels_col_ref, weights, vec_ref,
    x_ref, mixed_ref, heads_ref, hat_one_ref, first_ref, active_ref, slope_ref, hat_two_ref,
    stats_ref, acts_ref, y_scr, bias_scr, sum_scr, bias_in_scr,
):
    rows, width = y_scr.shape

    @pl.when(layer == 0)
    def _():
        fresh = fresh_ref[0] > 0
        last = y_scr[rows - 16 : rows, :].astype(F32)
        head_rows = pltpu.roll(last, 10, 0)
        number = lax.broadcasted_iota(jnp.int32, (16, width), 0)
        top = jnp.where(fresh, init_ref[0], head_rows)
        low = jnp.where(fresh, init_ref[1], last)
        x_ref[0] = text_ref[0, 0]
        x_ref[0, 0:16, :] = jnp.where(number < 10, top, text_ref[0, 0, 0:16, :].astype(F32)).astype(BF16)
        x_ref[0, rows - 16 : rows, :] = jnp.where(
            number >= 6, low, text_ref[0, 0, rows - 16 : rows, :].astype(F32)
        ).astype(BF16)

    @pl.when(layer == 1)
    def _():
        x_ref[0] = y_scr[...]

    row_side = labels_row_ref[0, 0]
    col_side = labels_col_ref[0, 0]
    allowed = (row_side == col_side) | (row_side < 0) | (col_side < 0)
    bias_scr[...] = jnp.where(allowed, 0.0, MASKED)

    before_mix()
    vec = vector_rows(vec_ref, at_layer)
    low, high = vec_ref[0, at_layer].astype(F32), vec_ref[1, at_layer].astype(F32)
    for part, row in enumerate((low[4:5], high[0:1], high[1:2], high[2:3])):
        bias_in_scr[part] = row
    inputs = x_ref[0]
    for tile in range(3):
        mixed = dot_nn(inputs, weight_tile(weights, "qkv", tile, at_layer))
        if tile == 0:
            mixed = mixed + vec["bias_q"]
        if tile == 2:
            mixed = mixed + vec["bias_v"]
        mixed_ref[0, :, tile * width : (tile + 1) * width] = mixed.astype(BF16)

    group = 4 * HEAD_DIM
    stat_lane = lax.broadcasted_iota(jnp.int32, (rows, 128), 1)
    stats = jnp.zeros((rows, 128), F32)
    for number in range(width // group):
        at = number * group
        queries = mixed_ref[0, :, at : at + group] * BF16(HEAD_DIM**-0.5)
        keys = mixed_ref[0, :, width + at : width + at + group]
        values = mixed_ref[0, :, 2 * width + at : 2 * width + at + group]
        total = jnp.zeros((rows, group), F32)
        for head in range(4):
            mine = head_lanes((rows, group), head)
            scores = dot_nt(jnp.where(mine, queries, 0), keys) + bias_scr[...]
            peak = jnp.max(scores, axis=-1, keepdims=True)
            expo = jnp.exp(scores - peak)
            norm = jnp.sum(expo, axis=-1, keepdims=True)
            probs = (expo * (1.0 / norm)).astype(BF16)
            total = total + dot_nn(probs, jnp.where(mine, values, 0))
            stats = jnp.where(stat_lane == number * 4 + head, peak + jnp.log(norm), stats)
        heads_ref[0, :, at : at + group] = total.astype(BF16)
    stats_ref[0] = stats

    before_out()
    attn = dot_nn(heads_ref[0], weight_tile(weights, "out", 0, at_layer)) + vec["bias_o"]
    hat, scale = norm_forward(x_ref[0].astype(F32) + attn)
    hat_one_ref[0] = hat.astype(BF16)
    stats = jnp.where(stat_lane == HEADS, scale, stats_ref[0])
    first = hat * vec["gain_one"] + vec["shift_one"]
    first_ref[0] = first.astype(BF16)
    sum_scr[...] = first + vec["bias_hid"]

    def ff_tile(tile, _):
        at = pl.multiple_of(tile * width, width)
        inner = dot_nn(first_ref[0], weight_tile(weights, "in", tile, at_layer)) + bias_in_scr[tile]
        phi, density = erf_parts(inner)
        active = (inner * phi).astype(BF16)
        active_ref[0, :, pl.ds(at, width)] = active
        slope_ref[0, :, pl.ds(at, width)] = (phi + inner * density).astype(BF16)
        sum_scr[...] += dot_nn(active, weight_tile(weights, "hid", tile, at_layer))
        return _

    lax.fori_loop(0, 4, ff_tile, 0)
    hat, scale = norm_forward(sum_scr[...])
    hat_two_ref[0] = hat.astype(BF16)
    stats_ref[0] = jnp.where(stat_lane == HEADS + 1, scale, stats)
    result = (hat * vec["gain_two"] + vec["shift_two"]).astype(BF16)
    y_scr[...] = result

    @pl.when(layer == 1)
    def _():
        acts_ref[0, 0] = jnp.where(live_ref[0] > 0, result, 0)


def saved_shapes(rows, width):
    return dict(
        x=((rows, width), BF16),
        mixed=((rows, 3 * width), BF16),
        heads=((rows, width), BF16),
        hat_one=((rows, width), BF16),
        first=((rows, width), BF16),
        active=((rows, 4 * width), BF16),
        slope=((rows, 4 * width), BF16),
        hat_two=((rows, width), BF16),
        stats=((rows, 128), F32),
    )


def forward_io(text, fresh, live, init, labels):
    items, segs, rows, width = text.shape
    count = 2 * items * segs
    saved = saved_shapes(rows, width)
    by_seg = lambda t: (t // (2 * segs), (t // 2) % segs, 0, 0)
    by_flag = lambda t: (t // 2, 0, 0)
    operands = [fresh, live, text, init, labels[:, :, :, None], labels[:, :, None, :]]
    in_specs = [
        pl.BlockSpec((1, 1, width), by_flag),
        pl.BlockSpec((1, 1, width), by_flag),
        pl.BlockSpec((1, 1, rows, width), by_seg),
        pl.BlockSpec(init.shape, lambda t: (0, 0, 0)),
        pl.BlockSpec((1, 1, rows, 1), by_seg),
        pl.BlockSpec((1, 1, 1, rows), by_seg),
    ]
    out_specs = [pl.BlockSpec((1,) + shape, lambda t: (t, 0, 0)) for shape, _ in saved.values()]
    out_specs.append(pl.BlockSpec((1, 1, rows, width), by_seg))
    out_shape = [jax.ShapeDtypeStruct((count,) + shape, kind) for shape, kind in saved.values()]
    out_shape.append(jax.ShapeDtypeStruct(text.shape, BF16))
    scratch = [
        pltpu.VMEM((rows, width), BF16),
        pltpu.VMEM((rows, rows), F32),
        pltpu.VMEM((rows, width), F32),
        pltpu.VMEM((4, 1, width), F32),
    ]
    return count, operands, in_specs, out_specs, out_shape, scratch


def nothing():
    pass


def forward_body(*refs):
    step = pl.program_id(0)
    y_scr = refs[21]

    @pl.when(step == 0)
    def _():
        y_scr[...] = jnp.zeros_like(y_scr)

    forward_layer(step, step % 2, 0, nothing, nothing, *refs[:6], refs[6:10], *refs[10:])


def forward_steps(text, fresh, live, init, labels, weights, vec):
    count, operands, in_specs, out_specs, out_shape, scratch = forward_io(text, fresh, live, init, labels)
    layer_of = lambda t: t % 2
    *saved, acts = pl.pallas_call(
        forward_body,
        grid=(count,),
        in_specs=in_specs
        + weight_specs([weight.shape for weight in weights], layer_of)
        + [pl.BlockSpec((2, 1) + vec.shape[2:], lambda t: (0, t % 2, 0, 0))],
        out_specs=out_specs,
        out_shape=out_shape,
        scratch_shapes=scratch,
        compiler_params=pltpu.CompilerParams(vmem_limit_bytes=VMEM_BYTES),
        name="forward_steps",
    )(*operands, *weights, vec)
    return dict(zip(saved_shapes(*text.shape[2:]), saved)), acts


def norm_backward(grad, hat, scale, gain):
    scaled = grad * gain
    mean_one = jnp.mean(scaled, axis=-1, keepdims=True)
    mean_two = jnp.mean(scaled * hat, axis=-1, keepdims=True)
    return (scaled - mean_one - hat * mean_two) * scale


def column_sum(values):
    return jnp.sum(values, axis=0, keepdims=True)


def backward_body(
    count, segs, fresh_ref, live_ref, cot_ref, labels_row_ref, labels_col_ref, qkv_ref, w_out_ref,
    in_ref, hid_ref, vec_ref, mixed_ref, heads_ref, hat_one_ref, slope_ref, hat_two_ref, stats_ref,
    branch_ref, inner_ref, attn_ref, mix_ref, sums_ref, inputs_ref, init_ref,
    g_scr, carry_scr, bias_scr, sum_scr, go_scr,
):
    step = count - 1 - pl.program_id(0)
    layer = step % 2
    seg = (step // 2) % segs
    rows, width = g_scr.shape
    weights = (qkv_ref, w_out_ref, in_ref, hid_ref)
    gain_one = vec_ref[0, 0].astype(F32)[5:6]
    gain_two = vec_ref[1, 0].astype(F32)[5:6]

    @pl.when(pl.program_id(0) == 0)
    def _():
        carry_scr[...] = jnp.zeros_like(carry_scr)
        init_ref[...] = jnp.zeros_like(init_ref)

    @pl.when(layer == 1)
    def _():
        cot = jnp.where(live_ref[0] > 0, cot_ref[0, 0], 0)
        g_scr[...] = cot
        carried = jnp.where(seg == segs - 1, 0.0, carry_scr[...])
        g_scr[rows - 16 : rows, :] = (cot[rows - 16 : rows].astype(F32) + carried).astype(BF16)

    row_side = labels_row_ref[0, 0]
    col_side = labels_col_ref[0, 0]
    allowed = (row_side == col_side) | (row_side < 0) | (col_side < 0)
    bias_scr[...] = jnp.where(allowed, 0.0, MASKED)

    stats = stats_ref[0]
    scale_one = stats[:, HEADS : HEADS + 1]
    scale_two = stats[:, HEADS + 1 : HEADS + 2]
    grad = g_scr[...].astype(F32)
    hat = hat_two_ref[0].astype(F32)
    sums_ref[0, :, 0:width] = column_sum(grad * hat)
    sums_ref[0, :, width : 2 * width] = column_sum(grad)
    grad_second = norm_backward(grad, hat, scale_two, gain_two)
    branch = grad_second.astype(BF16)
    branch_ref[0] = branch
    sums_ref[0, :, 2 * width : 3 * width] = column_sum(branch.astype(F32))
    sum_scr[...] = grad_second

    def ff_tile(tile, _):
        at = pl.multiple_of(tile * width, width)
        active = dot_nt(branch, weight_tile(weights, "hid", tile, 0))
        inner = (active * slope_ref[0, :, pl.ds(at, width)].astype(F32)).astype(BF16)
        inner_ref[0, :, pl.ds(at, width)] = inner
        sums_ref[0, :, pl.ds(8 * width + at, width)] = column_sum(inner.astype(F32))
        sum_scr[...] += dot_nt(inner, weight_tile(weights, "in", tile, 0))
        return _

    lax.fori_loop(0, 4, ff_tile, 0)
    grad = sum_scr[...]
    hat = hat_one_ref[0].astype(F32)
    sums_ref[0, :, 3 * width : 4 * width] = column_sum(grad * hat)
    sums_ref[0, :, 4 * width : 5 * width] = column_sum(grad)
    resid = norm_backward(grad, hat, scale_one, gain_one)
    sum_scr[...] = resid
    attn = resid.astype(BF16)
    attn_ref[0] = attn
    sums_ref[0, :, 5 * width : 6 * width] = column_sum(attn.astype(F32))
    go = dot_nt(attn, weight_tile(weights, "out", 0, 0)).astype(BF16)
    go_scr[...] = go
    product = go.astype(F32) * heads_ref[0].astype(F32)
    high = product.astype(BF16)
    low = (product - high.astype(F32)).astype(BF16)
    picks = (
        lax.broadcasted_iota(jnp.int32, (16, width), 1) // HEAD_DIM
        == lax.broadcasted_iota(jnp.int32, (16, width), 0)
    ).astype(BF16)
    centres = dot_nt(picks, high) + dot_nt(picks, low)
    logs = jnp.transpose(stats)

    group = 4 * HEAD_DIM
    for number in range(width // group):
        at = number * group
        queries = mixed_ref[0, :, at : at + group] * BF16(HEAD_DIM**-0.5)
        keys = mixed_ref[0, :, width + at : width + at + group]
        values = mixed_ref[0, :, 2 * width + at : 2 * width + at + group]
        outs = go_scr[:, at : at + group]
        grad_q = jnp.zeros((rows, group), F32)
        grad_k = jnp.zeros((rows, group), F32)
        grad_v = jnp.zeros((rows, group), F32)
        for head in range(4):
            mine = head_lanes((rows, group), head)
            row = number * 4 + head
            keys_h = jnp.where(mine, keys, 0)
            scores = dot_nt(keys_h, queries) + bias_scr[...]
            probs = jnp.exp(scores - logs[row : row + 1, :])
            grad_p = dot_nt(jnp.where(mine, values, 0), outs)
            grad_s = (probs * (grad_p - centres[row : row + 1, :])).astype(BF16)
            grad_v = grad_v + dot_nn(probs.astype(BF16), jnp.where(mine, outs, 0))
            grad_k = grad_k + dot_nn(grad_s, jnp.where(mine, queries, 0))
            grad_q = grad_q + dot_tn(grad_s, keys_h)
        mix_ref[0, :, at : at + group] = (grad_q * HEAD_DIM**-0.5).astype(BF16)
        mix_ref[0, :, width + at : width + at + group] = grad_k.astype(BF16)
        mix_ref[0, :, 2 * width + at : 2 * width + at + group] = grad_v.astype(BF16)

    sums_ref[0, :, 6 * width : 7 * width] = column_sum(mix_ref[0, :, 0:width].astype(F32))
    sums_ref[0, :, 7 * width : 8 * width] = column_sum(mix_ref[0, :, 2 * width : 3 * width].astype(F32))
    total = sum_scr[...]
    for tile in range(3):
        total = total + dot_nt(
            mix_ref[0, :, tile * width : (tile + 1) * width], weight_tile(weights, "qkv", tile, 0)
        )
    result = total.astype(BF16)
    g_scr[...] = result

    @pl.when(layer == 0)
    def _():
        inputs_ref[0, 0] = result
        fresh = fresh_ref[0] > 0
        number = lax.broadcasted_iota(jnp.int32, (16, width), 0)
        folded = result[rows - 16 : rows].astype(F32) + pltpu.roll(result[0:16].astype(F32), 6, 0)
        folded = jnp.where(number >= 6, folded, 0.0).astype(BF16).astype(F32)
        init_ref[...] += jnp.where(fresh, folded, 0.0)
        carry_scr[...] = jnp.where(fresh, 0.0, folded)


def backward_steps(cot, fresh, live, labels, weights, vec, saved):
    items, segs, rows, width = cot.shape
    count = 2 * items * segs
    at = lambda t: count - 1 - t
    by_seg = lambda t: (at(t) // (2 * segs), (at(t) // 2) % segs, 0, 0)
    by_flag = lambda t: (at(t) // 2, 0, 0)
    by_step = lambda t: (at(t), 0, 0)
    names = ("mixed", "heads", "hat_one", "slope", "hat_two", "stats")
    outs = dict(
        branch=(rows, width), inner=(rows, 4 * width), attn=(rows, width), mix=(rows, 3 * width),
    )
    *grads, sums, inputs, memory = pl.pallas_call(
        functools.partial(backward_body, count, segs),
        grid=(count,),
        in_specs=[
            pl.BlockSpec((1, 1, width), by_flag),
            pl.BlockSpec((1, 1, width), by_flag),
            pl.BlockSpec((1, 1, rows, width), by_seg),
            pl.BlockSpec((1, 1, rows, 1), by_seg),
            pl.BlockSpec((1, 1, 1, rows), by_seg),
        ]
        + weight_specs([weight.shape for weight in weights], lambda t: at(t) % 2)
        + [pl.BlockSpec((2, 1) + vec.shape[2:], lambda t: (0, at(t) % 2, 0, 0))]
        + [pl.BlockSpec((1,) + saved[name].shape[1:], by_step) for name in names],
        out_specs=[pl.BlockSpec((1,) + shape, by_step) for shape in outs.values()]
        + [
            pl.BlockSpec((1, 1, 12 * width), by_step),
            pl.BlockSpec((1, 1, rows, width), by_seg),
            pl.BlockSpec((16, width), lambda t: (0, 0)),
        ],
        out_shape=[jax.ShapeDtypeStruct((count,) + shape, BF16) for shape in outs.values()]
        + [
            jax.ShapeDtypeStruct((count, 1, 12 * width), F32),
            jax.ShapeDtypeStruct(cot.shape, BF16),
            jax.ShapeDtypeStruct((16, width), F32),
        ],
        scratch_shapes=[
            pltpu.VMEM((rows, width), BF16),
            pltpu.VMEM((16, width), F32),
            pltpu.VMEM((rows, rows), F32),
            pltpu.VMEM((rows, width), F32),
            pltpu.VMEM((rows, width), BF16),
        ],
        compiler_params=pltpu.CompilerParams(vmem_limit_bytes=VMEM_BYTES),
        name="backward_steps",
    )(
        fresh, live, cot, labels[:, :, :, None], labels[:, :, None, :], *weights, vec,
        *[saved[name] for name in names],
    )
    return dict(zip(outs, grads)), sums, inputs, memory


def gather_forward_body(count, *refs):
    io = refs[:6]
    sources = refs[6:10]
    vec_source = refs[10]
    outs = refs[11:21]
    full_outs = refs[21:25]
    vec_out = refs[25]
    forward_scratch = refs[26:30]
    weights = refs[30:34]
    vec = refs[34]
    (
        load_sems, hid_load_sems, store_sems, x_sems, y_sems, fx_sems, fy_sems, core_sems,
        line_core_sems, up_sems, down_sems, vec_sems, vec_load_sem,
    ) = refs[35:]
    step = pl.program_id(0)
    section, place = lax.axis_index("section"), lax.axis_index("dp")
    x, y = section % 2, section // 2
    core, z = place % 2, place // 2
    hid = weights[3]
    depth = hid.shape[0]
    x_dev = (y * 2 + 1 - x, place)
    y_dev = ((1 - y) * 2 + x, place)
    core_dev = (section, z * 2 + 1 - core)
    up_dev = (section, (z + 1) % depth * 2 + core)
    down_dev = (section, (z + depth - 1) % depth * 2 + core)
    blocks = ((y, 1 - x), (1 - y, x), (1 - y, 1 - x))

    def remote(source, target, sems, index, device):
        return pltpu.make_async_remote_copy(
            src_ref=source, dst_ref=target, send_sem=sems.at[(0, *index)], recv_sem=sems.at[(1, *index)],
            device_id=device, device_id_type=MESH,
        )

    def slot(number, block, first=None, part=None):
        lead = (z if first is None else first, core) if number == 3 else (core,)
        view = weights[number].at[(*lead, *block)]
        if part is not None:
            tall = weights[number].shape[-2] // 2
            view = view.at[pl.ds(part * tall, tall)]
        return view

    def own(number):
        tall = weights[number].shape[-2]
        at = (z * 2 + core) if number == 3 else core
        return sources[number].at[0, pl.ds(pl.multiple_of(at * tall, tall), tall)]

    def x_copy(number):
        return remote(own(number), slot(number, (y, x)), x_sems, (number,), x_dev)

    def y_copy(number):
        return remote(own(number), slot(number, (y, x)), y_sems, (number,), y_dev)

    def fy_copy(number):
        piece = slot(number, blocks[0], part=0)
        return remote(piece, piece, fy_sems, (number,), y_dev)

    def fx_copy(number):
        piece = slot(number, blocks[1], part=1)
        return remote(piece, piece, fx_sems, (number,), x_dev)

    def core_copy(number, kind):
        piece = slot(number, blocks[kind]) if kind < 2 else slot(number, blocks[2], part=kind - 2)
        return remote(piece, piece, core_sems, (number, kind), core_dev)

    def line_core_copy(at, kind):
        piece = slot(3, blocks[kind], first=at)
        return remote(piece, piece, line_core_sems, (at, kind), core_dev)

    def up_copy(at, kind):
        piece = slot(3, blocks[kind], first=at)
        return remote(piece, piece, up_sems, (at, kind), up_dev)

    def down_copy(at, kind):
        piece = slot(3, blocks[kind], first=at)
        return remote(piece, piece, down_sems, (at, kind), down_dev)

    def vec_copy(kind):
        block = ((y, x), (y, x), (y, 1 - x))[kind]
        source = vec_source if kind < 2 else vec.at[block]
        return remote(source, vec.at[block], vec_sems, (kind,), (x_dev, y_dev, y_dev)[kind])

    def loads():
        copies = [
            pltpu.make_async_copy(
                sources[number].at[0, pl.ds(side * weights[number].shape[-2], weights[number].shape[-2])],
                weights[number].at[side, y, x],
                load_sems.at[number, side],
            )
            for number in range(3)
            for side in range(2)
        ]
        tall = hid.shape[-2]
        copies += [
            pltpu.make_async_copy(
                sources[3].at[0, pl.ds((at * 2 + side) * tall, tall)],
                hid.at[at, side, y, x],
                hid_load_sems.at[at, side],
            )
            for at in range(depth)
            for side in range(2)
        ]
        return copies + [pltpu.make_async_copy(vec_source, vec.at[y, x], vec_load_sem)]

    def full_stores():
        copies = [
            pltpu.make_async_copy(weights[number], full_outs[number], store_sems.at[number])
            for number in range(4)
        ]
        return copies + [pltpu.make_async_copy(vec, vec_out, store_sems.at[4])]

    def spread(kind):
        @pl.when(z < depth - 1)
        def _():
            up_copy(z, kind).start()

        @pl.when(z > 0)
        def _():
            down_copy(z, kind).start()

        line_core_copy(z, kind).start()

    def hop(distance):
        @pl.when(z >= distance)
        def _():
            for kind in range(3):
                up_copy(z - distance, kind).wait_recv()

                @pl.when(z < depth - 1)
                def _():
                    up_copy(z - distance, kind).start()

                line_core_copy(z - distance, kind).start()

        @pl.when(z + distance < depth)
        def _():
            for kind in range(3):
                down_copy(z + distance, kind).wait_recv()

                @pl.when(z > 0)
                def _():
                    down_copy(z + distance, kind).start()

                line_core_copy(z + distance, kind).start()

    def direct(number):
        x_copy(number).wait_recv()
        fy_copy(number).start()
        core_copy(number, 0).start()
        y_copy(number).wait_recv()
        fx_copy(number).start()
        core_copy(number, 1).start()

    def diagonal(number):
        fy_copy(number).wait_recv()
        core_copy(number, 2).start()
        fx_copy(number).wait_recv()
        core_copy(number, 3).start()

    def complete(number):
        for kind in range(4):
            core_copy(number, kind).wait_recv()

    def before_mix():
        @pl.when(step == 0)
        def _():
            for copy in loads():
                copy.start()
            barrier = pltpu.get_barrier_semaphore()
            for device in (x_dev, y_dev, core_dev):
                pl.semaphore_signal(barrier, inc=1, device_id=device, device_id_type=MESH)

            @pl.when(z < depth - 1)
            def _():
                pl.semaphore_signal(barrier, inc=1, device_id=up_dev, device_id_type=MESH)

            @pl.when(z > 0)
            def _():
                pl.semaphore_signal(barrier, inc=1, device_id=down_dev, device_id_type=MESH)

            pl.semaphore_wait(barrier, 3 + jnp.where(z > 0, 1, 0) + jnp.where(z < depth - 1, 1, 0))
            x_copy(3).start()
            y_copy(3).start()
            vec_copy(0).start()
            vec_copy(1).start()
            for number in (0, 1):
                x_copy(number).start()
                y_copy(number).start()
            x_copy(3).wait_recv()
            fy_copy(3).start()
            spread(0)
            y_copy(3).wait_recv()
            fx_copy(3).start()
            spread(1)
            vec_copy(0).wait_recv()
            vec_copy(2).start()
            x_copy(2).start()
            y_copy(2).start()
            fy_copy(3).wait_recv()
            fx_copy(3).wait_recv()
            spread(2)
            direct(0)
            direct(1)
            hop(1)
            diagonal(0)
            diagonal(1)
            vec_copy(1).wait_recv()
            vec_copy(2).wait_recv()
            complete(0)
            for copy in loads():
                copy.wait()

    def before_out():
        @pl.when(step == 0)
        def _():
            hop(2)
            direct(2)
            hop(3)
            diagonal(2)
            complete(1)
            complete(2)
            for at in range(depth):
                for kind in range(3):
                    line_core_copy(at, kind).wait_recv()

        @pl.when(step == 1)
        def _():
            for copy in full_stores():
                copy.start()

    forward_layer(
        step, step % 2, step % 2, before_mix, before_out, *io, weights, vec, *outs, *forward_scratch
    )

    @pl.when(step == count - 1)
    def _():
        for copy in full_stores():
            copy.wait()
        for number in range(4):
            x_copy(number).wait_send()
            y_copy(number).wait_send()
            fx_copy(number).wait_send()
            fy_copy(number).wait_send()
            if number < 3:
                for kind in range(4):
                    core_copy(number, kind).wait_send()
        for kind in range(3):
            vec_copy(kind).wait_send()
            for at in range(depth):
                line_core_copy(at, kind).wait_send()

                @pl.when((z >= at) & (z < depth - 1))
                def _():
                    up_copy(at, kind).wait_send()

                @pl.when((z <= at) & (z > 0))
                def _():
                    down_copy(at, kind).wait_send()


def full_weight_shapes(w_qkv, w_out, w_in, w_hid):
    half, width = w_out.shape[1:]
    return [(2, 2, 2, half // 2, block.shape[2]) for block in (w_qkv, w_out, w_in)] + [
        (4, 2, 2, 2, w_hid.shape[1] // 8, width)
    ]


def gather_forward(text, fresh, live, init, labels, blocks, vec):
    count, operands, in_specs, out_specs, out_shape, scratch = forward_io(text, fresh, live, init, labels)
    shapes = full_weight_shapes(*blocks)
    vec_shape = (2, 2) + vec.shape
    any_spec = pl.BlockSpec(memory_space=pl.ANY)
    dma = pltpu.SemaphoreType.DMA
    depth = shapes[3][0]
    saved_count = len(out_specs)
    outs = pl.pallas_call(
        functools.partial(gather_forward_body, count),
        grid=(count,),
        in_specs=in_specs + [any_spec] * 5,
        out_specs=out_specs + [any_spec] * 5,
        out_shape=out_shape + [jax.ShapeDtypeStruct(shape, BF16) for shape in (*shapes, vec_shape)],
        scratch_shapes=scratch
        + [pltpu.VMEM(shape, BF16) for shape in (*shapes, vec_shape)]
        + [
            dma((3, 2)), dma((depth, 2)), dma((5,)), dma((2, 4)), dma((2, 4)), dma((2, 4)), dma((2, 4)),
            dma((2, 3, 4)), dma((2, depth, 3)), dma((2, depth, 3)), dma((2, depth, 3)), dma((2, 3)), dma,
        ],
        compiler_params=pltpu.CompilerParams(
            vmem_limit_bytes=VMEM_BYTES, collective_id=1, has_side_effects=True
        ),
        name="gather_forward",
    )(*operands, *blocks, vec)
    saved = dict(zip(saved_shapes(*text.shape[2:]), outs))
    return saved, outs[saved_count - 1], outs[saved_count : saved_count + 4], outs[saved_count + 4]


def gather_apart(blocks, vec):
    shapes = full_weight_shapes(*blocks)
    full = []
    for block, shape in zip(blocks, shapes):
        gathered = lax.all_gather(block[0], "section")
        lead = len(shape) - 4
        gathered = gathered.reshape(2, 2, *shape[: lead], *shape[-2:])
        order = (*range(2, 2 + lead), 0, 1, 2 + lead, 3 + lead)
        full.append(gathered.transpose(order))
    vec_full = lax.all_gather(vec, "section").reshape(2, 2, *vec.shape)
    return full, vec_full


GRAD_NAMES = ("first", "inner", "active", "branch", "x", "mix", "heads", "attn")


def weight_grad_body(
    layer, segs_all, dp, *refs,
):
    sources = refs[:8]
    extra_ref, mine_ref, theirs_ref = refs[8:11]
    held = refs[11:19]
    wire, in_sems, extra_sem, out_sems = refs[19:23]
    core = lax.axis_index("dp") % 2
    rows = sources[0].shape[1]
    width = sources[0].shape[2]
    half = width // 2
    lanes = wire.shape[-1]
    thin = width // dp
    wide = 3 * thin

    def loads(number):
        return [
            pltpu.make_async_copy(
                sources[number].at[2 * at + layer],
                held[number].at[pl.ds(at * rows, rows)],
                in_sems.at[number, at],
            )
            for at in range(segs_all)
        ]

    for number in range(8):
        for copy in loads(number):
            copy.start()
    extra = pltpu.make_async_copy(extra_ref, wire.at[:, :, :, :, pl.ds(half, extra_ref.shape[4])], extra_sem)
    extra.start()

    def ready(*numbers):
        for number in numbers:
            for copy in loads(number):
                copy.wait()

    def stores(kind):
        return [
            pltpu.make_async_copy(wire.at[kind, core], mine_ref.at[kind], out_sems.at[kind, 0]),
            pltpu.make_async_copy(wire.at[kind, 1 - core], theirs_ref.at[kind], out_sems.at[kind, 1]),
        ]

    first, inner, active, branch, inputs, mix, heads, attn = held
    extra.wait()

    ready(0, 1)
    per_tile = width // lanes

    def in_tile(tile, _):
        right = inner[:, pl.ds(pl.multiple_of(tile * width, width), width)]
        for side in range(2):
            result = dot_tn(first[:, side * half : (side + 1) * half], right).astype(BF16)
            for at in range(per_tile):
                wire[1, at % 2, tile * (per_tile // 2) + at // 2, side, 0:half, :] = result[
                    :, at * lanes : (at + 1) * lanes
                ]
        return _

    lax.fori_loop(0, 4, in_tile, 0)
    for copy in stores(1):
        copy.start()

    ready(2, 3)
    def hid_tile(side, _):
        for part in range(4):
            left = active[:, pl.ds(pl.multiple_of(side * 4 * half + part * half, half), half)]
            result = dot_tn(left, branch[...]).astype(BF16)
            for at in range(dp):
                wire[2, at % 2, at // 2, side, 0:half, part * thin : (part + 1) * thin] = result[
                    :, at * thin : (at + 1) * thin
                ]
        return _
    lax.fori_loop(0, 2, hid_tile, 0)
    for copy in stores(2):
        copy.start()

    ready(4, 5, 6, 7)
    for side in range(2):
        left = inputs[:, side * half : (side + 1) * half]
        for tile in range(2):
            result = dot_tn(left, mix[:, tile * 3 * half : (tile + 1) * 3 * half]).astype(BF16)
            for at in range(dp // 2):
                place = tile * (dp // 2) + at
                wire[0, place % 2, place // 2, side, 0:half, 0:wide] = result[
                    :, at * wide : (at + 1) * wide
                ]
        result = dot_tn(heads[:, side * half : (side + 1) * half], attn[...]).astype(BF16)
        for at in range(dp):
            wire[0, at % 2, at // 2, side, 0:half, wide:lanes] = result[:, at * thin : (at + 1) * thin]
    for copy in stores(0):
        copy.start()
    for kind in range(3):
        for copy in stores(kind):
            copy.wait()


def weight_grads(layer, dp, saved, extras):
    sources = [saved[name] for name in GRAD_NAMES]
    steps, rows, width = sources[0].shape
    segs_all = steps // 2
    half = width // 2
    lanes = 4 * width // dp
    extra_rows = extras.shape[4]
    kind = jax.ShapeDtypeStruct((3, dp // 2, 2, half + extra_rows, lanes), BF16)
    any_spec = pl.BlockSpec(memory_space=pl.ANY)
    return pl.pallas_call(
        functools.partial(weight_grad_body, layer, segs_all, dp),
        in_specs=[any_spec] * 9,
        out_specs=[any_spec] * 2,
        out_shape=[kind, kind],
        scratch_shapes=[pltpu.VMEM((segs_all * rows, source.shape[2]), BF16) for source in sources]
        + [
            pltpu.VMEM((3, 2, dp // 2, 2, half + extra_rows, lanes), BF16),
            pltpu.SemaphoreType.DMA((8, segs_all)),
            pltpu.SemaphoreType.DMA,
            pltpu.SemaphoreType.DMA((3, 2)),
        ],
        compiler_params=pltpu.CompilerParams(vmem_limit_bytes=VMEM_BYTES),
        name="weight_grads",
    )(*sources, extras)


def add_into(ref, other):
    ref[...] = (ref[...].astype(F32) + other[...].astype(F32)).astype(BF16)


def grad_reduce_body(dp, segs_all, *refs):
    sources = refs[:8]
    extra_ref = refs[8]
    qkv_out, out_out, in_out, hid_out, extra_out = refs[9:14]
    held = refs[14:22]
    mine, theirs, landed, xp, xq, yq, yp, from_low, from_high = refs[22:31]
    in_sems, extra_sems, core_sems, free_sem, xp_sems, xq_sems, yq_sems, yp_sems, up_sems, down_sems = refs[31:41]
    section, place = lax.axis_index("section"), lax.axis_index("dp")
    x, y = section % 2, section // 2
    core, z = place % 2, place // 2
    depth = dp // 2
    cut = depth // 2
    rows, width = sources[0].shape[1:]
    half = width // 2
    lanes = mine.shape[-1]
    thin = width // dp
    wide = 3 * thin
    x_dev = (y * 2 + 1 - x, place)
    y_dev = ((1 - y) * 2 + x, place)
    core_dev = (section, z * 2 + 1 - core)
    up_dev = (section, (z + 1) % depth * 2 + core)
    down_dev = (section, (z + depth - 1) % depth * 2 + core)
    kinds = (1, 2, 0)
    used = {1: (0, 1), 2: (2, 3), 0: (4, 5, 6, 7)}
    first, inner, active, branch, inputs, mix, heads, attn = held

    def loads(side, kind):
        layer = (1 - x) if side == 0 else x
        return [
            pltpu.make_async_copy(
                sources[number].at[2 * at + layer],
                held[number].at[pl.ds(at * rows, rows)],
                in_sems.at[number, at],
            )
            for number in used[kind]
            for at in range(segs_all)
        ]

    for kind in kinds:
        for copy in loads(0, kind):
            copy.start()

    barrier = pltpu.get_barrier_semaphore()
    for device in (x_dev, y_dev, core_dev):
        pl.semaphore_signal(barrier, inc=1, device_id=device, device_id_type=MESH)

    @pl.when(z < depth - 1)
    def _():
        pl.semaphore_signal(barrier, inc=1, device_id=up_dev, device_id_type=MESH)

    @pl.when(z > 0)
    def _():
        pl.semaphore_signal(barrier, inc=1, device_id=down_dev, device_id_type=MESH)

    pl.semaphore_wait(barrier, 3 + jnp.where(z > 0, 1, 0) + jnp.where(z < depth - 1, 1, 0))

    def remote(source, target, sems, index, device):
        return pltpu.make_async_remote_copy(
            src_ref=source, dst_ref=target, send_sem=sems.at[(0, *index)], recv_sem=sems.at[(1, *index)],
            device_id=device, device_id_type=MESH,
        )

    def core_copy(unit):
        return remote(theirs.at[unit % 2], landed.at[unit % 2], core_sems, (unit,), core_dev)

    def xp_copy(kind):
        return remote(mine.at[0, kind, pl.ds(0, cut)], xp.at[kind], xp_sems, (kind,), x_dev)

    def yq_copy(side, kind):
        return remote(
            mine.at[side, kind, pl.ds(cut, depth - cut), 1 - y], yq.at[side, kind], yq_sems,
            (side, kind), y_dev,
        )

    def xq_copy(kind):
        return remote(mine.at[0, kind, pl.ds(cut, depth - cut), y], xq.at[kind], xq_sems, (kind,), x_dev)

    def yp_copy(kind):
        return remote(mine.at[1, kind, pl.ds(0, cut), 1 - y], yp.at[kind], yp_sems, (kind,), y_dev)

    def up_copy(kind, at):
        return remote(mine.at[1, kind, at, y], from_low.at[kind, at], up_sems, (kind, at), up_dev)

    def down_copy(kind, at):
        return remote(mine.at[1, kind, at, y], from_high.at[kind, at], down_sems, (kind, at), down_dev)

    def multiply(side, kind, unit):
        slot = unit % 2

        def put(at, block, piece, start, stop):
            if isinstance(at, int):
                chunk_core, chunk_z = at % 2, at // 2
            else:
                chunk_core, chunk_z = at

            @pl.when(core == chunk_core)
            def _():
                mine[side, kind, chunk_z, block, 0:half, start:stop] = piece

            @pl.when(core != chunk_core)
            def _():
                theirs[slot, chunk_z, block, 0:half, start:stop] = piece

        if kind == 1:
            per_tile = width // lanes

            def in_tile(tile, _):
                right = inner[:, pl.ds(pl.multiple_of(tile * width, width), width)]
                for block in range(2):
                    result = dot_tn(first[:, block * half : (block + 1) * half], right).astype(BF16)
                    for at in range(per_tile):
                        put(
                            (at % 2, tile * (per_tile // 2) + at // 2), block,
                            result[:, at * lanes : (at + 1) * lanes], 0, lanes,
                        )
                return _

            lax.fori_loop(0, 4, in_tile, 0)
        elif kind == 2:

            def hid_tile(block, _):
                for part in range(4):
                    left = active[:, pl.ds(pl.multiple_of((block * 4 + part) * half, half), half)]
                    result = dot_tn(left, branch[...]).astype(BF16)
                    for at in range(dp):
                        put(
                            at, block, result[:, at * thin : (at + 1) * thin], part * thin,
                            (part + 1) * thin,
                        )
                return _

            lax.fori_loop(0, 2, hid_tile, 0)
        else:
            for block in range(2):
                left = inputs[:, block * half : (block + 1) * half]
                for tile in range(2):
                    result = dot_tn(left, mix[:, tile * 3 * half : (tile + 1) * 3 * half]).astype(BF16)
                    for at in range(depth):
                        put(
                            tile * depth + at, block, result[:, at * wide : (at + 1) * wide], 0, wide
                        )
                result = dot_tn(heads[:, block * half : (block + 1) * half], attn[...]).astype(BF16)
                for at in range(dp):
                    put(at, block, result[:, at * thin : (at + 1) * thin], wide, lanes)

    def after_core(side, kind, unit):
        core_copy(unit).wait_recv()

        def add(at, _):
            add_into(mine.at[side, kind, at], landed.at[unit % 2, at])
            return _

        lax.fori_loop(0, depth, add, 0)
        if unit + 2 < 6:
            pl.semaphore_signal(free_sem, inc=1, device_id=core_dev, device_id_type=MESH)
        if side == 0:
            xp_copy(kind).start()
        yq_copy(side, kind).start()

    def forward_q(kind):
        yq_copy(0, kind).wait_recv()

        def add(at, _):
            add_into(mine.at[0, kind, cut + at, y], yq.at[0, kind, at])
            return _

        lax.fori_loop(0, depth - cut, add, 0)
        xq_copy(kind).start()

    def forward_p(kind):
        xp_copy(kind).wait_recv()

        def add(at, _):
            add_into(mine.at[1, kind, at], xp.at[kind, at])
            return _

        lax.fori_loop(0, cut, add, 0)
        yp_copy(kind).start()

    def finish_plane(kind):
        yq_copy(1, kind).wait_recv()
        xq_copy(kind).wait_recv()

        def add_two(at, _):
            ref = mine.at[1, kind, cut + at, y]
            total = ref[...].astype(F32) + yq[1, kind, at].astype(F32) + xq[kind, at].astype(F32)
            ref[...] = total.astype(BF16)
            return _

        lax.fori_loop(0, depth - cut, add_two, 0)
        yp_copy(kind).wait_recv()

        def add(at, _):
            add_into(mine.at[1, kind, at, y], yp.at[kind, at])
            return _

        lax.fori_loop(0, cut, add, 0)

    def line(kind):
        def hop(count, _):
            high, low = depth - 1 - count, count

            @pl.when(z < high)
            def _():
                @pl.when(z > 0)
                def _():
                    up_copy(kind, high).wait_recv()
                    add_into(mine.at[1, kind, high, y], from_low.at[kind, high])

                up_copy(kind, high).start()

            @pl.when(z > low)
            def _():
                @pl.when(z < depth - 1)
                def _():
                    down_copy(kind, low).wait_recv()
                    add_into(mine.at[1, kind, low, y], from_high.at[kind, low])

                down_copy(kind, low).start()

            return 0

        lax.fori_loop(0, depth - 1, hop, 0)

    def finish(kind):
        @pl.when(z > 0)
        def _():
            up_copy(kind, z).wait_recv()
            add_into(mine.at[1, kind, z, y], from_low.at[kind, z])

        @pl.when(z < depth - 1)
        def _():
            down_copy(kind, z).wait_recv()
            add_into(mine.at[1, kind, z, y], from_high.at[kind, z])

        total = mine[1, kind, z, y].astype(F32)
        extra_out[kind] = total[half:, :]
        if kind == 0:
            qkv_out[0] = total[:half, 0:wide]
            out_out[0] = total[:half, wide:lanes]
        elif kind == 1:
            in_out[0] = total[:half]
        else:
            for part in range(4):
                hid_out[0, part * half : (part + 1) * half, :] = total[:half, part * thin : (part + 1) * thin]

    units = [(side, kind) for side in range(2) for kind in kinds]
    for unit, (side, kind) in enumerate(units):
        layer = (1 - x) if side == 0 else x
        for copy in loads(side, kind):
            copy.wait()
        if unit >= 2:
            core_copy(unit - 2).wait_send()
        extra_rows = extra_ref.shape[5]
        extras = [
            pltpu.make_async_copy(
                extra_ref.at[layer, kind, core], mine.at[side, kind, :, :, pl.ds(half, extra_rows)],
                extra_sems.at[0],
            ),
            pltpu.make_async_copy(
                extra_ref.at[layer, kind, 1 - core], theirs.at[unit % 2, :, :, pl.ds(half, extra_rows)],
                extra_sems.at[1],
            ),
        ]
        for copy in extras:
            copy.start()
        multiply(side, kind, unit)
        for copy in extras:
            copy.wait()
        if unit >= 2:
            pl.semaphore_wait(free_sem, 1)
        core_copy(unit).start()
        if side == 0:
            for copy in loads(1, kind):
                copy.start()
        if unit >= 1:
            after_core(*units[unit - 1], unit - 1)
        if unit == 4:
            forward_q(kinds[0])
        if unit == 5:
            forward_q(kinds[1])
    after_core(*units[5], 5)
    forward_p(kinds[0])
    forward_q(kinds[2])
    forward_p(kinds[1])
    forward_p(kinds[2])
    finish_plane(kinds[0])
    line(kinds[0])
    finish_plane(kinds[1])
    line(kinds[1])
    finish(kinds[0])
    finish_plane(kinds[2])
    line(kinds[2])
    finish(kinds[1])
    finish(kinds[2])
    core_copy(4).wait_send()
    core_copy(5).wait_send()
    for kind in kinds:
        xp_copy(kind).wait_send()
        xq_copy(kind).wait_send()
        yp_copy(kind).wait_send()
        for side in range(2):
            yq_copy(side, kind).wait_send()

        def sent(at, _):
            @pl.when(at > z)
            def _():
                up_copy(kind, at).wait_send()

            @pl.when(at < z)
            def _():
                down_copy(kind, at).wait_send()

            return 0

        lax.fori_loop(0, depth, sent, 0)


def grad_reduce_shapes(dp, steps, rows, width, extra_rows):
    half = width // 2
    lanes = 4 * width // dp
    depth = dp // 2
    cut = depth // 2
    tall = half + extra_rows
    held = [width, 4 * width, 4 * width, width, width, 3 * width, width, width]
    return [pltpu.VMEM((steps // 2 * rows, columns), BF16) for columns in held] + [
        pltpu.VMEM(shape + (tall, lanes), BF16)
        for shape in (
            (2, 3, depth, 2), (2, depth, 2), (2, depth, 2), (3, cut, 2), (3, depth - cut),
            (2, 3, depth - cut), (3, cut), (3, depth), (3, depth),
        )
    ]


def padded_bytes(shapes):
    total = 0
    for shape in shapes:
        *lead, tall, lanes = shape.shape
        size = 2 * tall * -(-lanes // 128) * 128
        for count in lead:
            size *= count
        total += size
    return total


def grad_reduce(dp, saved, extras):
    sources = [saved[name] for name in GRAD_NAMES]
    steps, rows, width = sources[0].shape
    segs_all = steps // 2
    half = width // 2
    lanes = 4 * width // dp
    thin = width // dp
    extra_rows = extras.shape[5]
    depth = dp // 2
    any_spec = pl.BlockSpec(memory_space=pl.ANY)
    dma = pltpu.SemaphoreType.DMA
    return pl.pallas_call(
        functools.partial(grad_reduce_body, dp, segs_all),
        in_specs=[any_spec] * 9,
        out_specs=[pl.BlockSpec(memory_space=pltpu.VMEM)] * 5,
        out_shape=[
            jax.ShapeDtypeStruct(shape, F32)
            for shape in (
                (1, half, 3 * thin), (1, half, thin), (1, half, lanes), (1, 4 * half, thin),
                (3, extra_rows, lanes),
            )
        ],
        scratch_shapes=grad_reduce_shapes(dp, steps, rows, width, extra_rows)
        + [
            dma((8, segs_all)), dma((2,)), dma((2, 6)), pltpu.SemaphoreType.REGULAR, dma((2, 3)),
            dma((2, 3)), dma((2, 2, 3)), dma((2, 3)), dma((2, 3, depth)), dma((2, 3, depth)),
        ],
        compiler_params=pltpu.CompilerParams(
            vmem_limit_bytes=VMEM_BYTES, collective_id=0, has_side_effects=True
        ),
        name="grad_reduce",
    )(*sources, extras)


def other_core(block, dp):
    return lax.ppermute(block, "dp", [(at, at ^ 1) for at in range(dp)])


def per_device(
    text_rows,
    memory_init,
    cotangent,
    w_qkv,
    w_out,
    w_in,
    w_hid,
    biases,
    norm_gains,
    boundaries,
    mem_resets,
    seg_counts,
):
    items, segs, text_len, width = text_rows.shape
    mem_rows = memory_init.shape[0]
    rows = text_len + 2 * mem_rows
    half = width // 2
    dp = lax.axis_size("dp")
    vector_len = biases.shape[1]

    blocks = (w_qkv, w_out, w_in, w_hid)
    vec = jnp.concatenate([biases[0], norm_gains[0]])
    vec = jnp.pad(vec, (0, 16 * width - vec.shape[0])).reshape(16, width)
    filler = jnp.full((items, segs, mem_rows), -1, jnp.int32)
    labels = jnp.concatenate([filler, jnp.cumsum(boundaries, axis=-1), filler], axis=-1)

    def flags(values):
        return jnp.broadcast_to(values.astype(jnp.int32).reshape(-1, 1, 1), (items * segs, 1, width))

    live = flags(jnp.arange(segs)[None] < seg_counts[:, None])
    fresh = flags((jnp.arange(segs)[None] == 0) | (mem_resets > 0))
    text = jnp.pad(text_rows, ((0, 0), (0, 0), (mem_rows, mem_rows), (0, 0)))
    start = memory_init.astype(F32)
    init = jnp.stack(
        [jnp.pad(start, ((0, 16 - mem_rows), (0, 0))), jnp.pad(start, ((16 - mem_rows, 0), (0, 0)))]
    )

    steps = 2 * items * segs
    if dp == 8:
        saved, activations, weights, vecs = gather_forward(text, fresh, live, init, labels, blocks, vec)
    else:
        weights, vecs = gather_apart(blocks, vec)
        saved, activations = forward_steps(text, fresh, live, init, labels, weights, vecs)
    grads, sums, input_grads, memory_grad = backward_steps(
        cotangent, fresh, live, labels, weights, vecs, saved
    )
    saved.update(grads)

    lanes = 4 * width // dp
    memory_part = memory_grad[16 - mem_rows :].reshape(-1)
    memory_len = -(-memory_part.shape[0] // lanes) * lanes
    memory_part = jnp.pad(memory_part, (0, memory_len - memory_part.shape[0]))
    vector_part = vector_len // dp
    gain_part = width // dp
    used = memory_len + vector_part + gain_part
    extra_rows = -(-used // (3 * 16 * lanes)) * 16
    extras = []
    for layer in range(2):
        total = sums.reshape(steps // 2, 2, 12 * width)[:, layer].sum(axis=0)
        gain_two, shift_two, bias_hid, gain_one, shift_one, bias_o, bias_q, bias_v = [
            total[at * width : (at + 1) * width] for at in range(8)
        ]
        vector = jnp.concatenate(
            [bias_q, bias_v, bias_o, shift_one, total[8 * width :], bias_hid, shift_two]
        ).reshape(2, dp, vector_part)
        gain = jnp.stack([gain_one, gain_two]).reshape(2, dp, gain_part)
        extra = jnp.concatenate(
            [jnp.broadcast_to(memory_part, (2, dp, memory_len)), vector, gain], axis=-1
        )
        extra = jnp.pad(extra, ((0, 0), (0, 0), (0, 3 * extra_rows * lanes - used)))
        extra = extra.reshape(2, dp // 2, 2, 3, extra_rows, lanes).transpose(3, 2, 1, 0, 4, 5)
        extras.append(extra.astype(BF16))
    extras = jnp.stack(extras)
    reduce = grad_reduce
    if padded_bytes(grad_reduce_shapes(dp, steps, rows, width, extra_rows)) > 60 * 2**20:
        reduce = grad_reduce_apart
    *grads, flat = reduce(dp, saved, extras)
    flat = flat.reshape(-1)
    return (
        activations,
        input_grads,
        flat[: mem_rows * width].reshape(mem_rows, width),
        *grads,
        flat[memory_len : memory_len + vector_part][None],
        flat[memory_len + vector_part : used][None],
    )


def grad_reduce_apart(dp, saved, extras):
    wires = [weight_grads(layer, dp, saved, extras[layer]) for layer in range(2)]
    mine = jnp.stack([wires[0][0], wires[1][0]])
    theirs = other_core(jnp.stack([wires[0][1], wires[1][1]]), dp)
    both = mine.astype(F32) + theirs.astype(F32)
    both = both.transpose(3, 0, 2, 1, 4, 5).astype(BF16)
    tall, lanes = both.shape[-2:]
    both = both.reshape(4, dp // 2, 3, tall, lanes)
    own = lax.psum_scatter(both, "section", scatter_dimension=0, tiled=True)[0]
    groups = [[2 * at + side for at in range(dp // 2)] for side in range(2)]
    own = lax.psum_scatter(
        own, "dp", scatter_dimension=0, axis_index_groups=groups, tiled=True
    )[0].astype(F32)
    half = tall - extras.shape[5]
    thin = lanes // 4
    body = own[:, :half]
    hid = body[2].reshape(half, 4, thin).transpose(1, 0, 2).reshape(4 * half, thin)
    return (
        body[0, :, : 3 * thin][None],
        body[0, :, 3 * thin :][None],
        body[1][None],
        hid[None],
        own[:, half:],
    )


def solution(mesh):
    in_specs = (
        P(("section", "dp"), None, None, None),
        P(),
        P(("section", "dp"), None, None, None),
        P("section", None, None),
        P("section", None, None),
        P("section", None, None),
        P("section", None, None),
        P("section", None),
        P("section", None),
        P(("section", "dp"), None, None),
        P(("section", "dp"), None),
        P(("section", "dp")),
    )
    out_specs = (
        P(("section", "dp"), None, None, None),
        P(("section", "dp"), None, None, None),
        P(),
        P("section", None, "dp"),
        P("section", None, "dp"),
        P("section", None, "dp"),
        P("section", None, "dp"),
        P("section", "dp"),
        P("section", "dp"),
    )
    return jax.shard_map(
        per_device, mesh=mesh, in_specs=in_specs, out_specs=out_specs, check_vma=False
    )
```

```python
import functools

import jax
import jax.numpy as jnp
from jax import lax
from jax.experimental import pallas as pl
from jax.experimental.pallas import tpu as pltpu
from jax.sharding import PartitionSpec as P

HEADS = 12
HEAD_DIM = 64
EPS = 1e-05
MASKED = -1e30
VMEM_BYTES = 63 * 2**20
F32 = jnp.float32
BF16 = jnp.bfloat16
MESH = pl.DeviceIdType.MESH


def dot_nn(one, two):
    return jnp.dot(one, two, preferred_element_type=F32)


def dot_nt(one, two):
    return lax.dot_general(one, two, (((1,), (1,)), ((), ())), preferred_element_type=F32)


def dot_tn(one, two):
    return lax.dot_general(one, two, (((0,), (0,)), ((), ())), preferred_element_type=F32)


def weight_tile(refs, kind, tile, layer):
    qkv_ref, in_ref, end_ref = refs
    quarters, _, _, _, tall, width = end_ref.shape
    thin = tall // 5
    if kind == "out":
        pieces = [
            end_ref[quarter, core, half, layer, 0:thin]
            for half in range(2)
            for quarter in range(quarters)
            for core in range(2)
        ]
    elif kind == "hid":
        pieces = [
            end_ref[(tile % 2) * (quarters // 2) + at, core, tile // 2, layer, thin:tall]
            for at in range(quarters // 2)
            for core in range(2)
        ]
    else:
        ref = qkv_ref if kind == "qkv" else in_ref
        at = tile * width if isinstance(tile, int) else pl.multiple_of(tile * width, width)
        pieces = [ref[core, half, layer, :, pl.ds(at, width)] for half in range(2) for core in range(2)]
    return jnp.concatenate(pieces, axis=0)


def weight_specs(shapes, layer_of):
    specs = []
    for shape in shapes:
        lead = len(shape) - 3
        block = shape[:lead] + (1,) + shape[lead + 1 :]
        specs.append(
            pl.BlockSpec(block, lambda t, *_, lead=lead: (0,) * lead + (layer_of(t), 0, 0))
        )
    return specs


def head_lanes(shape, head):
    lanes = lax.broadcasted_iota(jnp.int32, shape, 1)
    return (lanes // HEAD_DIM) == head


def erf_parts(values):
    density = jnp.exp(-0.5 * values * values) * 0.3989422804014327
    phi = 0.5 * (1.0 + lax.erf(values * 0.7071067811865476))
    return phi, density


def vector_rows(vec_ref, layer, width):
    row = lambda half, at: vec_ref[half, layer, :, at * width : (at + 1) * width]
    return dict(
        bias_q=row(0, 0), bias_v=row(0, 1), bias_o=row(0, 2), shift_one=row(0, 3),
        bias_in=(row(0, 4), row(1, 0), row(1, 1), row(1, 2)),
        bias_hid=row(1, 3), shift_two=row(1, 4), gain_one=row(0, 5), gain_two=row(1, 5),
    )


def ones_where(shape, condition):
    rows = lax.broadcasted_iota(jnp.int32, shape, 0)
    columns = lax.broadcasted_iota(jnp.int32, shape, 1)
    return condition(rows, columns).astype(BF16)


def document_bias(bounds, rows, mem):
    text = bounds.shape[1]
    eight = jnp.broadcast_to(bounds, (8, text)).astype(BF16)
    upto = ones_where((text, rows), lambda r, c: r <= c - mem)
    below = ones_where((rows, text), lambda r, c: c <= r - mem)
    columns = dot_nn(eight, upto)[0:1]
    lines = dot_nt(below, eight)[:, 0:1]
    place = lax.broadcasted_iota(jnp.int32, (1, rows), 1)
    columns = jnp.where((place < mem) | (place >= mem + text), -1.0, columns)
    place = lax.broadcasted_iota(jnp.int32, (rows, 1), 0)
    lines = jnp.where((place < mem) | (place >= mem + text), -1.0, lines)
    allowed = (lines == columns) | (lines < 0) | (columns < 0)
    return jnp.where(allowed, 0.0, MASKED)


def norm_forward(values):
    offset = values - jnp.mean(values, axis=-1, keepdims=True)
    scale = lax.rsqrt(jnp.mean(offset * offset, axis=-1, keepdims=True) + EPS)
    return offset * scale, scale


def forward_layer(
    step, segs, at_layer, before_mix, before_out, resets_ref, counts_ref, text_ref, init_ref,
    bounds_ref, weights, vec_ref,
    x_ref, mixed_ref, heads_ref, hat_one_ref, first_ref, active_ref, slope_ref, hat_two_ref,
    stats_ref, acts_ref, y_scr, bias_scr, sum_scr, bias_in_scr,
):
    rows, width = y_scr.shape
    text_len, mem = text_ref.shape[2], init_ref.shape[0]
    layer, seg, item = step % 2, (step // 2) % segs, step // (2 * segs)

    @pl.when(layer == 0)
    def _():
        fresh = (seg == 0) | (resets_ref[item, seg] > 0)
        place = ones_where((rows, text_len), lambda r, c: r - mem == c)
        start = ones_where((rows, mem), lambda r, c: (r == c) | (r - mem - text_len == c))
        again = ones_where(
            (rows, rows),
            lambda r, c: ((r < mem) & (r + mem + text_len == c)) | ((r >= mem + text_len) & (r == c)),
        )
        memory = jnp.where(fresh, dot_nn(start, init_ref[...]), dot_nn(again, y_scr[...]))
        x_ref[0] = (dot_nn(place, text_ref[0, 0]) + memory).astype(BF16)
        bias_scr[...] = document_bias(bounds_ref[0, pl.ds(seg, 1), :], rows, mem)

    @pl.when(layer == 1)
    def _():
        x_ref[0] = y_scr[...]

    before_mix()
    vec = vector_rows(vec_ref, at_layer, width)
    for part in range(4):
        bias_in_scr[part] = vec["bias_in"][part]
    inputs = x_ref[0]
    for tile in range(3):
        mixed = dot_nn(inputs, weight_tile(weights, "qkv", tile, at_layer))
        if tile == 0:
            mixed = mixed + vec["bias_q"]
        if tile == 2:
            mixed = mixed + vec["bias_v"]
        mixed_ref[0, :, tile * width : (tile + 1) * width] = mixed.astype(BF16)

    group = 4 * HEAD_DIM
    stat_lane = lax.broadcasted_iota(jnp.int32, (rows, 128), 1)
    stats = jnp.zeros((rows, 128), F32)
    for number in range(width // group):
        at = number * group
        queries = mixed_ref[0, :, at : at + group] * BF16(HEAD_DIM**-0.5)
        keys = mixed_ref[0, :, width + at : width + at + group]
        values = mixed_ref[0, :, 2 * width + at : 2 * width + at + group]
        total = jnp.zeros((rows, group), F32)
        for head in range(4):
            mine = head_lanes((rows, group), head)
            scores = dot_nt(jnp.where(mine, queries, 0), keys) + bias_scr[...]
            peak = jnp.max(scores, axis=-1, keepdims=True)
            expo = jnp.exp(scores - peak)
            norm = jnp.sum(expo, axis=-1, keepdims=True)
            probs = (expo * (1.0 / norm)).astype(BF16)
            total = total + dot_nn(probs, jnp.where(mine, values, 0))
            stats = jnp.where(stat_lane == number * 4 + head, peak + jnp.log(norm), stats)
        heads_ref[0, :, at : at + group] = total.astype(BF16)
    stats_ref[0] = stats

    before_out()
    attn = dot_nn(heads_ref[0], weight_tile(weights, "out", 0, at_layer)) + vec["bias_o"]
    hat, scale = norm_forward(x_ref[0].astype(F32) + attn)
    hat_one_ref[0] = hat.astype(BF16)
    stats = jnp.where(stat_lane == HEADS, scale, stats_ref[0])
    first = hat * vec["gain_one"] + vec["shift_one"]
    first_ref[0] = first.astype(BF16)
    sum_scr[...] = first + vec["bias_hid"]

    def ff_tile(tile, _):
        at = pl.multiple_of(tile * width, width)
        inner = dot_nn(first_ref[0], weight_tile(weights, "in", tile, at_layer)) + bias_in_scr[tile]
        phi, density = erf_parts(inner)
        active = (inner * phi).astype(BF16)
        active_ref[0, :, pl.ds(at, width)] = active
        slope_ref[0, :, pl.ds(at, width)] = (phi + inner * density).astype(BF16)
        sum_scr[...] += dot_nn(active, weight_tile(weights, "hid", tile, at_layer))
        return _

    lax.fori_loop(0, 4, ff_tile, 0)
    hat, scale = norm_forward(sum_scr[...])
    hat_two_ref[0] = hat.astype(BF16)
    stats_ref[0] = jnp.where(stat_lane == HEADS + 1, scale, stats)
    result = (hat * vec["gain_two"] + vec["shift_two"]).astype(BF16)
    y_scr[...] = result

    @pl.when(layer == 1)
    def _():
        acts_ref[0, 0] = jnp.where(seg < counts_ref[item], result, 0)


def saved_shapes(rows, width):
    return dict(
        x=((rows, width), BF16),
        mixed=((rows, 3 * width), BF16),
        heads=((rows, width), BF16),
        hat_one=((rows, width), BF16),
        first=((rows, width), BF16),
        active=((rows, 4 * width), BF16),
        slope=((rows, 4 * width), BF16),
        hat_two=((rows, width), BF16),
        stats=((rows, 128), F32),
    )


def forward_io(text, resets, counts, init, bounds):
    items, segs, text_len, width = text.shape
    rows = text_len + 2 * init.shape[0]
    steps = 2 * items * segs
    saved = saved_shapes(rows, width)
    by_seg = lambda t: (t // (2 * segs), (t // 2) % segs, 0, 0)
    operands = [resets, counts, text, init, bounds]
    in_specs = [
        pl.BlockSpec(memory_space=pltpu.SMEM),
        pl.BlockSpec(memory_space=pltpu.SMEM),
        pl.BlockSpec((1, 1, text_len, width), by_seg),
        pl.BlockSpec(init.shape, lambda t: (0, 0)),
        pl.BlockSpec((1, segs, text_len), lambda t: (t // (2 * segs), 0, 0)),
    ]
    out_specs = [pl.BlockSpec((1,) + shape, lambda t: (t, 0, 0)) for shape, _ in saved.values()]
    out_specs.append(pl.BlockSpec((1, 1, rows, width), by_seg))
    out_shape = [jax.ShapeDtypeStruct((steps,) + shape, kind) for shape, kind in saved.values()]
    out_shape.append(jax.ShapeDtypeStruct((items, segs, rows, width), BF16))
    scratch = [
        pltpu.VMEM((rows, width), BF16),
        pltpu.VMEM((rows, rows), F32),
        pltpu.VMEM((rows, width), F32),
        pltpu.VMEM((4, 1, width), F32),
    ]
    return steps, saved, operands, in_specs, out_specs, out_shape, scratch


def nothing():
    pass


def forward_body(segs, *refs):
    step = pl.program_id(0)
    y_scr = refs[19]

    @pl.when(step == 0)
    def _():
        y_scr[...] = jnp.zeros_like(y_scr)

    forward_layer(step, segs, 0, nothing, nothing, *refs[:5], refs[5:8], *refs[8:])


def forward_steps(text, resets, counts, init, bounds, weights, vec):
    steps, saved, operands, in_specs, out_specs, out_shape, scratch = forward_io(
        text, resets, counts, init, bounds
    )
    *outs, acts = pl.pallas_call(
        functools.partial(forward_body, text.shape[1]),
        grid=(steps,),
        in_specs=in_specs
        + weight_specs([weight.shape for weight in weights], lambda t: t % 2)
        + [pl.BlockSpec((2, 1) + vec.shape[2:], lambda t: (0, t % 2, 0, 0))],
        out_specs=out_specs,
        out_shape=out_shape,
        scratch_shapes=scratch,
        compiler_params=pltpu.CompilerParams(vmem_limit_bytes=VMEM_BYTES),
        name="forward_steps",
    )(*operands, *weights, vec)
    return dict(zip(saved, outs)), acts


def norm_backward(grad, hat, scale, gain):
    scaled = grad * gain
    mean_one = jnp.mean(scaled, axis=-1, keepdims=True)
    mean_two = jnp.mean(scaled * hat, axis=-1, keepdims=True)
    return (scaled - mean_one - hat * mean_two) * scale


def column_sum(values):
    return jnp.sum(values, axis=0, keepdims=True)


def backward_body(
    count, segs, mem, resets_ref, counts_ref, cot_ref, bounds_ref, acts_ref, qkv_ref, in_ref, end_ref,
    vec_ref, mixed_ref, heads_ref, hat_one_ref, slope_ref, hat_two_ref, stats_ref,
    branch_ref, inner_ref, attn_ref, mix_ref, sums_ref, inputs_ref, init_ref, acts_out_ref,
    g_scr, carry_scr, bias_scr, sum_scr, go_scr,
):
    step = count - 1 - pl.program_id(0)
    layer = step % 2
    seg = (step // 2) % segs
    rows, width = g_scr.shape
    item = step // (2 * segs)
    weights = (qkv_ref, in_ref, end_ref)
    vec = vector_rows(vec_ref, 0, width)
    gain_one, gain_two = vec["gain_one"], vec["gain_two"]

    @pl.when(pl.program_id(0) == 0)
    def _():
        carry_scr[...] = jnp.zeros_like(carry_scr)
        init_ref[...] = jnp.zeros_like(init_ref)

    @pl.when(layer == 1)
    def _():
        acts_out_ref[...] = acts_ref[...]
        bias_scr[...] = document_bias(bounds_ref[0, pl.ds(seg, 1), :], rows, mem)
        cot = jnp.where(seg < counts_ref[item], cot_ref[0, 0], 0)
        g_scr[...] = cot
        carried = jnp.where(seg == segs - 1, 0.0, carry_scr[...])
        g_scr[rows - 16 : rows, :] = (cot[rows - 16 : rows].astype(F32) + carried).astype(BF16)

    stats = stats_ref[0]
    scale_one = stats[:, HEADS : HEADS + 1]
    scale_two = stats[:, HEADS + 1 : HEADS + 2]
    grad = g_scr[...].astype(F32)
    hat = hat_two_ref[0].astype(F32)
    sums_ref[0, :, 0:width] = column_sum(grad * hat)
    sums_ref[0, :, width : 2 * width] = column_sum(grad)
    grad_second = norm_backward(grad, hat, scale_two, gain_two)
    branch = grad_second.astype(BF16)
    branch_ref[0] = branch
    sums_ref[0, :, 2 * width : 3 * width] = column_sum(branch.astype(F32))
    sum_scr[...] = grad_second

    def ff_tile(tile, _):
        at = pl.multiple_of(tile * width, width)
        active = dot_nt(branch, weight_tile(weights, "hid", tile, 0))
        inner = (active * slope_ref[0, :, pl.ds(at, width)].astype(F32)).astype(BF16)
        inner_ref[0, :, pl.ds(at, width)] = inner
        sums_ref[0, :, pl.ds(8 * width + at, width)] = column_sum(inner.astype(F32))
        sum_scr[...] += dot_nt(inner, weight_tile(weights, "in", tile, 0))
        return _

    lax.fori_loop(0, 4, ff_tile, 0)
    grad = sum_scr[...]
    hat = hat_one_ref[0].astype(F32)
    sums_ref[0, :, 3 * width : 4 * width] = column_sum(grad * hat)
    sums_ref[0, :, 4 * width : 5 * width] = column_sum(grad)
    resid = norm_backward(grad, hat, scale_one, gain_one)
    sum_scr[...] = resid
    attn = resid.astype(BF16)
    attn_ref[0] = attn
    sums_ref[0, :, 5 * width : 6 * width] = column_sum(attn.astype(F32))
    go = dot_nt(attn, weight_tile(weights, "out", 0, 0)).astype(BF16)
    go_scr[...] = go
    product = go.astype(F32) * heads_ref[0].astype(F32)
    high = product.astype(BF16)
    low = (product - high.astype(F32)).astype(BF16)
    picks = (
        lax.broadcasted_iota(jnp.int32, (16, width), 1) // HEAD_DIM
        == lax.broadcasted_iota(jnp.int32, (16, width), 0)
    ).astype(BF16)
    centres = dot_nt(picks, high) + dot_nt(picks, low)
    logs = jnp.transpose(stats)

    group = 4 * HEAD_DIM
    for number in range(width // group):
        at = number * group
        queries = mixed_ref[0, :, at : at + group] * BF16(HEAD_DIM**-0.5)
        keys = mixed_ref[0, :, width + at : width + at + group]
        values = mixed_ref[0, :, 2 * width + at : 2 * width + at + group]
        outs = go_scr[:, at : at + group]
        grad_q = jnp.zeros((rows, group), F32)
        grad_k = jnp.zeros((rows, group), F32)
        grad_v = jnp.zeros((rows, group), F32)
        for head in range(4):
            mine = head_lanes((rows, group), head)
            row = number * 4 + head
            keys_h = jnp.where(mine, keys, 0)
            scores = dot_nt(keys_h, queries) + bias_scr[...]
            probs = jnp.exp(scores - logs[row : row + 1, :])
            grad_p = dot_nt(jnp.where(mine, values, 0), outs)
            grad_s = (probs * (grad_p - centres[row : row + 1, :])).astype(BF16)
            grad_v = grad_v + dot_nn(probs.astype(BF16), jnp.where(mine, outs, 0))
            grad_k = grad_k + dot_nn(grad_s, jnp.where(mine, queries, 0))
            grad_q = grad_q + dot_tn(grad_s, keys_h)
        mix_ref[0, :, at : at + group] = (grad_q * HEAD_DIM**-0.5).astype(BF16)
        mix_ref[0, :, width + at : width + at + group] = grad_k.astype(BF16)
        mix_ref[0, :, 2 * width + at : 2 * width + at + group] = grad_v.astype(BF16)

    sums_ref[0, :, 6 * width : 7 * width] = column_sum(mix_ref[0, :, 0:width].astype(F32))
    sums_ref[0, :, 7 * width : 8 * width] = column_sum(mix_ref[0, :, 2 * width : 3 * width].astype(F32))
    total = sum_scr[...]
    for tile in range(3):
        total = total + dot_nt(
            mix_ref[0, :, tile * width : (tile + 1) * width], weight_tile(weights, "qkv", tile, 0)
        )
    result = total.astype(BF16)
    g_scr[...] = result

    @pl.when(layer == 0)
    def _():
        inputs_ref[0, 0] = result
        fresh = (seg == 0) | (resets_ref[item, seg] > 0)
        number = lax.broadcasted_iota(jnp.int32, (16, width), 0)
        folded = result[rows - 16 : rows].astype(F32) + pltpu.roll(
            result[0:16].astype(F32), 16 - mem, 0
        )
        folded = jnp.where(number >= 16 - mem, folded, 0.0).astype(BF16).astype(F32)
        init_ref[...] += jnp.where(fresh, folded, 0.0)
        carry_scr[...] = jnp.where(fresh, 0.0, folded)


def backward_steps(cot, resets, counts, bounds, mem, acts, weights, vec, saved):
    items, segs, rows, width = cot.shape
    steps = 2 * items * segs
    at = lambda t: steps - 1 - t
    by_seg = lambda t: (at(t) // (2 * segs), (at(t) // 2) % segs, 0, 0)
    by_step = lambda t: (at(t), 0, 0)
    names = ("mixed", "heads", "hat_one", "slope", "hat_two", "stats")
    outs = dict(
        branch=(rows, width), inner=(rows, 4 * width), attn=(rows, width), mix=(rows, 3 * width),
    )
    *grads, sums, inputs, memory, acts = pl.pallas_call(
        functools.partial(backward_body, steps, segs, mem),
        grid=(steps,),
        in_specs=[
            pl.BlockSpec(memory_space=pltpu.SMEM),
            pl.BlockSpec(memory_space=pltpu.SMEM),
            pl.BlockSpec((1, 1, rows, width), by_seg),
            pl.BlockSpec((1,) + bounds.shape[1:], lambda t: (at(t) // (2 * segs), 0, 0)),
            pl.BlockSpec((1, 1, rows, width), by_seg),
        ]
        + weight_specs([weight.shape for weight in weights], lambda t: at(t) % 2)
        + [pl.BlockSpec((2, 1) + vec.shape[2:], lambda t: (0, at(t) % 2, 0, 0))]
        + [pl.BlockSpec((1,) + saved[name].shape[1:], by_step) for name in names],
        out_specs=[pl.BlockSpec((1,) + shape, by_step) for shape in outs.values()]
        + [
            pl.BlockSpec((1, 1, 12 * width), by_step),
            pl.BlockSpec((1, 1, rows, width), by_seg),
            pl.BlockSpec((16, width), lambda t: (0, 0)),
            pl.BlockSpec((1, 1, rows, width), by_seg),
        ],
        out_shape=[jax.ShapeDtypeStruct((steps,) + shape, BF16) for shape in outs.values()]
        + [
            jax.ShapeDtypeStruct((steps, 1, 12 * width), F32),
            jax.ShapeDtypeStruct(cot.shape, BF16),
            jax.ShapeDtypeStruct((16, width), F32),
            jax.ShapeDtypeStruct(cot.shape, BF16),
        ],
        scratch_shapes=[
            pltpu.VMEM((rows, width), BF16),
            pltpu.VMEM((16, width), F32),
            pltpu.VMEM((rows, rows), F32),
            pltpu.VMEM((rows, width), F32),
            pltpu.VMEM((rows, width), BF16),
        ],
        compiler_params=pltpu.CompilerParams(vmem_limit_bytes=VMEM_BYTES),
        name="backward_steps",
    )(resets, counts, cot, bounds, acts, *weights, vec, *[saved[name] for name in names])
    return dict(zip(outs, grads)), sums, inputs, memory, acts


def gather_forward_body(steps, segs, *refs):
    io = refs[:5]
    qkv_src, in_src, out_src, hid_src, vec_src = refs[5:10]
    outs = refs[10:20]
    full_outs = refs[20:24]
    forward_scratch = refs[24:28]
    weights = refs[28:31]
    vec = refs[31]
    (
        load_sems, end_load_sems, store_sems, x_sems, y_sems, fx_sems, fy_sems, core_sems, end_sems,
        line_core_sems, up_sems, down_sems, vec_sems, vec_load_sem,
    ) = refs[32:]
    step = pl.program_id(0)
    section, place = lax.axis_index("section"), lax.axis_index("dp")
    x, y = section % 2, section // 2
    core, z = place % 2, place // 2
    end = weights[2]
    depth, _, _, _, tall, _ = end.shape
    thin = tall // 5
    x_dev = (y * 2 + 1 - x, place)
    y_dev = ((1 - y) * 2 + x, place)
    core_dev = (section, z * 2 + 1 - core)
    up_dev = (section, (z + 1) % depth * 2 + core)
    down_dev = (section, (z + depth - 1) % depth * 2 + core)
    own_block = (y, x)
    blocks = ((y, 1 - x), (1 - y, x), (1 - y, 1 - x))

    def remote(source, target, sems, index, device):
        return pltpu.make_async_remote_copy(
            src_ref=source, dst_ref=target, send_sem=sems.at[(0, *index)], recv_sem=sems.at[(1, *index)],
            device_id=device, device_id_type=MESH,
        )


    def part_of(number, block, part):
        rows = weights[number].shape[-2] // 2
        return weights[number].at[core, block[0], block[1], pl.ds(part * rows, rows)]

    def own_part(number, part):
        rows = weights[number].shape[-2] // 2
        at = pl.multiple_of((core * 2 + part) * rows, rows)
        return (qkv_src, in_src)[number].at[0, pl.ds(at, rows)]

    def x_copy(number, part):
        return remote(own_part(number, part), part_of(number, own_block, part), x_sems, (number, part), x_dev)

    def y_copy(number, part):
        return remote(own_part(number, part), part_of(number, own_block, part), y_sems, (number, part), y_dev)

    def fy_copy(number):
        piece = part_of(number, blocks[0], 0)
        return remote(piece, piece, fy_sems, (number,), y_dev)

    def fx_copy(number):
        piece = part_of(number, blocks[1], 1)
        return remote(piece, piece, fx_sems, (number,), x_dev)

    def core_copy(number, kind, part):
        piece = part_of(number, blocks[kind], part)
        return remote(piece, piece, core_sems, (number, kind, part), core_dev)


    def eighth(at, block, first=0, rows=None):
        view = end.at[at, core, block[0], block[1]]
        return view if rows is None else view.at[pl.ds(first, rows)]

    def own_eighth(first):
        source, rows = (out_src, thin) if first == 0 else (hid_src, tall - thin)
        return source.at[0, pl.ds(pl.multiple_of((z * 2 + core) * rows, rows), rows)]

    def end_copy(axis, first):
        rows = thin if first == 0 else tall - thin
        return remote(
            own_eighth(first), eighth(z, own_block, first, rows), end_sems, (axis, 0 if first == 0 else 1),
            (x_dev, y_dev)[axis],
        )

    low = tall // 32 * 16

    def end_fy_copy():
        piece = eighth(z, blocks[0], 0, low)
        return remote(piece, piece, fy_sems, (2,), y_dev)

    def end_fx_copy():
        piece = eighth(z, blocks[1], low, tall - low)
        return remote(piece, piece, fx_sems, (2,), x_dev)

    def line_core_copy(at, kind):
        piece = eighth(at, blocks[kind])
        return remote(piece, piece, line_core_sems, (at, kind), core_dev)

    def up_copy(at, kind):
        piece = eighth(at, blocks[kind])
        return remote(piece, piece, up_sems, (at, kind), up_dev)

    def down_copy(at, kind):
        piece = eighth(at, blocks[kind])
        return remote(piece, piece, down_sems, (at, kind), down_dev)

    def vec_copy(kind):
        block = (own_block, own_block, blocks[0])[kind]
        source = vec_src if kind < 2 else vec.at[block]
        return remote(source, vec.at[block], vec_sems, (kind,), (x_dev, y_dev, y_dev)[kind])

    def loads():
        copies = []
        for number, source in enumerate((qkv_src, in_src)):
            rows = weights[number].shape[-2]
            for side in range(2):
                copies.append(
                    pltpu.make_async_copy(
                        source.at[0, pl.ds(side * rows, rows)], weights[number].at[side, y, x],
                        load_sems.at[number, side],
                    )
                )
        for at in range(depth):
            for side in range(2):
                for number, (source, first, rows) in enumerate(
                    ((out_src, 0, thin), (hid_src, thin, tall - thin))
                ):
                    copies.append(
                        pltpu.make_async_copy(
                            source.at[0, pl.ds((at * 2 + side) * rows, rows)],
                            end.at[at, side, y, x, pl.ds(first, rows)],
                            end_load_sems.at[at, side, number],
                        )
                    )
        return copies + [pltpu.make_async_copy(vec_src, vec.at[y, x], vec_load_sem)]

    def full_stores():
        return [
            pltpu.make_async_copy(source, target, store_sems.at[number])
            for number, (source, target) in enumerate(zip((*weights, vec), full_outs))
        ]

    def spread(kind):
        @pl.when(z < depth - 1)
        def _():
            up_copy(z, kind).start()

        @pl.when(z > 0)
        def _():
            down_copy(z, kind).start()

        line_core_copy(z, kind).start()

    def hop(distance):
        for kind in range(3):

            @pl.when(z >= distance)
            def _():
                up_copy(z - distance, kind).wait_recv()

                @pl.when(z < depth - 1)
                def _():
                    up_copy(z - distance, kind).start()

                line_core_copy(z - distance, kind).start()

            @pl.when(z + distance < depth)
            def _():
                down_copy(z + distance, kind).wait_recv()

                @pl.when(z > 0)
                def _():
                    down_copy(z + distance, kind).start()

                line_core_copy(z + distance, kind).start()

    def near(number):
        x_copy(number, 0).wait_recv()
        fy_copy(number).start()
        core_copy(number, 0, 0).start()
        y_copy(number, 1).wait_recv()
        fx_copy(number).start()
        core_copy(number, 1, 1).start()

    def rest(number):
        x_copy(number, 1).wait_recv()
        core_copy(number, 0, 1).start()
        y_copy(number, 0).wait_recv()
        core_copy(number, 1, 0).start()

    def diagonal(number):
        fy_copy(number).wait_recv()
        core_copy(number, 2, 0).start()
        fx_copy(number).wait_recv()
        core_copy(number, 2, 1).start()

    def complete(number):
        for kind in range(3):
            for part in range(2):
                core_copy(number, kind, part).wait_recv()

    def before_mix():
        @pl.when(step == 0)
        def _():
            barrier = pltpu.get_barrier_semaphore()
            for device in (x_dev, y_dev, core_dev):
                pl.semaphore_signal(barrier, inc=1, device_id=device, device_id_type=MESH)

            @pl.when(z < depth - 1)
            def _():
                pl.semaphore_signal(barrier, inc=1, device_id=up_dev, device_id_type=MESH)

            @pl.when(z > 0)
            def _():
                pl.semaphore_signal(barrier, inc=1, device_id=down_dev, device_id_type=MESH)

            pl.semaphore_wait(barrier, 3 + jnp.where(z > 0, 1, 0) + jnp.where(z < depth - 1, 1, 0))
            for first in (0, thin):
                end_copy(0, first).start()
                end_copy(1, first).start()
            vec_copy(0).start()
            vec_copy(1).start()
            x_copy(0, 0).start()
            y_copy(0, 1).start()
            x_copy(0, 1).start()
            y_copy(0, 0).start()
            for copy in loads():
                copy.start()
            for axis in range(2):
                for first in (0, thin):
                    end_copy(axis, first).wait_recv()
                (end_fy_copy, end_fx_copy)[axis]().start()
                spread(axis)
            vec_copy(0).wait_recv()
            vec_copy(2).start()
            end_fy_copy().wait_recv()
            end_fx_copy().wait_recv()
            spread(2)
            near(0)
            x_copy(1, 0).start()
            y_copy(1, 1).start()
            rest(0)
            x_copy(1, 1).start()
            y_copy(1, 0).start()
            hop(1)
            diagonal(0)
            vec_copy(1).wait_recv()
            vec_copy(2).wait_recv()
            complete(0)
            for copy in loads():
                copy.wait()

    def before_out():
        @pl.when(step == 0)
        def _():
            near(1)
            hop(2)
            rest(1)
            diagonal(1)
            hop(3)
            complete(1)
            for at in range(depth):
                for kind in range(3):
                    line_core_copy(at, kind).wait_recv()

        @pl.when(step == 1)
        def _():
            for copy in full_stores():
                copy.start()

    @pl.when(step == 0)
    def _():
        forward_scratch[0][...] = jnp.zeros_like(forward_scratch[0])

    forward_layer(
        step, segs, step % 2, before_mix, before_out, *io, weights, vec, *outs, *forward_scratch
    )

    @pl.when(step == steps - 1)
    def _():
        for copy in full_stores():
            copy.wait()
        for number in range(2):
            for part in range(2):
                x_copy(number, part).wait_send()
                y_copy(number, part).wait_send()
                for kind in range(3):
                    core_copy(number, kind, part).wait_send()
            fx_copy(number).wait_send()
            fy_copy(number).wait_send()
            for first in (0, thin):
                end_copy(number, first).wait_send()
        end_fx_copy().wait_send()
        end_fy_copy().wait_send()
        for kind in range(3):
            vec_copy(kind).wait_send()
            for at in range(depth):
                line_core_copy(at, kind).wait_send()

                @pl.when((z >= at) & (z < depth - 1))
                def _():
                    up_copy(at, kind).wait_send()

                @pl.when((z <= at) & (z > 0))
                def _():
                    down_copy(at, kind).wait_send()


def full_weight_shapes(w_qkv, w_out, w_in, w_hid):
    half, width = w_out.shape[1:]
    return [(2, 2, 2, half // 2, block.shape[2]) for block in (w_qkv, w_in)] + [
        (4, 2, 2, 2, (half + w_hid.shape[1]) // 8, width)
    ]


def gather_forward(text, resets, counts, init, bounds, blocks, vec):
    steps, saved, operands, in_specs, out_specs, out_shape, scratch = forward_io(
        text, resets, counts, init, bounds
    )
    shapes = full_weight_shapes(*blocks)
    full = [pltpu.VMEM(shape, BF16) for shape in shapes] + [pltpu.VMEM((2, 2) + vec.shape, F32)]
    any_spec = pl.BlockSpec(memory_space=pl.ANY)
    dma = pltpu.SemaphoreType.DMA
    depth = shapes[2][0]
    *outs, acts, qkv, w_in, end, vecs = pl.pallas_call(
        functools.partial(gather_forward_body, steps, text.shape[1]),
        grid=(steps,),
        in_specs=in_specs + [any_spec] * 5,
        out_specs=out_specs + [any_spec] * 4,
        out_shape=out_shape + [jax.ShapeDtypeStruct(ref.shape, ref.dtype) for ref in full],
        scratch_shapes=scratch
        + full
        + [
            dma((2, 2)), dma((depth, 2, 2)), dma((4,)), dma((2, 2, 2)), dma((2, 2, 2)), dma((2, 3)),
            dma((2, 3)), dma((2, 2, 3, 2)), dma((2, 2, 2)), dma((2, depth, 3)), dma((2, depth, 3)),
            dma((2, depth, 3)), dma((2, 3)), dma,
        ],
        compiler_params=pltpu.CompilerParams(
            vmem_limit_bytes=VMEM_BYTES, collective_id=1, has_side_effects=True
        ),
        name="gather_forward",
    )(*operands, blocks[0], blocks[2], blocks[1], blocks[3], vec)
    return dict(zip(saved, outs)), acts, (qkv, w_in, end), vecs


def gather_apart(blocks, vec):
    w_qkv, w_out, w_in, w_hid = [
        lax.all_gather(block[0], "section").reshape(2, 2, *block.shape[1:]) for block in blocks
    ]
    half, width = w_out.shape[2:]
    full = [
        block.reshape(2, 2, 2, half // 2, -1).transpose(2, 0, 1, 3, 4) for block in (w_qkv, w_in)
    ]
    ends = [block.reshape(2, 2, 4, 2, -1, width).transpose(2, 3, 0, 1, 4, 5) for block in (w_out, w_hid)]
    vecs = lax.all_gather(vec, "section").reshape(2, 2, *vec.shape)
    return (*full, jnp.concatenate(ends, axis=4)), vecs


GRAD_NAMES = ("first", "inner", "active", "branch", "x", "mix", "heads", "attn")


def weight_grad_body(
    layer, segs_all, dp, *refs,
):
    sources = refs[:8]
    extra_ref, mine_ref, theirs_ref = refs[8:11]
    held = refs[11:19]
    wire, in_sems, extra_sem, out_sems = refs[19:23]
    core = lax.axis_index("dp") % 2
    rows = sources[0].shape[1]
    width = sources[0].shape[2]
    half = width // 2
    lanes = wire.shape[-1]
    thin = width // dp
    wide = 3 * thin

    def loads(number):
        return [
            pltpu.make_async_copy(
                sources[number].at[2 * at + layer],
                held[number].at[pl.ds(at * rows, rows)],
                in_sems.at[number, at],
            )
            for at in range(segs_all)
        ]

    for number in range(8):
        for copy in loads(number):
            copy.start()
    extra = pltpu.make_async_copy(extra_ref, wire.at[:, :, :, :, pl.ds(half, extra_ref.shape[4])], extra_sem)
    extra.start()

    def ready(*numbers):
        for number in numbers:
            for copy in loads(number):
                copy.wait()

    def stores(kind):
        return [
            pltpu.make_async_copy(wire.at[kind, core], mine_ref.at[kind], out_sems.at[kind, 0]),
            pltpu.make_async_copy(wire.at[kind, 1 - core], theirs_ref.at[kind], out_sems.at[kind, 1]),
        ]

    first, inner, active, branch, inputs, mix, heads, attn = held
    extra.wait()

    ready(0, 1)
    per_tile = width // lanes

    def in_tile(tile, _):
        right = inner[:, pl.ds(pl.multiple_of(tile * width, width), width)]
        for side in range(2):
            result = dot_tn(first[:, side * half : (side + 1) * half], right).astype(BF16)
            for at in range(per_tile):
                wire[1, at % 2, tile * (per_tile // 2) + at // 2, side, 0:half, :] = result[
                    :, at * lanes : (at + 1) * lanes
                ]
        return _

    lax.fori_loop(0, 4, in_tile, 0)
    for copy in stores(1):
        copy.start()

    ready(2, 3)
    def hid_tile(side, _):
        for part in range(4):
            left = active[:, pl.ds(pl.multiple_of(side * 4 * half + part * half, half), half)]
            result = dot_tn(left, branch[...]).astype(BF16)
            for at in range(dp):
                wire[2, at % 2, at // 2, side, 0:half, part * thin : (part + 1) * thin] = result[
                    :, at * thin : (at + 1) * thin
                ]
        return _
    lax.fori_loop(0, 2, hid_tile, 0)
    for copy in stores(2):
        copy.start()

    ready(4, 5, 6, 7)
    for side in range(2):
        left = inputs[:, side * half : (side + 1) * half]
        for tile in range(2):
            result = dot_tn(left, mix[:, tile * 3 * half : (tile + 1) * 3 * half]).astype(BF16)
            for at in range(dp // 2):
                place = tile * (dp // 2) + at
                wire[0, place % 2, place // 2, side, 0:half, 0:wide] = result[
                    :, at * wide : (at + 1) * wide
                ]
        result = dot_tn(heads[:, side * half : (side + 1) * half], attn[...]).astype(BF16)
        for at in range(dp):
            wire[0, at % 2, at // 2, side, 0:half, wide:lanes] = result[:, at * thin : (at + 1) * thin]
    for copy in stores(0):
        copy.start()
    for kind in range(3):
        for copy in stores(kind):
            copy.wait()


def weight_grads(layer, dp, saved, extras):
    sources = [saved[name] for name in GRAD_NAMES]
    steps, rows, width = sources[0].shape
    segs_all = steps // 2
    half = width // 2
    lanes = 4 * width // dp
    extra_rows = extras.shape[4]
    kind = jax.ShapeDtypeStruct((3, dp // 2, 2, half + extra_rows, lanes), BF16)
    any_spec = pl.BlockSpec(memory_space=pl.ANY)
    return pl.pallas_call(
        functools.partial(weight_grad_body, layer, segs_all, dp),
        in_specs=[any_spec] * 9,
        out_specs=[any_spec] * 2,
        out_shape=[kind, kind],
        scratch_shapes=[pltpu.VMEM((segs_all * rows, source.shape[2]), BF16) for source in sources]
        + [
            pltpu.VMEM((3, 2, dp // 2, 2, half + extra_rows, lanes), BF16),
            pltpu.SemaphoreType.DMA((8, segs_all)),
            pltpu.SemaphoreType.DMA,
            pltpu.SemaphoreType.DMA((3, 2)),
        ],
        compiler_params=pltpu.CompilerParams(vmem_limit_bytes=VMEM_BYTES),
        name="weight_grads",
    )(*sources, extras)


def add_into(ref, other):
    ref[...] = (ref[...].astype(F32) + other[...].astype(F32)).astype(BF16)


def build_extra(sums_ref, memory_ref, extra):
    steps = sums_ref.shape[0]
    width = memory_ref.shape[1]
    lanes = extra.shape[-1]
    mem = 10
    extra[...] = jnp.zeros_like(extra)
    for layer in range(2):
        total = sums_ref[layer]
        for step in range(layer + 2, steps, 2):
            total = total + sums_ref[step]
        for block, parts in enumerate(((6, 7, 5, 4, 8, 3), (9, 10, 11, 2, 1, 0))):
            for piece in range(width // lanes):
                extra[layer, block, piece * mem : (piece + 1) * mem, :] = memory_ref[
                    16 - mem : 16, piece * lanes : (piece + 1) * lanes
                ]
                for at, part in enumerate(parts):
                    row = mem * (width // lanes) + at * (width // lanes) + piece
                    first = part * width + piece * lanes
                    extra[layer, block, row : row + 1, :] = total[:, first : first + lanes]


def grad_reduce_body(dp, segs_all, *refs):
    sources = refs[:8]
    sums_ref, memory_ref = refs[8:10]
    piece_out = refs[10]
    held = refs[11:19]
    mine, theirs, landed, xp, xq, yq, yp, from_low, from_high = refs[19:28]
    extra = refs[28]
    in_sems, core_sems, free_sem, xp_sems, xq_sems, yq_sems, yp_sems, up_sems, down_sems = refs[29:38]
    section, place = lax.axis_index("section"), lax.axis_index("dp")
    x, y = section % 2, section // 2
    core, z = place % 2, place // 2
    depth = dp // 2
    cut = depth // 2
    rows, width = sources[0].shape[1:]
    half = width // 2
    lanes = mine.shape[-1]
    thin = width // dp
    wide = 3 * thin
    x_dev = (y * 2 + 1 - x, place)
    y_dev = ((1 - y) * 2 + x, place)
    core_dev = (section, z * 2 + 1 - core)
    up_dev = (section, (z + 1) % depth * 2 + core)
    down_dev = (section, (z + depth - 1) % depth * 2 + core)
    kinds = (1, 2, 0)
    used = {1: (0, 1), 2: (2, 3), 0: (4, 5, 6, 7)}
    first, inner, active, branch, inputs, mix, heads, attn = held

    def loads(side, kind):
        layer = (1 - x) if side == 0 else x
        return [
            pltpu.make_async_copy(
                sources[number].at[2 * at + layer],
                held[number].at[pl.ds(at * rows, rows)],
                in_sems.at[number, at],
            )
            for number in used[kind]
            for at in range(segs_all)
        ]

    for kind in kinds:
        for copy in loads(0, kind):
            copy.start()

    build_extra(sums_ref, memory_ref, extra)
    extra_rows = extra.shape[2] // 3
    barrier = pltpu.get_barrier_semaphore()
    for device in (x_dev, y_dev, core_dev):
        pl.semaphore_signal(barrier, inc=1, device_id=device, device_id_type=MESH)

    @pl.when(z < depth - 1)
    def _():
        pl.semaphore_signal(barrier, inc=1, device_id=up_dev, device_id_type=MESH)

    @pl.when(z > 0)
    def _():
        pl.semaphore_signal(barrier, inc=1, device_id=down_dev, device_id_type=MESH)

    pl.semaphore_wait(barrier, 3 + jnp.where(z > 0, 1, 0) + jnp.where(z < depth - 1, 1, 0))

    def remote(source, target, sems, index, device):
        return pltpu.make_async_remote_copy(
            src_ref=source, dst_ref=target, send_sem=sems.at[(0, *index)], recv_sem=sems.at[(1, *index)],
            device_id=device, device_id_type=MESH,
        )

    def core_copy(unit):
        return remote(theirs.at[unit % 2], landed.at[unit % 2], core_sems, (unit,), core_dev)

    def xp_copy(kind):
        return remote(mine.at[0, kind, pl.ds(0, cut)], xp.at[kind], xp_sems, (kind,), x_dev)

    def yq_copy(side, kind):
        return remote(
            mine.at[side, kind, pl.ds(cut, depth - cut), 1 - y], yq.at[side, kind], yq_sems,
            (side, kind), y_dev,
        )

    def xq_copy(kind):
        return remote(mine.at[0, kind, pl.ds(cut, depth - cut), y], xq.at[kind], xq_sems, (kind,), x_dev)

    def yp_copy(kind):
        return remote(mine.at[1, kind, pl.ds(0, cut), 1 - y], yp.at[kind], yp_sems, (kind,), y_dev)

    def up_copy(kind, at):
        return remote(mine.at[1, kind, at, y], from_low.at[kind, at], up_sems, (kind, at), up_dev)

    def down_copy(kind, at):
        return remote(mine.at[1, kind, at, y], from_high.at[kind, at], down_sems, (kind, at), down_dev)

    def multiply(side, kind, unit):
        slot = unit % 2

        def put(at, block, piece, start, stop):
            if isinstance(at, int):
                chunk_core, chunk_z = at % 2, at // 2
            else:
                chunk_core, chunk_z = at

            @pl.when(core == chunk_core)
            def _():
                mine[side, kind, chunk_z, block, 0:half, start:stop] = piece

            @pl.when(core != chunk_core)
            def _():
                theirs[slot, chunk_z, block, 0:half, start:stop] = piece

        if kind == 1:
            per_tile = width // lanes

            def in_tile(tile, _):
                right = inner[:, pl.ds(pl.multiple_of(tile * width, width), width)]
                for block in range(2):
                    result = dot_tn(first[:, block * half : (block + 1) * half], right).astype(BF16)
                    for at in range(per_tile):
                        put(
                            (at % 2, tile * (per_tile // 2) + at // 2), block,
                            result[:, at * lanes : (at + 1) * lanes], 0, lanes,
                        )
                return _

            lax.fori_loop(0, 4, in_tile, 0)
        elif kind == 2:

            def hid_tile(block, _):
                for part in range(4):
                    left = active[:, pl.ds(pl.multiple_of((block * 4 + part) * half, half), half)]
                    result = dot_tn(left, branch[...]).astype(BF16)
                    for at in range(dp):
                        put(
                            at, block, result[:, at * thin : (at + 1) * thin], part * thin,
                            (part + 1) * thin,
                        )
                return _

            lax.fori_loop(0, 2, hid_tile, 0)
        else:
            for block in range(2):
                left = inputs[:, block * half : (block + 1) * half]
                for tile in range(2):
                    result = dot_tn(left, mix[:, tile * 3 * half : (tile + 1) * 3 * half]).astype(BF16)
                    for at in range(depth):
                        put(
                            tile * depth + at, block, result[:, at * wide : (at + 1) * wide], 0, wide
                        )
                result = dot_tn(heads[:, block * half : (block + 1) * half], attn[...]).astype(BF16)
                for at in range(dp):
                    put(at, block, result[:, at * thin : (at + 1) * thin], wide, lanes)

    def after_core(side, kind, unit):
        core_copy(unit).wait_recv()

        def add(at, _):
            add_into(mine.at[side, kind, at], landed.at[unit % 2, at])
            return _

        lax.fori_loop(0, depth, add, 0)
        if unit + 2 < 6:
            pl.semaphore_signal(free_sem, inc=1, device_id=core_dev, device_id_type=MESH)
        if side == 0:
            xp_copy(kind).start()
        yq_copy(side, kind).start()

    def forward_q(kind):
        yq_copy(0, kind).wait_recv()

        def add(at, _):
            add_into(mine.at[0, kind, cut + at, y], yq.at[0, kind, at])
            return _

        lax.fori_loop(0, depth - cut, add, 0)
        xq_copy(kind).start()

    def forward_p(kind):
        xp_copy(kind).wait_recv()

        def add(at, _):
            add_into(mine.at[1, kind, at], xp.at[kind, at])
            return _

        lax.fori_loop(0, cut, add, 0)
        yp_copy(kind).start()

    def finish_plane(kind):
        yq_copy(1, kind).wait_recv()
        xq_copy(kind).wait_recv()

        def add_two(at, _):
            ref = mine.at[1, kind, cut + at, y]
            total = ref[...].astype(F32) + yq[1, kind, at].astype(F32) + xq[kind, at].astype(F32)
            ref[...] = total.astype(BF16)
            return _

        lax.fori_loop(0, depth - cut, add_two, 0)
        yp_copy(kind).wait_recv()

        def add(at, _):
            add_into(mine.at[1, kind, at, y], yp.at[kind, at])
            return _

        lax.fori_loop(0, cut, add, 0)

    def line(kind):
        def hop(count, _):
            high, low = depth - 1 - count, count

            @pl.when(z < high)
            def _():
                @pl.when(z > 0)
                def _():
                    up_copy(kind, high).wait_recv()
                    add_into(mine.at[1, kind, high, y], from_low.at[kind, high])

                @pl.when((z == 0) & (count > 0))
                def _():
                    up_copy(kind, high + 1).wait_send()

                up_copy(kind, high).start()

            @pl.when(z > low)
            def _():
                @pl.when(z < depth - 1)
                def _():
                    down_copy(kind, low).wait_recv()
                    add_into(mine.at[1, kind, low, y], from_high.at[kind, low])

                @pl.when((z == depth - 1) & (count > 0))
                def _():
                    down_copy(kind, low - 1).wait_send()

                down_copy(kind, low).start()

            return 0

        lax.fori_loop(0, depth - 1, hop, 0)

    def finish(kind):
        @pl.when(z > 0)
        def _():
            up_copy(kind, z).wait_recv()
            add_into(mine.at[1, kind, z, y], from_low.at[kind, z])

        @pl.when(z < depth - 1)
        def _():
            down_copy(kind, z).wait_recv()
            add_into(mine.at[1, kind, z, y], from_high.at[kind, z])

        piece_out[kind] = mine[1, kind, z, y]

    units = [(side, kind) for side in range(2) for kind in kinds]
    for unit, (side, kind) in enumerate(units):
        layer = (1 - x) if side == 0 else x
        for copy in loads(side, kind):
            copy.wait()
        if unit >= 2:
            core_copy(unit - 2).wait_send()
        for block in range(2):
            rows_now = extra[layer, block, kind * extra_rows : (kind + 1) * extra_rows, :].astype(BF16)
            for at in range(depth):
                mine[side, kind, at, block, half:, :] = rows_now
                theirs[unit % 2, at, block, half:, :] = rows_now
        multiply(side, kind, unit)
        if unit >= 2:
            pl.semaphore_wait(free_sem, 1)
        core_copy(unit).start()
        if side == 0:
            for copy in loads(1, kind):
                copy.start()
        if unit >= 1:
            after_core(*units[unit - 1], unit - 1)
        if unit == 4:
            forward_q(kinds[0])
        if unit == 5:
            forward_q(kinds[1])
    after_core(*units[5], 5)
    forward_p(kinds[0])
    forward_q(kinds[2])
    forward_p(kinds[1])
    forward_p(kinds[2])
    finish_plane(kinds[0])
    line(kinds[0])
    finish_plane(kinds[1])
    line(kinds[1])
    finish(kinds[0])
    finish_plane(kinds[2])
    line(kinds[2])
    finish(kinds[1])
    finish(kinds[2])
    core_copy(4).wait_send()
    core_copy(5).wait_send()
    for kind in kinds:
        xp_copy(kind).wait_send()
        xq_copy(kind).wait_send()
        yp_copy(kind).wait_send()
        for side in range(2):
            yq_copy(side, kind).wait_send()

        def sent(at, _):
            @pl.when((at > z) & ((z > 0) | (at == 1)))
            def _():
                up_copy(kind, at).wait_send()

            @pl.when((at < z) & ((z < depth - 1) | (at == depth - 2)))
            def _():
                down_copy(kind, at).wait_send()

            return 0

        lax.fori_loop(0, depth, sent, 0)


def grad_reduce_shapes(dp, steps, rows, width):
    half = width // 2
    lanes = 4 * width // dp
    depth = dp // 2
    cut = depth // 2
    extra_rows = 16
    tall = half + extra_rows
    held = [width, 4 * width, 4 * width, width, width, 3 * width, width, width]
    return (
        [pltpu.VMEM((steps // 2 * rows, columns), BF16) for columns in held]
        + [
            pltpu.VMEM(shape + (tall, lanes), BF16)
            for shape in (
                (2, 3, depth, 2), (2, depth, 2), (2, depth, 2), (3, cut, 2), (3, depth - cut),
                (2, 3, depth - cut), (3, cut), (3, depth), (3, depth),
            )
        ]
        + [pltpu.VMEM((2, 2, 3 * extra_rows, lanes), F32)]
    )


def unpack_body(mem, piece_ref, qkv_ref, out_ref, in_ref, hid_ref, memory_ref, vec_ref):
    half = qkv_ref.shape[1]
    wide, thin, lanes = qkv_ref.shape[2], out_ref.shape[2], in_ref.shape[2]
    width = memory_ref.shape[1]
    qkv_ref[0] = piece_ref[0, 0:half, 0:wide].astype(F32)
    out_ref[0] = piece_ref[0, 0:half, wide:lanes].astype(F32)
    in_ref[0] = piece_ref[1, 0:half, :].astype(F32)
    for part in range(4):
        hid_ref[0, part * half : (part + 1) * half, :] = piece_ref[
            2, 0:half, part * thin : (part + 1) * thin
        ].astype(F32)
    extra = jnp.concatenate([piece_ref[kind, half:, :].astype(F32) for kind in range(3)], axis=0)
    pieces = width // lanes
    for piece in range(pieces):
        memory_ref[:, piece * lanes : (piece + 1) * lanes] = extra[piece * mem : (piece + 1) * mem, :]
    for at in range(6 * pieces):
        row = mem * pieces + at
        vec_ref[:, at * lanes : (at + 1) * lanes] = extra[row : row + 1, :]


def grad_reduce(dp, mem, saved, sums, memory):
    sources = [saved[name] for name in GRAD_NAMES]
    steps, rows, width = sources[0].shape
    segs_all = steps // 2
    half = width // 2
    lanes = 4 * width // dp
    thin = width // dp
    depth = dp // 2
    any_spec = pl.BlockSpec(memory_space=pl.ANY)
    dma = pltpu.SemaphoreType.DMA
    shapes = grad_reduce_shapes(dp, steps, rows, width)
    piece = pl.pallas_call(
        functools.partial(grad_reduce_body, dp, segs_all),
        in_specs=[any_spec] * 8 + [pl.BlockSpec(memory_space=pltpu.VMEM)] * 2,
        out_specs=pl.BlockSpec(memory_space=pltpu.VMEM),
        out_shape=jax.ShapeDtypeStruct((3,) + shapes[8].shape[-2:], BF16),
        scratch_shapes=shapes
        + [
            dma((8, segs_all)), dma((2, 6)), pltpu.SemaphoreType.REGULAR, dma((2, 3)), dma((2, 3)),
            dma((2, 2, 3)), dma((2, 3)), dma((2, 3, depth)), dma((2, 3, depth)),
        ],
        compiler_params=pltpu.CompilerParams(
            vmem_limit_bytes=VMEM_BYTES, collective_id=0, has_side_effects=True
        ),
        name="grad_reduce",
    )(*sources, sums, memory)
    *grads, memory, vec = pl.pallas_call(
        functools.partial(unpack_body, mem),
        out_shape=[
            jax.ShapeDtypeStruct(shape, F32)
            for shape in (
                (1, half, 3 * thin), (1, half, thin), (1, half, lanes), (1, 4 * half, thin),
                (mem, width), (1, 6 * width),
            )
        ],
        name="unpack",
    )(piece)
    place = lax.axis_index("dp")
    bias_len = 5 * width // dp
    bias = lax.dynamic_slice(vec, (0, place * bias_len), (1, bias_len))
    gain = lax.dynamic_slice(vec, (0, 5 * width + place * thin), (1, thin))
    return (memory, *grads, bias, gain)


def padded_bytes(shapes):
    total = 0
    for shape in shapes:
        *lead, tall, lanes = shape.shape
        size = (4 if shape.dtype == F32 else 2) * tall * -(-lanes // 128) * 128
        for count in lead:
            size *= count
        total += size
    return total


def other_core(block, dp):
    return lax.ppermute(block, "dp", [(at, at ^ 1) for at in range(dp)])


def per_device(
    text_rows,
    memory_init,
    cotangent,
    w_qkv,
    w_out,
    w_in,
    w_hid,
    biases,
    norm_gains,
    boundaries,
    mem_resets,
    seg_counts,
):
    items, segs, text_len, width = text_rows.shape
    mem_rows = memory_init.shape[0]
    rows = text_len + 2 * mem_rows
    half = width // 2
    dp = lax.axis_size("dp")
    blocks = (w_qkv, w_out, w_in, w_hid)
    vec = jnp.concatenate([biases, norm_gains], axis=1).astype(F32)
    steps = 2 * items * segs
    if dp == 8:
        saved, acts, weights, vecs = gather_forward(
            text_rows, mem_resets, seg_counts, memory_init, boundaries, blocks, vec
        )
    else:
        weights, vecs = gather_apart(blocks, vec)
        saved, acts = forward_steps(
            text_rows, mem_resets, seg_counts, memory_init, boundaries, weights, vecs
        )
    grads, sums, input_grads, memory_grad, acts = backward_steps(
        cotangent, mem_resets, seg_counts, boundaries, mem_rows, acts, weights, vecs, saved
    )
    saved.update(grads)
    reduce = grad_reduce
    if padded_bytes(grad_reduce_shapes(dp, steps, rows, width)) > 60 * 2**20:
        reduce = grad_reduce_apart
    return (acts, input_grads, *reduce(dp, mem_rows, saved, sums, memory_grad))


def grad_reduce_apart(dp, mem_rows, saved, sums, memory_grad):
    steps, width = sums.shape[0], memory_grad.shape[1]
    half = width // 2
    vector_len = 5 * width
    lanes = 4 * width // dp
    memory_part = memory_grad[16 - mem_rows :].reshape(-1)
    memory_len = -(-memory_part.shape[0] // lanes) * lanes
    memory_part = jnp.pad(memory_part, (0, memory_len - memory_part.shape[0]))
    vector_part = vector_len // dp
    gain_part = width // dp
    used = memory_len + vector_part + gain_part
    extra_rows = -(-used // (3 * 16 * lanes)) * 16
    extras = []
    for layer in range(2):
        total = sums.reshape(steps // 2, 2, 12 * width)[:, layer].sum(axis=0)
        gain_two, shift_two, bias_hid, gain_one, shift_one, bias_o, bias_q, bias_v = [
            total[at * width : (at + 1) * width] for at in range(8)
        ]
        vector = jnp.concatenate(
            [bias_q, bias_v, bias_o, shift_one, total[8 * width :], bias_hid, shift_two]
        ).reshape(2, dp, vector_part)
        gain = jnp.stack([gain_one, gain_two]).reshape(2, dp, gain_part)
        extra = jnp.concatenate(
            [jnp.broadcast_to(memory_part, (2, dp, memory_len)), vector, gain], axis=-1
        )
        extra = jnp.pad(extra, ((0, 0), (0, 0), (0, 3 * extra_rows * lanes - used)))
        extra = extra.reshape(2, dp // 2, 2, 3, extra_rows, lanes).transpose(3, 2, 1, 0, 4, 5)
        extras.append(extra.astype(BF16))
    extras = jnp.stack(extras)
    wires = [weight_grads(layer, dp, saved, extras[layer]) for layer in range(2)]
    mine = jnp.stack([wires[0][0], wires[1][0]])
    theirs = other_core(jnp.stack([wires[0][1], wires[1][1]]), dp)
    both = mine.astype(F32) + theirs.astype(F32)
    both = both.transpose(3, 0, 2, 1, 4, 5).astype(BF16)
    tall, lanes = both.shape[-2:]
    both = both.reshape(4, dp // 2, 3, tall, lanes)
    own = lax.psum_scatter(both, "section", scatter_dimension=0, tiled=True)[0]
    groups = [[2 * at + side for at in range(dp // 2)] for side in range(2)]
    own = lax.psum_scatter(
        own, "dp", scatter_dimension=0, axis_index_groups=groups, tiled=True
    )[0].astype(F32)
    thin = lanes // 4
    body = own[:, :half]
    hid = body[2].reshape(half, 4, thin).transpose(1, 0, 2).reshape(4 * half, thin)
    flat = own[:, half:].reshape(-1)
    return (
        flat[: mem_rows * width].reshape(mem_rows, width),
        body[0, :, : 3 * thin][None],
        body[0, :, 3 * thin :][None],
        body[1][None],
        hid[None],
        flat[memory_len : memory_len + vector_part][None],
        flat[memory_len + vector_part : used][None],
    )


def solution(mesh):
    in_specs = (
        P(("section", "dp"), None, None, None),
        P(),
        P(("section", "dp"), None, None, None),
        P("section", None, None),
        P("section", None, None),
        P("section", None, None),
        P("section", None, None),
        P("section", None),
        P("section", None),
        P(("section", "dp"), None, None),
        P(("section", "dp"), None),
        P(("section", "dp")),
    )
    out_specs = (
        P(("section", "dp"), None, None, None),
        P(("section", "dp"), None, None, None),
        P(),
        P("section", None, "dp"),
        P("section", None, "dp"),
        P("section", None, "dp"),
        P("section", None, "dp"),
        P("section", "dp"),
        P("section", "dp"),
    )
    return jax.shard_map(
        per_device, mesh=mesh, in_specs=in_specs, out_specs=out_specs, check_vma=False
    )
```

```python
import functools

import jax
import jax.numpy as jnp
from jax import lax
from jax.experimental import pallas as pl
from jax.experimental.pallas import tpu as pltpu
from jax.sharding import PartitionSpec as P

HEADS = 12
HEAD_DIM = 64
EPS = 1e-05
MASKED = -1e30
VMEM_BYTES = 63 * 2**20
F32 = jnp.float32
BF16 = jnp.bfloat16
MESH = pl.DeviceIdType.MESH


def dot_nn(one, two):
    return jnp.dot(one, two, preferred_element_type=F32)


def dot_nt(one, two):
    return lax.dot_general(one, two, (((1,), (1,)), ((), ())), preferred_element_type=F32)


def dot_tn(one, two):
    return lax.dot_general(one, two, (((0,), (0,)), ((), ())), preferred_element_type=F32)


def weight_tile(refs, kind, tile, layer):
    qkv_ref, in_ref, end_ref = refs
    quarters, _, _, _, tall, width = end_ref.shape
    thin = tall // 5
    if kind == "out":
        pieces = [
            end_ref[quarter, core, half, layer, 0:thin]
            for half in range(2)
            for quarter in range(quarters)
            for core in range(2)
        ]
    elif kind == "hid":
        pieces = [
            end_ref[(tile % 2) * (quarters // 2) + at, core, tile // 2, layer, thin:tall]
            for at in range(quarters // 2)
            for core in range(2)
        ]
    else:
        ref = qkv_ref if kind == "qkv" else in_ref
        at = tile * width if isinstance(tile, int) else pl.multiple_of(tile * width, width)
        pieces = [ref[core, half, layer, :, pl.ds(at, width)] for half in range(2) for core in range(2)]
    return jnp.concatenate(pieces, axis=0)


def weight_specs(shapes, layer_of):
    specs = []
    for shape in shapes:
        lead = len(shape) - 3
        block = shape[:lead] + (1,) + shape[lead + 1 :]
        specs.append(
            pl.BlockSpec(block, lambda t, *_, lead=lead: (0,) * lead + (layer_of(t), 0, 0))
        )
    return specs


def head_lanes(shape, head):
    lanes = lax.broadcasted_iota(jnp.int32, shape, 1)
    return (lanes // HEAD_DIM) == head


def erf_parts(values):
    density = jnp.exp(-0.5 * values * values) * 0.3989422804014327
    phi = 0.5 * (1.0 + lax.erf(values * 0.7071067811865476))
    return phi, density


def vector_rows(vec_ref, layer, width):
    row = lambda half, at: vec_ref[half, layer, :, at * width : (at + 1) * width]
    return dict(
        bias_q=row(0, 0), bias_v=row(0, 1), bias_o=row(0, 2), shift_one=row(0, 3),
        bias_in=(row(0, 4), row(1, 0), row(1, 1), row(1, 2)),
        bias_hid=row(1, 3), shift_two=row(1, 4), gain_one=row(0, 5), gain_two=row(1, 5),
    )


def ones_where(shape, condition):
    rows = lax.broadcasted_iota(jnp.int32, shape, 0)
    columns = lax.broadcasted_iota(jnp.int32, shape, 1)
    return condition(rows, columns).astype(BF16)


def document_bias(bounds, rows, mem):
    text = bounds.shape[1]
    eight = jnp.broadcast_to(bounds, (8, text)).astype(BF16)
    upto = ones_where((text, rows), lambda r, c: r <= c - mem)
    below = ones_where((rows, text), lambda r, c: c <= r - mem)
    columns = dot_nn(eight, upto)[0:1]
    lines = dot_nt(below, eight)[:, 0:1]
    place = lax.broadcasted_iota(jnp.int32, (1, rows), 1)
    columns = jnp.where((place < mem) | (place >= mem + text), -1.0, columns)
    place = lax.broadcasted_iota(jnp.int32, (rows, 1), 0)
    lines = jnp.where((place < mem) | (place >= mem + text), -1.0, lines)
    allowed = (lines == columns) | (lines < 0) | (columns < 0)
    return jnp.where(allowed, 0.0, MASKED)


def norm_forward(values):
    offset = values - jnp.mean(values, axis=-1, keepdims=True)
    scale = lax.rsqrt(jnp.mean(offset * offset, axis=-1, keepdims=True) + EPS)
    return offset * scale, scale


def forward_layer(
    step, segs, at_layer, before_mix, before_out, resets_ref, counts_ref, text_ref, init_ref,
    bounds_ref, weights, vec_ref,
    x_ref, mixed_ref, heads_ref, hat_one_ref, first_ref, active_ref, slope_ref, hat_two_ref,
    stats_ref, acts_ref, y_scr, bias_scr, sum_scr, bias_in_scr,
):
    rows, width = y_scr.shape
    text_len, mem = text_ref.shape[2], init_ref.shape[0]
    layer, seg, item = step % 2, (step // 2) % segs, step // (2 * segs)

    @pl.when(layer == 0)
    def _():
        fresh = (seg == 0) | (resets_ref[item, seg] > 0)
        place = ones_where((rows, text_len), lambda r, c: r - mem == c)
        start = ones_where((rows, mem), lambda r, c: (r == c) | (r - mem - text_len == c))
        again = ones_where(
            (rows, rows),
            lambda r, c: ((r < mem) & (r + mem + text_len == c)) | ((r >= mem + text_len) & (r == c)),
        )
        memory = jnp.where(fresh, dot_nn(start, init_ref[...]), dot_nn(again, y_scr[...]))
        x_ref[0] = (dot_nn(place, text_ref[0, 0]) + memory).astype(BF16)
        bias_scr[...] = document_bias(bounds_ref[0, pl.ds(seg, 1), :], rows, mem)

    @pl.when(layer == 1)
    def _():
        x_ref[0] = y_scr[...]

    before_mix()
    vec = vector_rows(vec_ref, at_layer, width)
    for part in range(4):
        bias_in_scr[part] = vec["bias_in"][part]
    inputs = x_ref[0]
    for tile in range(3):
        mixed = dot_nn(inputs, weight_tile(weights, "qkv", tile, at_layer))
        if tile == 0:
            mixed = mixed + vec["bias_q"]
        if tile == 2:
            mixed = mixed + vec["bias_v"]
        mixed_ref[0, :, tile * width : (tile + 1) * width] = mixed.astype(BF16)

    group = 4 * HEAD_DIM
    stat_lane = lax.broadcasted_iota(jnp.int32, (rows, 128), 1)
    stats = jnp.zeros((rows, 128), F32)
    for number in range(width // group):
        at = number * group
        queries = mixed_ref[0, :, at : at + group] * BF16(HEAD_DIM**-0.5)
        keys = mixed_ref[0, :, width + at : width + at + group]
        values = mixed_ref[0, :, 2 * width + at : 2 * width + at + group]
        lanes = lax.broadcasted_iota(jnp.int32, (rows, group), 1) // HEAD_DIM
        stacked = jnp.concatenate([jnp.where(lanes == head, queries, 0) for head in range(4)], axis=0)
        scores = dot_nt(stacked, keys)
        probs = []
        for head in range(4):
            part = scores[head * rows : (head + 1) * rows] + bias_scr[...]
            peak = jnp.max(part, axis=-1, keepdims=True)
            expo = jnp.exp(part - peak)
            norm = jnp.sum(expo, axis=-1, keepdims=True)
            probs.append((expo * (1.0 / norm)).astype(BF16))
            stats = jnp.where(stat_lane == number * 4 + head, peak + jnp.log(norm), stats)
        result = dot_nn(jnp.concatenate(probs, axis=0), values)
        total = result[0:rows]
        for head in range(1, 4):
            total = jnp.where(lanes == head, result[head * rows : (head + 1) * rows], total)
        heads_ref[0, :, at : at + group] = total.astype(BF16)
    stats_ref[0] = stats

    before_out()
    attn = dot_nn(heads_ref[0], weight_tile(weights, "out", 0, at_layer)) + vec["bias_o"]
    hat, scale = norm_forward(x_ref[0].astype(F32) + attn)
    hat_one_ref[0] = hat.astype(BF16)
    stats = jnp.where(stat_lane == HEADS, scale, stats_ref[0])
    first = hat * vec["gain_one"] + vec["shift_one"]
    first_ref[0] = first.astype(BF16)
    sum_scr[...] = first + vec["bias_hid"]

    def ff_tile(tile, _):
        at = tile * width
        inner = dot_nn(first_ref[0], weight_tile(weights, "in", tile, at_layer)) + bias_in_scr[tile]
        phi, density = erf_parts(inner)
        active = (inner * phi).astype(BF16)
        active_ref[0, :, pl.ds(at, width)] = active
        slope_ref[0, :, pl.ds(at, width)] = (phi + inner * density).astype(BF16)
        sum_scr[...] += dot_nn(active, weight_tile(weights, "hid", tile, at_layer))
        return _

    for tile in range(4):
        ff_tile(tile, 0)
    hat, scale = norm_forward(sum_scr[...])
    hat_two_ref[0] = hat.astype(BF16)
    stats_ref[0] = jnp.where(stat_lane == HEADS + 1, scale, stats)
    result = (hat * vec["gain_two"] + vec["shift_two"]).astype(BF16)
    y_scr[...] = result

    @pl.when(layer == 1)
    def _():
        acts_ref[0, 0] = jnp.where(seg < counts_ref[item], result, 0)


def saved_shapes(rows, width):
    return dict(
        x=((rows, width), BF16),
        mixed=((rows, 3 * width), BF16),
        heads=((rows, width), BF16),
        hat_one=((rows, width), BF16),
        first=((rows, width), BF16),
        active=((rows, 4 * width), BF16),
        slope=((rows, 4 * width), BF16),
        hat_two=((rows, width), BF16),
        stats=((rows, 128), F32),
    )


def forward_io(text, resets, counts, init, bounds):
    items, segs, text_len, width = text.shape
    rows = text_len + 2 * init.shape[0]
    steps = 2 * items * segs
    saved = saved_shapes(rows, width)
    by_seg = lambda t: (t // (2 * segs), (t // 2) % segs, 0, 0)
    operands = [resets, counts, text, init, bounds]
    in_specs = [
        pl.BlockSpec(memory_space=pltpu.SMEM),
        pl.BlockSpec(memory_space=pltpu.SMEM),
        pl.BlockSpec((1, 1, text_len, width), by_seg),
        pl.BlockSpec(init.shape, lambda t: (0, 0)),
        pl.BlockSpec((1, segs, text_len), lambda t: (t // (2 * segs), 0, 0)),
    ]
    out_specs = [pl.BlockSpec((1,) + shape, lambda t: (t, 0, 0)) for shape, _ in saved.values()]
    out_specs.append(pl.BlockSpec((1, 1, rows, width), by_seg))
    out_shape = [jax.ShapeDtypeStruct((steps,) + shape, kind) for shape, kind in saved.values()]
    out_shape.append(jax.ShapeDtypeStruct((items, segs, rows, width), BF16))
    scratch = [
        pltpu.VMEM((rows, width), BF16),
        pltpu.VMEM((rows, rows), F32),
        pltpu.VMEM((rows, width), F32),
        pltpu.VMEM((4, 1, width), F32),
    ]
    return steps, saved, operands, in_specs, out_specs, out_shape, scratch


def nothing():
    pass


def forward_body(segs, *refs):
    step = pl.program_id(0)
    y_scr = refs[19]

    @pl.when(step == 0)
    def _():
        y_scr[...] = jnp.zeros_like(y_scr)

    forward_layer(step, segs, 0, nothing, nothing, *refs[:5], refs[5:8], *refs[8:])


def forward_steps(text, resets, counts, init, bounds, weights, vec):
    steps, saved, operands, in_specs, out_specs, out_shape, scratch = forward_io(
        text, resets, counts, init, bounds
    )
    *outs, acts = pl.pallas_call(
        functools.partial(forward_body, text.shape[1]),
        grid=(steps,),
        in_specs=in_specs
        + weight_specs([weight.shape for weight in weights], lambda t: t % 2)
        + [pl.BlockSpec((2, 1) + vec.shape[2:], lambda t: (0, t % 2, 0, 0))],
        out_specs=out_specs,
        out_shape=out_shape,
        scratch_shapes=scratch,
        compiler_params=pltpu.CompilerParams(vmem_limit_bytes=VMEM_BYTES),
        name="forward_steps",
    )(*operands, *weights, vec)
    return dict(zip(saved, outs)), acts


def norm_backward(grad, hat, scale, gain):
    scaled = grad * gain
    mean_one = jnp.mean(scaled, axis=-1, keepdims=True)
    mean_two = jnp.mean(scaled * hat, axis=-1, keepdims=True)
    return (scaled - mean_one - hat * mean_two) * scale


def column_sum(values):
    return jnp.sum(values, axis=0, keepdims=True)


def backward_body(
    count, segs, mem, resets_ref, counts_ref, cot_ref, bounds_ref, acts_ref, qkv_ref, in_ref, end_ref,
    vec_ref, mixed_ref, heads_ref, hat_one_ref, slope_ref, hat_two_ref, stats_ref,
    branch_ref, inner_ref, attn_ref, mix_ref, sums_ref, inputs_ref, init_ref, acts_out_ref,
    g_scr, carry_scr, bias_scr, sum_scr, go_scr,
):
    step = count - 1 - pl.program_id(0)
    layer = step % 2
    seg = (step // 2) % segs
    rows, width = g_scr.shape
    item = step // (2 * segs)
    weights = (qkv_ref, in_ref, end_ref)
    vec = vector_rows(vec_ref, 0, width)
    gain_one, gain_two = vec["gain_one"], vec["gain_two"]

    @pl.when(pl.program_id(0) == 0)
    def _():
        carry_scr[...] = jnp.zeros_like(carry_scr)
        init_ref[...] = jnp.zeros_like(init_ref)

    @pl.when(layer == 1)
    def _():
        acts_out_ref[...] = acts_ref[...]
        bias_scr[...] = document_bias(bounds_ref[0, pl.ds(seg, 1), :], rows, mem)
        cot = jnp.where(seg < counts_ref[item], cot_ref[0, 0], 0)
        g_scr[...] = cot
        carried = jnp.where(seg == segs - 1, 0.0, carry_scr[...])
        g_scr[rows - 16 : rows, :] = (cot[rows - 16 : rows].astype(F32) + carried).astype(BF16)

    stats = stats_ref[0]
    scale_one = stats[:, HEADS : HEADS + 1]
    scale_two = stats[:, HEADS + 1 : HEADS + 2]
    grad = g_scr[...].astype(F32)
    hat = hat_two_ref[0].astype(F32)
    sums_ref[0, :, 0:width] = column_sum(grad * hat)
    sums_ref[0, :, width : 2 * width] = column_sum(grad)
    grad_second = norm_backward(grad, hat, scale_two, gain_two)
    branch = grad_second.astype(BF16)
    branch_ref[0] = branch
    sums_ref[0, :, 2 * width : 3 * width] = column_sum(branch.astype(F32))
    sum_scr[...] = grad_second

    def ff_tile(tile, _):
        at = tile * width
        active = dot_nt(branch, weight_tile(weights, "hid", tile, 0))
        inner = (active * slope_ref[0, :, pl.ds(at, width)].astype(F32)).astype(BF16)
        inner_ref[0, :, pl.ds(at, width)] = inner
        sums_ref[0, :, pl.ds(8 * width + at, width)] = column_sum(inner.astype(F32))
        sum_scr[...] += dot_nt(inner, weight_tile(weights, "in", tile, 0))
        return _

    for tile in range(4):
        ff_tile(tile, 0)
    grad = sum_scr[...]
    hat = hat_one_ref[0].astype(F32)
    sums_ref[0, :, 3 * width : 4 * width] = column_sum(grad * hat)
    sums_ref[0, :, 4 * width : 5 * width] = column_sum(grad)
    resid = norm_backward(grad, hat, scale_one, gain_one)
    sum_scr[...] = resid
    attn = resid.astype(BF16)
    attn_ref[0] = attn
    sums_ref[0, :, 5 * width : 6 * width] = column_sum(attn.astype(F32))
    go = dot_nt(attn, weight_tile(weights, "out", 0, 0)).astype(BF16)
    go_scr[...] = go
    product = go.astype(F32) * heads_ref[0].astype(F32)
    high = product.astype(BF16)
    low = (product - high.astype(F32)).astype(BF16)
    picks = (
        lax.broadcasted_iota(jnp.int32, (16, width), 1) // HEAD_DIM
        == lax.broadcasted_iota(jnp.int32, (16, width), 0)
    ).astype(BF16)
    centres = dot_nt(picks, high) + dot_nt(picks, low)
    logs = jnp.transpose(stats)

    group = 4 * HEAD_DIM
    for number in range(width // group):
        at = number * group
        queries = mixed_ref[0, :, at : at + group] * BF16(HEAD_DIM**-0.5)
        keys = mixed_ref[0, :, width + at : width + at + group]
        values = mixed_ref[0, :, 2 * width + at : 2 * width + at + group]
        outs = go_scr[:, at : at + group]
        lanes = lax.broadcasted_iota(jnp.int32, (rows, group), 1) // HEAD_DIM

        def stack(block):
            return jnp.concatenate([jnp.where(lanes == head, block, 0) for head in range(4)], axis=0)

        def unstack(block):
            total = block[0:rows]
            for head in range(1, 4):
                total = jnp.where(lanes == head, block[head * rows : (head + 1) * rows], total)
            return total

        keys_s = stack(keys)
        scores = dot_nt(keys_s, queries)
        grad_p = dot_nt(stack(values), outs)
        probs, grads = [], []
        for head in range(4):
            row = number * 4 + head
            part = slice(head * rows, (head + 1) * rows)
            prob = jnp.exp(scores[part] + bias_scr[...] - logs[row : row + 1, :])
            grads.append((prob * (grad_p[part] - centres[row : row + 1, :])).astype(BF16))
            probs.append(prob.astype(BF16))
        grads = jnp.concatenate(grads, axis=0)
        grad_v = unstack(dot_nn(jnp.concatenate(probs, axis=0), outs))
        grad_k = unstack(dot_nn(grads, queries))
        grad_q = dot_tn(grads, keys_s)
        mix_ref[0, :, at : at + group] = (grad_q * HEAD_DIM**-0.5).astype(BF16)
        mix_ref[0, :, width + at : width + at + group] = grad_k.astype(BF16)
        mix_ref[0, :, 2 * width + at : 2 * width + at + group] = grad_v.astype(BF16)

    sums_ref[0, :, 6 * width : 7 * width] = column_sum(mix_ref[0, :, 0:width].astype(F32))
    sums_ref[0, :, 7 * width : 8 * width] = column_sum(mix_ref[0, :, 2 * width : 3 * width].astype(F32))
    total = sum_scr[...]
    for tile in range(3):
        total = total + dot_nt(
            mix_ref[0, :, tile * width : (tile + 1) * width], weight_tile(weights, "qkv", tile, 0)
        )
    result = total.astype(BF16)
    g_scr[...] = result

    @pl.when(layer == 0)
    def _():
        inputs_ref[0, 0] = result
        fresh = (seg == 0) | (resets_ref[item, seg] > 0)
        number = lax.broadcasted_iota(jnp.int32, (16, width), 0)
        folded = result[rows - 16 : rows].astype(F32) + pltpu.roll(
            result[0:16].astype(F32), 16 - mem, 0
        )
        folded = jnp.where(number >= 16 - mem, folded, 0.0).astype(BF16).astype(F32)
        init_ref[...] += jnp.where(fresh, folded, 0.0)
        carry_scr[...] = jnp.where(fresh, 0.0, folded)


def backward_steps(cot, resets, counts, bounds, mem, acts, weights, vec, saved):
    items, segs, rows, width = cot.shape
    steps = 2 * items * segs
    at = lambda t: steps - 1 - t
    by_seg = lambda t: (at(t) // (2 * segs), (at(t) // 2) % segs, 0, 0)
    by_step = lambda t: (at(t), 0, 0)
    names = ("mixed", "heads", "hat_one", "slope", "hat_two", "stats")
    outs = dict(
        branch=(rows, width), inner=(rows, 4 * width), attn=(rows, width), mix=(rows, 3 * width),
    )
    *grads, sums, inputs, memory, acts = pl.pallas_call(
        functools.partial(backward_body, steps, segs, mem),
        grid=(steps,),
        in_specs=[
            pl.BlockSpec(memory_space=pltpu.SMEM),
            pl.BlockSpec(memory_space=pltpu.SMEM),
            pl.BlockSpec((1, 1, rows, width), by_seg),
            pl.BlockSpec((1,) + bounds.shape[1:], lambda t: (at(t) // (2 * segs), 0, 0)),
            pl.BlockSpec((1, 1, rows, width), by_seg),
        ]
        + weight_specs([weight.shape for weight in weights], lambda t: at(t) % 2)
        + [pl.BlockSpec((2, 1) + vec.shape[2:], lambda t: (0, at(t) % 2, 0, 0))]
        + [pl.BlockSpec((1,) + saved[name].shape[1:], by_step) for name in names],
        out_specs=[pl.BlockSpec((1,) + shape, by_step) for shape in outs.values()]
        + [
            pl.BlockSpec((1, 1, 12 * width), by_step),
            pl.BlockSpec((1, 1, rows, width), by_seg),
            pl.BlockSpec((16, width), lambda t: (0, 0)),
            pl.BlockSpec((1, 1, rows, width), by_seg),
        ],
        out_shape=[jax.ShapeDtypeStruct((steps,) + shape, BF16) for shape in outs.values()]
        + [
            jax.ShapeDtypeStruct((steps, 1, 12 * width), F32),
            jax.ShapeDtypeStruct(cot.shape, BF16),
            jax.ShapeDtypeStruct((16, width), F32),
            jax.ShapeDtypeStruct(cot.shape, BF16),
        ],
        scratch_shapes=[
            pltpu.VMEM((rows, width), BF16),
            pltpu.VMEM((16, width), F32),
            pltpu.VMEM((rows, rows), F32),
            pltpu.VMEM((rows, width), F32),
            pltpu.VMEM((rows, width), BF16),
        ],
        compiler_params=pltpu.CompilerParams(vmem_limit_bytes=VMEM_BYTES),
        name="backward_steps",
    )(resets, counts, cot, bounds, acts, *weights, vec, *[saved[name] for name in names])
    return dict(zip(outs, grads)), sums, inputs, memory, acts


def gather_forward_body(steps, segs, *refs):
    io = refs[:5]
    qkv_src, in_src, out_src, hid_src, vec_src = refs[5:10]
    outs = refs[10:20]
    full_outs = refs[20:24]
    forward_scratch = refs[24:28]
    weights = refs[28:31]
    vec = refs[31]
    (
        load_sems, end_load_sems, store_sems, x_sems, y_sems, fx_sems, fy_sems, core_sems, end_sems,
        line_core_sems, up_sems, down_sems, vec_sems, vec_load_sem,
    ) = refs[32:]
    step = pl.program_id(0)
    section, place = lax.axis_index("section"), lax.axis_index("dp")
    x, y = section % 2, section // 2
    core, z = place % 2, place // 2
    end = weights[2]
    depth, _, _, _, tall, _ = end.shape
    thin = tall // 5
    x_dev = (y * 2 + 1 - x, place)
    y_dev = ((1 - y) * 2 + x, place)
    core_dev = (section, z * 2 + 1 - core)
    up_dev = (section, (z + 1) % depth * 2 + core)
    down_dev = (section, (z + depth - 1) % depth * 2 + core)
    own_block = (y, x)
    blocks = ((y, 1 - x), (1 - y, x), (1 - y, 1 - x))

    def remote(source, target, sems, index, device):
        return pltpu.make_async_remote_copy(
            src_ref=source, dst_ref=target, send_sem=sems.at[(0, *index)], recv_sem=sems.at[(1, *index)],
            device_id=device, device_id_type=MESH,
        )


    def part_of(number, block, part):
        rows = weights[number].shape[-2] // 2
        return weights[number].at[core, block[0], block[1], pl.ds(part * rows, rows)]

    def own_part(number, part):
        rows = weights[number].shape[-2] // 2
        at = pl.multiple_of((core * 2 + part) * rows, rows)
        return (qkv_src, in_src)[number].at[0, pl.ds(at, rows)]

    def x_copy(number, part):
        return remote(own_part(number, part), part_of(number, own_block, part), x_sems, (number, part), x_dev)

    def y_copy(number, part):
        return remote(own_part(number, part), part_of(number, own_block, part), y_sems, (number, part), y_dev)

    def fy_copy(number):
        piece = part_of(number, blocks[0], 0)
        return remote(piece, piece, fy_sems, (number,), y_dev)

    def fx_copy(number):
        piece = part_of(number, blocks[1], 1)
        return remote(piece, piece, fx_sems, (number,), x_dev)

    def core_copy(number, kind, part):
        piece = part_of(number, blocks[kind], part)
        return remote(piece, piece, core_sems, (number, kind, part), core_dev)


    def eighth(at, block, first=0, rows=None):
        view = end.at[at, core, block[0], block[1]]
        return view if rows is None else view.at[pl.ds(first, rows)]

    def own_eighth(first):
        source, rows = (out_src, thin) if first == 0 else (hid_src, tall - thin)
        return source.at[0, pl.ds(pl.multiple_of((z * 2 + core) * rows, rows), rows)]

    def end_copy(axis, first):
        rows = thin if first == 0 else tall - thin
        return remote(
            own_eighth(first), eighth(z, own_block, first, rows), end_sems, (axis, 0 if first == 0 else 1),
            (x_dev, y_dev)[axis],
        )

    low = tall // 32 * 16

    def end_fy_copy():
        piece = eighth(z, blocks[0], 0, low)
        return remote(piece, piece, fy_sems, (2,), y_dev)

    def end_fx_copy():
        piece = eighth(z, blocks[1], low, tall - low)
        return remote(piece, piece, fx_sems, (2,), x_dev)

    def line_core_copy(at, kind):
        piece = eighth(at, blocks[kind])
        return remote(piece, piece, line_core_sems, (at, kind), core_dev)

    def up_copy(at, kind):
        piece = eighth(at, blocks[kind])
        return remote(piece, piece, up_sems, (at, kind), up_dev)

    def down_copy(at, kind):
        piece = eighth(at, blocks[kind])
        return remote(piece, piece, down_sems, (at, kind), down_dev)

    def vec_copy(kind):
        block = (own_block, own_block, blocks[0])[kind]
        source = vec_src if kind < 2 else vec.at[block]
        return remote(source, vec.at[block], vec_sems, (kind,), (x_dev, y_dev, y_dev)[kind])

    def loads():
        copies = []
        for number, source in enumerate((qkv_src, in_src)):
            rows = weights[number].shape[-2]
            for side in range(2):
                copies.append(
                    pltpu.make_async_copy(
                        source.at[0, pl.ds(side * rows, rows)], weights[number].at[side, y, x],
                        load_sems.at[number, side],
                    )
                )
        for at in range(depth):
            for side in range(2):
                for number, (source, first, rows) in enumerate(
                    ((out_src, 0, thin), (hid_src, thin, tall - thin))
                ):
                    copies.append(
                        pltpu.make_async_copy(
                            source.at[0, pl.ds((at * 2 + side) * rows, rows)],
                            end.at[at, side, y, x, pl.ds(first, rows)],
                            end_load_sems.at[at, side, number],
                        )
                    )
        return copies + [pltpu.make_async_copy(vec_src, vec.at[y, x], vec_load_sem)]

    def full_stores():
        return [
            pltpu.make_async_copy(source, target, store_sems.at[number])
            for number, (source, target) in enumerate(zip((*weights, vec), full_outs))
        ]

    def spread(kind):
        @pl.when(z < depth - 1)
        def _():
            up_copy(z, kind).start()

        @pl.when(z > 0)
        def _():
            down_copy(z, kind).start()

        line_core_copy(z, kind).start()

    def hop(distance):
        for kind in range(3):

            @pl.when(z >= distance)
            def _():
                up_copy(z - distance, kind).wait_recv()

                @pl.when(z < depth - 1)
                def _():
                    up_copy(z - distance, kind).start()

                line_core_copy(z - distance, kind).start()

            @pl.when(z + distance < depth)
            def _():
                down_copy(z + distance, kind).wait_recv()

                @pl.when(z > 0)
                def _():
                    down_copy(z + distance, kind).start()

                line_core_copy(z + distance, kind).start()

    def near(number):
        x_copy(number, 0).wait_recv()
        fy_copy(number).start()
        core_copy(number, 0, 0).start()
        y_copy(number, 1).wait_recv()
        fx_copy(number).start()
        core_copy(number, 1, 1).start()

    def rest(number):
        x_copy(number, 1).wait_recv()
        core_copy(number, 0, 1).start()
        y_copy(number, 0).wait_recv()
        core_copy(number, 1, 0).start()

    def diagonal(number):
        fy_copy(number).wait_recv()
        core_copy(number, 2, 0).start()
        fx_copy(number).wait_recv()
        core_copy(number, 2, 1).start()

    def complete(number):
        for kind in range(3):
            for part in range(2):
                core_copy(number, kind, part).wait_recv()

    def before_mix():
        @pl.when(step == 0)
        def _():
            barrier = pltpu.get_barrier_semaphore()
            for device in (x_dev, y_dev, core_dev):
                pl.semaphore_signal(barrier, inc=1, device_id=device, device_id_type=MESH)

            @pl.when(z < depth - 1)
            def _():
                pl.semaphore_signal(barrier, inc=1, device_id=up_dev, device_id_type=MESH)

            @pl.when(z > 0)
            def _():
                pl.semaphore_signal(barrier, inc=1, device_id=down_dev, device_id_type=MESH)

            pl.semaphore_wait(barrier, 3 + jnp.where(z > 0, 1, 0) + jnp.where(z < depth - 1, 1, 0))
            for first in (0, thin):
                end_copy(0, first).start()
                end_copy(1, first).start()
            vec_copy(0).start()
            vec_copy(1).start()
            x_copy(0, 0).start()
            y_copy(0, 1).start()
            x_copy(0, 1).start()
            y_copy(0, 0).start()
            for copy in loads():
                copy.start()
            for axis in range(2):
                for first in (0, thin):
                    end_copy(axis, first).wait_recv()
                (end_fy_copy, end_fx_copy)[axis]().start()
                spread(axis)
            vec_copy(0).wait_recv()
            vec_copy(2).start()
            end_fy_copy().wait_recv()
            end_fx_copy().wait_recv()
            spread(2)
            near(0)
            x_copy(1, 0).start()
            y_copy(1, 1).start()
            rest(0)
            x_copy(1, 1).start()
            y_copy(1, 0).start()
            hop(1)
            diagonal(0)
            vec_copy(1).wait_recv()
            vec_copy(2).wait_recv()
            complete(0)
            for copy in loads():
                copy.wait()

    def before_out():
        @pl.when(step == 0)
        def _():
            near(1)
            hop(2)
            rest(1)
            diagonal(1)
            hop(3)
            complete(1)
            for at in range(depth):
                for kind in range(3):
                    line_core_copy(at, kind).wait_recv()

        @pl.when(step == 1)
        def _():
            for copy in full_stores():
                copy.start()

    @pl.when(step == 0)
    def _():
        forward_scratch[0][...] = jnp.zeros_like(forward_scratch[0])

    forward_layer(
        step, segs, step % 2, before_mix, before_out, *io, weights, vec, *outs, *forward_scratch
    )

    @pl.when(step == steps - 1)
    def _():
        for copy in full_stores():
            copy.wait()
        for number in range(2):
            for part in range(2):
                x_copy(number, part).wait_send()
                y_copy(number, part).wait_send()
                for kind in range(3):
                    core_copy(number, kind, part).wait_send()
            fx_copy(number).wait_send()
            fy_copy(number).wait_send()
            for first in (0, thin):
                end_copy(number, first).wait_send()
        end_fx_copy().wait_send()
        end_fy_copy().wait_send()
        for kind in range(3):
            vec_copy(kind).wait_send()
            for at in range(depth):
                line_core_copy(at, kind).wait_send()

                @pl.when((z >= at) & (z < depth - 1))
                def _():
                    up_copy(at, kind).wait_send()

                @pl.when((z <= at) & (z > 0))
                def _():
                    down_copy(at, kind).wait_send()


def full_weight_shapes(w_qkv, w_out, w_in, w_hid):
    half, width = w_out.shape[1:]
    return [(2, 2, 2, half // 2, block.shape[2]) for block in (w_qkv, w_in)] + [
        (4, 2, 2, 2, (half + w_hid.shape[1]) // 8, width)
    ]


def gather_forward(text, resets, counts, init, bounds, blocks, vec):
    steps, saved, operands, in_specs, out_specs, out_shape, scratch = forward_io(
        text, resets, counts, init, bounds
    )
    shapes = full_weight_shapes(*blocks)
    full = [pltpu.VMEM(shape, BF16) for shape in shapes] + [pltpu.VMEM((2, 2) + vec.shape, F32)]
    any_spec = pl.BlockSpec(memory_space=pl.ANY)
    dma = pltpu.SemaphoreType.DMA
    depth = shapes[2][0]
    *outs, acts, qkv, w_in, end, vecs = pl.pallas_call(
        functools.partial(gather_forward_body, steps, text.shape[1]),
        grid=(steps,),
        in_specs=in_specs + [any_spec] * 5,
        out_specs=out_specs + [any_spec] * 4,
        out_shape=out_shape + [jax.ShapeDtypeStruct(ref.shape, ref.dtype) for ref in full],
        scratch_shapes=scratch
        + full
        + [
            dma((2, 2)), dma((depth, 2, 2)), dma((4,)), dma((2, 2, 2)), dma((2, 2, 2)), dma((2, 3)),
            dma((2, 3)), dma((2, 2, 3, 2)), dma((2, 2, 2)), dma((2, depth, 3)), dma((2, depth, 3)),
            dma((2, depth, 3)), dma((2, 3)), dma,
        ],
        compiler_params=pltpu.CompilerParams(
            vmem_limit_bytes=VMEM_BYTES, collective_id=1, has_side_effects=True
        ),
        name="gather_forward",
    )(*operands, blocks[0], blocks[2], blocks[1], blocks[3], vec)
    return dict(zip(saved, outs)), acts, (qkv, w_in, end), vecs


def gather_apart(blocks, vec):
    w_qkv, w_out, w_in, w_hid = [
        lax.all_gather(block[0], "section").reshape(2, 2, *block.shape[1:]) for block in blocks
    ]
    half, width = w_out.shape[2:]
    full = [
        block.reshape(2, 2, 2, half // 2, -1).transpose(2, 0, 1, 3, 4) for block in (w_qkv, w_in)
    ]
    ends = [block.reshape(2, 2, 4, 2, -1, width).transpose(2, 3, 0, 1, 4, 5) for block in (w_out, w_hid)]
    vecs = lax.all_gather(vec, "section").reshape(2, 2, *vec.shape)
    return (*full, jnp.concatenate(ends, axis=4)), vecs


GRAD_NAMES = ("first", "inner", "active", "branch", "x", "mix", "heads", "attn")


def weight_grad_body(
    layer, segs_all, dp, *refs,
):
    sources = refs[:8]
    extra_ref, mine_ref, theirs_ref = refs[8:11]
    held = refs[11:19]
    wire, in_sems, extra_sem, out_sems = refs[19:23]
    core = lax.axis_index("dp") % 2
    rows = sources[0].shape[1]
    width = sources[0].shape[2]
    half = width // 2
    lanes = wire.shape[-1]
    thin = width // dp
    wide = 3 * thin

    def loads(number):
        return [
            pltpu.make_async_copy(
                sources[number].at[2 * at + layer],
                held[number].at[pl.ds(at * rows, rows)],
                in_sems.at[number, at],
            )
            for at in range(segs_all)
        ]

    for number in range(8):
        for copy in loads(number):
            copy.start()
    extra = pltpu.make_async_copy(extra_ref, wire.at[:, :, :, :, pl.ds(half, extra_ref.shape[4])], extra_sem)
    extra.start()

    def ready(*numbers):
        for number in numbers:
            for copy in loads(number):
                copy.wait()

    def stores(kind):
        return [
            pltpu.make_async_copy(wire.at[kind, core], mine_ref.at[kind], out_sems.at[kind, 0]),
            pltpu.make_async_copy(wire.at[kind, 1 - core], theirs_ref.at[kind], out_sems.at[kind, 1]),
        ]

    first, inner, active, branch, inputs, mix, heads, attn = held
    extra.wait()

    ready(0, 1)
    per_tile = width // lanes

    def in_tile(tile, _):
        right = inner[:, pl.ds(pl.multiple_of(tile * width, width), width)]
        for side in range(2):
            result = dot_tn(first[:, side * half : (side + 1) * half], right).astype(BF16)
            for at in range(per_tile):
                wire[1, at % 2, tile * (per_tile // 2) + at // 2, side, 0:half, :] = result[
                    :, at * lanes : (at + 1) * lanes
                ]
        return _

    lax.fori_loop(0, 4, in_tile, 0)
    for copy in stores(1):
        copy.start()

    ready(2, 3)
    def hid_tile(side, _):
        for part in range(4):
            left = active[:, pl.ds(pl.multiple_of(side * 4 * half + part * half, half), half)]
            result = dot_tn(left, branch[...]).astype(BF16)
            for at in range(dp):
                wire[2, at % 2, at // 2, side, 0:half, part * thin : (part + 1) * thin] = result[
                    :, at * thin : (at + 1) * thin
                ]
        return _
    lax.fori_loop(0, 2, hid_tile, 0)
    for copy in stores(2):
        copy.start()

    ready(4, 5, 6, 7)
    for side in range(2):
        left = inputs[:, side * half : (side + 1) * half]
        for tile in range(2):
            result = dot_tn(left, mix[:, tile * 3 * half : (tile + 1) * 3 * half]).astype(BF16)
            for at in range(dp // 2):
                place = tile * (dp // 2) + at
                wire[0, place % 2, place // 2, side, 0:half, 0:wide] = result[
                    :, at * wide : (at + 1) * wide
                ]
        result = dot_tn(heads[:, side * half : (side + 1) * half], attn[...]).astype(BF16)
        for at in range(dp):
            wire[0, at % 2, at // 2, side, 0:half, wide:lanes] = result[:, at * thin : (at + 1) * thin]
    for copy in stores(0):
        copy.start()
    for kind in range(3):
        for copy in stores(kind):
            copy.wait()


def weight_grads(layer, dp, saved, extras):
    sources = [saved[name] for name in GRAD_NAMES]
    steps, rows, width = sources[0].shape
    segs_all = steps // 2
    half = width // 2
    lanes = 4 * width // dp
    extra_rows = extras.shape[4]
    kind = jax.ShapeDtypeStruct((3, dp // 2, 2, half + extra_rows, lanes), BF16)
    any_spec = pl.BlockSpec(memory_space=pl.ANY)
    return pl.pallas_call(
        functools.partial(weight_grad_body, layer, segs_all, dp),
        in_specs=[any_spec] * 9,
        out_specs=[any_spec] * 2,
        out_shape=[kind, kind],
        scratch_shapes=[pltpu.VMEM((segs_all * rows, source.shape[2]), BF16) for source in sources]
        + [
            pltpu.VMEM((3, 2, dp // 2, 2, half + extra_rows, lanes), BF16),
            pltpu.SemaphoreType.DMA((8, segs_all)),
            pltpu.SemaphoreType.DMA,
            pltpu.SemaphoreType.DMA((3, 2)),
        ],
        compiler_params=pltpu.CompilerParams(vmem_limit_bytes=VMEM_BYTES),
        name="weight_grads",
    )(*sources, extras)


def add_into(ref, other):
    ref[...] = (ref[...].astype(F32) + other[...].astype(F32)).astype(BF16)


def build_extra(sums_ref, memory_ref, extra):
    steps = sums_ref.shape[0]
    width = memory_ref.shape[1]
    lanes = extra.shape[-1]
    mem = 10
    extra[...] = jnp.zeros_like(extra)
    for layer in range(2):
        total = sums_ref[layer]
        for step in range(layer + 2, steps, 2):
            total = total + sums_ref[step]
        for block, parts in enumerate(((6, 7, 5, 4, 8, 3), (9, 10, 11, 2, 1, 0))):
            for piece in range(width // lanes):
                extra[layer, block, piece * mem : (piece + 1) * mem, :] = memory_ref[
                    16 - mem : 16, piece * lanes : (piece + 1) * lanes
                ]
                for at, part in enumerate(parts):
                    row = mem * (width // lanes) + at * (width // lanes) + piece
                    first = part * width + piece * lanes
                    extra[layer, block, row : row + 1, :] = total[:, first : first + lanes]


KIND_IN, KIND_HID, KIND_MIX = 1, 2, 0
CUTS = {KIND_HID: 2, KIND_MIX: 2}
PLAN = (
    ("mul", 0, 2), ("mul", 0, 1), ("core", 0, 2), ("P", 2, 0), ("QO", 2, 0), ("mul", 1, 2), ("P", 2, 1),
    ("QO", 2, 1), ("XQ", 2, 0), ("core", 0, 1), ("hop", "ZO", 1, 0, 0), ("core", 1, 2), ("QW", 2, 1),
    ("QW", 2, 0), ("YP", 2, 0), ("hop", "ZO", 1, 0, 1), ("mul", 0, 0), ("mul", 1, 1), ("XQ", 2, 1),
    ("YP", 2, 1), ("hop", "ZO", 1, 0, 2), ("core", 0, 0), ("QO", 0, 1), ("P", 0, 0), ("QO", 0, 0), ("P",
    0, 1), ("mul", 1, 0), ("core", 1, 0), ("QW", 0, 1), ("QW", 0, 0), ("YP", 0, 0), ("XQ", 0, 0),
    ("fin", "ZO", 1, 0), ("XQ", 0, 1), ("plane", 2, 1), ("hop", "Z", 2, 1, 0), ("hop", "Z", 2, 1, 1),
    ("hop", "Z", 2, 1, 2), ("YP", 0, 1), ("plane", 2, 0), ("hop", "Z", 2, 0, 0), ("hop", "Z", 2, 0, 1),
    ("core", 1, 1), ("QWA", 1), ("hop", "Z", 2, 0, 2), ("XO", 1), ("plane", 0, 0), ("hop", "Z", 0, 0,
    0), ("hop", "Z", 0, 0, 1), ("hop", "Z", 0, 0, 2), ("plane", 0, 1), ("hop", "Z", 0, 1, 0), ("hop",
    "Z", 0, 1, 1), ("fin", "Z", 2, 0), ("fin", "Z", 0, 0), ("hop", "Z", 0, 1, 2), ("fin", "Z", 0, 1),
    ("fin", "Z", 2, 1), ("YO", 1), ("plane", 1, 0), ("hop", "Z", 1, 0, 0), ("hop", "Z", 1, 0, 1),
    ("hop", "Z", 1, 0, 2), ("fin", "Z", 1, 0),
)


def row_parts(tall):
    first = -(-tall // 32) * 16
    return ((0, first), (first, tall - first))


def grad_reduce_body(dp, segs_all, *refs):
    sources = refs[:8]
    sums_ref, memory_ref = refs[8:10]
    piece_out = refs[10]
    held = refs[11:19]
    mine, theirs, landed, xp, xq, yqo, yqw, yp, ywall, xo, yo, z_low, z_high, zo_low, zo_high = refs[19:34]
    extra = refs[34]
    (
        in_sems, core_sems, free_sem, xp_sems, xq_sems, yqo_sems, yqw_sems, yp_sems, single_sems, up_sems,
        down_sems, zo_up_sems, zo_down_sems,
    ) = refs[35:]
    section, place = lax.axis_index("section"), lax.axis_index("dp")
    x, y = section % 2, section // 2
    core, z = place % 2, place // 2
    depth = dp // 2
    rows, width = sources[0].shape[1:]
    half = width // 2
    tall, lanes = mine.shape[-2:]
    thin = width // dp
    wide = 3 * thin
    parts = row_parts(tall)
    x_dev = (y * 2 + 1 - x, place)
    y_dev = ((1 - y) * 2 + x, place)
    core_dev = (section, z * 2 + 1 - core)
    up_dev = (section, (z + 1) % depth * 2 + core)
    down_dev = (section, (z + depth - 1) % depth * 2 + core)
    used = {KIND_IN: (0, 1), KIND_HID: (2, 3), KIND_MIX: (4, 5, 6, 7)}
    slots = {KIND_HID: 0, KIND_MIX: 1}
    first, inner, active, branch, inputs, mix, heads, attn = held
    units = [step[1:] for step in PLAN if step[0] == "mul"]

    def loads(side, kind):
        layer = (1 - x) if side == 0 else x
        return [
            pltpu.make_async_copy(
                sources[number].at[2 * at + layer],
                held[number].at[pl.ds(at * rows, rows)],
                in_sems.at[number, at],
            )
            for number in used[kind]
            for at in range(segs_all)
        ]

    for side, kind in units:
        if side == 0:
            for copy in loads(0, kind):
                copy.start()
    barrier = pltpu.get_barrier_semaphore()
    for device in (x_dev, y_dev, core_dev):
        pl.semaphore_signal(barrier, inc=1, device_id=device, device_id_type=MESH)

    @pl.when(z < depth - 1)
    def _():
        pl.semaphore_signal(barrier, inc=1, device_id=up_dev, device_id_type=MESH)

    @pl.when(z > 0)
    def _():
        pl.semaphore_signal(barrier, inc=1, device_id=down_dev, device_id_type=MESH)

    build_extra(sums_ref, memory_ref, extra)
    pl.semaphore_wait(barrier, 3 + jnp.where(z > 0, 1, 0) + jnp.where(z < depth - 1, 1, 0))

    def remote(source, target, sems, index, device):
        return pltpu.make_async_remote_copy(
            src_ref=source, dst_ref=target, send_sem=sems.at[(0, *index)], recv_sem=sems.at[(1, *index)],
            device_id=device, device_id_type=MESH,
        )

    def core_copy(unit):
        return remote(theirs.at[unit % 2], landed.at[unit % 2], core_sems, (unit,), core_dev)

    def p_copy(kind, part):
        at = pl.ds(0, CUTS[kind])
        some = pl.ds(*parts[part])
        return remote(
            mine.at[0, kind, at, :, some], xp.at[slots[kind], at, :, some], xp_sems, (slots[kind], part), x_dev
        )

    def q_copy(side, kind, part):
        some = pl.ds(*parts[part])
        count = depth - CUTS[kind]
        return remote(
            mine.at[side, kind, pl.ds(CUTS[kind], count), 1 - y, some],
            (yqo, yqw)[side].at[slots[kind], pl.ds(0, count), some],
            (yqo_sems, yqw_sems)[side], (slots[kind], part), y_dev,
        )

    def xq_copy(kind, part):
        some = pl.ds(*parts[part])
        count = depth - CUTS[kind]
        return remote(
            mine.at[0, kind, pl.ds(CUTS[kind], count), y, some],
            xq.at[slots[kind], pl.ds(0, count), some], xq_sems, (slots[kind], part), x_dev,
        )

    def yp_copy(kind, part):
        some = pl.ds(*parts[part])
        at = pl.ds(0, CUTS[kind])
        return remote(
            mine.at[1, kind, at, 1 - y, some], yp.at[slots[kind], at, some], yp_sems, (slots[kind], part), y_dev
        )

    def xo_copy():
        return remote(mine.at[0, KIND_IN, z], xo, single_sems, (0,), x_dev)

    def yo_copy():
        return remote(xo.at[1 - y], yo, single_sems, (1,), y_dev)

    def ywall_copy():
        return remote(mine.at[1, KIND_IN, :, 1 - y], ywall, single_sems, (2,), y_dev)

    def line_rows(kind, part):
        return pl.ds(0, tall) if kind == KIND_IN else pl.ds(*parts[part])

    def up_copy(name, kind, part, at):
        if name == "ZO":
            return remote(mine.at[0, kind, at], zo_low.at[at - 1], zo_up_sems, (at,), up_dev)
        some = line_rows(kind, part)
        return remote(
            mine.at[1, kind, at, y, some], z_low.at[kind, at - 1, some], up_sems, (kind, part, at), up_dev
        )

    def down_copy(name, kind, part, at):
        if name == "ZO":
            return remote(mine.at[0, kind, at], zo_high.at[at], zo_down_sems, (at,), down_dev)
        some = line_rows(kind, part)
        return remote(
            mine.at[1, kind, at, y, some], z_high.at[kind, at, some], down_sems, (kind, part, at), down_dev
        )

    def from_low(name, kind, part, at):
        up_copy(name, kind, part, at).wait_recv()
        if name == "ZO":
            for block in range(2):
                add_into(mine.at[0, kind, at, block], zo_low.at[at - 1, block])
        else:
            some = line_rows(kind, part)
            add_into(mine.at[1, kind, at, y, some], z_low.at[kind, at - 1, some])

    def from_high(name, kind, part, at):
        down_copy(name, kind, part, at).wait_recv()
        if name == "ZO":
            for block in range(2):
                add_into(mine.at[0, kind, at, block], zo_high.at[at, block])
        else:
            some = line_rows(kind, part)
            add_into(mine.at[1, kind, at, y, some], z_high.at[kind, at, some])

    def multiply(side, kind):
        unit = units.index((side, kind))
        slot = unit % 2

        def put(chunk_core, chunk_z, block, piece, start, stop):
            @pl.when(core == chunk_core)
            def _():
                mine[side, kind, chunk_z, block, start:stop, :] = piece

            @pl.when(core != chunk_core)
            def _():
                theirs[slot, chunk_z, block, start:stop, :] = piece

        for copy in loads(side, kind):
            copy.wait()
        if unit >= 2:
            core_copy(unit - 2).wait_send()
        layer = (1 - x) if side == 0 else x
        extra_rows = tall - half
        for block in range(2):
            added = extra[layer, block, kind * extra_rows : (kind + 1) * extra_rows, :].astype(BF16)
            for at in range(depth):
                mine[side, kind, at, block, half:, :] = added
                theirs[slot, at, block, half:, :] = added
        if kind == KIND_IN:
            per_tile = width // lanes

            def in_tile(tile, _):
                right = inner[:, pl.ds(pl.multiple_of(tile * width, width), width)]
                for block in range(2):
                    result = dot_tn(first[:, block * half : (block + 1) * half], right).astype(BF16)
                    for at in range(per_tile):
                        put(
                            at % 2, tile * (per_tile // 2) + at // 2, block,
                            result[:, at * lanes : (at + 1) * lanes], 0, half,
                        )
                return _

            lax.fori_loop(0, 4, in_tile, 0)
        elif kind == KIND_HID:

            def hid_tile(block, _):
                for pair in range(2):
                    right = active[:, pl.ds(pl.multiple_of((block * 2 + pair) * width, width), width)]
                    for side_rows in range(2):
                        result = dot_tn(
                            branch[:, side_rows * half : (side_rows + 1) * half], right
                        ).astype(BF16)
                        for at in range(dp // 2):
                            chunk = side_rows * (dp // 2) + at
                            for piece in range(2):
                                row = (pair * 2 + piece) * thin
                                put(
                                    chunk % 2, chunk // 2, block,
                                    result[at * thin : (at + 1) * thin, piece * half : (piece + 1) * half],
                                    row, row + thin,
                                )
                return _

            lax.fori_loop(0, 2, hid_tile, 0)
        else:

            def mix_tile(block, _):
                columns = pl.ds(pl.multiple_of(block * half, half), half)
                for tile in range(2):
                    result = dot_tn(
                        mix[:, tile * 3 * half : (tile + 1) * 3 * half], inputs[:, columns]
                    ).astype(BF16)
                    for at in range(depth):
                        chunk = tile * depth + at
                        put(chunk % 2, chunk // 2, block, result[at * wide : (at + 1) * wide], 0, wide)
                result = dot_tn(attn[...], heads[:, columns]).astype(BF16)
                for chunk in range(dp):
                    put(chunk % 2, chunk // 2, block, result[chunk * thin : (chunk + 1) * thin], wide, half)
                return _

            lax.fori_loop(0, 2, mix_tile, 0)
        if unit >= 2:
            pl.semaphore_wait(free_sem, 1)
        core_copy(unit).start()
        if side == 0:
            for copy in loads(1, kind):
                copy.start()

    def add_core(side, kind):
        unit = units.index((side, kind))
        core_copy(unit).wait_recv()

        def add(at, _):
            for block in range(2):
                add_into(mine.at[side, kind, at, block], landed.at[unit % 2, at, block])
            return _

        lax.fori_loop(0, depth, add, 0)
        if unit + 2 < len(units):
            pl.semaphore_signal(free_sem, inc=1, device_id=core_dev, device_id_type=MESH)

    def forward_q(kind, part):
        q_copy(0, kind, part).wait_recv()
        some = pl.ds(*parts[part])
        for at in range(depth - CUTS[kind]):
            add_into(mine.at[0, kind, CUTS[kind] + at, y, some], yqo.at[slots[kind], at, some])
        xq_copy(kind, part).start()

    def forward_p(kind, part):
        p_copy(kind, part).wait_recv()
        some = pl.ds(*parts[part])
        for at in range(CUTS[kind]):
            for block in range(2):
                add_into(mine.at[1, kind, at, block, some], xp.at[slots[kind], at, block, some])
        yp_copy(kind, part).start()

    def finish_plane(kind, part):
        if kind == KIND_IN:
            ywall_copy().wait_recv()
            for at in range(depth):
                add_into(mine.at[1, kind, at, y], ywall.at[at])
            return
        some = pl.ds(*parts[part])
        slot = slots[kind]
        q_copy(1, kind, part).wait_recv()
        xq_copy(kind, part).wait_recv()
        for at in range(depth - CUTS[kind]):
            ref = mine.at[1, kind, CUTS[kind] + at, y, some]
            total = ref[...].astype(F32) + yqw[slot, at, some].astype(F32) + xq[slot, at, some].astype(F32)
            ref[...] = total.astype(BF16)
        yp_copy(kind, part).wait_recv()
        for at in range(CUTS[kind]):
            add_into(mine.at[1, kind, at, y, some], yp.at[slot, at, some])

    def hop(name, kind, part, count):
        high = depth - 1 - count + z
        low = count - (depth - 1 - z)

        @pl.when(z <= count)
        def _():
            @pl.when(z > 0)
            def _():
                from_low(name, kind, part, high)

            up_copy(name, kind, part, high).start()

        @pl.when(low >= 0)
        def _():
            @pl.when(z < depth - 1)
            def _():
                from_high(name, kind, part, low)

            down_copy(name, kind, part, low).start()

    def finish(name, kind, part):
        @pl.when(z > 0)
        def _():
            from_low(name, kind, part, z)

        @pl.when(z < depth - 1)
        def _():
            from_high(name, kind, part, z)

        if name == "ZO":
            return
        if kind == KIND_IN:
            add_into(mine.at[1, kind, z, y], xo.at[y])
            yo_copy().wait_recv()
            add_into(mine.at[1, kind, z, y], yo)
        some = line_rows(kind, part)
        piece_out[kind, some, :] = mine[1, kind, z, y, some, :]

    def forward_o(kind):
        xo_copy().wait_recv()
        yo_copy().start()

    act = dict(
        mul=multiply,
        core=add_core,
        P=lambda kind, part: p_copy(kind, part).start(),
        QO=lambda kind, part: q_copy(0, kind, part).start(),
        QW=lambda kind, part: q_copy(1, kind, part).start(),
        XQ=forward_q,
        YP=forward_p,
        plane=finish_plane,
        hop=hop,
        fin=finish,
        XO=lambda kind: xo_copy().start(),
        YO=forward_o,
        QWA=lambda kind: ywall_copy().start(),
    )
    for name, *numbers in PLAN:
        act[name](*numbers)

    core_copy(4).wait_send()
    core_copy(5).wait_send()
    for copy in (xo_copy(), yo_copy(), ywall_copy()):
        copy.wait_send()
    for kind in CUTS:
        for part in range(2):
            p_copy(kind, part).wait_send()
            xq_copy(kind, part).wait_send()
            yp_copy(kind, part).wait_send()
            for side in range(2):
                q_copy(side, kind, part).wait_send()
    lines = [("ZO", KIND_IN, 0), ("Z", KIND_IN, 0)]
    lines += [("Z", kind, part) for kind in CUTS for part in range(2)]
    for line in lines:
        for at in range(depth):

            @pl.when(at > z)
            def _():
                up_copy(*line, at).wait_send()

            @pl.when(at < z)
            def _():
                down_copy(*line, at).wait_send()


def grad_reduce_shapes(dp, steps, rows, width):
    half = width // 2
    lanes = 4 * width // dp
    depth = dp // 2
    extra_rows = 16
    tall = half + extra_rows
    most, least = max(CUTS.values()), depth - min(CUTS.values())
    held = [width, 4 * width, 4 * width, width, width, 3 * width, width, width]
    return (
        [pltpu.VMEM((steps // 2 * rows, columns), BF16) for columns in held]
        + [
            pltpu.VMEM(shape + (tall, lanes), BF16)
            for shape in (
                (2, 3, depth, 2), (2, depth, 2), (2, depth, 2), (2, most, 2), (2, least), (2, least),
                (2, least), (2, most), (depth,), (2,), (), (3, depth - 1), (3, depth - 1),
                (depth - 1, 2), (depth - 1, 2),
            )
        ]
        + [pltpu.VMEM((2, 2, 3 * extra_rows, lanes), F32)]
    )


def unpack_body(mem, piece_ref, qkv_ref, out_ref, in_ref, hid_ref, memory_ref, vec_ref):
    wide, half = qkv_ref.shape[1:]
    thin, lanes = out_ref.shape[1], in_ref.shape[2]
    width = memory_ref.shape[1]
    qkv_ref[0] = piece_ref[0, 0:wide, :].astype(F32)
    out_ref[0] = piece_ref[0, wide:half, :].astype(F32)
    in_ref[0] = piece_ref[1, 0:half, :].astype(F32)
    for part in range(4):
        hid_ref[0, :, part * half : (part + 1) * half] = piece_ref[
            2, part * thin : (part + 1) * thin, :
        ].astype(F32)
    extra = jnp.concatenate([piece_ref[kind, half:, :].astype(F32) for kind in range(3)], axis=0)
    pieces = width // lanes
    for piece in range(pieces):
        memory_ref[:, piece * lanes : (piece + 1) * lanes] = extra[piece * mem : (piece + 1) * mem, :]
    for at in range(6 * pieces):
        row = mem * pieces + at
        vec_ref[:, at * lanes : (at + 1) * lanes] = extra[row : row + 1, :]


def grad_reduce(dp, mem, saved, sums, memory):
    sources = [saved[name] for name in GRAD_NAMES]
    steps, rows, width = sources[0].shape
    segs_all = steps // 2
    half = width // 2
    lanes = 4 * width // dp
    thin = width // dp
    depth = dp // 2
    any_spec = pl.BlockSpec(memory_space=pl.ANY)
    dma = pltpu.SemaphoreType.DMA
    shapes = grad_reduce_shapes(dp, steps, rows, width)
    piece = pl.pallas_call(
        functools.partial(grad_reduce_body, dp, segs_all),
        in_specs=[any_spec] * 8 + [pl.BlockSpec(memory_space=pltpu.VMEM)] * 2,
        out_specs=pl.BlockSpec(memory_space=pltpu.VMEM),
        out_shape=jax.ShapeDtypeStruct((3,) + shapes[8].shape[-2:], BF16),
        scratch_shapes=shapes
        + [
            dma((8, segs_all)), dma((2, 6)), pltpu.SemaphoreType.REGULAR, dma((2, 2, 2)), dma((2, 2, 2)),
            dma((2, 2, 2)), dma((2, 2, 2)), dma((2, 2, 2)), dma((2, 3)), dma((2, 3, 2, depth)),
            dma((2, 3, 2, depth)), dma((2, depth)), dma((2, depth)),
        ],
        compiler_params=pltpu.CompilerParams(
            vmem_limit_bytes=VMEM_BYTES, collective_id=0, has_side_effects=True
        ),
        name="grad_reduce",
    )(*sources, sums, memory)
    qkv, out, w_in, hid, memory, vec = pl.pallas_call(
        functools.partial(unpack_body, mem),
        out_shape=[
            jax.ShapeDtypeStruct(shape, F32)
            for shape in (
                (1, 3 * thin, half), (1, thin, half), (1, half, lanes), (1, thin, 4 * half),
                (mem, width), (1, 6 * width),
            )
        ],
        name="unpack",
    )(piece)
    place = lax.axis_index("dp")
    bias_len = 5 * width // dp
    bias = lax.dynamic_slice(vec, (0, place * bias_len), (1, bias_len))
    gain = lax.dynamic_slice(vec, (0, 5 * width + place * thin), (1, thin))
    grads = (jnp.swapaxes(qkv, 1, 2), jnp.swapaxes(out, 1, 2), w_in, jnp.swapaxes(hid, 1, 2))
    return (memory, *grads, bias, gain)


def other_core(block, dp):
    return lax.ppermute(block, "dp", [(at, at ^ 1) for at in range(dp)])


def per_device(
    text_rows,
    memory_init,
    cotangent,
    w_qkv,
    w_out,
    w_in,
    w_hid,
    biases,
    norm_gains,
    boundaries,
    mem_resets,
    seg_counts,
):
    items, segs, text_len, width = text_rows.shape
    mem_rows = memory_init.shape[0]
    rows = text_len + 2 * mem_rows
    half = width // 2
    dp = lax.axis_size("dp")
    blocks = (w_qkv, w_out, w_in, w_hid)
    vec = jnp.concatenate([biases, norm_gains], axis=1).astype(F32)
    steps = 2 * items * segs
    if dp == 8:
        saved, acts, weights, vecs = gather_forward(
            text_rows, mem_resets, seg_counts, memory_init, boundaries, blocks, vec
        )
    else:
        weights, vecs = gather_apart(blocks, vec)
        saved, acts = forward_steps(
            text_rows, mem_resets, seg_counts, memory_init, boundaries, weights, vecs
        )
    grads, sums, input_grads, memory_grad, acts = backward_steps(
        cotangent, mem_resets, seg_counts, boundaries, mem_rows, acts, weights, vecs, saved
    )
    saved.update(grads)
    reduce = grad_reduce if dp == 8 else grad_reduce_apart
    return (acts, input_grads, *reduce(dp, mem_rows, saved, sums, memory_grad))


def grad_reduce_apart(dp, mem_rows, saved, sums, memory_grad):
    steps, width = sums.shape[0], memory_grad.shape[1]
    half = width // 2
    vector_len = 5 * width
    lanes = 4 * width // dp
    memory_part = memory_grad[16 - mem_rows :].reshape(-1)
    memory_len = -(-memory_part.shape[0] // lanes) * lanes
    memory_part = jnp.pad(memory_part, (0, memory_len - memory_part.shape[0]))
    vector_part = vector_len // dp
    gain_part = width // dp
    used = memory_len + vector_part + gain_part
    extra_rows = -(-used // (3 * 16 * lanes)) * 16
    extras = []
    for layer in range(2):
        total = sums.reshape(steps // 2, 2, 12 * width)[:, layer].sum(axis=0)
        gain_two, shift_two, bias_hid, gain_one, shift_one, bias_o, bias_q, bias_v = [
            total[at * width : (at + 1) * width] for at in range(8)
        ]
        vector = jnp.concatenate(
            [bias_q, bias_v, bias_o, shift_one, total[8 * width :], bias_hid, shift_two]
        ).reshape(2, dp, vector_part)
        gain = jnp.stack([gain_one, gain_two]).reshape(2, dp, gain_part)
        extra = jnp.concatenate(
            [jnp.broadcast_to(memory_part, (2, dp, memory_len)), vector, gain], axis=-1
        )
        extra = jnp.pad(extra, ((0, 0), (0, 0), (0, 3 * extra_rows * lanes - used)))
        extra = extra.reshape(2, dp // 2, 2, 3, extra_rows, lanes).transpose(3, 2, 1, 0, 4, 5)
        extras.append(extra.astype(BF16))
    extras = jnp.stack(extras)
    wires = [weight_grads(layer, dp, saved, extras[layer]) for layer in range(2)]
    mine = jnp.stack([wires[0][0], wires[1][0]])
    theirs = other_core(jnp.stack([wires[0][1], wires[1][1]]), dp)
    both = mine.astype(F32) + theirs.astype(F32)
    both = both.transpose(3, 0, 2, 1, 4, 5).astype(BF16)
    tall, lanes = both.shape[-2:]
    both = both.reshape(4, dp // 2, 3, tall, lanes)
    own = lax.psum_scatter(both, "section", scatter_dimension=0, tiled=True)[0]
    groups = [[2 * at + side for at in range(dp // 2)] for side in range(2)]
    own = lax.psum_scatter(
        own, "dp", scatter_dimension=0, axis_index_groups=groups, tiled=True
    )[0].astype(F32)
    thin = lanes // 4
    body = own[:, :half]
    hid = body[2].reshape(half, 4, thin).transpose(1, 0, 2).reshape(4 * half, thin)
    flat = own[:, half:].reshape(-1)
    return (
        flat[: mem_rows * width].reshape(mem_rows, width),
        body[0, :, : 3 * thin][None],
        body[0, :, 3 * thin :][None],
        body[1][None],
        hid[None],
        flat[memory_len : memory_len + vector_part][None],
        flat[memory_len + vector_part : used][None],
    )


def solution(mesh):
    in_specs = (
        P(("section", "dp"), None, None, None),
        P(),
        P(("section", "dp"), None, None, None),
        P("section", None, None),
        P("section", None, None),
        P("section", None, None),
        P("section", None, None),
        P("section", None),
        P("section", None),
        P(("section", "dp"), None, None),
        P(("section", "dp"), None),
        P(("section", "dp")),
    )
    out_specs = (
        P(("section", "dp"), None, None, None),
        P(("section", "dp"), None, None, None),
        P(),
        P("section", None, "dp"),
        P("section", None, "dp"),
        P("section", None, "dp"),
        P("section", None, "dp"),
        P("section", "dp"),
        P("section", "dp"),
    )
    return jax.shard_map(
        per_device, mesh=mesh, in_specs=in_specs, out_specs=out_specs, check_vma=False
    )
```

```python
import functools

import jax
import jax.numpy as jnp
from jax import lax
from jax.experimental import pallas as pl
from jax.experimental.pallas import tpu as pltpu
from jax.sharding import PartitionSpec as P

HEADS = 12
HEAD_DIM = 64
EPS = 1e-05
MASKED = -1e30
VMEM_BYTES = 63 * 2**20
F32 = jnp.float32
BF16 = jnp.bfloat16
MESH = pl.DeviceIdType.MESH


def dot_nn(one, two):
    return jnp.dot(one, two, preferred_element_type=F32)


def dot_nt(one, two):
    return lax.dot_general(one, two, (((1,), (1,)), ((), ())), preferred_element_type=F32)


def dot_tn(one, two):
    return lax.dot_general(one, two, (((0,), (0,)), ((), ())), preferred_element_type=F32)


def weight_tile(refs, kind, tile, layer):
    qkv_ref, in_ref, end_ref = refs
    quarters, _, _, _, tall, width = end_ref.shape
    thin = tall // 5
    if kind == "out":
        pieces = [
            end_ref[quarter, core, half, layer, 0:thin]
            for half in range(2)
            for quarter in range(quarters)
            for core in range(2)
        ]
    elif kind == "hid":
        pieces = [
            end_ref[(tile % 2) * (quarters // 2) + at, core, tile // 2, layer, thin:tall]
            for at in range(quarters // 2)
            for core in range(2)
        ]
    else:
        ref = qkv_ref if kind == "qkv" else in_ref
        at = tile * width if isinstance(tile, int) else pl.multiple_of(tile * width, width)
        pieces = [ref[core, half, layer, :, pl.ds(at, width)] for half in range(2) for core in range(2)]
    return jnp.concatenate(pieces, axis=0)


def weight_specs(shapes, layer_of):
    specs = []
    for shape in shapes:
        lead = len(shape) - 3
        block = shape[:lead] + (1,) + shape[lead + 1 :]
        specs.append(
            pl.BlockSpec(block, lambda t, *_, lead=lead: (0,) * lead + (layer_of(t), 0, 0))
        )
    return specs


def head_lanes(shape, head):
    lanes = lax.broadcasted_iota(jnp.int32, shape, 1)
    return (lanes // HEAD_DIM) == head


def erf_parts(values):
    density = jnp.exp(-0.5 * values * values) * 0.3989422804014327
    phi = 0.5 * (1.0 + lax.erf(values * 0.7071067811865476))
    return phi, density


def vector_rows(vec_ref, layer, width):
    row = lambda half, at: vec_ref[half, layer, :, at * width : (at + 1) * width]
    return dict(
        bias_q=row(0, 0), bias_v=row(0, 1), bias_o=row(0, 2), shift_one=row(0, 3),
        bias_in=(row(0, 4), row(1, 0), row(1, 1), row(1, 2)),
        bias_hid=row(1, 3), shift_two=row(1, 4), gain_one=row(0, 5), gain_two=row(1, 5),
    )


def ones_where(shape, condition):
    rows = lax.broadcasted_iota(jnp.int32, shape, 0)
    columns = lax.broadcasted_iota(jnp.int32, shape, 1)
    return condition(rows, columns).astype(BF16)


def document_bias(bounds, rows, mem):
    text = bounds.shape[1]
    eight = jnp.broadcast_to(bounds, (8, text)).astype(BF16)
    upto = ones_where((text, rows), lambda r, c: r <= c - mem)
    below = ones_where((rows, text), lambda r, c: c <= r - mem)
    columns = dot_nn(eight, upto)[0:1]
    lines = dot_nt(below, eight)[:, 0:1]
    place = lax.broadcasted_iota(jnp.int32, (1, rows), 1)
    columns = jnp.where((place < mem) | (place >= mem + text), -1.0, columns)
    place = lax.broadcasted_iota(jnp.int32, (rows, 1), 0)
    lines = jnp.where((place < mem) | (place >= mem + text), -1.0, lines)
    allowed = (lines == columns) | (lines < 0) | (columns < 0)
    return jnp.where(allowed, 0.0, MASKED)


def norm_forward(values):
    offset = values - jnp.mean(values, axis=-1, keepdims=True)
    scale = lax.rsqrt(jnp.mean(offset * offset, axis=-1, keepdims=True) + EPS)
    return offset * scale, scale


def forward_layer(
    step, segs, at_layer, before_mix, before_out, resets_ref, counts_ref, text_ref, init_ref,
    bounds_ref, weights, vec_ref,
    x_ref, mixed_ref, heads_ref, hat_one_ref, first_ref, active_ref, slope_ref, hat_two_ref,
    stats_ref, acts_ref, y_scr, bias_scr, sum_scr, bias_in_scr,
):
    rows, width = y_scr.shape
    text_len, mem = text_ref.shape[2], init_ref.shape[0]
    layer, seg, item = step % 2, (step // 2) % segs, step // (2 * segs)

    @pl.when(layer == 0)
    def _():
        fresh = (seg == 0) | (resets_ref[item, seg] > 0)
        place = ones_where((rows, text_len), lambda r, c: r - mem == c)
        start = ones_where((rows, mem), lambda r, c: (r == c) | (r - mem - text_len == c))
        again = ones_where(
            (rows, rows),
            lambda r, c: ((r < mem) & (r + mem + text_len == c)) | ((r >= mem + text_len) & (r == c)),
        )
        memory = jnp.where(fresh, dot_nn(start, init_ref[...]), dot_nn(again, y_scr[...]))
        x_ref[0] = (dot_nn(place, text_ref[0, 0]) + memory).astype(BF16)
        bias_scr[...] = document_bias(bounds_ref[0, pl.ds(seg, 1), :], rows, mem)

    @pl.when(layer == 1)
    def _():
        x_ref[0] = y_scr[...]

    before_mix()
    vec = vector_rows(vec_ref, at_layer, width)
    for part in range(4):
        bias_in_scr[part] = vec["bias_in"][part]
    inputs = x_ref[0]
    for tile in range(3):
        mixed = dot_nn(inputs, weight_tile(weights, "qkv", tile, at_layer))
        if tile == 0:
            mixed = mixed + vec["bias_q"]
        if tile == 2:
            mixed = mixed + vec["bias_v"]
        mixed_ref[0, :, tile * width : (tile + 1) * width] = mixed.astype(BF16)

    group = 4 * HEAD_DIM
    stat_lane = lax.broadcasted_iota(jnp.int32, (rows, 128), 1)
    stats = jnp.zeros((rows, 128), F32)
    for number in range(width // group):
        at = number * group
        queries = mixed_ref[0, :, at : at + group] * BF16(HEAD_DIM**-0.5)
        keys = mixed_ref[0, :, width + at : width + at + group]
        values = mixed_ref[0, :, 2 * width + at : 2 * width + at + group]
        lanes = lax.broadcasted_iota(jnp.int32, (rows, group), 1) // HEAD_DIM
        stacked = jnp.concatenate([jnp.where(lanes == head, queries, 0) for head in range(4)], axis=0)
        scores = dot_nt(stacked, keys)
        probs = []
        for head in range(4):
            part = scores[head * rows : (head + 1) * rows] + bias_scr[...]
            peak = jnp.max(part, axis=-1, keepdims=True)
            expo = jnp.exp(part - peak)
            norm = jnp.sum(expo, axis=-1, keepdims=True)
            probs.append((expo * (1.0 / norm)).astype(BF16))
            stats = jnp.where(stat_lane == number * 4 + head, peak + jnp.log(norm), stats)
        result = dot_nn(jnp.concatenate(probs, axis=0), values)
        total = result[0:rows]
        for head in range(1, 4):
            total = jnp.where(lanes == head, result[head * rows : (head + 1) * rows], total)
        heads_ref[0, :, at : at + group] = total.astype(BF16)
    stats_ref[0] = stats

    before_out()
    attn = dot_nn(heads_ref[0], weight_tile(weights, "out", 0, at_layer)) + vec["bias_o"]
    hat, scale = norm_forward(x_ref[0].astype(F32) + attn)
    hat_one_ref[0] = hat.astype(BF16)
    stats = jnp.where(stat_lane == HEADS, scale, stats_ref[0])
    first = hat * vec["gain_one"] + vec["shift_one"]
    first_ref[0] = first.astype(BF16)
    sum_scr[...] = first + vec["bias_hid"]

    def ff_tile(tile, _):
        at = tile * width
        inner = dot_nn(first_ref[0], weight_tile(weights, "in", tile, at_layer)) + bias_in_scr[tile]
        phi, density = erf_parts(inner)
        active = (inner * phi).astype(BF16)
        active_ref[0, :, pl.ds(at, width)] = active
        slope_ref[0, :, pl.ds(at, width)] = (phi + inner * density).astype(BF16)
        sum_scr[...] += dot_nn(active, weight_tile(weights, "hid", tile, at_layer))
        return _

    for tile in range(4):
        ff_tile(tile, 0)
    hat, scale = norm_forward(sum_scr[...])
    hat_two_ref[0] = hat.astype(BF16)
    stats_ref[0] = jnp.where(stat_lane == HEADS + 1, scale, stats)
    result = (hat * vec["gain_two"] + vec["shift_two"]).astype(BF16)
    y_scr[...] = result

    @pl.when(layer == 1)
    def _():
        acts_ref[0, 0] = jnp.where(seg < counts_ref[item], result, 0)


def saved_shapes(rows, width):
    return dict(
        x=((rows, width), BF16),
        mixed=((rows, 3 * width), BF16),
        heads=((rows, width), BF16),
        hat_one=((rows, width), BF16),
        first=((rows, width), BF16),
        active=((rows, 4 * width), BF16),
        slope=((rows, 4 * width), BF16),
        hat_two=((rows, width), BF16),
        stats=((rows, 128), F32),
    )


def forward_io(text, resets, counts, init, bounds):
    items, segs, text_len, width = text.shape
    rows = text_len + 2 * init.shape[0]
    steps = 2 * items * segs
    saved = saved_shapes(rows, width)
    by_seg = lambda t: (t // (2 * segs), (t // 2) % segs, 0, 0)
    operands = [resets, counts, text, init, bounds]
    in_specs = [
        pl.BlockSpec(memory_space=pltpu.SMEM),
        pl.BlockSpec(memory_space=pltpu.SMEM),
        pl.BlockSpec((1, 1, text_len, width), by_seg),
        pl.BlockSpec(init.shape, lambda t: (0, 0)),
        pl.BlockSpec((1, segs, text_len), lambda t: (t // (2 * segs), 0, 0)),
    ]
    out_specs = [pl.BlockSpec((1,) + shape, lambda t: (t, 0, 0)) for shape, _ in saved.values()]
    out_specs.append(pl.BlockSpec((1, 1, rows, width), by_seg))
    out_shape = [jax.ShapeDtypeStruct((steps,) + shape, kind) for shape, kind in saved.values()]
    out_shape.append(jax.ShapeDtypeStruct((items, segs, rows, width), BF16))
    scratch = [
        pltpu.VMEM((rows, width), BF16),
        pltpu.VMEM((rows, rows), F32),
        pltpu.VMEM((rows, width), F32),
        pltpu.VMEM((4, 1, width), F32),
    ]
    return steps, saved, operands, in_specs, out_specs, out_shape, scratch


def nothing():
    pass


def forward_body(segs, *refs):
    step = pl.program_id(0)
    y_scr = refs[19]

    @pl.when(step == 0)
    def _():
        y_scr[...] = jnp.zeros_like(y_scr)

    forward_layer(step, segs, 0, nothing, nothing, *refs[:5], refs[5:8], *refs[8:])


def forward_steps(text, resets, counts, init, bounds, weights, vec):
    steps, saved, operands, in_specs, out_specs, out_shape, scratch = forward_io(
        text, resets, counts, init, bounds
    )
    *outs, acts = pl.pallas_call(
        functools.partial(forward_body, text.shape[1]),
        grid=(steps,),
        in_specs=in_specs
        + weight_specs([weight.shape for weight in weights], lambda t: t % 2)
        + [pl.BlockSpec((2, 1) + vec.shape[2:], lambda t: (0, t % 2, 0, 0))],
        out_specs=out_specs,
        out_shape=out_shape,
        scratch_shapes=scratch,
        compiler_params=pltpu.CompilerParams(vmem_limit_bytes=VMEM_BYTES),
        name="forward_steps",
    )(*operands, *weights, vec)
    return dict(zip(saved, outs)), acts


def norm_backward(grad, hat, scale, gain):
    scaled = grad * gain
    mean_one = jnp.mean(scaled, axis=-1, keepdims=True)
    mean_two = jnp.mean(scaled * hat, axis=-1, keepdims=True)
    return (scaled - mean_one - hat * mean_two) * scale


def column_sum(values):
    return jnp.sum(values, axis=0, keepdims=True)


def backward_body(
    count, segs, mem, resets_ref, counts_ref, cot_ref, bounds_ref, acts_ref, qkv_ref, in_ref, end_ref,
    vec_ref, mixed_ref, heads_ref, hat_one_ref, slope_ref, hat_two_ref, stats_ref,
    branch_ref, inner_ref, attn_ref, mix_ref, sums_ref, inputs_ref, init_ref, acts_out_ref,
    g_scr, carry_scr, bias_scr, sum_scr, go_scr,
):
    step = count - 1 - pl.program_id(0)
    layer = step % 2
    seg = (step // 2) % segs
    rows, width = g_scr.shape
    item = step // (2 * segs)
    weights = (qkv_ref, in_ref, end_ref)
    vec = vector_rows(vec_ref, 0, width)
    gain_one, gain_two = vec["gain_one"], vec["gain_two"]

    @pl.when(pl.program_id(0) == 0)
    def _():
        carry_scr[...] = jnp.zeros_like(carry_scr)
        init_ref[...] = jnp.zeros_like(init_ref)

    @pl.when(layer == 1)
    def _():
        acts_out_ref[...] = acts_ref[...]
        bias_scr[...] = document_bias(bounds_ref[0, pl.ds(seg, 1), :], rows, mem)
        cot = jnp.where(seg < counts_ref[item], cot_ref[0, 0], 0)
        g_scr[...] = cot
        carried = jnp.where(seg == segs - 1, 0.0, carry_scr[...])
        g_scr[rows - 16 : rows, :] = (cot[rows - 16 : rows].astype(F32) + carried).astype(BF16)

    stats = stats_ref[0]
    scale_one = stats[:, HEADS : HEADS + 1]
    scale_two = stats[:, HEADS + 1 : HEADS + 2]
    grad = g_scr[...].astype(F32)
    hat = hat_two_ref[0].astype(F32)
    sums_ref[0, :, 0:width] = column_sum(grad * hat)
    sums_ref[0, :, width : 2 * width] = column_sum(grad)
    grad_second = norm_backward(grad, hat, scale_two, gain_two)
    branch = grad_second.astype(BF16)
    branch_ref[0] = branch
    sums_ref[0, :, 2 * width : 3 * width] = column_sum(branch.astype(F32))
    sum_scr[...] = grad_second

    def ff_tile(tile, _):
        at = tile * width
        active = dot_nt(branch, weight_tile(weights, "hid", tile, 0))
        inner = (active * slope_ref[0, :, pl.ds(at, width)].astype(F32)).astype(BF16)
        inner_ref[0, :, pl.ds(at, width)] = inner
        sums_ref[0, :, pl.ds(8 * width + at, width)] = column_sum(inner.astype(F32))
        sum_scr[...] += dot_nt(inner, weight_tile(weights, "in", tile, 0))
        return _

    for tile in range(4):
        ff_tile(tile, 0)
    grad = sum_scr[...]
    hat = hat_one_ref[0].astype(F32)
    sums_ref[0, :, 3 * width : 4 * width] = column_sum(grad * hat)
    sums_ref[0, :, 4 * width : 5 * width] = column_sum(grad)
    resid = norm_backward(grad, hat, scale_one, gain_one)
    sum_scr[...] = resid
    attn = resid.astype(BF16)
    attn_ref[0] = attn
    sums_ref[0, :, 5 * width : 6 * width] = column_sum(attn.astype(F32))
    go = dot_nt(attn, weight_tile(weights, "out", 0, 0)).astype(BF16)
    go_scr[...] = go
    product = go.astype(F32) * heads_ref[0].astype(F32)
    high = product.astype(BF16)
    low = (product - high.astype(F32)).astype(BF16)
    picks = (
        lax.broadcasted_iota(jnp.int32, (16, width), 1) // HEAD_DIM
        == lax.broadcasted_iota(jnp.int32, (16, width), 0)
    ).astype(BF16)
    centres = dot_nt(picks, high) + dot_nt(picks, low)
    logs = jnp.transpose(stats)

    group = 4 * HEAD_DIM
    for number in range(width // group):
        at = number * group
        queries = mixed_ref[0, :, at : at + group] * BF16(HEAD_DIM**-0.5)
        keys = mixed_ref[0, :, width + at : width + at + group]
        values = mixed_ref[0, :, 2 * width + at : 2 * width + at + group]
        outs = go_scr[:, at : at + group]
        lanes = lax.broadcasted_iota(jnp.int32, (rows, group), 1) // HEAD_DIM

        def stack(block):
            return jnp.concatenate([jnp.where(lanes == head, block, 0) for head in range(4)], axis=0)

        def unstack(block):
            total = block[0:rows]
            for head in range(1, 4):
                total = jnp.where(lanes == head, block[head * rows : (head + 1) * rows], total)
            return total

        keys_s = stack(keys)
        scores = dot_nt(keys_s, queries)
        grad_p = dot_nt(stack(values), outs)
        probs, grads = [], []
        for head in range(4):
            row = number * 4 + head
            part = slice(head * rows, (head + 1) * rows)
            prob = jnp.exp(scores[part] + bias_scr[...] - logs[row : row + 1, :])
            grads.append((prob * (grad_p[part] - centres[row : row + 1, :])).astype(BF16))
            probs.append(prob.astype(BF16))
        grads = jnp.concatenate(grads, axis=0)
        grad_v = unstack(dot_nn(jnp.concatenate(probs, axis=0), outs))
        grad_k = unstack(dot_nn(grads, queries))
        grad_q = dot_tn(grads, keys_s)
        mix_ref[0, :, at : at + group] = (grad_q * HEAD_DIM**-0.5).astype(BF16)
        mix_ref[0, :, width + at : width + at + group] = grad_k.astype(BF16)
        mix_ref[0, :, 2 * width + at : 2 * width + at + group] = grad_v.astype(BF16)

    sums_ref[0, :, 6 * width : 7 * width] = column_sum(mix_ref[0, :, 0:width].astype(F32))
    sums_ref[0, :, 7 * width : 8 * width] = column_sum(mix_ref[0, :, 2 * width : 3 * width].astype(F32))
    total = sum_scr[...]
    for tile in range(3):
        total = total + dot_nt(
            mix_ref[0, :, tile * width : (tile + 1) * width], weight_tile(weights, "qkv", tile, 0)
        )
    result = total.astype(BF16)
    g_scr[...] = result

    @pl.when(layer == 0)
    def _():
        inputs_ref[0, 0] = result
        fresh = (seg == 0) | (resets_ref[item, seg] > 0)
        number = lax.broadcasted_iota(jnp.int32, (16, width), 0)
        folded = result[rows - 16 : rows].astype(F32) + pltpu.roll(
            result[0:16].astype(F32), 16 - mem, 0
        )
        folded = jnp.where(number >= 16 - mem, folded, 0.0).astype(BF16).astype(F32)
        init_ref[...] += jnp.where(fresh, folded, 0.0)
        carry_scr[...] = jnp.where(fresh, 0.0, folded)


def backward_steps(cot, resets, counts, bounds, mem, acts, weights, vec, saved):
    items, segs, rows, width = cot.shape
    steps = 2 * items * segs
    at = lambda t: steps - 1 - t
    by_seg = lambda t: (at(t) // (2 * segs), (at(t) // 2) % segs, 0, 0)
    by_step = lambda t: (at(t), 0, 0)
    names = ("mixed", "heads", "hat_one", "slope", "hat_two", "stats")
    outs = dict(
        branch=(rows, width), inner=(rows, 4 * width), attn=(rows, width), mix=(rows, 3 * width),
    )
    *grads, sums, inputs, memory, acts = pl.pallas_call(
        functools.partial(backward_body, steps, segs, mem),
        grid=(steps,),
        in_specs=[
            pl.BlockSpec(memory_space=pltpu.SMEM),
            pl.BlockSpec(memory_space=pltpu.SMEM),
            pl.BlockSpec((1, 1, rows, width), by_seg),
            pl.BlockSpec((1,) + bounds.shape[1:], lambda t: (at(t) // (2 * segs), 0, 0)),
            pl.BlockSpec((1, 1, rows, width), by_seg),
        ]
        + weight_specs([weight.shape for weight in weights], lambda t: at(t) % 2)
        + [pl.BlockSpec((2, 1) + vec.shape[2:], lambda t: (0, at(t) % 2, 0, 0))]
        + [pl.BlockSpec((1,) + saved[name].shape[1:], by_step) for name in names],
        out_specs=[pl.BlockSpec((1,) + shape, by_step) for shape in outs.values()]
        + [
            pl.BlockSpec((1, 1, 12 * width), by_step),
            pl.BlockSpec((1, 1, rows, width), by_seg),
            pl.BlockSpec((16, width), lambda t: (0, 0)),
            pl.BlockSpec((1, 1, rows, width), by_seg),
        ],
        out_shape=[jax.ShapeDtypeStruct((steps,) + shape, BF16) for shape in outs.values()]
        + [
            jax.ShapeDtypeStruct((steps, 1, 12 * width), F32),
            jax.ShapeDtypeStruct(cot.shape, BF16),
            jax.ShapeDtypeStruct((16, width), F32),
            jax.ShapeDtypeStruct(cot.shape, BF16),
        ],
        scratch_shapes=[
            pltpu.VMEM((rows, width), BF16),
            pltpu.VMEM((16, width), F32),
            pltpu.VMEM((rows, rows), F32),
            pltpu.VMEM((rows, width), F32),
            pltpu.VMEM((rows, width), BF16),
        ],
        compiler_params=pltpu.CompilerParams(vmem_limit_bytes=VMEM_BYTES),
        name="backward_steps",
    )(resets, counts, cot, bounds, acts, *weights, vec, *[saved[name] for name in names])
    return dict(zip(outs, grads)), sums, inputs, memory, acts


def gather_forward_body(steps, segs, *refs):
    io = refs[:5]
    qkv_src, in_src, out_src, hid_src, biases_ref, gains_ref = refs[5:11]
    outs = refs[11:21]
    full_outs = refs[21:25]
    forward_scratch = refs[25:29]
    weights = refs[29:32]
    vec = refs[32]
    (
        load_sems, end_load_sems, store_sems, x_sems, y_sems, fx_sems, fy_sems, core_sems, end_sems,
        line_core_sems, up_sems, down_sems, vec_sems,
    ) = refs[33:]
    step = pl.program_id(0)
    section, place = lax.axis_index("section"), lax.axis_index("dp")
    x, y = section % 2, section // 2
    core, z = place % 2, place // 2
    end = weights[2]
    depth, _, _, _, tall, _ = end.shape
    thin = tall // 5
    x_dev = (y * 2 + 1 - x, place)
    y_dev = ((1 - y) * 2 + x, place)
    core_dev = (section, z * 2 + 1 - core)
    up_dev = (section, (z + 1) % depth * 2 + core)
    down_dev = (section, (z + depth - 1) % depth * 2 + core)
    own_block = (y, x)
    blocks = ((y, 1 - x), (1 - y, x), (1 - y, 1 - x))

    def remote(source, target, sems, index, device):
        return pltpu.make_async_remote_copy(
            src_ref=source, dst_ref=target, send_sem=sems.at[(0, *index)], recv_sem=sems.at[(1, *index)],
            device_id=device, device_id_type=MESH,
        )


    def part_of(number, block, part):
        rows = weights[number].shape[-2] // 2
        return weights[number].at[core, block[0], block[1], pl.ds(part * rows, rows)]

    def own_part(number, part):
        rows = weights[number].shape[-2] // 2
        at = pl.multiple_of((core * 2 + part) * rows, rows)
        return (qkv_src, in_src)[number].at[0, pl.ds(at, rows)]

    def x_copy(number, part):
        return remote(own_part(number, part), part_of(number, own_block, part), x_sems, (number, part), x_dev)

    def y_copy(number, part):
        return remote(own_part(number, part), part_of(number, own_block, part), y_sems, (number, part), y_dev)

    def fy_copy(number):
        piece = part_of(number, blocks[0], 0)
        return remote(piece, piece, fy_sems, (number,), y_dev)

    def fx_copy(number):
        piece = part_of(number, blocks[1], 1)
        return remote(piece, piece, fx_sems, (number,), x_dev)

    def core_copy(number, kind, part):
        piece = part_of(number, blocks[kind], part)
        return remote(piece, piece, core_sems, (number, kind, part), core_dev)


    def eighth(at, block, first=0, rows=None):
        view = end.at[at, core, block[0], block[1]]
        return view if rows is None else view.at[pl.ds(first, rows)]

    def own_eighth(first):
        source, rows = (out_src, thin) if first == 0 else (hid_src, tall - thin)
        return source.at[0, pl.ds(pl.multiple_of((z * 2 + core) * rows, rows), rows)]

    def end_copy(axis, first):
        rows = thin if first == 0 else tall - thin
        return remote(
            own_eighth(first), eighth(z, own_block, first, rows), end_sems, (axis, 0 if first == 0 else 1),
            (x_dev, y_dev)[axis],
        )

    low = tall // 32 * 16

    def end_fy_copy():
        piece = eighth(z, blocks[0], 0, low)
        return remote(piece, piece, fy_sems, (2,), y_dev)

    def end_fx_copy():
        piece = eighth(z, blocks[1], low, tall - low)
        return remote(piece, piece, fx_sems, (2,), x_dev)

    def line_core_copy(at, kind):
        piece = eighth(at, blocks[kind])
        return remote(piece, piece, line_core_sems, (at, kind), core_dev)

    def up_copy(at, kind):
        piece = eighth(at, blocks[kind])
        return remote(piece, piece, up_sems, (at, kind), up_dev)

    def down_copy(at, kind):
        piece = eighth(at, blocks[kind])
        return remote(piece, piece, down_sems, (at, kind), down_dev)

    def vec_copy(kind):
        row = vec.at[(own_block, own_block, blocks[0])[kind]]
        return remote(row, row, vec_sems, (kind,), (x_dev, y_dev, y_dev)[kind])

    def loads():
        copies = []
        for number, source in enumerate((qkv_src, in_src)):
            rows = weights[number].shape[-2]
            for side in range(2):
                copies.append(
                    pltpu.make_async_copy(
                        source.at[0, pl.ds(side * rows, rows)], weights[number].at[side, y, x],
                        load_sems.at[number, side],
                    )
                )
        for at in range(depth):
            for side in range(2):
                for number, (source, first, rows) in enumerate(
                    ((out_src, 0, thin), (hid_src, thin, tall - thin))
                ):
                    copies.append(
                        pltpu.make_async_copy(
                            source.at[0, pl.ds((at * 2 + side) * rows, rows)],
                            end.at[at, side, y, x, pl.ds(first, rows)],
                            end_load_sems.at[at, side, number],
                        )
                    )
        return copies

    def full_stores():
        return [
            pltpu.make_async_copy(source, target, store_sems.at[number])
            for number, (source, target) in enumerate(zip((*weights, vec), full_outs))
        ]

    def spread(kind):
        @pl.when(z < depth - 1)
        def _():
            up_copy(z, kind).start()

        @pl.when(z > 0)
        def _():
            down_copy(z, kind).start()

        line_core_copy(z, kind).start()

    def hop(distance):
        for kind in range(3):

            @pl.when(z >= distance)
            def _():
                up_copy(z - distance, kind).wait_recv()

                @pl.when(z < depth - 1)
                def _():
                    up_copy(z - distance, kind).start()

                line_core_copy(z - distance, kind).start()

            @pl.when(z + distance < depth)
            def _():
                down_copy(z + distance, kind).wait_recv()

                @pl.when(z > 0)
                def _():
                    down_copy(z + distance, kind).start()

                line_core_copy(z + distance, kind).start()

    def near(number):
        x_copy(number, 0).wait_recv()
        fy_copy(number).start()
        core_copy(number, 0, 0).start()
        y_copy(number, 1).wait_recv()
        fx_copy(number).start()
        core_copy(number, 1, 1).start()

    def rest(number):
        x_copy(number, 1).wait_recv()
        core_copy(number, 0, 1).start()
        y_copy(number, 0).wait_recv()
        core_copy(number, 1, 0).start()

    def diagonal(number):
        fy_copy(number).wait_recv()
        core_copy(number, 2, 0).start()
        fx_copy(number).wait_recv()
        core_copy(number, 2, 1).start()

    def complete(number):
        for kind in range(3):
            for part in range(2):
                core_copy(number, kind, part).wait_recv()

    def before_mix():
        @pl.when(step == 0)
        def _():
            barrier = pltpu.get_barrier_semaphore()
            for device in (x_dev, y_dev, core_dev):
                pl.semaphore_signal(barrier, inc=1, device_id=device, device_id_type=MESH)

            @pl.when(z < depth - 1)
            def _():
                pl.semaphore_signal(barrier, inc=1, device_id=up_dev, device_id_type=MESH)

            @pl.when(z > 0)
            def _():
                pl.semaphore_signal(barrier, inc=1, device_id=down_dev, device_id_type=MESH)

            pl.semaphore_wait(barrier, 3 + jnp.where(z > 0, 1, 0) + jnp.where(z < depth - 1, 1, 0))
            for first in (0, thin):
                end_copy(0, first).start()
                end_copy(1, first).start()
            vec[y, x] = jnp.concatenate([biases_ref[...].astype(F32), gains_ref[...].astype(F32)], axis=1)
            vec_copy(0).start()
            vec_copy(1).start()
            x_copy(0, 0).start()
            y_copy(0, 1).start()
            x_copy(0, 1).start()
            y_copy(0, 0).start()
            for copy in loads():
                copy.start()
            for axis in range(2):
                for first in (0, thin):
                    end_copy(axis, first).wait_recv()
                (end_fy_copy, end_fx_copy)[axis]().start()
                spread(axis)
            vec_copy(0).wait_recv()
            vec_copy(2).start()
            end_fy_copy().wait_recv()
            end_fx_copy().wait_recv()
            spread(2)
            near(0)
            x_copy(1, 0).start()
            y_copy(1, 1).start()
            rest(0)
            x_copy(1, 1).start()
            y_copy(1, 0).start()
            hop(1)
            diagonal(0)
            vec_copy(1).wait_recv()
            vec_copy(2).wait_recv()
            complete(0)
            for copy in loads():
                copy.wait()

    def before_out():
        @pl.when(step == 0)
        def _():
            near(1)
            hop(2)
            rest(1)
            diagonal(1)
            hop(3)
            complete(1)
            for at in range(depth):
                for kind in range(3):
                    line_core_copy(at, kind).wait_recv()

        @pl.when(step == 1)
        def _():
            for copy in full_stores():
                copy.start()

    @pl.when(step == 0)
    def _():
        forward_scratch[0][...] = jnp.zeros_like(forward_scratch[0])

    forward_layer(
        step, segs, step % 2, before_mix, before_out, *io, weights, vec, *outs, *forward_scratch
    )

    @pl.when(step == steps - 1)
    def _():
        for copy in full_stores():
            copy.wait()
        for number in range(2):
            for part in range(2):
                x_copy(number, part).wait_send()
                y_copy(number, part).wait_send()
                for kind in range(3):
                    core_copy(number, kind, part).wait_send()
            fx_copy(number).wait_send()
            fy_copy(number).wait_send()
            for first in (0, thin):
                end_copy(number, first).wait_send()
        end_fx_copy().wait_send()
        end_fy_copy().wait_send()
        for kind in range(3):
            vec_copy(kind).wait_send()
            for at in range(depth):
                line_core_copy(at, kind).wait_send()

                @pl.when((z >= at) & (z < depth - 1))
                def _():
                    up_copy(at, kind).wait_send()

                @pl.when((z <= at) & (z > 0))
                def _():
                    down_copy(at, kind).wait_send()


def full_weight_shapes(w_qkv, w_out, w_in, w_hid):
    half, width = w_out.shape[1:]
    return [(2, 2, 2, half // 2, block.shape[2]) for block in (w_qkv, w_in)] + [
        (4, 2, 2, 2, (half + w_hid.shape[1]) // 8, width)
    ]


def gather_forward(text, resets, counts, init, bounds, blocks, biases, gains):
    steps, saved, operands, in_specs, out_specs, out_shape, scratch = forward_io(
        text, resets, counts, init, bounds
    )
    shapes = full_weight_shapes(*blocks)
    full = [pltpu.VMEM(shape, BF16) for shape in shapes] + [pltpu.VMEM((2, 2, 1, biases.shape[1] + gains.shape[1]), F32)]
    any_spec = pl.BlockSpec(memory_space=pl.ANY)
    dma = pltpu.SemaphoreType.DMA
    depth = shapes[2][0]
    *outs, acts, qkv, w_in, end, vecs = pl.pallas_call(
        functools.partial(gather_forward_body, steps, text.shape[1]),
        grid=(steps,),
        in_specs=in_specs + [any_spec] * 4 + [pl.BlockSpec(vector.shape, lambda t: (0, 0)) for vector in (biases, gains)],
        out_specs=out_specs + [any_spec] * 4,
        out_shape=out_shape + [jax.ShapeDtypeStruct(ref.shape, ref.dtype) for ref in full],
        scratch_shapes=scratch
        + full
        + [
            dma((2, 2)), dma((depth, 2, 2)), dma((4,)), dma((2, 2, 2)), dma((2, 2, 2)), dma((2, 3)),
            dma((2, 3)), dma((2, 2, 3, 2)), dma((2, 2, 2)), dma((2, depth, 3)), dma((2, depth, 3)),
            dma((2, depth, 3)), dma((2, 3)),
        ],
        compiler_params=pltpu.CompilerParams(
            vmem_limit_bytes=VMEM_BYTES, collective_id=1, has_side_effects=True
        ),
        name="gather_forward",
    )(*operands, blocks[0], blocks[2], blocks[1], blocks[3], biases, gains)
    return dict(zip(saved, outs)), acts, (qkv, w_in, end), vecs


def gather_apart(blocks, biases, gains):
    vec = jnp.concatenate([biases, gains], axis=1).astype(F32)
    w_qkv, w_out, w_in, w_hid = [
        lax.all_gather(block[0], "section").reshape(2, 2, *block.shape[1:]) for block in blocks
    ]
    half, width = w_out.shape[2:]
    full = [
        block.reshape(2, 2, 2, half // 2, -1).transpose(2, 0, 1, 3, 4) for block in (w_qkv, w_in)
    ]
    ends = [block.reshape(2, 2, 4, 2, -1, width).transpose(2, 3, 0, 1, 4, 5) for block in (w_out, w_hid)]
    vecs = lax.all_gather(vec, "section").reshape(2, 2, *vec.shape)
    return (*full, jnp.concatenate(ends, axis=4)), vecs


GRAD_NAMES = ("first", "inner", "active", "branch", "x", "mix", "heads", "attn")


def weight_grad_body(
    layer, segs_all, dp, *refs,
):
    sources = refs[:8]
    extra_ref, mine_ref, theirs_ref = refs[8:11]
    held = refs[11:19]
    wire, in_sems, extra_sem, out_sems = refs[19:23]
    core = lax.axis_index("dp") % 2
    rows = sources[0].shape[1]
    width = sources[0].shape[2]
    half = width // 2
    lanes = wire.shape[-1]
    thin = width // dp
    wide = 3 * thin

    def loads(number):
        return [
            pltpu.make_async_copy(
                sources[number].at[2 * at + layer],
                held[number].at[pl.ds(at * rows, rows)],
                in_sems.at[number, at],
            )
            for at in range(segs_all)
        ]

    for number in range(8):
        for copy in loads(number):
            copy.start()
    extra = pltpu.make_async_copy(extra_ref, wire.at[:, :, :, :, pl.ds(half, extra_ref.shape[4])], extra_sem)
    extra.start()

    def ready(*numbers):
        for number in numbers:
            for copy in loads(number):
                copy.wait()

    def stores(kind):
        return [
            pltpu.make_async_copy(wire.at[kind, core], mine_ref.at[kind], out_sems.at[kind, 0]),
            pltpu.make_async_copy(wire.at[kind, 1 - core], theirs_ref.at[kind], out_sems.at[kind, 1]),
        ]

    first, inner, active, branch, inputs, mix, heads, attn = held
    extra.wait()

    ready(0, 1)
    per_tile = width // lanes

    def in_tile(tile, _):
        right = inner[:, pl.ds(pl.multiple_of(tile * width, width), width)]
        for side in range(2):
            result = dot_tn(first[:, side * half : (side + 1) * half], right).astype(BF16)
            for at in range(per_tile):
                wire[1, at % 2, tile * (per_tile // 2) + at // 2, side, 0:half, :] = result[
                    :, at * lanes : (at + 1) * lanes
                ]
        return _

    lax.fori_loop(0, 4, in_tile, 0)
    for copy in stores(1):
        copy.start()

    ready(2, 3)
    def hid_tile(side, _):
        for part in range(4):
            left = active[:, pl.ds(pl.multiple_of(side * 4 * half + part * half, half), half)]
            result = dot_tn(left, branch[...]).astype(BF16)
            for at in range(dp):
                wire[2, at % 2, at // 2, side, 0:half, part * thin : (part + 1) * thin] = result[
                    :, at * thin : (at + 1) * thin
                ]
        return _
    lax.fori_loop(0, 2, hid_tile, 0)
    for copy in stores(2):
        copy.start()

    ready(4, 5, 6, 7)
    for side in range(2):
        left = inputs[:, side * half : (side + 1) * half]
        for tile in range(2):
            result = dot_tn(left, mix[:, tile * 3 * half : (tile + 1) * 3 * half]).astype(BF16)
            for at in range(dp // 2):
                place = tile * (dp // 2) + at
                wire[0, place % 2, place // 2, side, 0:half, 0:wide] = result[
                    :, at * wide : (at + 1) * wide
                ]
        result = dot_tn(heads[:, side * half : (side + 1) * half], attn[...]).astype(BF16)
        for at in range(dp):
            wire[0, at % 2, at // 2, side, 0:half, wide:lanes] = result[:, at * thin : (at + 1) * thin]
    for copy in stores(0):
        copy.start()
    for kind in range(3):
        for copy in stores(kind):
            copy.wait()


def weight_grads(layer, dp, saved, extras):
    sources = [saved[name] for name in GRAD_NAMES]
    steps, rows, width = sources[0].shape
    segs_all = steps // 2
    half = width // 2
    lanes = 4 * width // dp
    extra_rows = extras.shape[4]
    kind = jax.ShapeDtypeStruct((3, dp // 2, 2, half + extra_rows, lanes), BF16)
    any_spec = pl.BlockSpec(memory_space=pl.ANY)
    return pl.pallas_call(
        functools.partial(weight_grad_body, layer, segs_all, dp),
        in_specs=[any_spec] * 9,
        out_specs=[any_spec] * 2,
        out_shape=[kind, kind],
        scratch_shapes=[pltpu.VMEM((segs_all * rows, source.shape[2]), BF16) for source in sources]
        + [
            pltpu.VMEM((3, 2, dp // 2, 2, half + extra_rows, lanes), BF16),
            pltpu.SemaphoreType.DMA((8, segs_all)),
            pltpu.SemaphoreType.DMA,
            pltpu.SemaphoreType.DMA((3, 2)),
        ],
        compiler_params=pltpu.CompilerParams(vmem_limit_bytes=VMEM_BYTES),
        name="weight_grads",
    )(*sources, extras)


def add_into(ref, other):
    ref[...] = (ref[...].astype(F32) + other[...].astype(F32)).astype(BF16)


def build_extra(mem, sums_ref, memory_ref, extra):
    steps = sums_ref.shape[0]
    width = memory_ref.shape[1]
    lanes = extra.shape[-1]
    extra[...] = jnp.zeros_like(extra)
    for layer in range(2):
        total = sums_ref[layer]
        for step in range(layer + 2, steps, 2):
            total = total + sums_ref[step]
        for block, parts in enumerate(((6, 7, 5, 4, 8, 3), (9, 10, 11, 2, 1, 0))):
            for piece in range(width // lanes):
                extra[layer, block, piece * mem : (piece + 1) * mem, :] = memory_ref[
                    16 - mem : 16, piece * lanes : (piece + 1) * lanes
                ]
                for at, part in enumerate(parts):
                    row = mem * (width // lanes) + at * (width // lanes) + piece
                    first = part * width + piece * lanes
                    extra[layer, block, row : row + 1, :] = total[:, first : first + lanes]


KIND_IN, KIND_HID, KIND_MIX = 1, 2, 0
CUTS = {KIND_HID: 2, KIND_MIX: 3}
PLAN = (
    ("mul", 0, 2, 0), ("mul", 0, 2, 1), ("core", 0, 2, 0), ("QO", 2, 0), ("P", 2, 0), ("mul", 0, 1, 0),
    ("core", 0, 2, 1), ("QO", 2, 1), ("P", 2, 1), ("mul", 1, 2, 0), ("mul", 1, 2, 1), ("core", 0, 1, 0),
    ("hop", "ZO", 1, 0, 0), ("XQ", 2, 0), ("XQ", 2, 1), ("core", 1, 2, 0), ("QW", 2, 0), ("YP", 2, 0),
    ("mul", 1, 1, 0), ("core", 1, 2, 1), ("QW", 2, 1), ("hop", "ZO", 1, 0, 1), ("mul", 0, 0, 0), ("YP",
    2, 1), ("core", 0, 0, 0), ("P", 0, 0), ("P", 0, 1), ("QO", 0, 0), ("hop", "ZO", 1, 0, 2), ("core",
    1, 1, 0), ("QWA", 1, 0), ("QWA", 1, 1), ("mul", 1, 0, 0), ("plane", 2, 0), ("hop", "Z", 2, 0, 0),
    ("hop", "Z", 2, 0, 1), ("hop", "Z", 2, 0, 2), ("plane", 2, 1), ("hop", "Z", 2, 1, 0), ("hop", "Z",
    2, 1, 1), ("hop", "Z", 2, 1, 2), ("core", 1, 0, 0), ("QW", 0, 0), ("YP", 0, 0), ("QW", 0, 1), ("QO",
    0, 1), ("plane", 1, 0), ("hop", "Z", 1, 0, 0), ("hop", "Z", 1, 0, 1), ("hop", "Z", 1, 0, 2), ("XQ",
    0, 0), ("fin", "ZO", 1, 0), ("XO", 1), ("plane", 1, 1), ("hop", "Z", 1, 1, 0), ("hop", "Z", 1, 1,
    1), ("fin", "Z", 2, 0), ("YP", 0, 1), ("plane", 0, 0), ("hop", "Z", 0, 0, 0), ("hop", "Z", 0, 0, 1),
    ("hop", "Z", 0, 0, 2), ("hop", "Z", 1, 1, 2), ("YO", 1), ("XQ", 0, 1), ("plane", 0, 1), ("hop", "Z",
    0, 1, 0), ("hop", "Z", 0, 1, 1), ("hop", "Z", 0, 1, 2), ("fin", "Z", 2, 1), ("fin", "Z", 0, 0),
    ("fin", "Z", 1, 1), ("fin", "Z", 1, 0), ("fin", "Z", 0, 1),
)


def row_parts(tall, thin):
    first = -(-tall // 32) * 16
    some = ((0, first), (first, tall - first))
    return {KIND_IN: some, KIND_MIX: some, KIND_HID: ((0, 2 * thin), (2 * thin, tall - 2 * thin))}


def grad_reduce_body(dp, mem, segs_all, *refs):
    sources = refs[:8]
    sums_ref, memory_ref = refs[8:10]
    piece_out = refs[10]
    held = refs[11:19]
    mine, theirs, landed, xp, xq, yqo, yqw, yp, ywall, xo, yo, z_low, z_high, zo_low, zo_high = refs[19:34]
    extra = refs[34]
    (
        in_sems, core_sems, free_sem, xp_sems, xq_sems, yqo_sems, yqw_sems, yp_sems, single_sems, up_sems,
        down_sems, zo_up_sems, zo_down_sems,
    ) = refs[35:]
    section, place = lax.axis_index("section"), lax.axis_index("dp")
    x, y = section % 2, section // 2
    core, z = place % 2, place // 2
    depth = dp // 2
    rows, width = sources[0].shape[1:]
    half = width // 2
    tall, lanes = mine.shape[-2:]
    thin = width // dp
    wide = 3 * thin
    parts = row_parts(tall, thin)
    x_dev = (y * 2 + 1 - x, place)
    y_dev = ((1 - y) * 2 + x, place)
    core_dev = (section, z * 2 + 1 - core)
    up_dev = (section, (z + 1) % depth * 2 + core)
    down_dev = (section, (z + depth - 1) % depth * 2 + core)
    used = {KIND_IN: (0, 1), KIND_HID: (2, 3), KIND_MIX: (4, 5, 6, 7)}
    slots = {KIND_HID: 0, KIND_MIX: 1}
    first, inner, active, branch, inputs, mix, heads, attn = held
    units = [step[1:3] for step in PLAN if step[0] == "mul" and step[3] == 0]

    def loads(side, kind):
        layer = (1 - x) if side == 0 else x
        return [
            pltpu.make_async_copy(
                sources[number].at[2 * at + layer],
                held[number].at[pl.ds(at * rows, rows)],
                in_sems.at[number, at],
            )
            for number in used[kind]
            for at in range(segs_all)
        ]

    for side, kind in units:
        if side == 0:
            for copy in loads(0, kind):
                copy.start()
    barrier = pltpu.get_barrier_semaphore()
    for device in (x_dev, y_dev, core_dev):
        pl.semaphore_signal(barrier, inc=1, device_id=device, device_id_type=MESH)

    @pl.when(z < depth - 1)
    def _():
        pl.semaphore_signal(barrier, inc=1, device_id=up_dev, device_id_type=MESH)

    @pl.when(z > 0)
    def _():
        pl.semaphore_signal(barrier, inc=1, device_id=down_dev, device_id_type=MESH)

    build_extra(mem, sums_ref, memory_ref, extra)
    pl.semaphore_wait(barrier, 3 + jnp.where(z > 0, 1, 0) + jnp.where(z < depth - 1, 1, 0))

    def remote(source, target, sems, index, device):
        return pltpu.make_async_remote_copy(
            src_ref=source, dst_ref=target, send_sem=sems.at[(0, *index)], recv_sem=sems.at[(1, *index)],
            device_id=device, device_id_type=MESH,
        )

    def core_parts(kind):
        return range(2) if kind == KIND_HID else range(1)

    def core_rows(kind, part):
        return parts[kind][part] if kind == KIND_HID else (0, tall)

    def core_copy(unit, part):
        some = pl.ds(*core_rows(units[unit][1], part))
        return remote(
            theirs.at[unit % 2, :, :, some], landed.at[unit % 2, :, :, some], core_sems, (unit, part), core_dev
        )

    def p_copy(kind, part):
        at = pl.ds(0, CUTS[kind])
        some = pl.ds(*parts[kind][part])
        return remote(
            mine.at[0, kind, at, :, some], xp.at[slots[kind], at, :, some], xp_sems, (slots[kind], part), x_dev
        )

    def q_copy(side, kind, part):
        some = pl.ds(*parts[kind][part])
        count = depth - CUTS[kind]
        return remote(
            mine.at[side, kind, pl.ds(CUTS[kind], count), 1 - y, some],
            (yqo, yqw)[side].at[slots[kind], pl.ds(0, count), some],
            (yqo_sems, yqw_sems)[side], (slots[kind], part), y_dev,
        )

    def xq_copy(kind, part):
        some = pl.ds(*parts[kind][part])
        count = depth - CUTS[kind]
        return remote(
            mine.at[0, kind, pl.ds(CUTS[kind], count), y, some],
            xq.at[slots[kind], pl.ds(0, count), some], xq_sems, (slots[kind], part), x_dev,
        )

    def yp_copy(kind, part):
        some = pl.ds(*parts[kind][part])
        at = pl.ds(0, CUTS[kind])
        return remote(
            mine.at[1, kind, at, 1 - y, some], yp.at[slots[kind], at, some], yp_sems, (slots[kind], part), y_dev
        )

    def xo_copy():
        return remote(mine.at[0, KIND_IN, z], xo, single_sems, (0,), x_dev)

    def yo_copy():
        return remote(xo.at[1 - y], yo, single_sems, (1,), y_dev)

    def ywall_copy(part):
        some = pl.ds(*parts[KIND_IN][part])
        return remote(
            mine.at[1, KIND_IN, :, 1 - y, some], ywall.at[:, some], single_sems, (2 + part,), y_dev
        )

    def line_rows(kind, part):
        return pl.ds(*parts[kind][part])

    def up_copy(name, kind, part, at):
        if name == "ZO":
            return remote(mine.at[0, kind, at], zo_low.at[at - 1], zo_up_sems, (at,), up_dev)
        some = line_rows(kind, part)
        return remote(
            mine.at[1, kind, at, y, some], z_low.at[kind, at - 1, some], up_sems, (kind, part, at), up_dev
        )

    def down_copy(name, kind, part, at):
        if name == "ZO":
            return remote(mine.at[0, kind, at], zo_high.at[at], zo_down_sems, (at,), down_dev)
        some = line_rows(kind, part)
        return remote(
            mine.at[1, kind, at, y, some], z_high.at[kind, at, some], down_sems, (kind, part, at), down_dev
        )

    def from_low(name, kind, part, at):
        up_copy(name, kind, part, at).wait_recv()
        if name == "ZO":
            for block in range(2):
                add_into(mine.at[0, kind, at, block], zo_low.at[at - 1, block])
        else:
            some = line_rows(kind, part)
            add_into(mine.at[1, kind, at, y, some], z_low.at[kind, at - 1, some])

    def from_high(name, kind, part, at):
        down_copy(name, kind, part, at).wait_recv()
        if name == "ZO":
            for block in range(2):
                add_into(mine.at[0, kind, at, block], zo_high.at[at, block])
        else:
            some = line_rows(kind, part)
            add_into(mine.at[1, kind, at, y, some], z_high.at[kind, at, some])

    def multiply(side, kind, part):
        unit = units.index((side, kind))
        slot = unit % 2

        def put(chunk_core, chunk_z, block, piece, start, stop):
            @pl.when(core == chunk_core)
            def _():
                mine[side, kind, chunk_z, block, start:stop, :] = piece

            @pl.when(core != chunk_core)
            def _():
                theirs[slot, chunk_z, block, start:stop, :] = piece

        if part == 0:
            for copy in loads(side, kind):
                copy.wait()
            if unit >= 2:
                for earlier in core_parts(units[unit - 2][1]):
                    core_copy(unit - 2, earlier).wait_send()
            layer = (1 - x) if side == 0 else x
            extra_rows = tall - half
            for block in range(2):
                added = extra[layer, block, kind * extra_rows : (kind + 1) * extra_rows, :].astype(BF16)
                for at in range(depth):
                    mine[side, kind, at, block, half:, :] = added
                    theirs[slot, at, block, half:, :] = added
        if kind == KIND_IN:
            per_tile = width // lanes

            def in_tile(tile, _):
                right = inner[:, pl.ds(pl.multiple_of(tile * width, width), width)]
                for block in range(2):
                    result = dot_tn(first[:, block * half : (block + 1) * half], right).astype(BF16)
                    for at in range(per_tile):
                        put(
                            at % 2, tile * (per_tile // 2) + at // 2, block,
                            result[:, at * lanes : (at + 1) * lanes], 0, half,
                        )
                return _

            lax.fori_loop(0, 4, in_tile, 0)
        elif kind == KIND_HID:

            def hid_tile(block, _):
                right = active[:, pl.ds(pl.multiple_of((block * 2 + part) * width, width), width)]
                for side_rows in range(2):
                    result = dot_tn(
                        branch[:, side_rows * half : (side_rows + 1) * half], right
                    ).astype(BF16)
                    for at in range(dp // 2):
                        chunk = side_rows * (dp // 2) + at
                        for piece in range(2):
                            row = (part * 2 + piece) * thin
                            put(
                                chunk % 2, chunk // 2, block,
                                result[at * thin : (at + 1) * thin, piece * half : (piece + 1) * half],
                                row, row + thin,
                            )
                return _

            lax.fori_loop(0, 2, hid_tile, 0)
        else:

            def mix_tile(block, _):
                columns = pl.ds(pl.multiple_of(block * half, half), half)
                for tile in range(2):
                    result = dot_tn(
                        mix[:, tile * 3 * half : (tile + 1) * 3 * half], inputs[:, columns]
                    ).astype(BF16)
                    for at in range(depth):
                        chunk = tile * depth + at
                        put(chunk % 2, chunk // 2, block, result[at * wide : (at + 1) * wide], 0, wide)
                result = dot_tn(attn[...], heads[:, columns]).astype(BF16)
                for chunk in range(dp):
                    put(chunk % 2, chunk // 2, block, result[chunk * thin : (chunk + 1) * thin], wide, half)
                return _

            lax.fori_loop(0, 2, mix_tile, 0)
        if unit >= 2 and part == 0:
            pl.semaphore_wait(free_sem, 1)
        core_copy(unit, part).start()
        if side == 0 and part == core_parts(kind)[-1]:
            for copy in loads(1, kind):
                copy.start()

    def add_core(side, kind, part):
        unit = units.index((side, kind))
        some = pl.ds(*core_rows(kind, part))
        core_copy(unit, part).wait_recv()

        def add(at, _):
            for block in range(2):
                add_into(mine.at[side, kind, at, block, some], landed.at[unit % 2, at, block, some])
            return _

        lax.fori_loop(0, depth, add, 0)
        if unit + 2 < len(units) and part == core_parts(kind)[-1]:
            pl.semaphore_signal(free_sem, inc=1, device_id=core_dev, device_id_type=MESH)

    def forward_q(kind, part):
        q_copy(0, kind, part).wait_recv()
        some = pl.ds(*parts[kind][part])
        for at in range(depth - CUTS[kind]):
            add_into(mine.at[0, kind, CUTS[kind] + at, y, some], yqo.at[slots[kind], at, some])
        xq_copy(kind, part).start()

    def forward_p(kind, part):
        p_copy(kind, part).wait_recv()
        some = pl.ds(*parts[kind][part])
        for at in range(CUTS[kind]):
            for block in range(2):
                add_into(mine.at[1, kind, at, block, some], xp.at[slots[kind], at, block, some])
        yp_copy(kind, part).start()

    def finish_plane(kind, part):
        some = pl.ds(*parts[kind][part])
        if kind == KIND_IN:
            ywall_copy(part).wait_recv()
            for at in range(depth):
                add_into(mine.at[1, kind, at, y, some], ywall.at[at, some])
            return
        slot = slots[kind]
        q_copy(1, kind, part).wait_recv()
        xq_copy(kind, part).wait_recv()
        for at in range(depth - CUTS[kind]):
            ref = mine.at[1, kind, CUTS[kind] + at, y, some]
            total = ref[...].astype(F32) + yqw[slot, at, some].astype(F32) + xq[slot, at, some].astype(F32)
            ref[...] = total.astype(BF16)
        yp_copy(kind, part).wait_recv()
        for at in range(CUTS[kind]):
            add_into(mine.at[1, kind, at, y, some], yp.at[slot, at, some])

    def hop(name, kind, part, count):
        high = depth - 1 - count + z
        low = count - (depth - 1 - z)

        @pl.when(z <= count)
        def _():
            @pl.when(z > 0)
            def _():
                from_low(name, kind, part, high)

            up_copy(name, kind, part, high).start()

        @pl.when(low >= 0)
        def _():
            @pl.when(z < depth - 1)
            def _():
                from_high(name, kind, part, low)

            down_copy(name, kind, part, low).start()

    finished = []

    def finish(name, kind, part):
        @pl.when(z > 0)
        def _():
            from_low(name, kind, part, z)

        @pl.when(z < depth - 1)
        def _():
            from_high(name, kind, part, z)

        if name == "ZO":
            return
        some = line_rows(kind, part)
        if kind == KIND_IN:
            add_into(mine.at[1, kind, z, y, some], xo.at[y, some])
            if (name, kind, 1 - part) not in finished:
                yo_copy().wait_recv()
            add_into(mine.at[1, kind, z, y, some], yo.at[some])
        finished.append((name, kind, part))
        piece_out[kind, some, :] = mine[1, kind, z, y, some, :]

    def forward_o(kind):
        xo_copy().wait_recv()
        yo_copy().start()

    act = dict(
        mul=multiply,
        core=add_core,
        P=lambda kind, part: p_copy(kind, part).start(),
        QO=lambda kind, part: q_copy(0, kind, part).start(),
        QW=lambda kind, part: q_copy(1, kind, part).start(),
        XQ=forward_q,
        YP=forward_p,
        plane=finish_plane,
        hop=hop,
        fin=finish,
        XO=lambda kind: xo_copy().start(),
        YO=forward_o,
        QWA=lambda kind, part: ywall_copy(part).start(),
    )
    for name, *numbers in PLAN:
        act[name](*numbers)

    for unit in (4, 5):
        for part in core_parts(units[unit][1]):
            core_copy(unit, part).wait_send()
    for copy in (xo_copy(), yo_copy(), ywall_copy(0), ywall_copy(1)):
        copy.wait_send()
    for kind in CUTS:
        for part in range(2):
            p_copy(kind, part).wait_send()
            xq_copy(kind, part).wait_send()
            yp_copy(kind, part).wait_send()
            for side in range(2):
                q_copy(side, kind, part).wait_send()
    lines = [("ZO", KIND_IN, 0)]
    lines += [("Z", kind, part) for kind in (KIND_IN, *CUTS) for part in range(2)]
    for line in lines:
        for at in range(depth):

            @pl.when(at > z)
            def _():
                up_copy(*line, at).wait_send()

            @pl.when(at < z)
            def _():
                down_copy(*line, at).wait_send()


def grad_reduce_shapes(dp, steps, rows, width):
    half = width // 2
    lanes = 4 * width // dp
    depth = dp // 2
    extra_rows = 16
    tall = half + extra_rows
    most, least = max(CUTS.values()), depth - min(CUTS.values())
    held = [width, 4 * width, 4 * width, width, width, 3 * width, width, width]
    return (
        [pltpu.VMEM((steps // 2 * rows, columns), BF16) for columns in held]
        + [
            pltpu.VMEM(shape + (tall, lanes), BF16)
            for shape in (
                (2, 3, depth, 2), (2, depth, 2), (2, depth, 2), (2, most, 2), (2, least), (2, least),
                (2, least), (2, most), (depth,), (2,), (), (3, depth - 1), (3, depth - 1),
                (depth - 1, 2), (depth - 1, 2),
            )
        ]
        + [pltpu.VMEM((2, 2, 3 * extra_rows, lanes), F32)]
    )


def unpack_body(mem, piece_ref, qkv_ref, out_ref, in_ref, hid_ref, memory_ref, bias_ref, gain_ref, vec_scr):
    wide, half = qkv_ref.shape[1:]
    thin, lanes = out_ref.shape[1], in_ref.shape[2]
    width = memory_ref.shape[1]
    qkv_ref[0] = piece_ref[0, 0:wide, :].astype(F32)
    out_ref[0] = piece_ref[0, wide:half, :].astype(F32)
    in_ref[0] = piece_ref[1, 0:half, :].astype(F32)
    for part in range(4):
        hid_ref[0, :, part * half : (part + 1) * half] = piece_ref[
            2, part * thin : (part + 1) * thin, :
        ].astype(F32)
    extra = jnp.concatenate([piece_ref[kind, half:, :].astype(F32) for kind in range(3)], axis=0)
    pieces = width // lanes
    for piece in range(pieces):
        memory_ref[:, piece * lanes : (piece + 1) * lanes] = extra[piece * mem : (piece + 1) * mem, :]
    for at in range(6 * pieces):
        row = mem * pieces + at
        vec_scr[0:1, at * lanes : (at + 1) * lanes] = extra[row : row + 1, :]
    place = lax.axis_index("dp")
    long = 5 * width
    for ref, first, last in ((bias_ref, 0, long), (gain_ref, long, long + width)):
        size = ref.shape[1]
        turned = pltpu.roll(vec_scr[:, first:last], (last - first - place * size) % (last - first), 1)
        ref[...] = turned[0:1, 0:size]


def grad_reduce(dp, mem, saved, sums, memory):
    sources = [saved[name] for name in GRAD_NAMES]
    steps, rows, width = sources[0].shape
    segs_all = steps // 2
    half = width // 2
    lanes = 4 * width // dp
    thin = width // dp
    depth = dp // 2
    any_spec = pl.BlockSpec(memory_space=pl.ANY)
    dma = pltpu.SemaphoreType.DMA
    shapes = grad_reduce_shapes(dp, steps, rows, width)
    piece = pl.pallas_call(
        functools.partial(grad_reduce_body, dp, mem, segs_all),
        in_specs=[any_spec] * 8 + [pl.BlockSpec(memory_space=pltpu.VMEM)] * 2,
        out_specs=pl.BlockSpec(memory_space=pltpu.VMEM),
        out_shape=jax.ShapeDtypeStruct((3,) + shapes[8].shape[-2:], BF16),
        scratch_shapes=shapes
        + [
            dma((8, segs_all)), dma((2, 6, 2)), pltpu.SemaphoreType.REGULAR, dma((2, 2, 2)), dma((2, 2, 2)),
            dma((2, 2, 2)), dma((2, 2, 2)), dma((2, 2, 2)), dma((2, 4)), dma((2, 3, 2, depth)),
            dma((2, 3, 2, depth)), dma((2, depth)), dma((2, depth)),
        ],
        compiler_params=pltpu.CompilerParams(
            vmem_limit_bytes=VMEM_BYTES, collective_id=0, has_side_effects=True
        ),
        name="grad_reduce",
    )(*sources, sums, memory)
    qkv, out, w_in, hid, memory, bias, gain = pl.pallas_call(
        functools.partial(unpack_body, mem),
        out_shape=[
            jax.ShapeDtypeStruct(shape, F32)
            for shape in (
                (1, 3 * thin, half), (1, thin, half), (1, half, lanes), (1, thin, 4 * half),
                (mem, width), (1, 5 * thin), (1, thin),
            )
        ],
        scratch_shapes=[pltpu.VMEM((8, 6 * width), F32)],
        name="unpack",
    )(piece)
    grads = (jnp.swapaxes(qkv, 1, 2), jnp.swapaxes(out, 1, 2), w_in, jnp.swapaxes(hid, 1, 2))
    return (memory, *grads, bias, gain)


def other_core(block, dp):
    return lax.ppermute(block, "dp", [(at, at ^ 1) for at in range(dp)])


def per_device(
    text_rows,
    memory_init,
    cotangent,
    w_qkv,
    w_out,
    w_in,
    w_hid,
    biases,
    norm_gains,
    boundaries,
    mem_resets,
    seg_counts,
):
    items, segs, text_len, width = text_rows.shape
    mem_rows = memory_init.shape[0]
    rows = text_len + 2 * mem_rows
    half = width // 2
    dp = lax.axis_size("dp")
    blocks = (w_qkv, w_out, w_in, w_hid)
    steps = 2 * items * segs
    if dp == 8:
        saved, acts, weights, vecs = gather_forward(
            text_rows, mem_resets, seg_counts, memory_init, boundaries, blocks, biases, norm_gains
        )
    else:
        weights, vecs = gather_apart(blocks, biases, norm_gains)
        saved, acts = forward_steps(
            text_rows, mem_resets, seg_counts, memory_init, boundaries, weights, vecs
        )
    grads, sums, input_grads, memory_grad, acts = backward_steps(
        cotangent, mem_resets, seg_counts, boundaries, mem_rows, acts, weights, vecs, saved
    )
    saved.update(grads)
    reduce = grad_reduce if dp == 8 else grad_reduce_apart
    return (acts, input_grads, *reduce(dp, mem_rows, saved, sums, memory_grad))


def grad_reduce_apart(dp, mem_rows, saved, sums, memory_grad):
    steps, width = sums.shape[0], memory_grad.shape[1]
    half = width // 2
    vector_len = 5 * width
    lanes = 4 * width // dp
    memory_part = memory_grad[16 - mem_rows :].reshape(-1)
    memory_len = -(-memory_part.shape[0] // lanes) * lanes
    memory_part = jnp.pad(memory_part, (0, memory_len - memory_part.shape[0]))
    vector_part = vector_len // dp
    gain_part = width // dp
    used = memory_len + vector_part + gain_part
    extra_rows = -(-used // (3 * 16 * lanes)) * 16
    extras = []
    for layer in range(2):
        total = sums.reshape(steps // 2, 2, 12 * width)[:, layer].sum(axis=0)
        gain_two, shift_two, bias_hid, gain_one, shift_one, bias_o, bias_q, bias_v = [
            total[at * width : (at + 1) * width] for at in range(8)
        ]
        vector = jnp.concatenate(
            [bias_q, bias_v, bias_o, shift_one, total[8 * width :], bias_hid, shift_two]
        ).reshape(2, dp, vector_part)
        gain = jnp.stack([gain_one, gain_two]).reshape(2, dp, gain_part)
        extra = jnp.concatenate(
            [jnp.broadcast_to(memory_part, (2, dp, memory_len)), vector, gain], axis=-1
        )
        extra = jnp.pad(extra, ((0, 0), (0, 0), (0, 3 * extra_rows * lanes - used)))
        extra = extra.reshape(2, dp // 2, 2, 3, extra_rows, lanes).transpose(3, 2, 1, 0, 4, 5)
        extras.append(extra.astype(BF16))
    extras = jnp.stack(extras)
    wires = [weight_grads(layer, dp, saved, extras[layer]) for layer in range(2)]
    mine = jnp.stack([wires[0][0], wires[1][0]])
    theirs = other_core(jnp.stack([wires[0][1], wires[1][1]]), dp)
    both = mine.astype(F32) + theirs.astype(F32)
    both = both.transpose(3, 0, 2, 1, 4, 5).astype(BF16)
    tall, lanes = both.shape[-2:]
    both = both.reshape(4, dp // 2, 3, tall, lanes)
    own = lax.psum_scatter(both, "section", scatter_dimension=0, tiled=True)[0]
    groups = [[2 * at + side for at in range(dp // 2)] for side in range(2)]
    own = lax.psum_scatter(
        own, "dp", scatter_dimension=0, axis_index_groups=groups, tiled=True
    )[0].astype(F32)
    thin = lanes // 4
    body = own[:, :half]
    hid = body[2].reshape(half, 4, thin).transpose(1, 0, 2).reshape(4 * half, thin)
    flat = own[:, half:].reshape(-1)
    return (
        flat[: mem_rows * width].reshape(mem_rows, width),
        body[0, :, : 3 * thin][None],
        body[0, :, 3 * thin :][None],
        body[1][None],
        hid[None],
        flat[memory_len : memory_len + vector_part][None],
        flat[memory_len + vector_part : used][None],
    )


def solution(mesh):
    in_specs = (
        P(("section", "dp"), None, None, None),
        P(),
        P(("section", "dp"), None, None, None),
        P("section", None, None),
        P("section", None, None),
        P("section", None, None),
        P("section", None, None),
        P("section", None),
        P("section", None),
        P(("section", "dp"), None, None),
        P(("section", "dp"), None),
        P(("section", "dp")),
    )
    out_specs = (
        P(("section", "dp"), None, None, None),
        P(("section", "dp"), None, None, None),
        P(),
        P("section", None, "dp"),
        P("section", None, "dp"),
        P("section", None, "dp"),
        P("section", None, "dp"),
        P("section", "dp"),
        P("section", "dp"),
    )
    return jax.shard_map(
        per_device, mesh=mesh, in_specs=in_specs, out_specs=out_specs, check_vma=False
    )
```

```python
import functools

import jax
import jax.numpy as jnp
from jax import lax
from jax.experimental import pallas as pl
from jax.experimental.pallas import tpu as pltpu
from jax.sharding import PartitionSpec as P

HEADS = 12
HEAD_DIM = 64
EPS = 1e-05
MASKED = -1e30
VMEM_BYTES = 63 * 2**20
F32 = jnp.float32
BF16 = jnp.bfloat16
MESH = pl.DeviceIdType.MESH


def dot_nn(one, two):
    return jnp.dot(one, two, preferred_element_type=F32)


def dot_nt(one, two):
    return lax.dot_general(one, two, (((1,), (1,)), ((), ())), preferred_element_type=F32)


def dot_tn(one, two):
    return lax.dot_general(one, two, (((0,), (0,)), ((), ())), preferred_element_type=F32)


def weight_tile(refs, kind, tile, layer):
    qkv_ref, in_ref, end_ref = refs
    quarters, _, _, _, tall, width = end_ref.shape
    thin = tall // 5
    if kind == "out":
        pieces = [
            end_ref[quarter, core, half, layer, 0:thin]
            for half in range(2)
            for quarter in range(quarters)
            for core in range(2)
        ]
    elif kind == "hid":
        pieces = [
            end_ref[(tile % 2) * (quarters // 2) + at, core, tile // 2, layer, thin:tall]
            for at in range(quarters // 2)
            for core in range(2)
        ]
    else:
        ref = qkv_ref if kind == "qkv" else in_ref
        at = tile * width if isinstance(tile, int) else pl.multiple_of(tile * width, width)
        pieces = [ref[core, half, layer, :, pl.ds(at, width)] for half in range(2) for core in range(2)]
    return jnp.concatenate(pieces, axis=0)


def weight_specs(shapes, layer_of):
    specs = []
    for shape in shapes:
        lead = len(shape) - 3
        block = shape[:lead] + (1,) + shape[lead + 1 :]
        specs.append(
            pl.BlockSpec(block, lambda t, *_, lead=lead: (0,) * lead + (layer_of(t), 0, 0))
        )
    return specs


def head_lanes(shape, head):
    lanes = lax.broadcasted_iota(jnp.int32, shape, 1)
    return (lanes // HEAD_DIM) == head


def erf_parts(values):
    density = jnp.exp(-0.5 * values * values) * 0.3989422804014327
    phi = 0.5 * (1.0 + lax.erf(values * 0.7071067811865476))
    return phi, density


def vector_rows(vec_ref, layer, width):
    row = lambda half, at: vec_ref[half, layer, :, at * width : (at + 1) * width]
    return dict(
        bias_q=row(0, 0), bias_v=row(0, 1), bias_o=row(0, 2), shift_one=row(0, 3),
        bias_in=(row(0, 4), row(1, 0), row(1, 1), row(1, 2)),
        bias_hid=row(1, 3), shift_two=row(1, 4), gain_one=row(0, 5), gain_two=row(1, 5),
    )


def ones_where(shape, condition):
    rows = lax.broadcasted_iota(jnp.int32, shape, 0)
    columns = lax.broadcasted_iota(jnp.int32, shape, 1)
    return condition(rows, columns).astype(BF16)


def document_bias(bounds, rows, mem):
    text = bounds.shape[1]
    eight = jnp.broadcast_to(bounds, (8, text)).astype(BF16)
    upto = ones_where((text, rows), lambda r, c: r <= c - mem)
    below = ones_where((rows, text), lambda r, c: c <= r - mem)
    columns = dot_nn(eight, upto)[0:1]
    lines = dot_nt(below, eight)[:, 0:1]
    place = lax.broadcasted_iota(jnp.int32, (1, rows), 1)
    columns = jnp.where((place < mem) | (place >= mem + text), -1.0, columns)
    place = lax.broadcasted_iota(jnp.int32, (rows, 1), 0)
    lines = jnp.where((place < mem) | (place >= mem + text), -1.0, lines)
    allowed = (lines == columns) | (lines < 0) | (columns < 0)
    return jnp.where(allowed, 0.0, MASKED)


def norm_forward(values):
    offset = values - jnp.mean(values, axis=-1, keepdims=True)
    scale = lax.rsqrt(jnp.mean(offset * offset, axis=-1, keepdims=True) + EPS)
    return offset * scale, scale


def forward_layer(
    step, segs, at_layer, before_mix, before_out, resets_ref, counts_ref, text_ref, init_ref,
    bounds_ref, weights, vec_ref,
    x_ref, mixed_ref, heads_ref, hat_one_ref, first_ref, active_ref, slope_ref, hat_two_ref,
    stats_ref, acts_ref, y_scr, bias_scr, sum_scr, bias_in_scr,
):
    rows, width = y_scr.shape
    text_len, mem = text_ref.shape[2], init_ref.shape[0]
    layer, seg, item = step % 2, (step // 2) % segs, step // (2 * segs)

    @pl.when(layer == 0)
    def _():
        fresh = (seg == 0) | (resets_ref[item, seg] > 0)
        place = ones_where((rows, text_len), lambda r, c: r - mem == c)
        start = ones_where((rows, mem), lambda r, c: (r == c) | (r - mem - text_len == c))
        again = ones_where(
            (rows, rows),
            lambda r, c: ((r < mem) & (r + mem + text_len == c)) | ((r >= mem + text_len) & (r == c)),
        )
        memory = jnp.where(fresh, dot_nn(start, init_ref[...]), dot_nn(again, y_scr[...]))
        x_ref[0] = (dot_nn(place, text_ref[0, 0]) + memory).astype(BF16)
        bias_scr[...] = document_bias(bounds_ref[0, pl.ds(seg, 1), :], rows, mem)

    @pl.when(layer == 1)
    def _():
        x_ref[0] = y_scr[...]

    before_mix()
    vec = vector_rows(vec_ref, at_layer, width)
    for part in range(4):
        bias_in_scr[part] = vec["bias_in"][part]
    inputs = x_ref[0]
    for tile in range(3):
        mixed = dot_nn(inputs, weight_tile(weights, "qkv", tile, at_layer))
        if tile == 0:
            mixed = mixed + vec["bias_q"]
        if tile == 2:
            mixed = mixed + vec["bias_v"]
        mixed_ref[0, :, tile * width : (tile + 1) * width] = mixed.astype(BF16)

    group = 4 * HEAD_DIM
    stat_lane = lax.broadcasted_iota(jnp.int32, (rows, 128), 1)
    stats = jnp.zeros((rows, 128), F32)
    for number in range(width // group):
        at = number * group
        queries = mixed_ref[0, :, at : at + group] * BF16(HEAD_DIM**-0.5)
        keys = mixed_ref[0, :, width + at : width + at + group]
        values = mixed_ref[0, :, 2 * width + at : 2 * width + at + group]
        lanes = lax.broadcasted_iota(jnp.int32, (rows, group), 1) // HEAD_DIM
        stacked = jnp.concatenate([jnp.where(lanes == head, queries, 0) for head in range(4)], axis=0)
        scores = dot_nt(stacked, keys)
        probs = []
        for head in range(4):
            part = scores[head * rows : (head + 1) * rows] + bias_scr[...]
            peak = jnp.max(part, axis=-1, keepdims=True)
            expo = jnp.exp(part - peak)
            norm = jnp.sum(expo, axis=-1, keepdims=True)
            probs.append((expo * (1.0 / norm)).astype(BF16))
            stats = jnp.where(stat_lane == number * 4 + head, peak + jnp.log(norm), stats)
        result = dot_nn(jnp.concatenate(probs, axis=0), values)
        total = result[0:rows]
        for head in range(1, 4):
            total = jnp.where(lanes == head, result[head * rows : (head + 1) * rows], total)
        heads_ref[0, :, at : at + group] = total.astype(BF16)
    stats_ref[0] = stats

    before_out()
    attn = dot_nn(heads_ref[0], weight_tile(weights, "out", 0, at_layer)) + vec["bias_o"]
    hat, scale = norm_forward(x_ref[0].astype(F32) + attn)
    hat_one_ref[0] = hat.astype(BF16)
    stats = jnp.where(stat_lane == HEADS, scale, stats_ref[0])
    first = hat * vec["gain_one"] + vec["shift_one"]
    first_ref[0] = first.astype(BF16)
    sum_scr[...] = first + vec["bias_hid"]

    def ff_tile(tile, _):
        at = tile * width
        inner = dot_nn(first_ref[0], weight_tile(weights, "in", tile, at_layer)) + bias_in_scr[tile]
        phi, density = erf_parts(inner)
        active = (inner * phi).astype(BF16)
        active_ref[0, :, pl.ds(at, width)] = active
        slope_ref[0, :, pl.ds(at, width)] = (phi + inner * density).astype(BF16)
        sum_scr[...] += dot_nn(active, weight_tile(weights, "hid", tile, at_layer))
        return _

    for tile in range(4):
        ff_tile(tile, 0)
    hat, scale = norm_forward(sum_scr[...])
    hat_two_ref[0] = hat.astype(BF16)
    stats_ref[0] = jnp.where(stat_lane == HEADS + 1, scale, stats)
    result = (hat * vec["gain_two"] + vec["shift_two"]).astype(BF16)
    y_scr[...] = result

    @pl.when(layer == 1)
    def _():
        acts_ref[0, 0] = jnp.where(seg < counts_ref[item], result, 0)


def saved_shapes(rows, width):
    return dict(
        x=((rows, width), BF16),
        mixed=((rows, 3 * width), BF16),
        heads=((rows, width), BF16),
        hat_one=((rows, width), BF16),
        first=((rows, width), BF16),
        active=((rows, 4 * width), BF16),
        slope=((rows, 4 * width), BF16),
        hat_two=((rows, width), BF16),
        stats=((rows, 128), F32),
    )


def forward_io(text, resets, counts, init, bounds):
    items, segs, text_len, width = text.shape
    rows = text_len + 2 * init.shape[0]
    steps = 2 * items * segs
    saved = saved_shapes(rows, width)
    by_seg = lambda t: (t // (2 * segs), (t // 2) % segs, 0, 0)
    operands = [resets, counts, text, init, bounds]
    in_specs = [
        pl.BlockSpec(memory_space=pltpu.SMEM),
        pl.BlockSpec(memory_space=pltpu.SMEM),
        pl.BlockSpec((1, 1, text_len, width), by_seg),
        pl.BlockSpec(init.shape, lambda t: (0, 0)),
        pl.BlockSpec((1, segs, text_len), lambda t: (t // (2 * segs), 0, 0)),
    ]
    out_specs = [pl.BlockSpec((1,) + shape, lambda t: (t, 0, 0)) for shape, _ in saved.values()]
    out_specs.append(pl.BlockSpec((1, 1, rows, width), by_seg))
    out_shape = [jax.ShapeDtypeStruct((steps,) + shape, kind) for shape, kind in saved.values()]
    out_shape.append(jax.ShapeDtypeStruct((items, segs, rows, width), BF16))
    scratch = [
        pltpu.VMEM((rows, width), BF16),
        pltpu.VMEM((rows, rows), F32),
        pltpu.VMEM((rows, width), F32),
        pltpu.VMEM((4, 1, width), F32),
    ]
    return steps, saved, operands, in_specs, out_specs, out_shape, scratch


def nothing():
    pass


def forward_body(segs, *refs):
    step = pl.program_id(0)
    y_scr = refs[19]

    @pl.when(step == 0)
    def _():
        y_scr[...] = jnp.zeros_like(y_scr)

    forward_layer(step, segs, 0, nothing, nothing, *refs[:5], refs[5:8], *refs[8:])


def forward_steps(text, resets, counts, init, bounds, weights, vec):
    steps, saved, operands, in_specs, out_specs, out_shape, scratch = forward_io(
        text, resets, counts, init, bounds
    )
    *outs, acts = pl.pallas_call(
        functools.partial(forward_body, text.shape[1]),
        grid=(steps,),
        in_specs=in_specs
        + weight_specs([weight.shape for weight in weights], lambda t: t % 2)
        + [pl.BlockSpec((2, 1) + vec.shape[2:], lambda t: (0, t % 2, 0, 0))],
        out_specs=out_specs,
        out_shape=out_shape,
        scratch_shapes=scratch,
        compiler_params=pltpu.CompilerParams(vmem_limit_bytes=VMEM_BYTES),
        name="forward_steps",
    )(*operands, *weights, vec)
    return dict(zip(saved, outs)), acts


def norm_backward(grad, hat, scale, gain):
    scaled = grad * gain
    mean_one = jnp.mean(scaled, axis=-1, keepdims=True)
    mean_two = jnp.mean(scaled * hat, axis=-1, keepdims=True)
    return (scaled - mean_one - hat * mean_two) * scale


def column_sum(values):
    return jnp.sum(values, axis=0, keepdims=True)


def backward_body(
    count, segs, mem, resets_ref, counts_ref, cot_ref, bounds_ref, acts_ref, qkv_ref, in_ref, end_ref,
    vec_ref, mixed_ref, heads_ref, hat_one_ref, slope_ref, hat_two_ref, stats_ref,
    branch_ref, inner_ref, attn_ref, mix_ref, sums_ref, inputs_ref, init_ref, acts_out_ref,
    g_scr, carry_scr, bias_scr, sum_scr, go_scr,
):
    step = count - 1 - pl.program_id(0)
    layer = step % 2
    seg = (step // 2) % segs
    rows, width = g_scr.shape
    item = step // (2 * segs)
    weights = (qkv_ref, in_ref, end_ref)
    vec = vector_rows(vec_ref, 0, width)
    gain_one, gain_two = vec["gain_one"], vec["gain_two"]

    @pl.when(pl.program_id(0) == 0)
    def _():
        carry_scr[...] = jnp.zeros_like(carry_scr)
        init_ref[...] = jnp.zeros_like(init_ref)

    @pl.when(layer == 1)
    def _():
        acts_out_ref[...] = acts_ref[...]
        bias_scr[...] = document_bias(bounds_ref[0, pl.ds(seg, 1), :], rows, mem)
        cot = jnp.where(seg < counts_ref[item], cot_ref[0, 0], 0)
        g_scr[...] = cot
        carried = jnp.where(seg == segs - 1, 0.0, carry_scr[...])
        g_scr[rows - 16 : rows, :] = (cot[rows - 16 : rows].astype(F32) + carried).astype(BF16)

    stats = stats_ref[0]
    scale_one = stats[:, HEADS : HEADS + 1]
    scale_two = stats[:, HEADS + 1 : HEADS + 2]
    grad = g_scr[...].astype(F32)
    hat = hat_two_ref[0].astype(F32)
    sums_ref[0, :, 0:width] = column_sum(grad * hat)
    sums_ref[0, :, width : 2 * width] = column_sum(grad)
    grad_second = norm_backward(grad, hat, scale_two, gain_two)
    branch = grad_second.astype(BF16)
    branch_ref[0] = branch
    sums_ref[0, :, 2 * width : 3 * width] = column_sum(branch.astype(F32))
    sum_scr[...] = grad_second

    def ff_tile(tile, _):
        at = tile * width
        active = dot_nt(branch, weight_tile(weights, "hid", tile, 0))
        inner = (active * slope_ref[0, :, pl.ds(at, width)].astype(F32)).astype(BF16)
        inner_ref[0, :, pl.ds(at, width)] = inner
        sums_ref[0, :, pl.ds(8 * width + at, width)] = column_sum(inner.astype(F32))
        sum_scr[...] += dot_nt(inner, weight_tile(weights, "in", tile, 0))
        return _

    for tile in range(4):
        ff_tile(tile, 0)
    grad = sum_scr[...]
    hat = hat_one_ref[0].astype(F32)
    sums_ref[0, :, 3 * width : 4 * width] = column_sum(grad * hat)
    sums_ref[0, :, 4 * width : 5 * width] = column_sum(grad)
    resid = norm_backward(grad, hat, scale_one, gain_one)
    sum_scr[...] = resid
    attn = resid.astype(BF16)
    attn_ref[0] = attn
    sums_ref[0, :, 5 * width : 6 * width] = column_sum(attn.astype(F32))
    go = dot_nt(attn, weight_tile(weights, "out", 0, 0)).astype(BF16)
    go_scr[...] = go
    product = go.astype(F32) * heads_ref[0].astype(F32)
    high = product.astype(BF16)
    low = (product - high.astype(F32)).astype(BF16)
    picks = (
        lax.broadcasted_iota(jnp.int32, (16, width), 1) // HEAD_DIM
        == lax.broadcasted_iota(jnp.int32, (16, width), 0)
    ).astype(BF16)
    centres = dot_nt(picks, high) + dot_nt(picks, low)
    logs = jnp.transpose(stats)

    group = 4 * HEAD_DIM
    for number in range(width // group):
        at = number * group
        queries = mixed_ref[0, :, at : at + group] * BF16(HEAD_DIM**-0.5)
        keys = mixed_ref[0, :, width + at : width + at + group]
        values = mixed_ref[0, :, 2 * width + at : 2 * width + at + group]
        outs = go_scr[:, at : at + group]
        lanes = lax.broadcasted_iota(jnp.int32, (rows, group), 1) // HEAD_DIM

        def stack(block):
            return jnp.concatenate([jnp.where(lanes == head, block, 0) for head in range(4)], axis=0)

        def unstack(block):
            total = block[0:rows]
            for head in range(1, 4):
                total = jnp.where(lanes == head, block[head * rows : (head + 1) * rows], total)
            return total

        keys_s = stack(keys)
        scores = dot_nt(keys_s, queries)
        grad_p = dot_nt(stack(values), outs)
        probs, grads = [], []
        for head in range(4):
            row = number * 4 + head
            part = slice(head * rows, (head + 1) * rows)
            prob = jnp.exp(scores[part] + bias_scr[...] - logs[row : row + 1, :])
            grads.append((prob * (grad_p[part] - centres[row : row + 1, :])).astype(BF16))
            probs.append(prob.astype(BF16))
        grads = jnp.concatenate(grads, axis=0)
        grad_v = unstack(dot_nn(jnp.concatenate(probs, axis=0), outs))
        grad_k = unstack(dot_nn(grads, queries))
        grad_q = dot_tn(grads, keys_s)
        mix_ref[0, :, at : at + group] = (grad_q * HEAD_DIM**-0.5).astype(BF16)
        mix_ref[0, :, width + at : width + at + group] = grad_k.astype(BF16)
        mix_ref[0, :, 2 * width + at : 2 * width + at + group] = grad_v.astype(BF16)

    sums_ref[0, :, 6 * width : 7 * width] = column_sum(mix_ref[0, :, 0:width].astype(F32))
    sums_ref[0, :, 7 * width : 8 * width] = column_sum(mix_ref[0, :, 2 * width : 3 * width].astype(F32))
    total = sum_scr[...]
    for tile in range(3):
        total = total + dot_nt(
            mix_ref[0, :, tile * width : (tile + 1) * width], weight_tile(weights, "qkv", tile, 0)
        )
    result = total.astype(BF16)
    g_scr[...] = result

    @pl.when(layer == 0)
    def _():
        inputs_ref[0, 0] = result
        fresh = (seg == 0) | (resets_ref[item, seg] > 0)
        number = lax.broadcasted_iota(jnp.int32, (16, width), 0)
        folded = result[rows - 16 : rows].astype(F32) + pltpu.roll(
            result[0:16].astype(F32), 16 - mem, 0
        )
        folded = jnp.where(number >= 16 - mem, folded, 0.0).astype(BF16).astype(F32)
        init_ref[...] += jnp.where(fresh, folded, 0.0)
        carry_scr[...] = jnp.where(fresh, 0.0, folded)


def backward_steps(cot, resets, counts, bounds, mem, acts, weights, vec, saved):
    items, segs, rows, width = cot.shape
    steps = 2 * items * segs
    at = lambda t: steps - 1 - t
    by_seg = lambda t: (at(t) // (2 * segs), (at(t) // 2) % segs, 0, 0)
    by_step = lambda t: (at(t), 0, 0)
    names = ("mixed", "heads", "hat_one", "slope", "hat_two", "stats")
    outs = dict(
        branch=(rows, width), inner=(rows, 4 * width), attn=(rows, width), mix=(rows, 3 * width),
    )
    *grads, sums, inputs, memory, acts = pl.pallas_call(
        functools.partial(backward_body, steps, segs, mem),
        grid=(steps,),
        in_specs=[
            pl.BlockSpec(memory_space=pltpu.SMEM),
            pl.BlockSpec(memory_space=pltpu.SMEM),
            pl.BlockSpec((1, 1, rows, width), by_seg),
            pl.BlockSpec((1,) + bounds.shape[1:], lambda t: (at(t) // (2 * segs), 0, 0)),
            pl.BlockSpec((1, 1, rows, width), by_seg),
        ]
        + weight_specs([weight.shape for weight in weights], lambda t: at(t) % 2)
        + [pl.BlockSpec((2, 1) + vec.shape[2:], lambda t: (0, at(t) % 2, 0, 0))]
        + [pl.BlockSpec((1,) + saved[name].shape[1:], by_step) for name in names],
        out_specs=[pl.BlockSpec((1,) + shape, by_step) for shape in outs.values()]
        + [
            pl.BlockSpec((1, 1, 12 * width), by_step),
            pl.BlockSpec((1, 1, rows, width), by_seg),
            pl.BlockSpec((16, width), lambda t: (0, 0)),
            pl.BlockSpec((1, 1, rows, width), by_seg),
        ],
        out_shape=[jax.ShapeDtypeStruct((steps,) + shape, BF16) for shape in outs.values()]
        + [
            jax.ShapeDtypeStruct((steps, 1, 12 * width), F32),
            jax.ShapeDtypeStruct(cot.shape, BF16),
            jax.ShapeDtypeStruct((16, width), F32),
            jax.ShapeDtypeStruct(cot.shape, BF16),
        ],
        scratch_shapes=[
            pltpu.VMEM((rows, width), BF16),
            pltpu.VMEM((16, width), F32),
            pltpu.VMEM((rows, rows), F32),
            pltpu.VMEM((rows, width), F32),
            pltpu.VMEM((rows, width), BF16),
        ],
        compiler_params=pltpu.CompilerParams(vmem_limit_bytes=VMEM_BYTES),
        name="backward_steps",
    )(resets, counts, cot, bounds, acts, *weights, vec, *[saved[name] for name in names])
    return dict(zip(outs, grads)), sums, inputs, memory, acts


GATHER_START = (
    ("start", 0, 0, 0), ("start", 1, 0, 1),
)
GATHER_FIRST = (
    ("forward_end", 0), ("spread", 0), ("forward_end", 1), ("forward_vec",), ("spread", 1), ("start", 0,
    0, 1), ("start", 1, 0, 0), ("spread", 2), ("forward_part", 0, 0), ("forward_part", 1, 0), ("start",
    0, 1, 0), ("start", 1, 1, 1), ("hop", 1, 0), ("hop", 1, 1), ("share_part", 0, 0), ("share_part", 1,
    0), ("start", 0, 1, 1), ("start", 1, 1, 0), ("hop", 1, 2), ("share_diagonal", 0),
)
GATHER_THEN = (
    ("hop", 2, 0), ("hop", 2, 1), ("forward_part", 0, 1), ("forward_part", 1, 1), ("hop", 2, 2),
    ("share_part", 0, 1), ("share_part", 1, 1), ("hop", 3, 0), ("hop", 3, 1), ("share_diagonal", 1),
    ("hop", 3, 2),
)


def gather_forward_body(steps, segs, *refs):
    io = refs[:5]
    qkv_src, in_src, out_src, hid_src, biases_ref, gains_ref = refs[5:11]
    outs = refs[11:21]
    full_outs = refs[21:25]
    forward_scratch = refs[25:29]
    weights = refs[29:32]
    vec = refs[32]
    (
        load_sems, end_load_sems, store_sems, x_sems, y_sems, fx_sems, fy_sems, core_sems, end_sems,
        line_core_sems, up_sems, down_sems, vec_sems,
    ) = refs[33:]
    step = pl.program_id(0)
    section, place = lax.axis_index("section"), lax.axis_index("dp")
    x, y = section % 2, section // 2
    core, z = place % 2, place // 2
    end = weights[2]
    depth, _, _, _, tall, _ = end.shape
    thin = tall // 5
    x_dev = (y * 2 + 1 - x, place)
    y_dev = ((1 - y) * 2 + x, place)
    core_dev = (section, z * 2 + 1 - core)
    up_dev = (section, (z + 1) % depth * 2 + core)
    down_dev = (section, (z + depth - 1) % depth * 2 + core)
    own_block = (y, x)
    blocks = ((y, 1 - x), (1 - y, x), (1 - y, 1 - x))

    def remote(source, target, sems, index, device):
        return pltpu.make_async_remote_copy(
            src_ref=source, dst_ref=target, send_sem=sems.at[(0, *index)], recv_sem=sems.at[(1, *index)],
            device_id=device, device_id_type=MESH,
        )


    def part_of(number, block, part):
        rows = weights[number].shape[-2] // 2
        return weights[number].at[core, block[0], block[1], pl.ds(part * rows, rows)]

    def own_part(number, part):
        rows = weights[number].shape[-2] // 2
        at = pl.multiple_of((core * 2 + part) * rows, rows)
        return (qkv_src, in_src)[number].at[0, pl.ds(at, rows)]

    def x_copy(number, part):
        return remote(own_part(number, part), part_of(number, own_block, part), x_sems, (number, part), x_dev)

    def y_copy(number, part):
        return remote(own_part(number, part), part_of(number, own_block, part), y_sems, (number, part), y_dev)

    def fy_copy(number):
        piece = part_of(number, blocks[0], 0)
        return remote(piece, piece, fy_sems, (number,), y_dev)

    def fx_copy(number):
        piece = part_of(number, blocks[1], 1)
        return remote(piece, piece, fx_sems, (number,), x_dev)

    def core_copy(number, kind, part):
        piece = part_of(number, blocks[kind], part)
        return remote(piece, piece, core_sems, (number, kind, part), core_dev)


    def eighth(at, block, first=0, rows=None):
        view = end.at[at, core, block[0], block[1]]
        return view if rows is None else view.at[pl.ds(first, rows)]

    def own_eighth(first):
        source, rows = (out_src, thin) if first == 0 else (hid_src, tall - thin)
        return source.at[0, pl.ds(pl.multiple_of((z * 2 + core) * rows, rows), rows)]

    def end_copy(axis, first):
        rows = thin if first == 0 else tall - thin
        return remote(
            own_eighth(first), eighth(z, own_block, first, rows), end_sems, (axis, 0 if first == 0 else 1),
            (x_dev, y_dev)[axis],
        )

    low = tall // 32 * 16

    def end_fy_copy():
        piece = eighth(z, blocks[0], 0, low)
        return remote(piece, piece, fy_sems, (2,), y_dev)

    def end_fx_copy():
        piece = eighth(z, blocks[1], low, tall - low)
        return remote(piece, piece, fx_sems, (2,), x_dev)

    def line_core_copy(at, kind):
        piece = eighth(at, blocks[kind])
        return remote(piece, piece, line_core_sems, (at, kind), core_dev)

    def up_copy(at, kind):
        piece = eighth(at, blocks[kind])
        return remote(piece, piece, up_sems, (at, kind), up_dev)

    def down_copy(at, kind):
        piece = eighth(at, blocks[kind])
        return remote(piece, piece, down_sems, (at, kind), down_dev)

    def vec_copy(kind):
        row = vec.at[(own_block, own_block, blocks[0])[kind]]
        return remote(row, row, vec_sems, (kind,), (x_dev, y_dev, y_dev)[kind])

    def loads():
        copies = []
        for number, source in enumerate((qkv_src, in_src)):
            rows = weights[number].shape[-2]
            for side in range(2):
                copies.append(
                    pltpu.make_async_copy(
                        source.at[0, pl.ds(side * rows, rows)], weights[number].at[side, y, x],
                        load_sems.at[number, side],
                    )
                )
        for at in range(depth):
            for side in range(2):
                for number, (source, first, rows) in enumerate(
                    ((out_src, 0, thin), (hid_src, thin, tall - thin))
                ):
                    copies.append(
                        pltpu.make_async_copy(
                            source.at[0, pl.ds((at * 2 + side) * rows, rows)],
                            end.at[at, side, y, x, pl.ds(first, rows)],
                            end_load_sems.at[at, side, number],
                        )
                    )
        return copies

    def full_stores():
        return [
            pltpu.make_async_copy(source, target, store_sems.at[number])
            for number, (source, target) in enumerate(zip((*weights, vec), full_outs))
        ]

    received = set()

    def arrived(*copies):
        for name, copy in copies:
            if name not in received:
                received.add(name)
                copy.wait_recv()

    def end_arrived(axis):
        arrived(*[((axis, first), end_copy(axis, first)) for first in (0, thin)])

    def start_end(axis):
        for first in (0, thin):
            end_copy(axis, first).start()

    def forward_end(axis):
        end_arrived(axis)
        (end_fy_copy, end_fx_copy)[axis]().start()

    def spread(kind):
        if kind < 2:
            end_arrived(kind)
        else:
            arrived(("fy", end_fy_copy()), ("fx", end_fx_copy()))

        @pl.when(z < depth - 1)
        def _():
            up_copy(z, kind).start()

        @pl.when(z > 0)
        def _():
            down_copy(z, kind).start()

        line_core_copy(z, kind).start()

    def hop(distance, kind):
        @pl.when(z >= distance)
        def _():
            up_copy(z - distance, kind).wait_recv()

            @pl.when(z < depth - 1)
            def _():
                up_copy(z - distance, kind).start()

            line_core_copy(z - distance, kind).start()

        @pl.when(z + distance < depth)
        def _():
            down_copy(z + distance, kind).wait_recv()

            @pl.when(z > 0)
            def _():
                down_copy(z + distance, kind).start()

            line_core_copy(z + distance, kind).start()

    def forward_part(axis, number):
        part = axis
        (x_copy, y_copy)[axis](number, part).wait_recv()
        (fy_copy, fx_copy)[axis](number).start()
        core_copy(number, axis, part).start()

    def share_part(axis, number):
        part = 1 - axis
        (x_copy, y_copy)[axis](number, part).wait_recv()
        core_copy(number, axis, part).start()

    def share_diagonal(number):
        fy_copy(number).wait_recv()
        core_copy(number, 2, 0).start()
        fx_copy(number).wait_recv()
        core_copy(number, 2, 1).start()

    def forward_vec():
        vec_copy(0).wait_recv()
        vec_copy(2).start()

    act = dict(
        forward_vec=forward_vec,
        start=lambda axis, number, part: (x_copy, y_copy)[axis](number, part).start(),
        forward_end=forward_end,
        spread=spread,
        hop=hop,
        forward_part=forward_part,
        share_part=share_part,
        share_diagonal=share_diagonal,
    )

    def complete(number):
        for kind in range(3):
            for part in range(2):
                core_copy(number, kind, part).wait_recv()

    def before_mix():
        @pl.when(step == 0)
        def _():
            barrier = pltpu.get_barrier_semaphore()
            for device in (x_dev, y_dev, core_dev):
                pl.semaphore_signal(barrier, inc=1, device_id=device, device_id_type=MESH)

            @pl.when(z < depth - 1)
            def _():
                pl.semaphore_signal(barrier, inc=1, device_id=up_dev, device_id_type=MESH)

            @pl.when(z > 0)
            def _():
                pl.semaphore_signal(barrier, inc=1, device_id=down_dev, device_id_type=MESH)

            pl.semaphore_wait(barrier, 3 + jnp.where(z > 0, 1, 0) + jnp.where(z < depth - 1, 1, 0))
            start_end(0)
            start_end(1)
            vec[y, x] = jnp.concatenate([biases_ref[...].astype(F32), gains_ref[...].astype(F32)], axis=1)
            vec_copy(0).start()
            vec_copy(1).start()
            for name, *numbers in GATHER_START:
                act[name](*numbers)
            for copy in loads():
                copy.start()
            for name, *numbers in GATHER_FIRST:
                act[name](*numbers)
            vec_copy(1).wait_recv()
            vec_copy(2).wait_recv()
            complete(0)
            for copy in loads():
                copy.wait()

    def before_out():
        @pl.when(step == 0)
        def _():
            for name, *numbers in GATHER_THEN:
                act[name](*numbers)
            complete(1)
            for at in range(depth):
                for kind in range(3):
                    line_core_copy(at, kind).wait_recv()

        @pl.when(step == 1)
        def _():
            for copy in full_stores():
                copy.start()

    @pl.when(step == 0)
    def _():
        forward_scratch[0][...] = jnp.zeros_like(forward_scratch[0])

    forward_layer(
        step, segs, step % 2, before_mix, before_out, *io, weights, vec, *outs, *forward_scratch
    )

    @pl.when(step == steps - 1)
    def _():
        for copy in full_stores():
            copy.wait()
        for number in range(2):
            for part in range(2):
                x_copy(number, part).wait_send()
                y_copy(number, part).wait_send()
                for kind in range(3):
                    core_copy(number, kind, part).wait_send()
            fx_copy(number).wait_send()
            fy_copy(number).wait_send()
            for first in (0, thin):
                end_copy(number, first).wait_send()
        end_fx_copy().wait_send()
        end_fy_copy().wait_send()
        for kind in range(3):
            vec_copy(kind).wait_send()
            for at in range(depth):
                line_core_copy(at, kind).wait_send()

                @pl.when((z >= at) & (z < depth - 1))
                def _():
                    up_copy(at, kind).wait_send()

                @pl.when((z <= at) & (z > 0))
                def _():
                    down_copy(at, kind).wait_send()


def full_weight_shapes(w_qkv, w_out, w_in, w_hid):
    half, width = w_out.shape[1:]
    return [(2, 2, 2, half // 2, block.shape[2]) for block in (w_qkv, w_in)] + [
        (4, 2, 2, 2, (half + w_hid.shape[1]) // 8, width)
    ]


def gather_forward(text, resets, counts, init, bounds, blocks, biases, gains):
    steps, saved, operands, in_specs, out_specs, out_shape, scratch = forward_io(
        text, resets, counts, init, bounds
    )
    shapes = full_weight_shapes(*blocks)
    full = [pltpu.VMEM(shape, BF16) for shape in shapes] + [pltpu.VMEM((2, 2, 1, biases.shape[1] + gains.shape[1]), F32)]
    any_spec = pl.BlockSpec(memory_space=pl.ANY)
    dma = pltpu.SemaphoreType.DMA
    depth = shapes[2][0]
    *outs, acts, qkv, w_in, end, vecs = pl.pallas_call(
        functools.partial(gather_forward_body, steps, text.shape[1]),
        grid=(steps,),
        in_specs=in_specs + [any_spec] * 4 + [pl.BlockSpec(vector.shape, lambda t: (0, 0)) for vector in (biases, gains)],
        out_specs=out_specs + [any_spec] * 4,
        out_shape=out_shape + [jax.ShapeDtypeStruct(ref.shape, ref.dtype) for ref in full],
        scratch_shapes=scratch
        + full
        + [
            dma((2, 2)), dma((depth, 2, 2)), dma((4,)), dma((2, 2, 2)), dma((2, 2, 2)), dma((2, 3)),
            dma((2, 3)), dma((2, 2, 3, 2)), dma((2, 2, 2)), dma((2, depth, 3)), dma((2, depth, 3)),
            dma((2, depth, 3)), dma((2, 3)),
        ],
        compiler_params=pltpu.CompilerParams(
            vmem_limit_bytes=VMEM_BYTES, collective_id=1, has_side_effects=True
        ),
        name="gather_forward",
    )(*operands, blocks[0], blocks[2], blocks[1], blocks[3], biases, gains)
    return dict(zip(saved, outs)), acts, (qkv, w_in, end), vecs


def gather_apart(blocks, biases, gains):
    vec = jnp.concatenate([biases, gains], axis=1).astype(F32)
    w_qkv, w_out, w_in, w_hid = [
        lax.all_gather(block[0], "section").reshape(2, 2, *block.shape[1:]) for block in blocks
    ]
    half, width = w_out.shape[2:]
    full = [
        block.reshape(2, 2, 2, half // 2, -1).transpose(2, 0, 1, 3, 4) for block in (w_qkv, w_in)
    ]
    ends = [block.reshape(2, 2, 4, 2, -1, width).transpose(2, 3, 0, 1, 4, 5) for block in (w_out, w_hid)]
    vecs = lax.all_gather(vec, "section").reshape(2, 2, *vec.shape)
    return (*full, jnp.concatenate(ends, axis=4)), vecs


GRAD_NAMES = ("first", "inner", "active", "branch", "x", "mix", "heads", "attn")


def weight_grad_body(
    layer, segs_all, dp, *refs,
):
    sources = refs[:8]
    extra_ref, mine_ref, theirs_ref = refs[8:11]
    held = refs[11:19]
    wire, in_sems, extra_sem, out_sems = refs[19:23]
    core = lax.axis_index("dp") % 2
    rows = sources[0].shape[1]
    width = sources[0].shape[2]
    half = width // 2
    lanes = wire.shape[-1]
    thin = width // dp
    wide = 3 * thin

    def loads(number):
        return [
            pltpu.make_async_copy(
                sources[number].at[2 * at + layer],
                held[number].at[pl.ds(at * rows, rows)],
                in_sems.at[number, at],
            )
            for at in range(segs_all)
        ]

    for number in range(8):
        for copy in loads(number):
            copy.start()
    extra = pltpu.make_async_copy(extra_ref, wire.at[:, :, :, :, pl.ds(half, extra_ref.shape[4])], extra_sem)
    extra.start()

    def ready(*numbers):
        for number in numbers:
            for copy in loads(number):
                copy.wait()

    def stores(kind):
        return [
            pltpu.make_async_copy(wire.at[kind, core], mine_ref.at[kind], out_sems.at[kind, 0]),
            pltpu.make_async_copy(wire.at[kind, 1 - core], theirs_ref.at[kind], out_sems.at[kind, 1]),
        ]

    first, inner, active, branch, inputs, mix, heads, attn = held
    extra.wait()

    ready(0, 1)
    per_tile = width // lanes

    def in_tile(tile, _):
        right = inner[:, pl.ds(pl.multiple_of(tile * width, width), width)]
        for side in range(2):
            result = dot_tn(first[:, side * half : (side + 1) * half], right).astype(BF16)
            for at in range(per_tile):
                wire[1, at % 2, tile * (per_tile // 2) + at // 2, side, 0:half, :] = result[
                    :, at * lanes : (at + 1) * lanes
                ]
        return _

    lax.fori_loop(0, 4, in_tile, 0)
    for copy in stores(1):
        copy.start()

    ready(2, 3)
    def hid_tile(side, _):
        for part in range(4):
            left = active[:, pl.ds(pl.multiple_of(side * 4 * half + part * half, half), half)]
            result = dot_tn(left, branch[...]).astype(BF16)
            for at in range(dp):
                wire[2, at % 2, at // 2, side, 0:half, part * thin : (part + 1) * thin] = result[
                    :, at * thin : (at + 1) * thin
                ]
        return _
    lax.fori_loop(0, 2, hid_tile, 0)
    for copy in stores(2):
        copy.start()

    ready(4, 5, 6, 7)
    for side in range(2):
        left = inputs[:, side * half : (side + 1) * half]
        for tile in range(2):
            result = dot_tn(left, mix[:, tile * 3 * half : (tile + 1) * 3 * half]).astype(BF16)
            for at in range(dp // 2):
                place = tile * (dp // 2) + at
                wire[0, place % 2, place // 2, side, 0:half, 0:wide] = result[
                    :, at * wide : (at + 1) * wide
                ]
        result = dot_tn(heads[:, side * half : (side + 1) * half], attn[...]).astype(BF16)
        for at in range(dp):
            wire[0, at % 2, at // 2, side, 0:half, wide:lanes] = result[:, at * thin : (at + 1) * thin]
    for copy in stores(0):
        copy.start()
    for kind in range(3):
        for copy in stores(kind):
            copy.wait()


def weight_grads(layer, dp, saved, extras):
    sources = [saved[name] for name in GRAD_NAMES]
    steps, rows, width = sources[0].shape
    segs_all = steps // 2
    half = width // 2
    lanes = 4 * width // dp
    extra_rows = extras.shape[4]
    kind = jax.ShapeDtypeStruct((3, dp // 2, 2, half + extra_rows, lanes), BF16)
    any_spec = pl.BlockSpec(memory_space=pl.ANY)
    return pl.pallas_call(
        functools.partial(weight_grad_body, layer, segs_all, dp),
        in_specs=[any_spec] * 9,
        out_specs=[any_spec] * 2,
        out_shape=[kind, kind],
        scratch_shapes=[pltpu.VMEM((segs_all * rows, source.shape[2]), BF16) for source in sources]
        + [
            pltpu.VMEM((3, 2, dp // 2, 2, half + extra_rows, lanes), BF16),
            pltpu.SemaphoreType.DMA((8, segs_all)),
            pltpu.SemaphoreType.DMA,
            pltpu.SemaphoreType.DMA((3, 2)),
        ],
        compiler_params=pltpu.CompilerParams(vmem_limit_bytes=VMEM_BYTES),
        name="weight_grads",
    )(*sources, extras)


def add_into(ref, other):
    ref[...] = (ref[...].astype(F32) + other[...].astype(F32)).astype(BF16)


def build_extra(mem, sums_ref, memory_ref, extra):
    steps = sums_ref.shape[0]
    width = memory_ref.shape[1]
    lanes = extra.shape[-1]
    extra[...] = jnp.zeros_like(extra)
    for layer in range(2):
        total = sums_ref[layer]
        for step in range(layer + 2, steps, 2):
            total = total + sums_ref[step]
        for block, parts in enumerate(((6, 7, 5, 4, 8, 3), (9, 10, 11, 2, 1, 0))):
            for piece in range(width // lanes):
                extra[layer, block, piece * mem : (piece + 1) * mem, :] = memory_ref[
                    16 - mem : 16, piece * lanes : (piece + 1) * lanes
                ]
                for at, part in enumerate(parts):
                    row = mem * (width // lanes) + at * (width // lanes) + piece
                    first = part * width + piece * lanes
                    extra[layer, block, row : row + 1, :] = total[:, first : first + lanes]


KIND_IN, KIND_HID, KIND_MIX = 1, 2, 0
CUTS = {KIND_HID: 2, KIND_MIX: 3}
PLAN = (
    ("mul", 0, 2, 0), ("mul", 0, 2, 1), ("core", 0, 2, 0), ("QO", 2, 0), ("P", 2, 0), ("mul", 0, 1, 0),
    ("core", 0, 2, 1), ("QO", 2, 1), ("P", 2, 1), ("mul", 1, 2, 0), ("mul", 1, 2, 1), ("core", 0, 1, 0),
    ("hop", "ZO", 1, 0, 0), ("XQ", 2, 0), ("XQ", 2, 1), ("core", 1, 2, 0), ("QW", 2, 0), ("YP", 2, 0),
    ("mul", 1, 1, 0), ("core", 1, 2, 1), ("QW", 2, 1), ("hop", "ZO", 1, 0, 1), ("mul", 0, 0, 0), ("YP",
    2, 1), ("core", 0, 0, 0), ("P", 0, 0), ("P", 0, 1), ("QO", 0, 0), ("hop", "ZO", 1, 0, 2), ("core",
    1, 1, 0), ("QWA", 1, 0), ("QWA", 1, 1), ("mul", 1, 0, 0), ("plane", 2, 0), ("hop", "Z", 2, 0, 0),
    ("hop", "Z", 2, 0, 1), ("hop", "Z", 2, 0, 2), ("plane", 2, 1), ("hop", "Z", 2, 1, 0), ("hop", "Z",
    2, 1, 1), ("hop", "Z", 2, 1, 2), ("core", 1, 0, 0), ("QW", 0, 0), ("YP", 0, 0), ("QW", 0, 1), ("QO",
    0, 1), ("plane", 1, 0), ("hop", "Z", 1, 0, 0), ("hop", "Z", 1, 0, 1), ("hop", "Z", 1, 0, 2), ("XQ",
    0, 0), ("fin", "ZO", 1, 0), ("XO", 1), ("plane", 1, 1), ("hop", "Z", 1, 1, 0), ("hop", "Z", 1, 1,
    1), ("fin", "Z", 2, 0), ("YP", 0, 1), ("plane", 0, 0), ("hop", "Z", 0, 0, 0), ("hop", "Z", 0, 0, 1),
    ("hop", "Z", 0, 0, 2), ("hop", "Z", 1, 1, 2), ("YO", 1), ("XQ", 0, 1), ("plane", 0, 1), ("hop", "Z",
    0, 1, 0), ("hop", "Z", 0, 1, 1), ("hop", "Z", 0, 1, 2), ("fin", "Z", 2, 1), ("fin", "Z", 0, 0),
    ("fin", "Z", 1, 1), ("fin", "Z", 1, 0), ("fin", "Z", 0, 1),
)


def row_parts(tall, thin):
    first = -(-tall // 32) * 16
    some = ((0, first), (first, tall - first))
    return {KIND_IN: some, KIND_MIX: some, KIND_HID: ((0, 2 * thin), (2 * thin, tall - 2 * thin))}


def grad_reduce_body(dp, mem, segs_all, *refs):
    sources = refs[:8]
    sums_ref, memory_ref = refs[8:10]
    piece_out = refs[10]
    held = refs[11:19]
    mine, theirs, landed, xp, xq, yqo, yqw, yp, ywall, xo, yo, z_low, z_high, zo_low, zo_high = refs[19:34]
    extra = refs[34]
    (
        in_sems, core_sems, free_sem, xp_sems, xq_sems, yqo_sems, yqw_sems, yp_sems, single_sems, up_sems,
        down_sems, zo_up_sems, zo_down_sems,
    ) = refs[35:]
    section, place = lax.axis_index("section"), lax.axis_index("dp")
    x, y = section % 2, section // 2
    core, z = place % 2, place // 2
    depth = dp // 2
    rows, width = sources[0].shape[1:]
    half = width // 2
    tall, lanes = mine.shape[-2:]
    thin = width // dp
    wide = 3 * thin
    parts = row_parts(tall, thin)
    x_dev = (y * 2 + 1 - x, place)
    y_dev = ((1 - y) * 2 + x, place)
    core_dev = (section, z * 2 + 1 - core)
    up_dev = (section, (z + 1) % depth * 2 + core)
    down_dev = (section, (z + depth - 1) % depth * 2 + core)
    used = {KIND_IN: (0, 1), KIND_HID: (2, 3), KIND_MIX: (4, 5, 6, 7)}
    slots = {KIND_HID: 0, KIND_MIX: 1}
    first, inner, active, branch, inputs, mix, heads, attn = held
    units = [step[1:3] for step in PLAN if step[0] == "mul" and step[3] == 0]

    def loads(side, kind):
        layer = (1 - x) if side == 0 else x
        return [
            pltpu.make_async_copy(
                sources[number].at[2 * at + layer],
                held[number].at[pl.ds(at * rows, rows)],
                in_sems.at[number, at],
            )
            for number in used[kind]
            for at in range(segs_all)
        ]

    for side, kind in units:
        if side == 0:
            for copy in loads(0, kind):
                copy.start()
    barrier = pltpu.get_barrier_semaphore()
    for device in (x_dev, y_dev, core_dev):
        pl.semaphore_signal(barrier, inc=1, device_id=device, device_id_type=MESH)

    @pl.when(z < depth - 1)
    def _():
        pl.semaphore_signal(barrier, inc=1, device_id=up_dev, device_id_type=MESH)

    @pl.when(z > 0)
    def _():
        pl.semaphore_signal(barrier, inc=1, device_id=down_dev, device_id_type=MESH)

    build_extra(mem, sums_ref, memory_ref, extra)
    pl.semaphore_wait(barrier, 3 + jnp.where(z > 0, 1, 0) + jnp.where(z < depth - 1, 1, 0))

    def remote(source, target, sems, index, device):
        return pltpu.make_async_remote_copy(
            src_ref=source, dst_ref=target, send_sem=sems.at[(0, *index)], recv_sem=sems.at[(1, *index)],
            device_id=device, device_id_type=MESH,
        )

    def core_parts(kind):
        return range(2) if kind == KIND_HID else range(1)

    def core_rows(kind, part):
        return parts[kind][part] if kind == KIND_HID else (0, tall)

    def core_copy(unit, part):
        some = pl.ds(*core_rows(units[unit][1], part))
        return remote(
            theirs.at[unit % 2, :, :, some], landed.at[unit % 2, :, :, some], core_sems, (unit, part), core_dev
        )

    def p_copy(kind, part):
        at = pl.ds(0, CUTS[kind])
        some = pl.ds(*parts[kind][part])
        return remote(
            mine.at[0, kind, at, :, some], xp.at[slots[kind], at, :, some], xp_sems, (slots[kind], part), x_dev
        )

    def q_copy(side, kind, part):
        some = pl.ds(*parts[kind][part])
        count = depth - CUTS[kind]
        return remote(
            mine.at[side, kind, pl.ds(CUTS[kind], count), 1 - y, some],
            (yqo, yqw)[side].at[slots[kind], pl.ds(0, count), some],
            (yqo_sems, yqw_sems)[side], (slots[kind], part), y_dev,
        )

    def xq_copy(kind, part):
        some = pl.ds(*parts[kind][part])
        count = depth - CUTS[kind]
        return remote(
            mine.at[0, kind, pl.ds(CUTS[kind], count), y, some],
            xq.at[slots[kind], pl.ds(0, count), some], xq_sems, (slots[kind], part), x_dev,
        )

    def yp_copy(kind, part):
        some = pl.ds(*parts[kind][part])
        at = pl.ds(0, CUTS[kind])
        return remote(
            mine.at[1, kind, at, 1 - y, some], yp.at[slots[kind], at, some], yp_sems, (slots[kind], part), y_dev
        )

    def xo_copy():
        return remote(mine.at[0, KIND_IN, z], xo, single_sems, (0,), x_dev)

    def yo_copy():
        return remote(xo.at[1 - y], yo, single_sems, (1,), y_dev)

    def ywall_copy(part):
        some = pl.ds(*parts[KIND_IN][part])
        return remote(
            mine.at[1, KIND_IN, :, 1 - y, some], ywall.at[:, some], single_sems, (2 + part,), y_dev
        )

    def line_rows(kind, part):
        return pl.ds(*parts[kind][part])

    def up_copy(name, kind, part, at):
        if name == "ZO":
            return remote(mine.at[0, kind, at], zo_low.at[at - 1], zo_up_sems, (at,), up_dev)
        some = line_rows(kind, part)
        return remote(
            mine.at[1, kind, at, y, some], z_low.at[kind, at - 1, some], up_sems, (kind, part, at), up_dev
        )

    def down_copy(name, kind, part, at):
        if name == "ZO":
            return remote(mine.at[0, kind, at], zo_high.at[at], zo_down_sems, (at,), down_dev)
        some = line_rows(kind, part)
        return remote(
            mine.at[1, kind, at, y, some], z_high.at[kind, at, some], down_sems, (kind, part, at), down_dev
        )

    def from_low(name, kind, part, at):
        up_copy(name, kind, part, at).wait_recv()
        if name == "ZO":
            for block in range(2):
                add_into(mine.at[0, kind, at, block], zo_low.at[at - 1, block])
        else:
            some = line_rows(kind, part)
            add_into(mine.at[1, kind, at, y, some], z_low.at[kind, at - 1, some])

    def from_high(name, kind, part, at):
        down_copy(name, kind, part, at).wait_recv()
        if name == "ZO":
            for block in range(2):
                add_into(mine.at[0, kind, at, block], zo_high.at[at, block])
        else:
            some = line_rows(kind, part)
            add_into(mine.at[1, kind, at, y, some], z_high.at[kind, at, some])

    def multiply(side, kind, part):
        unit = units.index((side, kind))
        slot = unit % 2

        def put(chunk_core, chunk_z, block, piece, start, stop):
            @pl.when(core == chunk_core)
            def _():
                mine[side, kind, chunk_z, block, start:stop, :] = piece

            @pl.when(core != chunk_core)
            def _():
                theirs[slot, chunk_z, block, start:stop, :] = piece

        if part == 0:
            for copy in loads(side, kind):
                copy.wait()
            if unit >= 2:
                for earlier in core_parts(units[unit - 2][1]):
                    core_copy(unit - 2, earlier).wait_send()
            layer = (1 - x) if side == 0 else x
            extra_rows = tall - half
            for block in range(2):
                added = extra[layer, block, kind * extra_rows : (kind + 1) * extra_rows, :].astype(BF16)
                for at in range(depth):
                    mine[side, kind, at, block, half:, :] = added
                    theirs[slot, at, block, half:, :] = added
        if kind == KIND_IN:
            per_tile = width // lanes

            def in_tile(tile, _):
                right = inner[:, pl.ds(pl.multiple_of(tile * width, width), width)]
                for block in range(2):
                    result = dot_tn(first[:, block * half : (block + 1) * half], right).astype(BF16)
                    for at in range(per_tile):
                        put(
                            at % 2, tile * (per_tile // 2) + at // 2, block,
                            result[:, at * lanes : (at + 1) * lanes], 0, half,
                        )
                return _

            lax.fori_loop(0, 4, in_tile, 0)
        elif kind == KIND_HID:

            def hid_tile(block, _):
                right = active[:, pl.ds(pl.multiple_of((block * 2 + part) * width, width), width)]
                for side_rows in range(2):
                    result = dot_tn(
                        branch[:, side_rows * half : (side_rows + 1) * half], right
                    ).astype(BF16)
                    for at in range(dp // 2):
                        chunk = side_rows * (dp // 2) + at
                        for piece in range(2):
                            row = (part * 2 + piece) * thin
                            put(
                                chunk % 2, chunk // 2, block,
                                result[at * thin : (at + 1) * thin, piece * half : (piece + 1) * half],
                                row, row + thin,
                            )
                return _

            lax.fori_loop(0, 2, hid_tile, 0)
        else:

            def mix_tile(block, _):
                columns = pl.ds(pl.multiple_of(block * half, half), half)
                for tile in range(2):
                    result = dot_tn(
                        mix[:, tile * 3 * half : (tile + 1) * 3 * half], inputs[:, columns]
                    ).astype(BF16)
                    for at in range(depth):
                        chunk = tile * depth + at
                        put(chunk % 2, chunk // 2, block, result[at * wide : (at + 1) * wide], 0, wide)
                result = dot_tn(attn[...], heads[:, columns]).astype(BF16)
                for chunk in range(dp):
                    put(chunk % 2, chunk // 2, block, result[chunk * thin : (chunk + 1) * thin], wide, half)
                return _

            lax.fori_loop(0, 2, mix_tile, 0)
        if unit >= 2 and part == 0:
            pl.semaphore_wait(free_sem, 1)
        core_copy(unit, part).start()
        if side == 0 and part == core_parts(kind)[-1]:
            for copy in loads(1, kind):
                copy.start()

    def add_core(side, kind, part):
        unit = units.index((side, kind))
        some = pl.ds(*core_rows(kind, part))
        core_copy(unit, part).wait_recv()

        def add(at, _):
            for block in range(2):
                add_into(mine.at[side, kind, at, block, some], landed.at[unit % 2, at, block, some])
            return _

        lax.fori_loop(0, depth, add, 0)
        if unit + 2 < len(units) and part == core_parts(kind)[-1]:
            pl.semaphore_signal(free_sem, inc=1, device_id=core_dev, device_id_type=MESH)

    def forward_q(kind, part):
        q_copy(0, kind, part).wait_recv()
        some = pl.ds(*parts[kind][part])
        for at in range(depth - CUTS[kind]):
            add_into(mine.at[0, kind, CUTS[kind] + at, y, some], yqo.at[slots[kind], at, some])
        xq_copy(kind, part).start()

    def forward_p(kind, part):
        p_copy(kind, part).wait_recv()
        some = pl.ds(*parts[kind][part])
        for at in range(CUTS[kind]):
            for block in range(2):
                add_into(mine.at[1, kind, at, block, some], xp.at[slots[kind], at, block, some])
        yp_copy(kind, part).start()

    def finish_plane(kind, part):
        some = pl.ds(*parts[kind][part])
        if kind == KIND_IN:
            ywall_copy(part).wait_recv()
            for at in range(depth):
                add_into(mine.at[1, kind, at, y, some], ywall.at[at, some])
            return
        slot = slots[kind]
        q_copy(1, kind, part).wait_recv()
        xq_copy(kind, part).wait_recv()
        for at in range(depth - CUTS[kind]):
            ref = mine.at[1, kind, CUTS[kind] + at, y, some]
            total = ref[...].astype(F32) + yqw[slot, at, some].astype(F32) + xq[slot, at, some].astype(F32)
            ref[...] = total.astype(BF16)
        yp_copy(kind, part).wait_recv()
        for at in range(CUTS[kind]):
            add_into(mine.at[1, kind, at, y, some], yp.at[slot, at, some])

    def hop(name, kind, part, count):
        high = depth - 1 - count + z
        low = count - (depth - 1 - z)

        @pl.when(z <= count)
        def _():
            @pl.when(z > 0)
            def _():
                from_low(name, kind, part, high)

            up_copy(name, kind, part, high).start()

        @pl.when(low >= 0)
        def _():
            @pl.when(z < depth - 1)
            def _():
                from_high(name, kind, part, low)

            down_copy(name, kind, part, low).start()

    finished = []

    def finish(name, kind, part):
        @pl.when(z > 0)
        def _():
            from_low(name, kind, part, z)

        @pl.when(z < depth - 1)
        def _():
            from_high(name, kind, part, z)

        if name == "ZO":
            return
        some = line_rows(kind, part)
        if kind == KIND_IN:
            add_into(mine.at[1, kind, z, y, some], xo.at[y, some])
            if (name, kind, 1 - part) not in finished:
                yo_copy().wait_recv()
            add_into(mine.at[1, kind, z, y, some], yo.at[some])
        finished.append((name, kind, part))
        piece_out[kind, some, :] = mine[1, kind, z, y, some, :]

    def forward_o(kind):
        xo_copy().wait_recv()
        yo_copy().start()

    act = dict(
        mul=multiply,
        core=add_core,
        P=lambda kind, part: p_copy(kind, part).start(),
        QO=lambda kind, part: q_copy(0, kind, part).start(),
        QW=lambda kind, part: q_copy(1, kind, part).start(),
        XQ=forward_q,
        YP=forward_p,
        plane=finish_plane,
        hop=hop,
        fin=finish,
        XO=lambda kind: xo_copy().start(),
        YO=forward_o,
        QWA=lambda kind, part: ywall_copy(part).start(),
    )
    for name, *numbers in PLAN:
        act[name](*numbers)

    for unit in (4, 5):
        for part in core_parts(units[unit][1]):
            core_copy(unit, part).wait_send()
    for copy in (xo_copy(), yo_copy(), ywall_copy(0), ywall_copy(1)):
        copy.wait_send()
    for kind in CUTS:
        for part in range(2):
            p_copy(kind, part).wait_send()
            xq_copy(kind, part).wait_send()
            yp_copy(kind, part).wait_send()
            for side in range(2):
                q_copy(side, kind, part).wait_send()
    lines = [("ZO", KIND_IN, 0)]
    lines += [("Z", kind, part) for kind in (KIND_IN, *CUTS) for part in range(2)]
    for line in lines:
        for at in range(depth):

            @pl.when(at > z)
            def _():
                up_copy(*line, at).wait_send()

            @pl.when(at < z)
            def _():
                down_copy(*line, at).wait_send()


def grad_reduce_shapes(dp, steps, rows, width):
    half = width // 2
    lanes = 4 * width // dp
    depth = dp // 2
    extra_rows = 16
    tall = half + extra_rows
    most, least = max(CUTS.values()), depth - min(CUTS.values())
    held = [width, 4 * width, 4 * width, width, width, 3 * width, width, width]
    return (
        [pltpu.VMEM((steps // 2 * rows, columns), BF16) for columns in held]
        + [
            pltpu.VMEM(shape + (tall, lanes), BF16)
            for shape in (
                (2, 3, depth, 2), (2, depth, 2), (2, depth, 2), (2, most, 2), (2, least), (2, least),
                (2, least), (2, most), (depth,), (2,), (), (3, depth - 1), (3, depth - 1),
                (depth - 1, 2), (depth - 1, 2),
            )
        ]
        + [pltpu.VMEM((2, 2, 3 * extra_rows, lanes), F32)]
    )


def unpack_body(mem, piece_ref, qkv_ref, out_ref, in_ref, hid_ref, memory_ref, bias_ref, gain_ref, vec_scr):
    wide, half = qkv_ref.shape[1:]
    thin, lanes = out_ref.shape[1], in_ref.shape[2]
    width = memory_ref.shape[1]
    qkv_ref[0] = piece_ref[0, 0:wide, :].astype(F32)
    out_ref[0] = piece_ref[0, wide:half, :].astype(F32)
    in_ref[0] = piece_ref[1, 0:half, :].astype(F32)
    for part in range(4):
        hid_ref[0, :, part * half : (part + 1) * half] = piece_ref[
            2, part * thin : (part + 1) * thin, :
        ].astype(F32)
    extra = jnp.concatenate([piece_ref[kind, half:, :].astype(F32) for kind in range(3)], axis=0)
    pieces = width // lanes
    for piece in range(pieces):
        memory_ref[:, piece * lanes : (piece + 1) * lanes] = extra[piece * mem : (piece + 1) * mem, :]
    for at in range(6 * pieces):
        row = mem * pieces + at
        vec_scr[0:1, at * lanes : (at + 1) * lanes] = extra[row : row + 1, :]
    place = lax.axis_index("dp")
    long = 5 * width
    for ref, first, last in ((bias_ref, 0, long), (gain_ref, long, long + width)):
        size = ref.shape[1]
        turned = pltpu.roll(vec_scr[:, first:last], (last - first - place * size) % (last - first), 1)
        ref[...] = turned[0:1, 0:size]


def grad_reduce(dp, mem, saved, sums, memory):
    sources = [saved[name] for name in GRAD_NAMES]
    steps, rows, width = sources[0].shape
    segs_all = steps // 2
    half = width // 2
    lanes = 4 * width // dp
    thin = width // dp
    depth = dp // 2
    any_spec = pl.BlockSpec(memory_space=pl.ANY)
    dma = pltpu.SemaphoreType.DMA
    shapes = grad_reduce_shapes(dp, steps, rows, width)
    piece = pl.pallas_call(
        functools.partial(grad_reduce_body, dp, mem, segs_all),
        in_specs=[any_spec] * 8 + [pl.BlockSpec(memory_space=pltpu.VMEM)] * 2,
        out_specs=pl.BlockSpec(memory_space=pltpu.VMEM),
        out_shape=jax.ShapeDtypeStruct((3,) + shapes[8].shape[-2:], BF16),
        scratch_shapes=shapes
        + [
            dma((8, segs_all)), dma((2, 6, 2)), pltpu.SemaphoreType.REGULAR, dma((2, 2, 2)), dma((2, 2, 2)),
            dma((2, 2, 2)), dma((2, 2, 2)), dma((2, 2, 2)), dma((2, 4)), dma((2, 3, 2, depth)),
            dma((2, 3, 2, depth)), dma((2, depth)), dma((2, depth)),
        ],
        compiler_params=pltpu.CompilerParams(
            vmem_limit_bytes=VMEM_BYTES, collective_id=0, has_side_effects=True
        ),
        name="grad_reduce",
    )(*sources, sums, memory)
    qkv, out, w_in, hid, memory, bias, gain = pl.pallas_call(
        functools.partial(unpack_body, mem),
        out_shape=[
            jax.ShapeDtypeStruct(shape, F32)
            for shape in (
                (1, 3 * thin, half), (1, thin, half), (1, half, lanes), (1, thin, 4 * half),
                (mem, width), (1, 5 * thin), (1, thin),
            )
        ],
        scratch_shapes=[pltpu.VMEM((8, 6 * width), F32)],
        name="unpack",
    )(piece)
    grads = (jnp.swapaxes(qkv, 1, 2), jnp.swapaxes(out, 1, 2), w_in, jnp.swapaxes(hid, 1, 2))
    return (memory, *grads, bias, gain)


def other_core(block, dp):
    return lax.ppermute(block, "dp", [(at, at ^ 1) for at in range(dp)])


def per_device(
    text_rows,
    memory_init,
    cotangent,
    w_qkv,
    w_out,
    w_in,
    w_hid,
    biases,
    norm_gains,
    boundaries,
    mem_resets,
    seg_counts,
):
    items, segs, text_len, width = text_rows.shape
    mem_rows = memory_init.shape[0]
    rows = text_len + 2 * mem_rows
    half = width // 2
    dp = lax.axis_size("dp")
    blocks = (w_qkv, w_out, w_in, w_hid)
    steps = 2 * items * segs
    if dp == 8:
        saved, acts, weights, vecs = gather_forward(
            text_rows, mem_resets, seg_counts, memory_init, boundaries, blocks, biases, norm_gains
        )
    else:
        weights, vecs = gather_apart(blocks, biases, norm_gains)
        saved, acts = forward_steps(
            text_rows, mem_resets, seg_counts, memory_init, boundaries, weights, vecs
        )
    grads, sums, input_grads, memory_grad, acts = backward_steps(
        cotangent, mem_resets, seg_counts, boundaries, mem_rows, acts, weights, vecs, saved
    )
    saved.update(grads)
    reduce = grad_reduce if dp == 8 else grad_reduce_apart
    return (acts, input_grads, *reduce(dp, mem_rows, saved, sums, memory_grad))


def grad_reduce_apart(dp, mem_rows, saved, sums, memory_grad):
    steps, width = sums.shape[0], memory_grad.shape[1]
    half = width // 2
    vector_len = 5 * width
    lanes = 4 * width // dp
    memory_part = memory_grad[16 - mem_rows :].reshape(-1)
    memory_len = -(-memory_part.shape[0] // lanes) * lanes
    memory_part = jnp.pad(memory_part, (0, memory_len - memory_part.shape[0]))
    vector_part = vector_len // dp
    gain_part = width // dp
    used = memory_len + vector_part + gain_part
    extra_rows = -(-used // (3 * 16 * lanes)) * 16
    extras = []
    for layer in range(2):
        total = sums.reshape(steps // 2, 2, 12 * width)[:, layer].sum(axis=0)
        gain_two, shift_two, bias_hid, gain_one, shift_one, bias_o, bias_q, bias_v = [
            total[at * width : (at + 1) * width] for at in range(8)
        ]
        vector = jnp.concatenate(
            [bias_q, bias_v, bias_o, shift_one, total[8 * width :], bias_hid, shift_two]
        ).reshape(2, dp, vector_part)
        gain = jnp.stack([gain_one, gain_two]).reshape(2, dp, gain_part)
        extra = jnp.concatenate(
            [jnp.broadcast_to(memory_part, (2, dp, memory_len)), vector, gain], axis=-1
        )
        extra = jnp.pad(extra, ((0, 0), (0, 0), (0, 3 * extra_rows * lanes - used)))
        extra = extra.reshape(2, dp // 2, 2, 3, extra_rows, lanes).transpose(3, 2, 1, 0, 4, 5)
        extras.append(extra.astype(BF16))
    extras = jnp.stack(extras)
    wires = [weight_grads(layer, dp, saved, extras[layer]) for layer in range(2)]
    mine = jnp.stack([wires[0][0], wires[1][0]])
    theirs = other_core(jnp.stack([wires[0][1], wires[1][1]]), dp)
    both = mine.astype(F32) + theirs.astype(F32)
    both = both.transpose(3, 0, 2, 1, 4, 5).astype(BF16)
    tall, lanes = both.shape[-2:]
    both = both.reshape(4, dp // 2, 3, tall, lanes)
    own = lax.psum_scatter(both, "section", scatter_dimension=0, tiled=True)[0]
    groups = [[2 * at + side for at in range(dp // 2)] for side in range(2)]
    own = lax.psum_scatter(
        own, "dp", scatter_dimension=0, axis_index_groups=groups, tiled=True
    )[0].astype(F32)
    thin = lanes // 4
    body = own[:, :half]
    hid = body[2].reshape(half, 4, thin).transpose(1, 0, 2).reshape(4 * half, thin)
    flat = own[:, half:].reshape(-1)
    return (
        flat[: mem_rows * width].reshape(mem_rows, width),
        body[0, :, : 3 * thin][None],
        body[0, :, 3 * thin :][None],
        body[1][None],
        hid[None],
        flat[memory_len : memory_len + vector_part][None],
        flat[memory_len + vector_part : used][None],
    )


def solution(mesh):
    in_specs = (
        P(("section", "dp"), None, None, None),
        P(),
        P(("section", "dp"), None, None, None),
        P("section", None, None),
        P("section", None, None),
        P("section", None, None),
        P("section", None, None),
        P("section", None),
        P("section", None),
        P(("section", "dp"), None, None),
        P(("section", "dp"), None),
        P(("section", "dp")),
    )
    out_specs = (
        P(("section", "dp"), None, None, None),
        P(("section", "dp"), None, None, None),
        P(),
        P("section", None, "dp"),
        P("section", None, "dp"),
        P("section", None, "dp"),
        P("section", None, "dp"),
        P("section", "dp"),
        P("section", "dp"),
    )
    return jax.shard_map(
        per_device, mesh=mesh, in_specs=in_specs, out_specs=out_specs, check_vma=False
    )
```

```python
import functools

import jax
import jax.numpy as jnp
from jax import lax
from jax.experimental import pallas as pl
from jax.experimental.pallas import tpu as pltpu
from jax.sharding import PartitionSpec as P

HEADS = 12
HEAD_DIM = 64
EPS = 1e-05
MASKED = -1e30
VMEM_BYTES = 63 * 2**20
F32 = jnp.float32
BF16 = jnp.bfloat16
MESH = pl.DeviceIdType.MESH


def dot_nn(one, two):
    return jnp.dot(one, two, preferred_element_type=F32)


def dot_nt(one, two):
    return lax.dot_general(one, two, (((1,), (1,)), ((), ())), preferred_element_type=F32)


def dot_tn(one, two):
    return lax.dot_general(one, two, (((0,), (0,)), ((), ())), preferred_element_type=F32)


def weight_tile(refs, kind, tile, layer):
    qkv_ref, in_ref, end_ref = refs
    quarters, _, _, _, tall, width = end_ref.shape
    thin = tall // 5
    if kind == "out":
        pieces = [
            end_ref[quarter, core, half, layer, 0:thin]
            for half in range(2)
            for quarter in range(quarters)
            for core in range(2)
        ]
    elif kind == "hid":
        pieces = [
            end_ref[(tile % 2) * (quarters // 2) + at, core, tile // 2, layer, thin:tall]
            for at in range(quarters // 2)
            for core in range(2)
        ]
    else:
        ref = qkv_ref if kind == "qkv" else in_ref
        at = tile * width if isinstance(tile, int) else pl.multiple_of(tile * width, width)
        pieces = [ref[core, half, layer, :, pl.ds(at, width)] for half in range(2) for core in range(2)]
    return jnp.concatenate(pieces, axis=0)


def weight_specs(shapes, layer_of):
    specs = []
    for shape in shapes:
        lead = len(shape) - 3
        block = shape[:lead] + (1,) + shape[lead + 1 :]
        specs.append(
            pl.BlockSpec(block, lambda t, *_, lead=lead: (0,) * lead + (layer_of(t), 0, 0))
        )
    return specs


def head_lanes(shape, head):
    lanes = lax.broadcasted_iota(jnp.int32, shape, 1)
    return (lanes // HEAD_DIM) == head


def erf_parts(values):
    density = jnp.exp(-0.5 * values * values) * 0.3989422804014327
    phi = 0.5 * (1.0 + lax.erf(values * 0.7071067811865476))
    return phi, density


def vector_rows(vec_ref, layer, width):
    row = lambda half, at: vec_ref[half, layer, :, at * width : (at + 1) * width]
    return dict(
        bias_q=row(0, 0), bias_v=row(0, 1), bias_o=row(0, 2), shift_one=row(0, 3),
        bias_in=(row(0, 4), row(1, 0), row(1, 1), row(1, 2)),
        bias_hid=row(1, 3), shift_two=row(1, 4), gain_one=row(0, 5), gain_two=row(1, 5),
    )


def ones_where(shape, condition):
    rows = lax.broadcasted_iota(jnp.int32, shape, 0)
    columns = lax.broadcasted_iota(jnp.int32, shape, 1)
    return condition(rows, columns).astype(BF16)


def document_bias(bounds, rows, mem):
    text = bounds.shape[1]
    eight = jnp.broadcast_to(bounds, (8, text)).astype(BF16)
    upto = ones_where((text, rows), lambda r, c: r <= c - mem)
    below = ones_where((rows, text), lambda r, c: c <= r - mem)
    columns = dot_nn(eight, upto)[0:1]
    lines = dot_nt(below, eight)[:, 0:1]
    place = lax.broadcasted_iota(jnp.int32, (1, rows), 1)
    columns = jnp.where((place < mem) | (place >= mem + text), -1.0, columns)
    place = lax.broadcasted_iota(jnp.int32, (rows, 1), 0)
    lines = jnp.where((place < mem) | (place >= mem + text), -1.0, lines)
    allowed = (lines == columns) | (lines < 0) | (columns < 0)
    return jnp.where(allowed, 0.0, MASKED)


def norm_forward(values):
    offset = values - jnp.mean(values, axis=-1, keepdims=True)
    scale = lax.rsqrt(jnp.mean(offset * offset, axis=-1, keepdims=True) + EPS)
    return offset * scale, scale


def forward_layer(
    step, segs, at_layer, before_mix, before_out, store, resets_ref, counts_ref, text_ref, init_ref,
    bounds_ref, weights, vec_ref,
    x_ref, mixed_ref, heads_ref, hat_one_ref, first_ref, active_ref, slope_ref, hat_two_ref,
    stats_ref, acts_ref, bias_ref, y_scr, bias_scr, sum_scr, bias_in_scr, text_scr,
):
    rows, width = y_scr.shape
    text_len, mem = text_ref.shape[1], init_ref.shape[0]
    layer, seg, item = step % 2, (step // 2) % segs, step // (2 * segs)

    def prepare():
        flat = text_ref[0].reshape(text_len * segs, width)
        for number in range(segs):
            pick = ones_where((rows, text_len * segs), lambda r, c: (r - mem) * segs + number == c)
            text_scr[number] = dot_nn(pick, flat).astype(BF16)
            bias_scr[number] = document_bias(bounds_ref[0, number : number + 1, :], rows, mem)

    @pl.when((layer == 0) & (seg == 0) & (step > 0))
    def _():
        prepare()

    before_mix(prepare)

    @pl.when(layer == 0)
    def _():
        fresh = (seg == 0) | (resets_ref[item, seg] > 0)
        start = ones_where((rows, mem), lambda r, c: (r == c) | (r - mem - text_len == c))
        again = ones_where(
            (rows, rows),
            lambda r, c: ((r < mem) & (r + mem + text_len == c)) | ((r >= mem + text_len) & (r == c)),
        )
        memory = jnp.where(fresh, dot_nn(start, init_ref[...]), dot_nn(again, y_scr[...]))
        x_ref[0] = (text_scr[seg].astype(F32) + memory).astype(BF16)
        bias_ref[0, 0] = bias_scr[seg]

    @pl.when(layer == 1)
    def _():
        x_ref[0] = y_scr[...]

    store("x")
    vec = vector_rows(vec_ref, at_layer, width)
    for part in range(4):
        bias_in_scr[part] = vec["bias_in"][part]
    inputs = x_ref[0]
    for tile in range(3):
        mixed = dot_nn(inputs, weight_tile(weights, "qkv", tile, at_layer))
        if tile == 0:
            mixed = mixed + vec["bias_q"]
        if tile == 2:
            mixed = mixed + vec["bias_v"]
        mixed_ref[0, :, tile * width : (tile + 1) * width] = mixed.astype(BF16)

    store("mixed")
    group = 4 * HEAD_DIM
    stat_lane = lax.broadcasted_iota(jnp.int32, (rows, 128), 1)
    stats = jnp.zeros((rows, 128), F32)
    for number in range(width // group):
        at = number * group
        queries = mixed_ref[0, :, at : at + group] * BF16(HEAD_DIM**-0.5)
        keys = mixed_ref[0, :, width + at : width + at + group]
        values = mixed_ref[0, :, 2 * width + at : 2 * width + at + group]
        lanes = lax.broadcasted_iota(jnp.int32, (rows, group), 1) // HEAD_DIM
        stacked = jnp.concatenate([jnp.where(lanes == head, queries, 0) for head in range(4)], axis=0)
        scores = dot_nt(stacked, keys)
        probs = []
        for head in range(4):
            part = scores[head * rows : (head + 1) * rows] + bias_ref[0, 0]
            peak = jnp.max(part, axis=-1, keepdims=True)
            expo = jnp.exp(part - peak)
            norm = jnp.sum(expo, axis=-1, keepdims=True)
            probs.append((expo * (1.0 / norm)).astype(BF16))
            stats = jnp.where(stat_lane == number * 4 + head, peak + jnp.log(norm), stats)
        result = dot_nn(jnp.concatenate(probs, axis=0), values)
        total = result[0:rows]
        for head in range(1, 4):
            total = jnp.where(lanes == head, result[head * rows : (head + 1) * rows], total)
        heads_ref[0, :, at : at + group] = total.astype(BF16)
    store("heads")
    stats_ref[0] = stats

    before_out()
    attn = dot_nn(heads_ref[0], weight_tile(weights, "out", 0, at_layer)) + vec["bias_o"]
    hat, scale = norm_forward(x_ref[0].astype(F32) + attn)
    hat_one_ref[0] = hat.astype(BF16)
    stats = jnp.where(stat_lane == HEADS, scale, stats_ref[0])
    first = hat * vec["gain_one"] + vec["shift_one"]
    first_ref[0] = first.astype(BF16)
    store("hat_one")
    store("first")
    sum_scr[...] = first + vec["bias_hid"]

    def ff_tile(tile, _):
        at = tile * width
        inner = dot_nn(first_ref[0], weight_tile(weights, "in", tile, at_layer)) + bias_in_scr[tile]
        phi, density = erf_parts(inner)
        active = (inner * phi).astype(BF16)
        active_ref[0, :, pl.ds(at, width)] = active
        slope_ref[0, :, pl.ds(at, width)] = (phi + inner * density).astype(BF16)
        store("active", tile)
        store("slope", tile)
        sum_scr[...] += dot_nn(active, weight_tile(weights, "hid", tile, at_layer))
        return _

    for tile in range(4):
        ff_tile(tile, 0)
    hat, scale = norm_forward(sum_scr[...])
    hat_two_ref[0] = hat.astype(BF16)
    stats_ref[0] = jnp.where(stat_lane == HEADS + 1, scale, stats)
    store("hat_two")
    store("stats")
    result = (hat * vec["gain_two"] + vec["shift_two"]).astype(BF16)
    y_scr[...] = result

    @pl.when(layer == 1)
    def _():
        acts_ref[0, 0] = jnp.where(seg < counts_ref[item], result, 0)


def saved_shapes(rows, width):
    return dict(
        x=((rows, width), BF16),
        mixed=((rows, 3 * width), BF16),
        heads=((rows, width), BF16),
        hat_one=((rows, width), BF16),
        first=((rows, width), BF16),
        active=((rows, 4 * width), BF16),
        slope=((rows, 4 * width), BF16),
        hat_two=((rows, width), BF16),
        stats=((rows, 128), F32),
    )


def forward_io(text, resets, counts, init, bounds):
    items, text_len, segs, width = text.shape
    rows = text_len + 2 * init.shape[0]
    steps = 2 * items * segs
    saved = saved_shapes(rows, width)
    by_seg = lambda t: (t // (2 * segs), (t // 2) % segs, 0, 0)
    operands = [resets, counts, text, init, bounds]
    in_specs = [
        pl.BlockSpec(memory_space=pltpu.SMEM),
        pl.BlockSpec(memory_space=pltpu.SMEM),
        pl.BlockSpec((1, text_len, segs, width), lambda t: (t // (2 * segs), 0, 0, 0)),
        pl.BlockSpec(init.shape, lambda t: (0, 0)),
        pl.BlockSpec((1, segs, text_len), lambda t: (t // (2 * segs), 0, 0)),
    ]
    out_specs = [pl.BlockSpec((1,) + shape, lambda t: (t, 0, 0)) for shape, _ in saved.values()]
    out_specs.append(pl.BlockSpec((1, 1, rows, width), by_seg))
    out_specs.append(pl.BlockSpec((1, 1, rows, rows), by_seg))
    out_shape = [jax.ShapeDtypeStruct((steps,) + shape, kind) for shape, kind in saved.values()]
    out_shape.append(jax.ShapeDtypeStruct((items, segs, rows, width), BF16))
    out_shape.append(jax.ShapeDtypeStruct((items, segs, rows, rows), F32))
    scratch = [
        pltpu.VMEM((rows, width), BF16),
        pltpu.VMEM((segs, rows, rows), F32),
        pltpu.VMEM((rows, width), F32),
        pltpu.VMEM((4, 1, width), F32),
        pltpu.VMEM((segs, rows, width), BF16),
    ]
    return steps, saved, operands, in_specs, out_specs, out_shape, scratch


def forward_body(segs, *refs):
    step = pl.program_id(0)
    y_scr = refs[20]

    @pl.when(step == 0)
    def _():
        y_scr[...] = jnp.zeros_like(y_scr)

    def before_mix(prepare):
        pl.when(step == 0)(prepare)

    forward_layer(
        step, segs, 0, before_mix, lambda: None, lambda *_: None, *refs[:5], refs[5:8], *refs[8:]
    )


def forward_steps(text, resets, counts, init, bounds, weights, vec):
    steps, saved, operands, in_specs, out_specs, out_shape, scratch = forward_io(
        text, resets, counts, init, bounds
    )
    *outs, acts, bias = pl.pallas_call(
        functools.partial(forward_body, text.shape[2]),
        grid=(steps,),
        in_specs=in_specs
        + weight_specs([weight.shape for weight in weights], lambda t: t % 2)
        + [pl.BlockSpec((2, 1) + vec.shape[2:], lambda t: (0, t % 2, 0, 0))],
        out_specs=out_specs,
        out_shape=out_shape,
        scratch_shapes=scratch,
        compiler_params=pltpu.CompilerParams(vmem_limit_bytes=VMEM_BYTES),
        name="forward_steps",
    )(*operands, *weights, vec)
    return dict(zip(saved, outs)), acts, bias


def norm_backward(grad, hat, scale, gain):
    scaled = grad * gain
    mean_one = jnp.mean(scaled, axis=-1, keepdims=True)
    mean_two = jnp.mean(scaled * hat, axis=-1, keepdims=True)
    return (scaled - mean_one - hat * mean_two) * scale


def column_sum(values):
    return jnp.sum(values, axis=0, keepdims=True)


def backward_body(
    count, segs, mem, resets_ref, counts_ref, cot_ref, bias_ref, acts_ref, qkv_ref, in_ref, end_ref,
    vec_ref, mixed_ref, heads_ref, hat_one_ref, slope_ref, hat_two_ref, stats_ref,
    branch_ref, inner_ref, attn_ref, mix_ref, sums_ref, inputs_ref, init_ref, acts_out_ref,
    g_scr, carry_scr, sum_scr, go_scr,
):
    step = count - 1 - pl.program_id(0)
    layer = step % 2
    seg = (step // 2) % segs
    rows, width = g_scr.shape
    item = step // (2 * segs)
    weights = (qkv_ref, in_ref, end_ref)
    vec = vector_rows(vec_ref, 0, width)
    gain_one, gain_two = vec["gain_one"], vec["gain_two"]

    @pl.when(pl.program_id(0) == 0)
    def _():
        carry_scr[...] = jnp.zeros_like(carry_scr)
        init_ref[...] = jnp.zeros_like(init_ref)

    @pl.when(layer == 1)
    def _():
        acts_out_ref[...] = acts_ref[...]
        cot = jnp.where(seg < counts_ref[item], cot_ref[0, 0], 0)
        g_scr[...] = cot
        carried = jnp.where(seg == segs - 1, 0.0, carry_scr[...])
        g_scr[rows - 16 : rows, :] = (cot[rows - 16 : rows].astype(F32) + carried).astype(BF16)

    stats = stats_ref[0]
    scale_one = stats[:, HEADS : HEADS + 1]
    scale_two = stats[:, HEADS + 1 : HEADS + 2]
    grad = g_scr[...].astype(F32)
    hat = hat_two_ref[0].astype(F32)
    sums_ref[0, :, 0:width] = column_sum(grad * hat)
    sums_ref[0, :, width : 2 * width] = column_sum(grad)
    grad_second = norm_backward(grad, hat, scale_two, gain_two)
    branch = grad_second.astype(BF16)
    branch_ref[0] = branch
    sums_ref[0, :, 2 * width : 3 * width] = column_sum(branch.astype(F32))
    sum_scr[...] = grad_second

    def ff_tile(tile, _):
        at = tile * width
        active = dot_nt(branch, weight_tile(weights, "hid", tile, 0))
        inner = (active * slope_ref[0, :, pl.ds(at, width)].astype(F32)).astype(BF16)
        inner_ref[0, :, pl.ds(at, width)] = inner
        sums_ref[0, :, pl.ds(8 * width + at, width)] = column_sum(inner.astype(F32))
        sum_scr[...] += dot_nt(inner, weight_tile(weights, "in", tile, 0))
        return _

    for tile in range(4):
        ff_tile(tile, 0)
    grad = sum_scr[...]
    hat = hat_one_ref[0].astype(F32)
    sums_ref[0, :, 3 * width : 4 * width] = column_sum(grad * hat)
    sums_ref[0, :, 4 * width : 5 * width] = column_sum(grad)
    resid = norm_backward(grad, hat, scale_one, gain_one)
    sum_scr[...] = resid
    attn = resid.astype(BF16)
    attn_ref[0] = attn
    sums_ref[0, :, 5 * width : 6 * width] = column_sum(attn.astype(F32))
    go = dot_nt(attn, weight_tile(weights, "out", 0, 0)).astype(BF16)
    go_scr[...] = go
    product = go.astype(F32) * heads_ref[0].astype(F32)
    high = product.astype(BF16)
    low = (product - high.astype(F32)).astype(BF16)
    picks = (
        lax.broadcasted_iota(jnp.int32, (16, width), 1) // HEAD_DIM
        == lax.broadcasted_iota(jnp.int32, (16, width), 0)
    ).astype(BF16)
    centres = dot_nt(picks, high) + dot_nt(picks, low)
    logs = jnp.transpose(stats)

    group = 4 * HEAD_DIM
    for number in range(width // group):
        at = number * group
        queries = mixed_ref[0, :, at : at + group] * BF16(HEAD_DIM**-0.5)
        keys = mixed_ref[0, :, width + at : width + at + group]
        values = mixed_ref[0, :, 2 * width + at : 2 * width + at + group]
        outs = go_scr[:, at : at + group]
        lanes = lax.broadcasted_iota(jnp.int32, (rows, group), 1) // HEAD_DIM

        def stack(block):
            return jnp.concatenate([jnp.where(lanes == head, block, 0) for head in range(4)], axis=0)

        def unstack(block):
            total = block[0:rows]
            for head in range(1, 4):
                total = jnp.where(lanes == head, block[head * rows : (head + 1) * rows], total)
            return total

        keys_s = stack(keys)
        scores = dot_nt(keys_s, queries)
        grad_p = dot_nt(stack(values), outs)
        probs, grads = [], []
        for head in range(4):
            row = number * 4 + head
            part = slice(head * rows, (head + 1) * rows)
            prob = jnp.exp(scores[part] + bias_ref[0, 0] - logs[row : row + 1, :])
            grads.append((prob * (grad_p[part] - centres[row : row + 1, :])).astype(BF16))
            probs.append(prob.astype(BF16))
        grads = jnp.concatenate(grads, axis=0)
        grad_v = unstack(dot_nn(jnp.concatenate(probs, axis=0), outs))
        grad_k = unstack(dot_nn(grads, queries))
        grad_q = dot_tn(grads, keys_s)
        mix_ref[0, :, at : at + group] = (grad_q * HEAD_DIM**-0.5).astype(BF16)
        mix_ref[0, :, width + at : width + at + group] = grad_k.astype(BF16)
        mix_ref[0, :, 2 * width + at : 2 * width + at + group] = grad_v.astype(BF16)

    sums_ref[0, :, 6 * width : 7 * width] = column_sum(mix_ref[0, :, 0:width].astype(F32))
    sums_ref[0, :, 7 * width : 8 * width] = column_sum(mix_ref[0, :, 2 * width : 3 * width].astype(F32))
    total = sum_scr[...]
    for tile in range(3):
        total = total + dot_nt(
            mix_ref[0, :, tile * width : (tile + 1) * width], weight_tile(weights, "qkv", tile, 0)
        )
    result = total.astype(BF16)
    g_scr[...] = result

    @pl.when(layer == 0)
    def _():
        inputs_ref[0, 0] = result
        fresh = (seg == 0) | (resets_ref[item, seg] > 0)
        number = lax.broadcasted_iota(jnp.int32, (16, width), 0)
        folded = result[rows - 16 : rows].astype(F32) + pltpu.roll(
            result[0:16].astype(F32), 16 - mem, 0
        )
        folded = jnp.where(number >= 16 - mem, folded, 0.0).astype(BF16).astype(F32)
        init_ref[...] += jnp.where(fresh, folded, 0.0)
        carry_scr[...] = jnp.where(fresh, 0.0, folded)


def backward_steps(cot, resets, counts, bias, mem, acts, weights, vec, saved):
    items, segs, rows, width = cot.shape
    steps = 2 * items * segs
    at = lambda t: steps - 1 - t
    by_seg = lambda t: (at(t) // (2 * segs), (at(t) // 2) % segs, 0, 0)
    by_step = lambda t: (at(t), 0, 0)
    names = ("mixed", "heads", "hat_one", "slope", "hat_two", "stats")
    outs = dict(
        branch=(rows, width), inner=(rows, 4 * width), attn=(rows, width), mix=(rows, 3 * width),
    )
    *grads, sums, inputs, memory, acts = pl.pallas_call(
        functools.partial(backward_body, steps, segs, mem),
        grid=(steps,),
        in_specs=[
            pl.BlockSpec(memory_space=pltpu.SMEM),
            pl.BlockSpec(memory_space=pltpu.SMEM),
            pl.BlockSpec((1, 1, rows, width), by_seg),
            pl.BlockSpec((1, 1, rows, rows), by_seg),
            pl.BlockSpec((1, 1, rows, width), by_seg),
        ]
        + weight_specs([weight.shape for weight in weights], lambda t: at(t) % 2)
        + [pl.BlockSpec((2, 1) + vec.shape[2:], lambda t: (0, at(t) % 2, 0, 0))]
        + [pl.BlockSpec((1,) + saved[name].shape[1:], by_step) for name in names],
        out_specs=[pl.BlockSpec((1,) + shape, by_step) for shape in outs.values()]
        + [
            pl.BlockSpec((1, 1, 12 * width), by_step),
            pl.BlockSpec((1, 1, rows, width), by_seg),
            pl.BlockSpec((16, width), lambda t: (0, 0)),
            pl.BlockSpec((1, 1, rows, width), by_seg),
        ],
        out_shape=[jax.ShapeDtypeStruct((steps,) + shape, BF16) for shape in outs.values()]
        + [
            jax.ShapeDtypeStruct((steps, 1, 12 * width), F32),
            jax.ShapeDtypeStruct(cot.shape, BF16),
            jax.ShapeDtypeStruct((16, width), F32),
            jax.ShapeDtypeStruct(cot.shape, BF16),
        ],
        scratch_shapes=[
            pltpu.VMEM((rows, width), BF16),
            pltpu.VMEM((16, width), F32),
            pltpu.VMEM((rows, width), F32),
            pltpu.VMEM((rows, width), BF16),
        ],
        compiler_params=pltpu.CompilerParams(vmem_limit_bytes=VMEM_BYTES),
        name="backward_steps",
    )(resets, counts, cot, bias, acts, *weights, vec, *[saved[name] for name in names])
    return dict(zip(outs, grads)), sums, inputs, memory, acts


GATHER_START = (
    ("start", 0, 0, 0), ("start", 1, 0, 1),
)
GATHER_FIRST = (
    ("forward_end", 0), ("spread", 0), ("forward_end", 1), ("forward_vec",), ("spread", 1), ("start", 0,
    0, 1), ("start", 1, 0, 0), ("spread", 2), ("forward_part", 0, 0), ("forward_part", 1, 0), ("start",
    0, 1, 0), ("start", 1, 1, 1), ("hop", 1, 0), ("hop", 1, 1), ("share_part", 0, 0), ("share_part", 1,
    0), ("start", 0, 1, 1), ("start", 1, 1, 0), ("hop", 1, 2), ("share_diagonal", 0),
)
GATHER_THEN = (
    ("hop", 2, 0), ("hop", 2, 1), ("forward_part", 0, 1), ("forward_part", 1, 1), ("hop", 2, 2),
    ("share_part", 0, 1), ("share_part", 1, 1), ("hop", 3, 0), ("hop", 3, 1), ("share_diagonal", 1),
    ("hop", 3, 2),
)


def gather_forward_body(steps, segs, *refs):
    io = refs[:5]
    qkv_src, in_src, out_src, hid_src, biases_ref, gains_ref = refs[5:11]
    outs = refs[11:22]
    full_outs = refs[22:26]
    forward_scratch = refs[26:31]
    weights = refs[31:34]
    vec = refs[34]
    slots = refs[35:44]
    (
        load_sems, end_load_sems, store_sems, x_sems, y_sems, fx_sems, fy_sems, core_sems, end_sems,
        line_core_sems, up_sems, down_sems, vec_sems, saved_sems,
    ) = refs[44:]
    step = pl.program_id(0)
    section, place = lax.axis_index("section"), lax.axis_index("dp")
    x, y = section % 2, section // 2
    core, z = place % 2, place // 2
    end = weights[2]
    depth, _, _, _, tall, _ = end.shape
    thin = tall // 5
    x_dev = (y * 2 + 1 - x, place)
    y_dev = ((1 - y) * 2 + x, place)
    core_dev = (section, z * 2 + 1 - core)
    up_dev = (section, (z + 1) % depth * 2 + core)
    down_dev = (section, (z + depth - 1) % depth * 2 + core)
    own_block = (y, x)
    blocks = ((y, 1 - x), (1 - y, x), (1 - y, 1 - x))

    def remote(source, target, sems, index, device):
        return pltpu.make_async_remote_copy(
            src_ref=source, dst_ref=target, send_sem=sems.at[(0, *index)], recv_sem=sems.at[(1, *index)],
            device_id=device, device_id_type=MESH,
        )


    def part_of(number, block, part):
        rows = weights[number].shape[-2] // 2
        return weights[number].at[core, block[0], block[1], pl.ds(part * rows, rows)]

    def own_part(number, part):
        rows = weights[number].shape[-2] // 2
        at = pl.multiple_of((core * 2 + part) * rows, rows)
        return (qkv_src, in_src)[number].at[0, pl.ds(at, rows)]

    def x_copy(number, part):
        return remote(own_part(number, part), part_of(number, own_block, part), x_sems, (number, part), x_dev)

    def y_copy(number, part):
        return remote(own_part(number, part), part_of(number, own_block, part), y_sems, (number, part), y_dev)

    def fy_copy(number):
        piece = part_of(number, blocks[0], 0)
        return remote(piece, piece, fy_sems, (number,), y_dev)

    def fx_copy(number):
        piece = part_of(number, blocks[1], 1)
        return remote(piece, piece, fx_sems, (number,), x_dev)

    def core_copy(number, kind, part):
        piece = part_of(number, blocks[kind], part)
        return remote(piece, piece, core_sems, (number, kind, part), core_dev)


    def eighth(at, block, first=0, rows=None):
        view = end.at[at, core, block[0], block[1]]
        return view if rows is None else view.at[pl.ds(first, rows)]

    def own_eighth(first):
        source, rows = (out_src, thin) if first == 0 else (hid_src, tall - thin)
        return source.at[0, pl.ds(pl.multiple_of((z * 2 + core) * rows, rows), rows)]

    def end_copy(axis, first):
        rows = thin if first == 0 else tall - thin
        return remote(
            own_eighth(first), eighth(z, own_block, first, rows), end_sems, (axis, 0 if first == 0 else 1),
            (x_dev, y_dev)[axis],
        )

    low = tall // 32 * 16

    def end_fy_copy():
        piece = eighth(z, blocks[0], 0, low)
        return remote(piece, piece, fy_sems, (2,), y_dev)

    def end_fx_copy():
        piece = eighth(z, blocks[1], low, tall - low)
        return remote(piece, piece, fx_sems, (2,), x_dev)

    def line_core_copy(at, kind):
        piece = eighth(at, blocks[kind])
        return remote(piece, piece, line_core_sems, (at, kind), core_dev)

    def up_copy(at, kind):
        piece = eighth(at, blocks[kind])
        return remote(piece, piece, up_sems, (at, kind), up_dev)

    def down_copy(at, kind):
        piece = eighth(at, blocks[kind])
        return remote(piece, piece, down_sems, (at, kind), down_dev)

    def vec_copy(kind):
        row = vec.at[(own_block, own_block, blocks[0])[kind]]
        return remote(row, row, vec_sems, (kind,), (x_dev, y_dev, y_dev)[kind])

    def loads():
        copies = []
        for number, source in enumerate((qkv_src, in_src)):
            rows = weights[number].shape[-2]
            for side in range(2):
                copies.append(
                    pltpu.make_async_copy(
                        source.at[0, pl.ds(side * rows, rows)], weights[number].at[side, y, x],
                        load_sems.at[number, side],
                    )
                )
        for at in range(depth):
            for side in range(2):
                for number, (source, first, rows) in enumerate(
                    ((out_src, 0, thin), (hid_src, thin, tall - thin))
                ):
                    copies.append(
                        pltpu.make_async_copy(
                            source.at[0, pl.ds((at * 2 + side) * rows, rows)],
                            end.at[at, side, y, x, pl.ds(first, rows)],
                            end_load_sems.at[at, side, number],
                        )
                    )
        return copies

    def full_stores():
        return [
            pltpu.make_async_copy(source, target, store_sems.at[number])
            for number, (source, target) in enumerate(zip((*weights, vec), full_outs))
        ]

    received = set()

    def arrived(*copies):
        for name, copy in copies:
            if name not in received:
                received.add(name)
                copy.wait_recv()

    def end_arrived(axis):
        arrived(*[((axis, first), end_copy(axis, first)) for first in (0, thin)])

    def start_end(axis):
        for first in (0, thin):
            end_copy(axis, first).start()

    def forward_end(axis):
        end_arrived(axis)
        (end_fy_copy, end_fx_copy)[axis]().start()

    def spread(kind):
        if kind < 2:
            end_arrived(kind)
        else:
            arrived(("fy", end_fy_copy()), ("fx", end_fx_copy()))

        @pl.when(z < depth - 1)
        def _():
            up_copy(z, kind).start()

        @pl.when(z > 0)
        def _():
            down_copy(z, kind).start()

        line_core_copy(z, kind).start()

    def hop(distance, kind):
        @pl.when(z >= distance)
        def _():
            up_copy(z - distance, kind).wait_recv()

            @pl.when(z < depth - 1)
            def _():
                up_copy(z - distance, kind).start()

            line_core_copy(z - distance, kind).start()

        @pl.when(z + distance < depth)
        def _():
            down_copy(z + distance, kind).wait_recv()

            @pl.when(z > 0)
            def _():
                down_copy(z + distance, kind).start()

            line_core_copy(z + distance, kind).start()

    def forward_part(axis, number):
        part = axis
        (x_copy, y_copy)[axis](number, part).wait_recv()
        (fy_copy, fx_copy)[axis](number).start()
        core_copy(number, axis, part).start()

    def share_part(axis, number):
        part = 1 - axis
        (x_copy, y_copy)[axis](number, part).wait_recv()
        core_copy(number, axis, part).start()

    def share_diagonal(number):
        fy_copy(number).wait_recv()
        core_copy(number, 2, 0).start()
        fx_copy(number).wait_recv()
        core_copy(number, 2, 1).start()

    def forward_vec():
        vec_copy(0).wait_recv()
        vec_copy(2).start()

    act = dict(
        forward_vec=forward_vec,
        start=lambda axis, number, part: (x_copy, y_copy)[axis](number, part).start(),
        forward_end=forward_end,
        spread=spread,
        hop=hop,
        forward_part=forward_part,
        share_part=share_part,
        share_diagonal=share_diagonal,
    )

    def complete(number):
        for kind in range(3):
            for part in range(2):
                core_copy(number, kind, part).wait_recv()

    def before_mix(prepare):
        @pl.when(step == 0)
        def _():
            barrier = pltpu.get_barrier_semaphore()
            for device in (x_dev, y_dev, core_dev):
                pl.semaphore_signal(barrier, inc=1, device_id=device, device_id_type=MESH)

            @pl.when(z < depth - 1)
            def _():
                pl.semaphore_signal(barrier, inc=1, device_id=up_dev, device_id_type=MESH)

            @pl.when(z > 0)
            def _():
                pl.semaphore_signal(barrier, inc=1, device_id=down_dev, device_id_type=MESH)

            pl.semaphore_wait(barrier, 3 + jnp.where(z > 0, 1, 0) + jnp.where(z < depth - 1, 1, 0))
            start_end(0)
            start_end(1)
            vec[y, x] = jnp.concatenate([biases_ref[...].astype(F32), gains_ref[...].astype(F32)], axis=1)
            vec_copy(0).start()
            vec_copy(1).start()
            for name, *numbers in GATHER_START:
                act[name](*numbers)
            for copy in loads():
                copy.start()
            forward_scratch[0][...] = jnp.zeros_like(forward_scratch[0])
            prepare()
            for name, *numbers in GATHER_FIRST:
                act[name](*numbers)
            vec_copy(1).wait_recv()
            vec_copy(2).wait_recv()
            complete(0)
            for copy in loads():
                copy.wait()

        @pl.when(step == 1)
        def _():
            for copy in full_stores():
                copy.start()

    def before_out():
        @pl.when(step == 0)
        def _():
            for name, *numbers in GATHER_THEN:
                act[name](*numbers)
            complete(1)
            for at in range(depth):
                for kind in range(3):
                    line_core_copy(at, kind).wait_recv()

    names = tuple(saved_shapes(*forward_scratch[0].shape))

    def saved_copies(which, name, tile=None):
        number = names.index(name)
        source, target = slots[number].at[which % 2], outs[number].at[which]
        if name not in ("active", "slope"):
            return [pltpu.make_async_copy(source, target, saved_sems.at[which % 2, number, 0])]
        size = source.shape[1] // 4
        return [
            pltpu.make_async_copy(
                source.at[:, pl.ds(at * size, size)], target.at[:, pl.ds(at * size, size)],
                saved_sems.at[which % 2, number, at],
            )
            for at in range(4)
            if tile is None or at == tile
        ]

    def store(name, tile=None):
        for copy in saved_copies(step, name, tile):
            copy.start()

    def stored(which):
        for name in names:
            for copy in saved_copies(which, name):
                copy.wait()

    @pl.when(step >= 2)
    def _():
        stored(step - 2)

    views = [slot.at[pl.ds(step % 2, 1)] for slot in slots]
    forward_layer(
        step, segs, step % 2, before_mix, before_out, store, *io, weights, vec, *views, *outs[9:],
        *forward_scratch,
    )

    @pl.when(step == steps - 1)
    def _():
        stored(steps - 2)
        stored(steps - 1)
        for copy in full_stores():
            copy.wait()
        for number in range(2):
            for part in range(2):
                x_copy(number, part).wait_send()
                y_copy(number, part).wait_send()
                for kind in range(3):
                    core_copy(number, kind, part).wait_send()
            fx_copy(number).wait_send()
            fy_copy(number).wait_send()
            for first in (0, thin):
                end_copy(number, first).wait_send()
        end_fx_copy().wait_send()
        end_fy_copy().wait_send()
        for kind in range(3):
            vec_copy(kind).wait_send()
            for at in range(depth):
                line_core_copy(at, kind).wait_send()

                @pl.when((z >= at) & (z < depth - 1))
                def _():
                    up_copy(at, kind).wait_send()

                @pl.when((z <= at) & (z > 0))
                def _():
                    down_copy(at, kind).wait_send()


def full_weight_shapes(w_qkv, w_out, w_in, w_hid):
    half, width = w_out.shape[1:]
    return [(2, 2, 2, half // 2, block.shape[2]) for block in (w_qkv, w_in)] + [
        (4, 2, 2, 2, (half + w_hid.shape[1]) // 8, width)
    ]


def gather_forward(text, resets, counts, init, bounds, blocks, biases, gains):
    steps, saved, operands, in_specs, out_specs, out_shape, scratch = forward_io(
        text, resets, counts, init, bounds
    )
    shapes = full_weight_shapes(*blocks)
    full = [pltpu.VMEM(shape, BF16) for shape in shapes] + [pltpu.VMEM((2, 2, 1, biases.shape[1] + gains.shape[1]), F32)]
    any_spec = pl.BlockSpec(memory_space=pl.ANY)
    dma = pltpu.SemaphoreType.DMA
    depth = shapes[2][0]
    *outs, acts, bias, qkv, w_in, end, vecs = pl.pallas_call(
        functools.partial(gather_forward_body, steps, text.shape[2]),
        grid=(steps,),
        in_specs=in_specs + [any_spec] * 4 + [pl.BlockSpec(vector.shape, lambda t: (0, 0)) for vector in (biases, gains)],
        out_specs=[any_spec] * len(saved) + out_specs[len(saved) :] + [any_spec] * 4,
        out_shape=out_shape + [jax.ShapeDtypeStruct(ref.shape, ref.dtype) for ref in full],
        scratch_shapes=scratch
        + full
        + [pltpu.VMEM((2,) + shape, kind) for shape, kind in saved.values()]
        + [
            dma((2, 2)), dma((depth, 2, 2)), dma((4,)), dma((2, 2, 2)), dma((2, 2, 2)), dma((2, 3)),
            dma((2, 3)), dma((2, 2, 3, 2)), dma((2, 2, 2)), dma((2, depth, 3)), dma((2, depth, 3)),
            dma((2, depth, 3)), dma((2, 3)), dma((2, len(saved), 4)),
        ],
        compiler_params=pltpu.CompilerParams(
            vmem_limit_bytes=VMEM_BYTES, collective_id=1, has_side_effects=True
        ),
        name="gather_forward",
    )(*operands, blocks[0], blocks[2], blocks[1], blocks[3], biases, gains)
    return dict(zip(saved, outs)), acts, bias, (qkv, w_in, end), vecs


def gather_apart(blocks, biases, gains):
    vec = jnp.concatenate([biases, gains], axis=1).astype(F32)
    w_qkv, w_out, w_in, w_hid = [
        lax.all_gather(block[0], "section").reshape(2, 2, *block.shape[1:]) for block in blocks
    ]
    half, width = w_out.shape[2:]
    full = [
        block.reshape(2, 2, 2, half // 2, -1).transpose(2, 0, 1, 3, 4) for block in (w_qkv, w_in)
    ]
    ends = [block.reshape(2, 2, 4, 2, -1, width).transpose(2, 3, 0, 1, 4, 5) for block in (w_out, w_hid)]
    vecs = lax.all_gather(vec, "section").reshape(2, 2, *vec.shape)
    return (*full, jnp.concatenate(ends, axis=4)), vecs


GRAD_NAMES = ("first", "inner", "active", "branch", "x", "mix", "heads", "attn")


def weight_grad_body(
    layer, segs_all, dp, *refs,
):
    sources = refs[:8]
    extra_ref, mine_ref, theirs_ref = refs[8:11]
    held = refs[11:19]
    wire, in_sems, extra_sem, out_sems = refs[19:23]
    core = lax.axis_index("dp") % 2
    rows = sources[0].shape[1]
    width = sources[0].shape[2]
    half = width // 2
    lanes = wire.shape[-1]
    thin = width // dp
    wide = 3 * thin

    def loads(number):
        return [
            pltpu.make_async_copy(
                sources[number].at[2 * at + layer],
                held[number].at[pl.ds(at * rows, rows)],
                in_sems.at[number, at],
            )
            for at in range(segs_all)
        ]

    for number in range(8):
        for copy in loads(number):
            copy.start()
    extra = pltpu.make_async_copy(extra_ref, wire.at[:, :, :, :, pl.ds(half, extra_ref.shape[4])], extra_sem)
    extra.start()

    def ready(*numbers):
        for number in numbers:
            for copy in loads(number):
                copy.wait()

    def stores(kind):
        return [
            pltpu.make_async_copy(wire.at[kind, core], mine_ref.at[kind], out_sems.at[kind, 0]),
            pltpu.make_async_copy(wire.at[kind, 1 - core], theirs_ref.at[kind], out_sems.at[kind, 1]),
        ]

    first, inner, active, branch, inputs, mix, heads, attn = held
    extra.wait()

    ready(0, 1)
    per_tile = width // lanes

    def in_tile(tile, _):
        right = inner[:, pl.ds(pl.multiple_of(tile * width, width), width)]
        for side in range(2):
            result = dot_tn(first[:, side * half : (side + 1) * half], right).astype(BF16)
            for at in range(per_tile):
                wire[1, at % 2, tile * (per_tile // 2) + at // 2, side, 0:half, :] = result[
                    :, at * lanes : (at + 1) * lanes
                ]
        return _

    lax.fori_loop(0, 4, in_tile, 0)
    for copy in stores(1):
        copy.start()

    ready(2, 3)
    def hid_tile(side, _):
        for part in range(4):
            left = active[:, pl.ds(pl.multiple_of(side * 4 * half + part * half, half), half)]
            result = dot_tn(left, branch[...]).astype(BF16)
            for at in range(dp):
                wire[2, at % 2, at // 2, side, 0:half, part * thin : (part + 1) * thin] = result[
                    :, at * thin : (at + 1) * thin
                ]
        return _
    lax.fori_loop(0, 2, hid_tile, 0)
    for copy in stores(2):
        copy.start()

    ready(4, 5, 6, 7)
    for side in range(2):
        left = inputs[:, side * half : (side + 1) * half]
        for tile in range(2):
            result = dot_tn(left, mix[:, tile * 3 * half : (tile + 1) * 3 * half]).astype(BF16)
            for at in range(dp // 2):
                place = tile * (dp // 2) + at
                wire[0, place % 2, place // 2, side, 0:half, 0:wide] = result[
                    :, at * wide : (at + 1) * wide
                ]
        result = dot_tn(heads[:, side * half : (side + 1) * half], attn[...]).astype(BF16)
        for at in range(dp):
            wire[0, at % 2, at // 2, side, 0:half, wide:lanes] = result[:, at * thin : (at + 1) * thin]
    for copy in stores(0):
        copy.start()
    for kind in range(3):
        for copy in stores(kind):
            copy.wait()


def weight_grads(layer, dp, saved, extras):
    sources = [saved[name] for name in GRAD_NAMES]
    steps, rows, width = sources[0].shape
    segs_all = steps // 2
    half = width // 2
    lanes = 4 * width // dp
    extra_rows = extras.shape[4]
    kind = jax.ShapeDtypeStruct((3, dp // 2, 2, half + extra_rows, lanes), BF16)
    any_spec = pl.BlockSpec(memory_space=pl.ANY)
    return pl.pallas_call(
        functools.partial(weight_grad_body, layer, segs_all, dp),
        in_specs=[any_spec] * 9,
        out_specs=[any_spec] * 2,
        out_shape=[kind, kind],
        scratch_shapes=[pltpu.VMEM((segs_all * rows, source.shape[2]), BF16) for source in sources]
        + [
            pltpu.VMEM((3, 2, dp // 2, 2, half + extra_rows, lanes), BF16),
            pltpu.SemaphoreType.DMA((8, segs_all)),
            pltpu.SemaphoreType.DMA,
            pltpu.SemaphoreType.DMA((3, 2)),
        ],
        compiler_params=pltpu.CompilerParams(vmem_limit_bytes=VMEM_BYTES),
        name="weight_grads",
    )(*sources, extras)


def add_into(ref, other):
    ref[...] = (ref[...].astype(F32) + other[...].astype(F32)).astype(BF16)


def build_extra(mem, sums_ref, memory_ref, extra):
    steps = sums_ref.shape[0]
    width = memory_ref.shape[1]
    lanes = extra.shape[-1]
    extra[...] = jnp.zeros_like(extra)
    for layer in range(2):
        total = sums_ref[layer]
        for step in range(layer + 2, steps, 2):
            total = total + sums_ref[step]
        for block, parts in enumerate(((6, 7, 5, 4, 8, 3), (9, 10, 11, 2, 1, 0))):
            for piece in range(width // lanes):
                extra[layer, block, piece * mem : (piece + 1) * mem, :] = memory_ref[
                    16 - mem : 16, piece * lanes : (piece + 1) * lanes
                ]
                for at, part in enumerate(parts):
                    row = mem * (width // lanes) + at * (width // lanes) + piece
                    first = part * width + piece * lanes
                    extra[layer, block, row : row + 1, :] = total[:, first : first + lanes]


KIND_IN, KIND_HID, KIND_MIX = 1, 2, 0
CUTS = {KIND_HID: 2, KIND_MIX: 3}
PLAN = (
    ("mul", 0, 2, 0), ("mul", 0, 2, 1), ("core", 0, 2, 0), ("QO", 2, 0), ("P", 2, 0), ("mul", 0, 1, 0),
    ("core", 0, 2, 1), ("QO", 2, 1), ("P", 2, 1), ("mul", 1, 2, 0), ("mul", 1, 2, 1), ("core", 0, 1, 0),
    ("hop", "ZO", 1, 0, 0), ("XQ", 2, 0), ("XQ", 2, 1), ("core", 1, 2, 0), ("QW", 2, 0), ("YP", 2, 0),
    ("mul", 1, 1, 0), ("core", 1, 2, 1), ("QW", 2, 1), ("hop", "ZO", 1, 0, 1), ("mul", 0, 0, 0), ("YP",
    2, 1), ("core", 0, 0, 0), ("P", 0, 0), ("P", 0, 1), ("QO", 0, 0), ("hop", "ZO", 1, 0, 2), ("core",
    1, 1, 0), ("QWA", 1, 0), ("QWA", 1, 1), ("mul", 1, 0, 0), ("plane", 2, 0), ("hop", "Z", 2, 0, 0),
    ("hop", "Z", 2, 0, 1), ("hop", "Z", 2, 0, 2), ("plane", 2, 1), ("hop", "Z", 2, 1, 0), ("hop", "Z",
    2, 1, 1), ("hop", "Z", 2, 1, 2), ("core", 1, 0, 0), ("QW", 0, 0), ("YP", 0, 0), ("QW", 0, 1), ("QO",
    0, 1), ("plane", 1, 0), ("hop", "Z", 1, 0, 0), ("hop", "Z", 1, 0, 1), ("hop", "Z", 1, 0, 2), ("XQ",
    0, 0), ("fin", "ZO", 1, 0), ("XO", 1), ("plane", 1, 1), ("hop", "Z", 1, 1, 0), ("hop", "Z", 1, 1,
    1), ("fin", "Z", 2, 0), ("YP", 0, 1), ("plane", 0, 0), ("hop", "Z", 0, 0, 0), ("hop", "Z", 0, 0, 1),
    ("hop", "Z", 0, 0, 2), ("hop", "Z", 1, 1, 2), ("YO", 1), ("XQ", 0, 1), ("plane", 0, 1), ("hop", "Z",
    0, 1, 0), ("hop", "Z", 0, 1, 1), ("hop", "Z", 0, 1, 2), ("fin", "Z", 2, 1), ("fin", "Z", 0, 0),
    ("fin", "Z", 1, 1), ("fin", "Z", 1, 0), ("fin", "Z", 0, 1),
)


def row_parts(tall, thin):
    first = -(-tall // 32) * 16
    some = ((0, first), (first, tall - first))
    return {KIND_IN: some, KIND_MIX: some, KIND_HID: ((0, 2 * thin), (2 * thin, tall - 2 * thin))}


def grad_reduce_body(dp, mem, segs_all, *refs):
    sources = refs[:8]
    sums_ref, memory_ref = refs[8:10]
    piece_out = refs[10]
    held = refs[11:19]
    mine, theirs, landed, xp, xq, yqo, yqw, yp, ywall, xo, yo, z_low, z_high, zo_low, zo_high = refs[19:34]
    extra = refs[34]
    (
        in_sems, core_sems, free_sem, xp_sems, xq_sems, yqo_sems, yqw_sems, yp_sems, single_sems, up_sems,
        down_sems, zo_up_sems, zo_down_sems,
    ) = refs[35:]
    section, place = lax.axis_index("section"), lax.axis_index("dp")
    x, y = section % 2, section // 2
    core, z = place % 2, place // 2
    depth = dp // 2
    rows, width = sources[0].shape[1:]
    half = width // 2
    tall, lanes = mine.shape[-2:]
    thin = width // dp
    wide = 3 * thin
    parts = row_parts(tall, thin)
    x_dev = (y * 2 + 1 - x, place)
    y_dev = ((1 - y) * 2 + x, place)
    core_dev = (section, z * 2 + 1 - core)
    up_dev = (section, (z + 1) % depth * 2 + core)
    down_dev = (section, (z + depth - 1) % depth * 2 + core)
    used = {KIND_IN: (0, 1), KIND_HID: (2, 3), KIND_MIX: (4, 5, 6, 7)}
    slots = {KIND_HID: 0, KIND_MIX: 1}
    first, inner, active, branch, inputs, mix, heads, attn = held
    units = [step[1:3] for step in PLAN if step[0] == "mul" and step[3] == 0]

    def loads(side, kind):
        layer = (1 - x) if side == 0 else x
        return [
            pltpu.make_async_copy(
                sources[number].at[2 * at + layer],
                held[number].at[pl.ds(at * rows, rows)],
                in_sems.at[number, at],
            )
            for number in used[kind]
            for at in range(segs_all)
        ]

    for side, kind in units:
        if side == 0:
            for copy in loads(0, kind):
                copy.start()
    barrier = pltpu.get_barrier_semaphore()
    for device in (x_dev, y_dev, core_dev):
        pl.semaphore_signal(barrier, inc=1, device_id=device, device_id_type=MESH)

    @pl.when(z < depth - 1)
    def _():
        pl.semaphore_signal(barrier, inc=1, device_id=up_dev, device_id_type=MESH)

    @pl.when(z > 0)
    def _():
        pl.semaphore_signal(barrier, inc=1, device_id=down_dev, device_id_type=MESH)

    build_extra(mem, sums_ref, memory_ref, extra)
    pl.semaphore_wait(barrier, 3 + jnp.where(z > 0, 1, 0) + jnp.where(z < depth - 1, 1, 0))

    def remote(source, target, sems, index, device):
        return pltpu.make_async_remote_copy(
            src_ref=source, dst_ref=target, send_sem=sems.at[(0, *index)], recv_sem=sems.at[(1, *index)],
            device_id=device, device_id_type=MESH,
        )

    def core_parts(kind):
        return range(2) if kind == KIND_HID else range(1)

    def core_rows(kind, part):
        return parts[kind][part] if kind == KIND_HID else (0, tall)

    def core_copy(unit, part):
        some = pl.ds(*core_rows(units[unit][1], part))
        return remote(
            theirs.at[unit % 2, :, :, some], landed.at[unit % 2, :, :, some], core_sems, (unit, part), core_dev
        )

    def p_copy(kind, part):
        at = pl.ds(0, CUTS[kind])
        some = pl.ds(*parts[kind][part])
        return remote(
            mine.at[0, kind, at, :, some], xp.at[slots[kind], at, :, some], xp_sems, (slots[kind], part), x_dev
        )

    def q_copy(side, kind, part):
        some = pl.ds(*parts[kind][part])
        count = depth - CUTS[kind]
        return remote(
            mine.at[side, kind, pl.ds(CUTS[kind], count), 1 - y, some],
            (yqo, yqw)[side].at[slots[kind], pl.ds(0, count), some],
            (yqo_sems, yqw_sems)[side], (slots[kind], part), y_dev,
        )

    def xq_copy(kind, part):
        some = pl.ds(*parts[kind][part])
        count = depth - CUTS[kind]
        return remote(
            mine.at[0, kind, pl.ds(CUTS[kind], count), y, some],
            xq.at[slots[kind], pl.ds(0, count), some], xq_sems, (slots[kind], part), x_dev,
        )

    def yp_copy(kind, part):
        some = pl.ds(*parts[kind][part])
        at = pl.ds(0, CUTS[kind])
        return remote(
            mine.at[1, kind, at, 1 - y, some], yp.at[slots[kind], at, some], yp_sems, (slots[kind], part), y_dev
        )

    def xo_copy():
        return remote(mine.at[0, KIND_IN, z], xo, single_sems, (0,), x_dev)

    def yo_copy():
        return remote(xo.at[1 - y], yo, single_sems, (1,), y_dev)

    def ywall_copy(part):
        some = pl.ds(*parts[KIND_IN][part])
        return remote(
            mine.at[1, KIND_IN, :, 1 - y, some], ywall.at[:, some], single_sems, (2 + part,), y_dev
        )

    def line_rows(kind, part):
        return pl.ds(*parts[kind][part])

    def up_copy(name, kind, part, at):
        if name == "ZO":
            return remote(mine.at[0, kind, at], zo_low.at[at - 1], zo_up_sems, (at,), up_dev)
        some = line_rows(kind, part)
        return remote(
            mine.at[1, kind, at, y, some], z_low.at[kind, at - 1, some], up_sems, (kind, part, at), up_dev
        )

    def down_copy(name, kind, part, at):
        if name == "ZO":
            return remote(mine.at[0, kind, at], zo_high.at[at], zo_down_sems, (at,), down_dev)
        some = line_rows(kind, part)
        return remote(
            mine.at[1, kind, at, y, some], z_high.at[kind, at, some], down_sems, (kind, part, at), down_dev
        )

    def from_low(name, kind, part, at):
        up_copy(name, kind, part, at).wait_recv()
        if name == "ZO":
            for block in range(2):
                add_into(mine.at[0, kind, at, block], zo_low.at[at - 1, block])
        else:
            some = line_rows(kind, part)
            add_into(mine.at[1, kind, at, y, some], z_low.at[kind, at - 1, some])

    def from_high(name, kind, part, at):
        down_copy(name, kind, part, at).wait_recv()
        if name == "ZO":
            for block in range(2):
                add_into(mine.at[0, kind, at, block], zo_high.at[at, block])
        else:
            some = line_rows(kind, part)
            add_into(mine.at[1, kind, at, y, some], z_high.at[kind, at, some])

    def multiply(side, kind, part):
        unit = units.index((side, kind))
        slot = unit % 2

        def put(chunk_core, chunk_z, block, piece, start, stop):
            @pl.when(core == chunk_core)
            def _():
                mine[side, kind, chunk_z, block, start:stop, :] = piece

            @pl.when(core != chunk_core)
            def _():
                theirs[slot, chunk_z, block, start:stop, :] = piece

        if part == 0:
            for copy in loads(side, kind):
                copy.wait()
            if unit >= 2:
                for earlier in core_parts(units[unit - 2][1]):
                    core_copy(unit - 2, earlier).wait_send()
            layer = (1 - x) if side == 0 else x
            extra_rows = tall - half
            for block in range(2):
                added = extra[layer, block, kind * extra_rows : (kind + 1) * extra_rows, :].astype(BF16)
                for at in range(depth):
                    mine[side, kind, at, block, half:, :] = added
                    theirs[slot, at, block, half:, :] = added
        if kind == KIND_IN:
            per_tile = width // lanes

            def in_tile(tile, _):
                right = inner[:, pl.ds(pl.multiple_of(tile * width, width), width)]
                for block in range(2):
                    result = dot_tn(first[:, block * half : (block + 1) * half], right).astype(BF16)
                    for at in range(per_tile):
                        put(
                            at % 2, tile * (per_tile // 2) + at // 2, block,
                            result[:, at * lanes : (at + 1) * lanes], 0, half,
                        )
                return _

            lax.fori_loop(0, 4, in_tile, 0)
        elif kind == KIND_HID:

            def hid_tile(block, _):
                right = active[:, pl.ds(pl.multiple_of((block * 2 + part) * width, width), width)]
                for side_rows in range(2):
                    result = dot_tn(
                        branch[:, side_rows * half : (side_rows + 1) * half], right
                    ).astype(BF16)
                    for at in range(dp // 2):
                        chunk = side_rows * (dp // 2) + at
                        for piece in range(2):
                            row = (part * 2 + piece) * thin
                            put(
                                chunk % 2, chunk // 2, block,
                                result[at * thin : (at + 1) * thin, piece * half : (piece + 1) * half],
                                row, row + thin,
                            )
                return _

            lax.fori_loop(0, 2, hid_tile, 0)
        else:

            def mix_tile(block, _):
                columns = pl.ds(pl.multiple_of(block * half, half), half)
                for tile in range(2):
                    result = dot_tn(
                        mix[:, tile * 3 * half : (tile + 1) * 3 * half], inputs[:, columns]
                    ).astype(BF16)
                    for at in range(depth):
                        chunk = tile * depth + at
                        put(chunk % 2, chunk // 2, block, result[at * wide : (at + 1) * wide], 0, wide)
                result = dot_tn(attn[...], heads[:, columns]).astype(BF16)
                for chunk in range(dp):
                    put(chunk % 2, chunk // 2, block, result[chunk * thin : (chunk + 1) * thin], wide, half)
                return _

            lax.fori_loop(0, 2, mix_tile, 0)
        if unit >= 2 and part == 0:
            pl.semaphore_wait(free_sem, 1)
        core_copy(unit, part).start()
        if side == 0 and part == core_parts(kind)[-1]:
            for copy in loads(1, kind):
                copy.start()

    def add_core(side, kind, part):
        unit = units.index((side, kind))
        some = pl.ds(*core_rows(kind, part))
        core_copy(unit, part).wait_recv()

        def add(at, _):
            for block in range(2):
                add_into(mine.at[side, kind, at, block, some], landed.at[unit % 2, at, block, some])
            return _

        lax.fori_loop(0, depth, add, 0)
        if unit + 2 < len(units) and part == core_parts(kind)[-1]:
            pl.semaphore_signal(free_sem, inc=1, device_id=core_dev, device_id_type=MESH)

    def forward_q(kind, part):
        q_copy(0, kind, part).wait_recv()
        some = pl.ds(*parts[kind][part])
        for at in range(depth - CUTS[kind]):
            add_into(mine.at[0, kind, CUTS[kind] + at, y, some], yqo.at[slots[kind], at, some])
        xq_copy(kind, part).start()

    def forward_p(kind, part):
        p_copy(kind, part).wait_recv()
        some = pl.ds(*parts[kind][part])
        for at in range(CUTS[kind]):
            for block in range(2):
                add_into(mine.at[1, kind, at, block, some], xp.at[slots[kind], at, block, some])
        yp_copy(kind, part).start()

    def finish_plane(kind, part):
        some = pl.ds(*parts[kind][part])
        if kind == KIND_IN:
            ywall_copy(part).wait_recv()
            for at in range(depth):
                add_into(mine.at[1, kind, at, y, some], ywall.at[at, some])
            return
        slot = slots[kind]
        q_copy(1, kind, part).wait_recv()
        xq_copy(kind, part).wait_recv()
        for at in range(depth - CUTS[kind]):
            ref = mine.at[1, kind, CUTS[kind] + at, y, some]
            total = ref[...].astype(F32) + yqw[slot, at, some].astype(F32) + xq[slot, at, some].astype(F32)
            ref[...] = total.astype(BF16)
        yp_copy(kind, part).wait_recv()
        for at in range(CUTS[kind]):
            add_into(mine.at[1, kind, at, y, some], yp.at[slot, at, some])

    def hop(name, kind, part, count):
        high = depth - 1 - count + z
        low = count - (depth - 1 - z)

        @pl.when(z <= count)
        def _():
            @pl.when(z > 0)
            def _():
                from_low(name, kind, part, high)

            up_copy(name, kind, part, high).start()

        @pl.when(low >= 0)
        def _():
            @pl.when(z < depth - 1)
            def _():
                from_high(name, kind, part, low)

            down_copy(name, kind, part, low).start()

    finished = []

    def finish(name, kind, part):
        @pl.when(z > 0)
        def _():
            from_low(name, kind, part, z)

        @pl.when(z < depth - 1)
        def _():
            from_high(name, kind, part, z)

        if name == "ZO":
            return
        some = line_rows(kind, part)
        if kind == KIND_IN:
            add_into(mine.at[1, kind, z, y, some], xo.at[y, some])
            if (name, kind, 1 - part) not in finished:
                yo_copy().wait_recv()
            add_into(mine.at[1, kind, z, y, some], yo.at[some])
        finished.append((name, kind, part))
        piece_out[kind, some, :] = mine[1, kind, z, y, some, :]

    def forward_o(kind):
        xo_copy().wait_recv()
        yo_copy().start()

    act = dict(
        mul=multiply,
        core=add_core,
        P=lambda kind, part: p_copy(kind, part).start(),
        QO=lambda kind, part: q_copy(0, kind, part).start(),
        QW=lambda kind, part: q_copy(1, kind, part).start(),
        XQ=forward_q,
        YP=forward_p,
        plane=finish_plane,
        hop=hop,
        fin=finish,
        XO=lambda kind: xo_copy().start(),
        YO=forward_o,
        QWA=lambda kind, part: ywall_copy(part).start(),
    )
    for name, *numbers in PLAN:
        act[name](*numbers)

    for unit in (4, 5):
        for part in core_parts(units[unit][1]):
            core_copy(unit, part).wait_send()
    for copy in (xo_copy(), yo_copy(), ywall_copy(0), ywall_copy(1)):
        copy.wait_send()
    for kind in CUTS:
        for part in range(2):
            p_copy(kind, part).wait_send()
            xq_copy(kind, part).wait_send()
            yp_copy(kind, part).wait_send()
            for side in range(2):
                q_copy(side, kind, part).wait_send()
    lines = [("ZO", KIND_IN, 0)]
    lines += [("Z", kind, part) for kind in (KIND_IN, *CUTS) for part in range(2)]
    for line in lines:
        for at in range(depth):

            @pl.when(at > z)
            def _():
                up_copy(*line, at).wait_send()

            @pl.when(at < z)
            def _():
                down_copy(*line, at).wait_send()


def grad_reduce_shapes(dp, steps, rows, width):
    half = width // 2
    lanes = 4 * width // dp
    depth = dp // 2
    extra_rows = 16
    tall = half + extra_rows
    most, least = max(CUTS.values()), depth - min(CUTS.values())
    held = [width, 4 * width, 4 * width, width, width, 3 * width, width, width]
    return (
        [pltpu.VMEM((steps // 2 * rows, columns), BF16) for columns in held]
        + [
            pltpu.VMEM(shape + (tall, lanes), BF16)
            for shape in (
                (2, 3, depth, 2), (2, depth, 2), (2, depth, 2), (2, most, 2), (2, least), (2, least),
                (2, least), (2, most), (depth,), (2,), (), (3, depth - 1), (3, depth - 1),
                (depth - 1, 2), (depth - 1, 2),
            )
        ]
        + [pltpu.VMEM((2, 2, 3 * extra_rows, lanes), F32)]
    )


def unpack_body(mem, piece_ref, qkv_ref, out_ref, in_ref, hid_ref, memory_ref, bias_ref, gain_ref, vec_scr):
    wide, half = qkv_ref.shape[1:]
    thin, lanes = out_ref.shape[1], in_ref.shape[2]
    width = memory_ref.shape[1]
    qkv_ref[0] = piece_ref[0, 0:wide, :].astype(F32)
    out_ref[0] = piece_ref[0, wide:half, :].astype(F32)
    in_ref[0] = piece_ref[1, 0:half, :].astype(F32)
    for part in range(4):
        hid_ref[0, :, part * half : (part + 1) * half] = piece_ref[
            2, part * thin : (part + 1) * thin, :
        ].astype(F32)
    extra = jnp.concatenate([piece_ref[kind, half:, :].astype(F32) for kind in range(3)], axis=0)
    pieces = width // lanes
    for piece in range(pieces):
        memory_ref[:, piece * lanes : (piece + 1) * lanes] = extra[piece * mem : (piece + 1) * mem, :]
    for at in range(6 * pieces):
        row = mem * pieces + at
        vec_scr[0:1, at * lanes : (at + 1) * lanes] = extra[row : row + 1, :]
    place = lax.axis_index("dp")
    long = 5 * width
    for ref, first, last in ((bias_ref, 0, long), (gain_ref, long, long + width)):
        size = ref.shape[1]
        turned = pltpu.roll(vec_scr[:, first:last], (last - first - place * size) % (last - first), 1)
        ref[...] = turned[0:1, 0:size]


def grad_reduce(dp, mem, saved, sums, memory):
    sources = [saved[name] for name in GRAD_NAMES]
    steps, rows, width = sources[0].shape
    segs_all = steps // 2
    half = width // 2
    lanes = 4 * width // dp
    thin = width // dp
    depth = dp // 2
    any_spec = pl.BlockSpec(memory_space=pl.ANY)
    dma = pltpu.SemaphoreType.DMA
    shapes = grad_reduce_shapes(dp, steps, rows, width)
    piece = pl.pallas_call(
        functools.partial(grad_reduce_body, dp, mem, segs_all),
        in_specs=[any_spec] * 8 + [pl.BlockSpec(memory_space=pltpu.VMEM)] * 2,
        out_specs=pl.BlockSpec(memory_space=pltpu.VMEM),
        out_shape=jax.ShapeDtypeStruct((3,) + shapes[8].shape[-2:], BF16),
        scratch_shapes=shapes
        + [
            dma((8, segs_all)), dma((2, 6, 2)), pltpu.SemaphoreType.REGULAR, dma((2, 2, 2)), dma((2, 2, 2)),
            dma((2, 2, 2)), dma((2, 2, 2)), dma((2, 2, 2)), dma((2, 4)), dma((2, 3, 2, depth)),
            dma((2, 3, 2, depth)), dma((2, depth)), dma((2, depth)),
        ],
        compiler_params=pltpu.CompilerParams(
            vmem_limit_bytes=VMEM_BYTES, collective_id=0, has_side_effects=True
        ),
        name="grad_reduce",
    )(*sources, sums, memory)
    qkv, out, w_in, hid, memory, bias, gain = pl.pallas_call(
        functools.partial(unpack_body, mem),
        out_shape=[
            jax.ShapeDtypeStruct(shape, F32)
            for shape in (
                (1, 3 * thin, half), (1, thin, half), (1, half, lanes), (1, thin, 4 * half),
                (mem, width), (1, 5 * thin), (1, thin),
            )
        ],
        scratch_shapes=[pltpu.VMEM((8, 6 * width), F32)],
        name="unpack",
    )(piece)
    grads = (jnp.swapaxes(qkv, 1, 2), jnp.swapaxes(out, 1, 2), w_in, jnp.swapaxes(hid, 1, 2))
    return (memory, *grads, bias, gain)


def other_core(block, dp):
    return lax.ppermute(block, "dp", [(at, at ^ 1) for at in range(dp)])


def per_device(
    text_rows,
    memory_init,
    cotangent,
    w_qkv,
    w_out,
    w_in,
    w_hid,
    biases,
    norm_gains,
    boundaries,
    mem_resets,
    seg_counts,
):
    items, segs, text_len, width = text_rows.shape
    mem_rows = memory_init.shape[0]
    rows = text_len + 2 * mem_rows
    half = width // 2
    dp = lax.axis_size("dp")
    blocks = (w_qkv, w_out, w_in, w_hid)
    steps = 2 * items * segs
    text = jnp.swapaxes(text_rows, 1, 2)
    if dp == 8:
        saved, acts, masks, weights, vecs = gather_forward(
            text, mem_resets, seg_counts, memory_init, boundaries, blocks, biases, norm_gains
        )
    else:
        weights, vecs = gather_apart(blocks, biases, norm_gains)
        saved, acts, masks = forward_steps(
            text, mem_resets, seg_counts, memory_init, boundaries, weights, vecs
        )
    grads, sums, input_grads, memory_grad, acts = backward_steps(
        cotangent, mem_resets, seg_counts, masks, mem_rows, acts, weights, vecs, saved
    )
    saved.update(grads)
    reduce = grad_reduce if dp == 8 else grad_reduce_apart
    return (acts, input_grads, *reduce(dp, mem_rows, saved, sums, memory_grad))


def grad_reduce_apart(dp, mem_rows, saved, sums, memory_grad):
    steps, width = sums.shape[0], memory_grad.shape[1]
    half = width // 2
    vector_len = 5 * width
    lanes = 4 * width // dp
    memory_part = memory_grad[16 - mem_rows :].reshape(-1)
    memory_len = -(-memory_part.shape[0] // lanes) * lanes
    memory_part = jnp.pad(memory_part, (0, memory_len - memory_part.shape[0]))
    vector_part = vector_len // dp
    gain_part = width // dp
    used = memory_len + vector_part + gain_part
    extra_rows = -(-used // (3 * 16 * lanes)) * 16
    extras = []
    for layer in range(2):
        total = sums.reshape(steps // 2, 2, 12 * width)[:, layer].sum(axis=0)
        gain_two, shift_two, bias_hid, gain_one, shift_one, bias_o, bias_q, bias_v = [
            total[at * width : (at + 1) * width] for at in range(8)
        ]
        vector = jnp.concatenate(
            [bias_q, bias_v, bias_o, shift_one, total[8 * width :], bias_hid, shift_two]
        ).reshape(2, dp, vector_part)
        gain = jnp.stack([gain_one, gain_two]).reshape(2, dp, gain_part)
        extra = jnp.concatenate(
            [jnp.broadcast_to(memory_part, (2, dp, memory_len)), vector, gain], axis=-1
        )
        extra = jnp.pad(extra, ((0, 0), (0, 0), (0, 3 * extra_rows * lanes - used)))
        extra = extra.reshape(2, dp // 2, 2, 3, extra_rows, lanes).transpose(3, 2, 1, 0, 4, 5)
        extras.append(extra.astype(BF16))
    extras = jnp.stack(extras)
    wires = [weight_grads(layer, dp, saved, extras[layer]) for layer in range(2)]
    mine = jnp.stack([wires[0][0], wires[1][0]])
    theirs = other_core(jnp.stack([wires[0][1], wires[1][1]]), dp)
    both = mine.astype(F32) + theirs.astype(F32)
    both = both.transpose(3, 0, 2, 1, 4, 5).astype(BF16)
    tall, lanes = both.shape[-2:]
    both = both.reshape(4, dp // 2, 3, tall, lanes)
    own = lax.psum_scatter(both, "section", scatter_dimension=0, tiled=True)[0]
    groups = [[2 * at + side for at in range(dp // 2)] for side in range(2)]
    own = lax.psum_scatter(
        own, "dp", scatter_dimension=0, axis_index_groups=groups, tiled=True
    )[0].astype(F32)
    thin = lanes // 4
    body = own[:, :half]
    hid = body[2].reshape(half, 4, thin).transpose(1, 0, 2).reshape(4 * half, thin)
    flat = own[:, half:].reshape(-1)
    return (
        flat[: mem_rows * width].reshape(mem_rows, width),
        body[0, :, : 3 * thin][None],
        body[0, :, 3 * thin :][None],
        body[1][None],
        hid[None],
        flat[memory_len : memory_len + vector_part][None],
        flat[memory_len + vector_part : used][None],
    )


def solution(mesh):
    in_specs = (
        P(("section", "dp"), None, None, None),
        P(),
        P(("section", "dp"), None, None, None),
        P("section", None, None),
        P("section", None, None),
        P("section", None, None),
        P("section", None, None),
        P("section", None),
        P("section", None),
        P(("section", "dp"), None, None),
        P(("section", "dp"), None),
        P(("section", "dp")),
    )
    out_specs = (
        P(("section", "dp"), None, None, None),
        P(("section", "dp"), None, None, None),
        P(),
        P("section", None, "dp"),
        P("section", None, "dp"),
        P("section", None, "dp"),
        P("section", None, "dp"),
        P("section", "dp"),
        P("section", "dp"),
    )
    return jax.shard_map(
        per_device, mesh=mesh, in_specs=in_specs, out_specs=out_specs, check_vma=False
    )
```

```python
import functools

import jax
import jax.numpy as jnp
from jax import lax
from jax.experimental import pallas as pl
from jax.experimental.pallas import tpu as pltpu
from jax.sharding import PartitionSpec as P

HEADS = 12
HEAD_DIM = 64
EPS = 1e-05
MASKED = -1e30
VMEM_BYTES = 63 * 2**20
F32 = jnp.float32
BF16 = jnp.bfloat16
MESH = pl.DeviceIdType.MESH


def dot_nn(one, two):
    return jnp.dot(one, two, preferred_element_type=F32)


def dot_nt(one, two):
    return lax.dot_general(one, two, (((1,), (1,)), ((), ())), preferred_element_type=F32)


def dot_tn(one, two):
    return lax.dot_general(one, two, (((0,), (0,)), ((), ())), preferred_element_type=F32)


def weight_tile(refs, kind, tile, layer):
    qkv_ref, in_ref, end_ref = refs
    quarters, _, _, _, tall, width = end_ref.shape
    thin = tall // 5
    if kind == "out":
        pieces = [
            end_ref[quarter, core, half, layer, 0:thin]
            for half in range(2)
            for quarter in range(quarters)
            for core in range(2)
        ]
    elif kind == "hid":
        pieces = [
            end_ref[(tile % 2) * (quarters // 2) + at, core, tile // 2, layer, thin:tall]
            for at in range(quarters // 2)
            for core in range(2)
        ]
    else:
        ref = qkv_ref if kind == "qkv" else in_ref
        at = tile * width if isinstance(tile, int) else pl.multiple_of(tile * width, width)
        pieces = [ref[core, half, layer, :, pl.ds(at, width)] for half in range(2) for core in range(2)]
    return jnp.concatenate(pieces, axis=0)


def weight_specs(shapes, layer_of):
    specs = []
    for shape in shapes:
        lead = len(shape) - 3
        block = shape[:lead] + (1,) + shape[lead + 1 :]
        specs.append(
            pl.BlockSpec(block, lambda t, *_, lead=lead: (0,) * lead + (layer_of(t), 0, 0))
        )
    return specs


def head_lanes(shape, head):
    lanes = lax.broadcasted_iota(jnp.int32, shape, 1)
    return (lanes // HEAD_DIM) == head


def erf_parts(values):
    density = jnp.exp(-0.5 * values * values) * 0.3989422804014327
    phi = 0.5 * (1.0 + lax.erf(values * 0.7071067811865476))
    return phi, density


def vector_rows(vec_ref, layer, width):
    row = lambda half, at: vec_ref[half, layer, :, at * width : (at + 1) * width]
    return dict(
        bias_q=row(0, 0), bias_v=row(0, 1), bias_o=row(0, 2), shift_one=row(0, 3),
        bias_in=(row(0, 4), row(1, 0), row(1, 1), row(1, 2)),
        bias_hid=row(1, 3), shift_two=row(1, 4), gain_one=row(0, 5), gain_two=row(1, 5),
    )


def ones_where(shape, condition):
    rows = lax.broadcasted_iota(jnp.int32, shape, 0)
    columns = lax.broadcasted_iota(jnp.int32, shape, 1)
    return condition(rows, columns).astype(BF16)


def document_bias(bounds, rows, mem):
    text = bounds.shape[1]
    eight = jnp.broadcast_to(bounds, (8, text)).astype(BF16)
    upto = ones_where((text, rows), lambda r, c: r <= c - mem)
    below = ones_where((rows, text), lambda r, c: c <= r - mem)
    columns = dot_nn(eight, upto)[0:1]
    lines = dot_nt(below, eight)[:, 0:1]
    place = lax.broadcasted_iota(jnp.int32, (1, rows), 1)
    columns = jnp.where((place < mem) | (place >= mem + text), -1.0, columns)
    place = lax.broadcasted_iota(jnp.int32, (rows, 1), 0)
    lines = jnp.where((place < mem) | (place >= mem + text), -1.0, lines)
    allowed = (lines == columns) | (lines < 0) | (columns < 0)
    return jnp.where(allowed, 0.0, MASKED)


def norm_forward(values):
    offset = values - jnp.mean(values, axis=-1, keepdims=True)
    scale = lax.rsqrt(jnp.mean(offset * offset, axis=-1, keepdims=True) + EPS)
    return offset * scale, scale


def forward_layer(
    step, segs, at_layer, before_mix, before_out, store, resets_ref, counts_ref, text_ref, init_ref,
    bounds_ref, weights, vec_ref,
    x_ref, mixed_ref, heads_ref, hat_one_ref, first_ref, active_ref, slope_ref, hat_two_ref,
    stats_ref, acts_ref, bias_ref, y_scr, bias_scr, sum_scr, bias_in_scr, text_scr,
):
    rows, width = y_scr.shape
    text_len, mem = text_ref.shape[1], init_ref.shape[0]
    layer, seg, item = step % 2, (step // 2) % segs, step // (2 * segs)

    def prepare():
        flat = text_ref[0].reshape(text_len * segs, width)
        for number in range(segs):
            pick = ones_where((rows, text_len * segs), lambda r, c: (r - mem) * segs + number == c)
            text_scr[number] = dot_nn(pick, flat).astype(BF16)
            bias_scr[number] = document_bias(bounds_ref[0, number : number + 1, :], rows, mem)

    @pl.when((layer == 0) & (seg == 0) & (step > 0))
    def _():
        prepare()

    before_mix(prepare)

    @pl.when(layer == 0)
    def _():
        fresh = (seg == 0) | (resets_ref[item, seg] > 0)
        start = ones_where((rows, mem), lambda r, c: (r == c) | (r - mem - text_len == c))
        again = ones_where(
            (rows, rows),
            lambda r, c: ((r < mem) & (r + mem + text_len == c)) | ((r >= mem + text_len) & (r == c)),
        )
        memory = jnp.where(fresh, dot_nn(start, init_ref[...]), dot_nn(again, y_scr[...]))
        x_ref[0] = (text_scr[seg].astype(F32) + memory).astype(BF16)
        bias_ref[0, 0] = bias_scr[seg]

    @pl.when(layer == 1)
    def _():
        x_ref[0] = y_scr[...]

    store("x")
    vec = vector_rows(vec_ref, at_layer, width)
    for part in range(4):
        bias_in_scr[part] = vec["bias_in"][part]
    inputs = x_ref[0]
    for tile in range(3):
        mixed = dot_nn(inputs, weight_tile(weights, "qkv", tile, at_layer))
        if tile == 0:
            mixed = mixed + vec["bias_q"]
        if tile == 2:
            mixed = mixed + vec["bias_v"]
        mixed_ref[0, :, tile * width : (tile + 1) * width] = mixed.astype(BF16)

    store("mixed")
    group = 4 * HEAD_DIM
    stat_lane = lax.broadcasted_iota(jnp.int32, (rows, 128), 1)
    stats = jnp.zeros((rows, 128), F32)
    for number in range(width // group):
        at = number * group
        queries = mixed_ref[0, :, at : at + group] * BF16(HEAD_DIM**-0.5)
        keys = mixed_ref[0, :, width + at : width + at + group]
        values = mixed_ref[0, :, 2 * width + at : 2 * width + at + group]
        lanes = lax.broadcasted_iota(jnp.int32, (rows, group), 1) // HEAD_DIM
        stacked = jnp.concatenate([jnp.where(lanes == head, queries, 0) for head in range(4)], axis=0)
        scores = dot_nt(stacked, keys)
        probs = []
        for head in range(4):
            part = scores[head * rows : (head + 1) * rows] + bias_ref[0, 0]
            peak = jnp.max(part, axis=-1, keepdims=True)
            expo = jnp.exp(part - peak)
            norm = jnp.sum(expo, axis=-1, keepdims=True)
            probs.append((expo * (1.0 / norm)).astype(BF16))
            stats = jnp.where(stat_lane == number * 4 + head, peak + jnp.log(norm), stats)
        result = dot_nn(jnp.concatenate(probs, axis=0), values)
        total = result[0:rows]
        for head in range(1, 4):
            total = jnp.where(lanes == head, result[head * rows : (head + 1) * rows], total)
        heads_ref[0, :, at : at + group] = total.astype(BF16)
    store("heads")
    stats_ref[0] = stats

    before_out()
    attn = dot_nn(heads_ref[0], weight_tile(weights, "out", 0, at_layer)) + vec["bias_o"]
    hat, scale = norm_forward(x_ref[0].astype(F32) + attn)
    hat_one_ref[0] = hat.astype(BF16)
    stats = jnp.where(stat_lane == HEADS, scale, stats_ref[0])
    first = hat * vec["gain_one"] + vec["shift_one"]
    first_ref[0] = first.astype(BF16)
    store("hat_one")
    store("first")
    sum_scr[...] = first + vec["bias_hid"]

    def ff_tile(tile, _):
        at = tile * width
        inner = dot_nn(first_ref[0], weight_tile(weights, "in", tile, at_layer)) + bias_in_scr[tile]
        phi, density = erf_parts(inner)
        active = (inner * phi).astype(BF16)
        active_ref[0, :, pl.ds(at, width)] = active
        slope_ref[0, :, pl.ds(at, width)] = (phi + inner * density).astype(BF16)
        store("active", tile)
        store("slope", tile)
        sum_scr[...] += dot_nn(active, weight_tile(weights, "hid", tile, at_layer))
        return _

    for tile in range(4):
        ff_tile(tile, 0)
    hat, scale = norm_forward(sum_scr[...])
    hat_two_ref[0] = hat.astype(BF16)
    stats_ref[0] = jnp.where(stat_lane == HEADS + 1, scale, stats)
    store("hat_two")
    store("stats")
    result = (hat * vec["gain_two"] + vec["shift_two"]).astype(BF16)
    y_scr[...] = result

    @pl.when(layer == 1)
    def _():
        acts_ref[0, 0] = jnp.where(seg < counts_ref[item], result, 0)


def saved_shapes(rows, width):
    return dict(
        x=((rows, width), BF16),
        mixed=((rows, 3 * width), BF16),
        heads=((rows, width), BF16),
        hat_one=((rows, width), BF16),
        first=((rows, width), BF16),
        active=((rows, 4 * width), BF16),
        slope=((rows, 4 * width), BF16),
        hat_two=((rows, width), BF16),
        stats=((rows, 128), F32),
    )


def forward_io(text, resets, counts, init, bounds):
    items, text_len, segs, width = text.shape
    rows = text_len + 2 * init.shape[0]
    steps = 2 * items * segs
    saved = saved_shapes(rows, width)
    by_seg = lambda t: (t // (2 * segs), (t // 2) % segs, 0, 0)
    operands = [resets, counts, text, init, bounds]
    in_specs = [
        pl.BlockSpec(memory_space=pltpu.SMEM),
        pl.BlockSpec(memory_space=pltpu.SMEM),
        pl.BlockSpec((1, text_len, segs, width), lambda t: (t // (2 * segs), 0, 0, 0)),
        pl.BlockSpec(init.shape, lambda t: (0, 0)),
        pl.BlockSpec((1, segs, text_len), lambda t: (t // (2 * segs), 0, 0)),
    ]
    out_specs = [pl.BlockSpec((1,) + shape, lambda t: (t, 0, 0)) for shape, _ in saved.values()]
    out_specs.append(pl.BlockSpec((1, 1, rows, width), by_seg))
    out_specs.append(pl.BlockSpec((1, 1, rows, rows), by_seg))
    out_shape = [jax.ShapeDtypeStruct((steps,) + shape, kind) for shape, kind in saved.values()]
    out_shape.append(jax.ShapeDtypeStruct((items, segs, rows, width), BF16))
    out_shape.append(jax.ShapeDtypeStruct((items, segs, rows, rows), F32))
    scratch = [
        pltpu.VMEM((rows, width), BF16),
        pltpu.VMEM((segs, rows, rows), F32),
        pltpu.VMEM((rows, width), F32),
        pltpu.VMEM((4, 1, width), F32),
        pltpu.VMEM((segs, rows, width), BF16),
    ]
    return steps, saved, operands, in_specs, out_specs, out_shape, scratch


def forward_body(segs, *refs):
    step = pl.program_id(0)
    y_scr = refs[20]

    @pl.when(step == 0)
    def _():
        y_scr[...] = jnp.zeros_like(y_scr)

    def before_mix(prepare):
        pl.when(step == 0)(prepare)

    forward_layer(
        step, segs, 0, before_mix, lambda: None, lambda *_: None, *refs[:5], refs[5:8], *refs[8:]
    )


def forward_steps(text, resets, counts, init, bounds, weights, vec):
    steps, saved, operands, in_specs, out_specs, out_shape, scratch = forward_io(
        text, resets, counts, init, bounds
    )
    *outs, acts, bias = pl.pallas_call(
        functools.partial(forward_body, text.shape[2]),
        grid=(steps,),
        in_specs=in_specs
        + weight_specs([weight.shape for weight in weights], lambda t: t % 2)
        + [pl.BlockSpec((2, 1) + vec.shape[2:], lambda t: (0, t % 2, 0, 0))],
        out_specs=out_specs,
        out_shape=out_shape,
        scratch_shapes=scratch,
        compiler_params=pltpu.CompilerParams(vmem_limit_bytes=VMEM_BYTES),
        name="forward_steps",
    )(*operands, *weights, vec)
    return dict(zip(saved, outs)), acts, bias


def norm_backward(grad, hat, scale, gain):
    scaled = grad * gain
    mean_one = jnp.mean(scaled, axis=-1, keepdims=True)
    mean_two = jnp.mean(scaled * hat, axis=-1, keepdims=True)
    return (scaled - mean_one - hat * mean_two) * scale


def column_sum(values):
    return jnp.sum(values, axis=0, keepdims=True)


def backward_layer(
    layer, count, segs, mem, resets_ref, counts_ref, cot_ref, bias_ref, acts_ref, qkv_ref, in_ref, end_ref,
    vec_ref, mixed_ref, heads_ref, hat_one_ref, slope_ref, hat_two_ref, stats_ref,
    branch_ref, inner_ref, attn_ref, mix_ref, sums_ref, inputs_ref, init_ref, acts_out_ref,
    g_scr, carry_scr, sum_scr, go_scr,
):
    step = count - 1 - pl.program_id(0)
    seg = (step // 2) % segs
    rows, width = g_scr.shape
    item = step // (2 * segs)
    weights = (qkv_ref, in_ref, end_ref)
    vec = vector_rows(vec_ref, 0, width)
    gain_one, gain_two = vec["gain_one"], vec["gain_two"]

    if layer == 1:
        acts_out_ref[...] = acts_ref[...]
        cot = jnp.where(seg < counts_ref[item], cot_ref[0, 0], 0)
        g_scr[...] = cot
        carried = jnp.where(seg == segs - 1, 0.0, carry_scr[...])
        g_scr[rows - 16 : rows, :] = (cot[rows - 16 : rows].astype(F32) + carried).astype(BF16)

    stats = stats_ref[0]
    scale_one = stats[:, HEADS : HEADS + 1]
    scale_two = stats[:, HEADS + 1 : HEADS + 2]
    grad = g_scr[...].astype(F32)
    hat = hat_two_ref[0].astype(F32)
    sums_ref[0, :, 0:width] = column_sum(grad * hat)
    sums_ref[0, :, width : 2 * width] = column_sum(grad)
    grad_second = norm_backward(grad, hat, scale_two, gain_two)
    branch = grad_second.astype(BF16)
    branch_ref[0] = branch
    sums_ref[0, :, 2 * width : 3 * width] = column_sum(branch.astype(F32))
    sum_scr[...] = grad_second

    def ff_tile(tile, _):
        at = tile * width
        active = dot_nt(branch, weight_tile(weights, "hid", tile, 0))
        inner = (active * slope_ref[0, :, pl.ds(at, width)].astype(F32)).astype(BF16)
        inner_ref[0, :, pl.ds(at, width)] = inner
        sums_ref[0, :, pl.ds(8 * width + at, width)] = column_sum(inner.astype(F32))
        sum_scr[...] += dot_nt(inner, weight_tile(weights, "in", tile, 0))
        return _

    for tile in range(4):
        ff_tile(tile, 0)
    grad = sum_scr[...]
    hat = hat_one_ref[0].astype(F32)
    sums_ref[0, :, 3 * width : 4 * width] = column_sum(grad * hat)
    sums_ref[0, :, 4 * width : 5 * width] = column_sum(grad)
    resid = norm_backward(grad, hat, scale_one, gain_one)
    sum_scr[...] = resid
    attn = resid.astype(BF16)
    attn_ref[0] = attn
    sums_ref[0, :, 5 * width : 6 * width] = column_sum(attn.astype(F32))
    go = dot_nt(attn, weight_tile(weights, "out", 0, 0)).astype(BF16)
    go_scr[...] = go
    product = go.astype(F32) * heads_ref[0].astype(F32)
    high = product.astype(BF16)
    low = (product - high.astype(F32)).astype(BF16)
    picks = (
        lax.broadcasted_iota(jnp.int32, (16, width), 1) // HEAD_DIM
        == lax.broadcasted_iota(jnp.int32, (16, width), 0)
    ).astype(BF16)
    centres = dot_nt(picks, high) + dot_nt(picks, low)
    logs = jnp.transpose(stats)

    group = 4 * HEAD_DIM
    for number in range(width // group):
        at = number * group
        queries = mixed_ref[0, :, at : at + group] * BF16(HEAD_DIM**-0.5)
        keys = mixed_ref[0, :, width + at : width + at + group]
        values = mixed_ref[0, :, 2 * width + at : 2 * width + at + group]
        outs = go_scr[:, at : at + group]
        lanes = lax.broadcasted_iota(jnp.int32, (rows, group), 1) // HEAD_DIM

        def stack(block):
            return jnp.concatenate([jnp.where(lanes == head, block, 0) for head in range(4)], axis=0)

        def unstack(block):
            total = block[0:rows]
            for head in range(1, 4):
                total = jnp.where(lanes == head, block[head * rows : (head + 1) * rows], total)
            return total

        keys_s = stack(keys)
        scores = dot_nt(keys_s, queries)
        grad_p = dot_nt(stack(values), outs)
        probs, grads = [], []
        for head in range(4):
            row = number * 4 + head
            part = slice(head * rows, (head + 1) * rows)
            prob = jnp.exp(scores[part] + bias_ref[0, 0] - logs[row : row + 1, :])
            grads.append((prob * (grad_p[part] - centres[row : row + 1, :])).astype(BF16))
            probs.append(prob.astype(BF16))
        grads = jnp.concatenate(grads, axis=0)
        grad_v = unstack(dot_nn(jnp.concatenate(probs, axis=0), outs))
        grad_k = unstack(dot_nn(grads, queries))
        grad_q = dot_tn(grads, keys_s)
        mix_ref[0, :, at : at + group] = (grad_q * HEAD_DIM**-0.5).astype(BF16)
        mix_ref[0, :, width + at : width + at + group] = grad_k.astype(BF16)
        mix_ref[0, :, 2 * width + at : 2 * width + at + group] = grad_v.astype(BF16)

    sums_ref[0, :, 6 * width : 7 * width] = column_sum(mix_ref[0, :, 0:width].astype(F32))
    sums_ref[0, :, 7 * width : 8 * width] = column_sum(mix_ref[0, :, 2 * width : 3 * width].astype(F32))
    total = sum_scr[...]
    for tile in range(3):
        total = total + dot_nt(
            mix_ref[0, :, tile * width : (tile + 1) * width], weight_tile(weights, "qkv", tile, 0)
        )
    result = total.astype(BF16)
    g_scr[...] = result

    if layer == 0:
        inputs_ref[0, 0] = result
        fresh = (seg == 0) | (resets_ref[item, seg] > 0)
        number = lax.broadcasted_iota(jnp.int32, (16, width), 0)
        folded = result[rows - 16 : rows].astype(F32) + pltpu.roll(
            result[0:16].astype(F32), 16 - mem, 0
        )
        folded = jnp.where(number >= 16 - mem, folded, 0.0).astype(BF16).astype(F32)
        init_ref[...] += jnp.where(fresh, folded, 0.0)
        carry_scr[...] = jnp.where(fresh, 0.0, folded)


def backward_body(count, segs, mem, *refs):
    init_ref, carry_scr = refs[21], refs[24]

    @pl.when(pl.program_id(0) == 0)
    def _():
        carry_scr[...] = jnp.zeros_like(carry_scr)
        init_ref[...] = jnp.zeros_like(init_ref)

    for layer in range(2):
        pl.when((count - 1 - pl.program_id(0)) % 2 == layer)(
            functools.partial(backward_layer, layer, count, segs, mem, *refs)
        )


def backward_steps(cot, resets, counts, bias, mem, acts, weights, vec, saved):
    items, segs, rows, width = cot.shape
    steps = 2 * items * segs
    at = lambda t: steps - 1 - t
    by_seg = lambda t: (at(t) // (2 * segs), (at(t) // 2) % segs, 0, 0)
    by_step = lambda t: (at(t), 0, 0)
    names = ("mixed", "heads", "hat_one", "slope", "hat_two", "stats")
    outs = dict(
        branch=(rows, width), inner=(rows, 4 * width), attn=(rows, width), mix=(rows, 3 * width),
    )
    *grads, sums, inputs, memory, acts = pl.pallas_call(
        functools.partial(backward_body, steps, segs, mem),
        grid=(steps,),
        in_specs=[
            pl.BlockSpec(memory_space=pltpu.SMEM),
            pl.BlockSpec(memory_space=pltpu.SMEM),
            pl.BlockSpec((1, 1, rows, width), by_seg),
            pl.BlockSpec((1, 1, rows, rows), by_seg),
            pl.BlockSpec((1, 1, rows, width), by_seg),
        ]
        + weight_specs([weight.shape for weight in weights], lambda t: at(t) % 2)
        + [pl.BlockSpec((2, 1) + vec.shape[2:], lambda t: (0, at(t) % 2, 0, 0))]
        + [pl.BlockSpec((1,) + saved[name].shape[1:], by_step) for name in names],
        out_specs=[pl.BlockSpec((1,) + shape, by_step) for shape in outs.values()]
        + [
            pl.BlockSpec((1, 1, 12 * width), by_step),
            pl.BlockSpec((1, 1, rows, width), by_seg),
            pl.BlockSpec((16, width), lambda t: (0, 0)),
            pl.BlockSpec((1, 1, rows, width), by_seg),
        ],
        out_shape=[jax.ShapeDtypeStruct((steps,) + shape, BF16) for shape in outs.values()]
        + [
            jax.ShapeDtypeStruct((steps, 1, 12 * width), F32),
            jax.ShapeDtypeStruct(cot.shape, BF16),
            jax.ShapeDtypeStruct((16, width), F32),
            jax.ShapeDtypeStruct(cot.shape, BF16),
        ],
        scratch_shapes=[
            pltpu.VMEM((rows, width), BF16),
            pltpu.VMEM((16, width), F32),
            pltpu.VMEM((rows, width), F32),
            pltpu.VMEM((rows, width), BF16),
        ],
        compiler_params=pltpu.CompilerParams(vmem_limit_bytes=VMEM_BYTES),
        name="backward_steps",
    )(resets, counts, cot, bias, acts, *weights, vec, *[saved[name] for name in names])
    return dict(zip(outs, grads)), sums, inputs, memory, acts


(START, FORWARD_END, FORWARD_VEC, SPREAD, MOVE, FORWARD_PART, SHARE_PART, SHARE_DIAGONAL) = range(8)
GATHER_START = (
    (START, 0, 0, 0), (START, 1, 0, 1),
)
GATHER_FIRST = (
    (FORWARD_END, 0), (SPREAD, 0), (FORWARD_END, 1), (FORWARD_VEC,), (SPREAD, 1), (START, 0,
    0, 1), (START, 1, 0, 0), (SPREAD, 2), (FORWARD_PART, 0, 0), (FORWARD_PART, 1, 0), (START,
    0, 1, 0), (START, 1, 1, 1), (MOVE, 1, 0), (MOVE, 1, 1), (SHARE_PART, 0, 0), (SHARE_PART, 1,
    0), (START, 0, 1, 1), (START, 1, 1, 0), (MOVE, 1, 2), (SHARE_DIAGONAL, 0),
)
GATHER_THEN = (
    (MOVE, 2, 0), (MOVE, 2, 1), (FORWARD_PART, 0, 1), (FORWARD_PART, 1, 1), (MOVE, 2, 2),
    (SHARE_PART, 0, 1), (SHARE_PART, 1, 1), (MOVE, 3, 0), (MOVE, 3, 1), (SHARE_DIAGONAL, 1),
    (MOVE, 3, 2),
)


def gather_forward_body(steps, segs, *refs):
    io = refs[:5]
    qkv_src, in_src, out_src, hid_src, biases_ref, gains_ref = refs[5:11]
    outs = refs[11:22]
    full_outs = refs[22:26]
    forward_scratch = refs[26:31]
    weights = refs[31:34]
    vec = refs[34]
    slots = refs[35:44]
    (
        load_sems, end_load_sems, store_sems, x_sems, y_sems, fx_sems, fy_sems, core_sems, end_sems,
        line_core_sems, up_sems, down_sems, vec_sems, saved_sems,
    ) = refs[44:]
    step = pl.program_id(0)
    section, place = lax.axis_index("section"), lax.axis_index("dp")
    x, y = section % 2, section // 2
    core, z = place % 2, place // 2
    end = weights[2]
    depth, _, _, _, tall, _ = end.shape
    thin = tall // 5
    x_dev = (y * 2 + 1 - x, place)
    y_dev = ((1 - y) * 2 + x, place)
    core_dev = (section, z * 2 + 1 - core)
    up_dev = (section, (z + 1) % depth * 2 + core)
    down_dev = (section, (z + depth - 1) % depth * 2 + core)
    own_block = (y, x)
    blocks = ((y, 1 - x), (1 - y, x), (1 - y, 1 - x))

    def remote(source, target, sems, index, device):
        return pltpu.make_async_remote_copy(
            src_ref=source, dst_ref=target, send_sem=sems.at[(0, *index)], recv_sem=sems.at[(1, *index)],
            device_id=device, device_id_type=MESH,
        )


    def part_of(number, block, part):
        rows = weights[number].shape[-2] // 2
        return weights[number].at[core, block[0], block[1], pl.ds(part * rows, rows)]

    def own_part(number, part):
        rows = weights[number].shape[-2] // 2
        at = pl.multiple_of((core * 2 + part) * rows, rows)
        return (qkv_src, in_src)[number].at[0, pl.ds(at, rows)]

    def x_copy(number, part):
        return remote(own_part(number, part), part_of(number, own_block, part), x_sems, (number, part), x_dev)

    def y_copy(number, part):
        return remote(own_part(number, part), part_of(number, own_block, part), y_sems, (number, part), y_dev)

    def fy_copy(number):
        piece = part_of(number, blocks[0], 0)
        return remote(piece, piece, fy_sems, (number,), y_dev)

    def fx_copy(number):
        piece = part_of(number, blocks[1], 1)
        return remote(piece, piece, fx_sems, (number,), x_dev)

    def core_copy(number, kind, part):
        piece = part_of(number, blocks[kind], part)
        return remote(piece, piece, core_sems, (number, kind, part), core_dev)


    def eighth(at, block, first=0, rows=None):
        view = end.at[at, core, block[0], block[1]]
        return view if rows is None else view.at[pl.ds(first, rows)]

    def own_eighth(first):
        source, rows = (out_src, thin) if first == 0 else (hid_src, tall - thin)
        return source.at[0, pl.ds(pl.multiple_of((z * 2 + core) * rows, rows), rows)]

    def end_copy(axis, first):
        rows = thin if first == 0 else tall - thin
        return remote(
            own_eighth(first), eighth(z, own_block, first, rows), end_sems, (axis, 0 if first == 0 else 1),
            (x_dev, y_dev)[axis],
        )

    low = tall // 32 * 16

    def end_fy_copy():
        piece = eighth(z, blocks[0], 0, low)
        return remote(piece, piece, fy_sems, (2,), y_dev)

    def end_fx_copy():
        piece = eighth(z, blocks[1], low, tall - low)
        return remote(piece, piece, fx_sems, (2,), x_dev)

    def line_core_copy(at, kind):
        piece = eighth(at, blocks[kind])
        return remote(piece, piece, line_core_sems, (at, kind), core_dev)

    def up_copy(at, kind):
        piece = eighth(at, blocks[kind])
        return remote(piece, piece, up_sems, (at, kind), up_dev)

    def down_copy(at, kind):
        piece = eighth(at, blocks[kind])
        return remote(piece, piece, down_sems, (at, kind), down_dev)

    def vec_copy(kind):
        row = vec.at[(own_block, own_block, blocks[0])[kind]]
        return remote(row, row, vec_sems, (kind,), (x_dev, y_dev, y_dev)[kind])

    def loads():
        copies = []
        for number, source in enumerate((qkv_src, in_src)):
            rows = weights[number].shape[-2]
            for side in range(2):
                copies.append(
                    pltpu.make_async_copy(
                        source.at[0, pl.ds(side * rows, rows)], weights[number].at[side, y, x],
                        load_sems.at[number, side],
                    )
                )
        for at in range(depth):
            for side in range(2):
                for number, (source, first, rows) in enumerate(
                    ((out_src, 0, thin), (hid_src, thin, tall - thin))
                ):
                    copies.append(
                        pltpu.make_async_copy(
                            source.at[0, pl.ds((at * 2 + side) * rows, rows)],
                            end.at[at, side, y, x, pl.ds(first, rows)],
                            end_load_sems.at[at, side, number],
                        )
                    )
        return copies

    def full_stores():
        return [
            pltpu.make_async_copy(source, target, store_sems.at[number])
            for number, (source, target) in enumerate(zip((*weights, vec), full_outs))
        ]

    received = set()

    def arrived(*copies):
        for name, copy in copies:
            if name not in received:
                received.add(name)
                copy.wait_recv()

    def end_arrived(axis):
        arrived(*[((axis, first), end_copy(axis, first)) for first in (0, thin)])

    def start_end(axis):
        for first in (0, thin):
            end_copy(axis, first).start()

    def forward_end(axis):
        end_arrived(axis)
        (end_fy_copy, end_fx_copy)[axis]().start()

    def spread(kind):
        if kind < 2:
            end_arrived(kind)
        else:
            arrived(("fy", end_fy_copy()), ("fx", end_fx_copy()))

        @pl.when(z < depth - 1)
        def _():
            up_copy(z, kind).start()

        @pl.when(z > 0)
        def _():
            down_copy(z, kind).start()

        line_core_copy(z, kind).start()

    def hop(distance, kind):
        @pl.when(z >= distance)
        def _():
            up_copy(z - distance, kind).wait_recv()

            @pl.when(z < depth - 1)
            def _():
                up_copy(z - distance, kind).start()

            line_core_copy(z - distance, kind).start()

        @pl.when(z + distance < depth)
        def _():
            down_copy(z + distance, kind).wait_recv()

            @pl.when(z > 0)
            def _():
                down_copy(z + distance, kind).start()

            line_core_copy(z + distance, kind).start()

    def forward_part(axis, number):
        part = axis
        (x_copy, y_copy)[axis](number, part).wait_recv()
        (fy_copy, fx_copy)[axis](number).start()
        core_copy(number, axis, part).start()

    def share_part(axis, number):
        part = 1 - axis
        (x_copy, y_copy)[axis](number, part).wait_recv()
        core_copy(number, axis, part).start()

    def share_diagonal(number):
        fy_copy(number).wait_recv()
        core_copy(number, 2, 0).start()
        fx_copy(number).wait_recv()
        core_copy(number, 2, 1).start()

    def forward_vec():
        vec_copy(0).wait_recv()
        vec_copy(2).start()

    act = {
        START: lambda axis, number, part: (x_copy, y_copy)[axis](number, part).start(),
        FORWARD_END: forward_end,
        FORWARD_VEC: forward_vec,
        SPREAD: spread,
        MOVE: hop,
        FORWARD_PART: forward_part,
        SHARE_PART: share_part,
        SHARE_DIAGONAL: share_diagonal,
    }

    def complete(number):
        for kind in range(3):
            for part in range(2):
                core_copy(number, kind, part).wait_recv()

    def before_mix(prepare):
        @pl.when(step == 0)
        def _():
            barrier = pltpu.get_barrier_semaphore()
            for device in (x_dev, y_dev, core_dev):
                pl.semaphore_signal(barrier, inc=1, device_id=device, device_id_type=MESH)

            @pl.when(z < depth - 1)
            def _():
                pl.semaphore_signal(barrier, inc=1, device_id=up_dev, device_id_type=MESH)

            @pl.when(z > 0)
            def _():
                pl.semaphore_signal(barrier, inc=1, device_id=down_dev, device_id_type=MESH)

            pl.semaphore_wait(barrier, 3 + jnp.where(z > 0, 1, 0) + jnp.where(z < depth - 1, 1, 0))
            start_end(0)
            start_end(1)
            vec[y, x] = jnp.concatenate([biases_ref[...].astype(F32), gains_ref[...].astype(F32)], axis=1)
            vec_copy(0).start()
            vec_copy(1).start()
            for name, *numbers in GATHER_START:
                act[name](*numbers)
            for copy in loads():
                copy.start()
            forward_scratch[0][...] = jnp.zeros_like(forward_scratch[0])
            prepare()
            for name, *numbers in GATHER_FIRST:
                act[name](*numbers)
            vec_copy(1).wait_recv()
            vec_copy(2).wait_recv()
            complete(0)
            for copy in loads():
                copy.wait()

        @pl.when(step == 1)
        def _():
            for copy in full_stores():
                copy.start()

    def before_out():
        @pl.when(step == 0)
        def _():
            for name, *numbers in GATHER_THEN:
                act[name](*numbers)
            complete(1)
            for at in range(depth):
                for kind in range(3):
                    line_core_copy(at, kind).wait_recv()

    names = tuple(saved_shapes(*forward_scratch[0].shape))

    def saved_copies(which, name, tile=None):
        number = names.index(name)
        source, target = slots[number].at[which % 2], outs[number].at[which]
        if name not in ("active", "slope"):
            return [pltpu.make_async_copy(source, target, saved_sems.at[which % 2, number, 0])]
        size = source.shape[1] // 4
        return [
            pltpu.make_async_copy(
                source.at[:, pl.ds(at * size, size)], target.at[:, pl.ds(at * size, size)],
                saved_sems.at[which % 2, number, at],
            )
            for at in range(4)
            if tile is None or at == tile
        ]

    def store(name, tile=None):
        for copy in saved_copies(step, name, tile):
            copy.start()

    def stored(which):
        for name in names:
            for copy in saved_copies(which, name):
                copy.wait()

    @pl.when(step >= 2)
    def _():
        stored(step - 2)

    views = [slot.at[pl.ds(step % 2, 1)] for slot in slots]
    forward_layer(
        step, segs, step % 2, before_mix, before_out, store, *io, weights, vec, *views, *outs[9:],
        *forward_scratch,
    )

    @pl.when(step == steps - 1)
    def _():
        stored(steps - 2)
        stored(steps - 1)
        for copy in full_stores():
            copy.wait()
        for number in range(2):
            for part in range(2):
                x_copy(number, part).wait_send()
                y_copy(number, part).wait_send()
                for kind in range(3):
                    core_copy(number, kind, part).wait_send()
            fx_copy(number).wait_send()
            fy_copy(number).wait_send()
            for first in (0, thin):
                end_copy(number, first).wait_send()
        end_fx_copy().wait_send()
        end_fy_copy().wait_send()
        for kind in range(3):
            vec_copy(kind).wait_send()
            for at in range(depth):
                line_core_copy(at, kind).wait_send()

                @pl.when((z >= at) & (z < depth - 1))
                def _():
                    up_copy(at, kind).wait_send()

                @pl.when((z <= at) & (z > 0))
                def _():
                    down_copy(at, kind).wait_send()


def full_weight_shapes(w_qkv, w_out, w_in, w_hid):
    half, width = w_out.shape[1:]
    return [(2, 2, 2, half // 2, block.shape[2]) for block in (w_qkv, w_in)] + [
        (4, 2, 2, 2, (half + w_hid.shape[1]) // 8, width)
    ]


def gather_forward(text, resets, counts, init, bounds, blocks, biases, gains):
    steps, saved, operands, in_specs, out_specs, out_shape, scratch = forward_io(
        text, resets, counts, init, bounds
    )
    shapes = full_weight_shapes(*blocks)
    full = [pltpu.VMEM(shape, BF16) for shape in shapes] + [pltpu.VMEM((2, 2, 1, biases.shape[1] + gains.shape[1]), F32)]
    any_spec = pl.BlockSpec(memory_space=pl.ANY)
    dma = pltpu.SemaphoreType.DMA
    depth = shapes[2][0]
    *outs, acts, bias, qkv, w_in, end, vecs = pl.pallas_call(
        functools.partial(gather_forward_body, steps, text.shape[2]),
        grid=(steps,),
        in_specs=in_specs + [any_spec] * 4 + [pl.BlockSpec(vector.shape, lambda t: (0, 0)) for vector in (biases, gains)],
        out_specs=[any_spec] * len(saved) + out_specs[len(saved) :] + [any_spec] * 4,
        out_shape=out_shape + [jax.ShapeDtypeStruct(ref.shape, ref.dtype) for ref in full],
        scratch_shapes=scratch
        + full
        + [pltpu.VMEM((2,) + shape, kind) for shape, kind in saved.values()]
        + [
            dma((2, 2)), dma((depth, 2, 2)), dma((4,)), dma((2, 2, 2)), dma((2, 2, 2)), dma((2, 3)),
            dma((2, 3)), dma((2, 2, 3, 2)), dma((2, 2, 2)), dma((2, depth, 3)), dma((2, depth, 3)),
            dma((2, depth, 3)), dma((2, 3)), dma((2, len(saved), 4)),
        ],
        compiler_params=pltpu.CompilerParams(
            vmem_limit_bytes=VMEM_BYTES, collective_id=1, has_side_effects=True
        ),
        name="gather_forward",
    )(*operands, blocks[0], blocks[2], blocks[1], blocks[3], biases, gains)
    return dict(zip(saved, outs)), acts, bias, (qkv, w_in, end), vecs


def gather_apart(blocks, biases, gains):
    vec = jnp.concatenate([biases, gains], axis=1).astype(F32)
    w_qkv, w_out, w_in, w_hid = [
        lax.all_gather(block[0], "section").reshape(2, 2, *block.shape[1:]) for block in blocks
    ]
    half, width = w_out.shape[2:]
    full = [
        block.reshape(2, 2, 2, half // 2, -1).transpose(2, 0, 1, 3, 4) for block in (w_qkv, w_in)
    ]
    ends = [block.reshape(2, 2, 4, 2, -1, width).transpose(2, 3, 0, 1, 4, 5) for block in (w_out, w_hid)]
    vecs = lax.all_gather(vec, "section").reshape(2, 2, *vec.shape)
    return (*full, jnp.concatenate(ends, axis=4)), vecs


GRAD_NAMES = ("first", "inner", "active", "branch", "x", "mix", "heads", "attn")


def weight_grad_body(
    layer, segs_all, dp, *refs,
):
    sources = refs[:8]
    extra_ref, mine_ref, theirs_ref = refs[8:11]
    held = refs[11:19]
    wire, in_sems, extra_sem, out_sems = refs[19:23]
    core = lax.axis_index("dp") % 2
    rows = sources[0].shape[1]
    width = sources[0].shape[2]
    half = width // 2
    lanes = wire.shape[-1]
    thin = width // dp
    wide = 3 * thin

    def loads(number):
        return [
            pltpu.make_async_copy(
                sources[number].at[2 * at + layer],
                held[number].at[pl.ds(at * rows, rows)],
                in_sems.at[number, at],
            )
            for at in range(segs_all)
        ]

    for number in range(8):
        for copy in loads(number):
            copy.start()
    extra = pltpu.make_async_copy(extra_ref, wire.at[:, :, :, :, pl.ds(half, extra_ref.shape[4])], extra_sem)
    extra.start()

    def ready(*numbers):
        for number in numbers:
            for copy in loads(number):
                copy.wait()

    def stores(kind):
        return [
            pltpu.make_async_copy(wire.at[kind, core], mine_ref.at[kind], out_sems.at[kind, 0]),
            pltpu.make_async_copy(wire.at[kind, 1 - core], theirs_ref.at[kind], out_sems.at[kind, 1]),
        ]

    first, inner, active, branch, inputs, mix, heads, attn = held
    extra.wait()

    ready(0, 1)
    per_tile = width // lanes

    def in_tile(tile, _):
        right = inner[:, pl.ds(pl.multiple_of(tile * width, width), width)]
        for side in range(2):
            result = dot_tn(first[:, side * half : (side + 1) * half], right).astype(BF16)
            for at in range(per_tile):
                wire[1, at % 2, tile * (per_tile // 2) + at // 2, side, 0:half, :] = result[
                    :, at * lanes : (at + 1) * lanes
                ]
        return _

    lax.fori_loop(0, 4, in_tile, 0)
    for copy in stores(1):
        copy.start()

    ready(2, 3)
    def hid_tile(side, _):
        for part in range(4):
            left = active[:, pl.ds(pl.multiple_of(side * 4 * half + part * half, half), half)]
            result = dot_tn(left, branch[...]).astype(BF16)
            for at in range(dp):
                wire[2, at % 2, at // 2, side, 0:half, part * thin : (part + 1) * thin] = result[
                    :, at * thin : (at + 1) * thin
                ]
        return _
    lax.fori_loop(0, 2, hid_tile, 0)
    for copy in stores(2):
        copy.start()

    ready(4, 5, 6, 7)
    for side in range(2):
        left = inputs[:, side * half : (side + 1) * half]
        for tile in range(2):
            result = dot_tn(left, mix[:, tile * 3 * half : (tile + 1) * 3 * half]).astype(BF16)
            for at in range(dp // 2):
                place = tile * (dp // 2) + at
                wire[0, place % 2, place // 2, side, 0:half, 0:wide] = result[
                    :, at * wide : (at + 1) * wide
                ]
        result = dot_tn(heads[:, side * half : (side + 1) * half], attn[...]).astype(BF16)
        for at in range(dp):
            wire[0, at % 2, at // 2, side, 0:half, wide:lanes] = result[:, at * thin : (at + 1) * thin]
    for copy in stores(0):
        copy.start()
    for kind in range(3):
        for copy in stores(kind):
            copy.wait()


def weight_grads(layer, dp, saved, extras):
    sources = [saved[name] for name in GRAD_NAMES]
    steps, rows, width = sources[0].shape
    segs_all = steps // 2
    half = width // 2
    lanes = 4 * width // dp
    extra_rows = extras.shape[4]
    kind = jax.ShapeDtypeStruct((3, dp // 2, 2, half + extra_rows, lanes), BF16)
    any_spec = pl.BlockSpec(memory_space=pl.ANY)
    return pl.pallas_call(
        functools.partial(weight_grad_body, layer, segs_all, dp),
        in_specs=[any_spec] * 9,
        out_specs=[any_spec] * 2,
        out_shape=[kind, kind],
        scratch_shapes=[pltpu.VMEM((segs_all * rows, source.shape[2]), BF16) for source in sources]
        + [
            pltpu.VMEM((3, 2, dp // 2, 2, half + extra_rows, lanes), BF16),
            pltpu.SemaphoreType.DMA((8, segs_all)),
            pltpu.SemaphoreType.DMA,
            pltpu.SemaphoreType.DMA((3, 2)),
        ],
        compiler_params=pltpu.CompilerParams(vmem_limit_bytes=VMEM_BYTES),
        name="weight_grads",
    )(*sources, extras)


def add_into(ref, other):
    ref[...] = (ref[...].astype(F32) + other[...].astype(F32)).astype(BF16)


def build_extra(mem, sums_ref, memory_ref, extra):
    steps = sums_ref.shape[0]
    width = memory_ref.shape[1]
    lanes = extra.shape[-1]
    extra[...] = jnp.zeros_like(extra)
    for layer in range(2):
        total = sums_ref[layer]
        for step in range(layer + 2, steps, 2):
            total = total + sums_ref[step]
        for block, parts in enumerate(((6, 7, 5, 4, 8, 3), (9, 10, 11, 2, 1, 0))):
            for piece in range(width // lanes):
                extra[layer, block, piece * mem : (piece + 1) * mem, :] = memory_ref[
                    16 - mem : 16, piece * lanes : (piece + 1) * lanes
                ]
                for at, part in enumerate(parts):
                    row = mem * (width // lanes) + at * (width // lanes) + piece
                    first = part * width + piece * lanes
                    extra[layer, block, row : row + 1, :] = total[:, first : first + lanes]


KIND_IN, KIND_HID, KIND_MIX = 1, 2, 0
CUTS = {KIND_HID: 2, KIND_MIX: 3}
(MUL, CORE, SEND_P, SEND_QO, SEND_QW, PASS_Q, PASS_P, PLANE, HOP, FIN, SEND_O, PASS_O, SEND_WALL) = range(13)
FIRST_LINE, LINE = range(2)
PLAN = (
    (MUL, 0, 2, 0), (MUL, 0, 2, 1), (CORE, 0, 2, 0), (SEND_P, 2, 0), (SEND_QO, 2, 0), (MUL, 0, 1, 0),
    (MUL, 0, 1, 1), (CORE, 0, 2, 1), (SEND_QO, 2, 1), (MUL, 1, 2, 0), (MUL, 0, 1, 2), (MUL, 0, 1, 3),
    (CORE, 0, 1, 0), (SEND_P, 2, 1), (CORE, 0, 1, 1), (HOP, FIRST_LINE, 1, 0, 0), (CORE, 1, 2, 0),
    (SEND_QW, 2, 0), (PASS_P, 2, 0), (PASS_Q, 2, 0), (MUL, 1, 2, 1), (CORE, 0, 1, 2), (CORE, 0, 1, 3),
    (MUL, 1, 1, 0), (HOP, FIRST_LINE, 1, 0, 1), (CORE, 1, 2, 1), (SEND_QW, 2, 1), (MUL, 0, 0, 0),
    (PASS_P, 2, 1), (PASS_Q, 2, 1), (MUL, 1, 1, 1), (MUL, 1, 1, 2), (MUL, 1, 1, 3), (PLANE, 2, 0), (HOP,
    LINE, 2, 0, 0), (CORE, 0, 0, 0), (SEND_P, 0, 1), (SEND_QO, 0, 1), (SEND_P, 0, 0), (SEND_QO, 0, 0),
    (PLANE, 2, 1), (HOP, LINE, 2, 1, 0), (HOP, LINE, 2, 1, 1), (HOP, FIRST_LINE, 1, 0, 2), (CORE, 1, 1,
    0), (CORE, 1, 1, 1), (CORE, 1, 1, 2), (CORE, 1, 1, 3), (SEND_WALL, 1, 1), (SEND_WALL, 1, 0), (MUL,
    1, 0, 0), (CORE, 1, 0, 0), (PASS_P, 0, 1), (SEND_QW, 0, 0), (PLANE, 1, 1), (SEND_QW, 0, 1), (HOP,
    LINE, 2, 1, 2), (PASS_Q, 0, 1), (HOP, LINE, 1, 1, 0), (HOP, LINE, 1, 1, 1), (HOP, LINE, 1, 1, 2),
    (HOP, LINE, 2, 0, 1), (HOP, LINE, 2, 0, 2), (FIN, LINE, 2, 1), (FIN, FIRST_LINE, 1, 0), (SEND_O, 1),
    (PLANE, 1, 0), (HOP, LINE, 1, 0, 0), (HOP, LINE, 1, 0, 1), (HOP, LINE, 1, 0, 2), (PASS_Q, 0, 0),
    (PASS_P, 0, 0), (PLANE, 0, 1), (HOP, LINE, 0, 1, 0), (HOP, LINE, 0, 1, 1), (HOP, LINE, 0, 1, 2),
    (PASS_O, 1), (PLANE, 0, 0), (HOP, LINE, 0, 0, 0), (HOP, LINE, 0, 0, 1), (HOP, LINE, 0, 0, 2), (FIN,
    LINE, 0, 1), (FIN, LINE, 1, 0), (FIN, LINE, 1, 1), (FIN, LINE, 2, 0), (FIN, LINE, 0, 0),
)


def row_parts(tall, thin):
    first = -(-tall // 32) * 16
    some = ((0, first), (first, tall - first))
    return {KIND_IN: some, KIND_MIX: some, KIND_HID: ((0, 2 * thin), (2 * thin, tall - 2 * thin))}


def grad_reduce_body(dp, mem, segs_all, *refs):
    sources = refs[:8]
    sums_ref, memory_ref = refs[8:10]
    piece_out = refs[10]
    held = refs[11:19]
    mine, theirs, landed, xp, xq, yqo, yqw, yp, ywall, xo, yo, z_low, z_high, zo_low, zo_high = refs[19:34]
    extra = refs[34]
    (
        in_sems, core_sems, free_sem, xp_sems, xq_sems, yqo_sems, yqw_sems, yp_sems, single_sems, up_sems,
        down_sems, zo_up_sems, zo_down_sems,
    ) = refs[35:]
    section, place = lax.axis_index("section"), lax.axis_index("dp")
    x, y = section % 2, section // 2
    core, z = place % 2, place // 2
    depth = dp // 2
    rows, width = sources[0].shape[1:]
    half = width // 2
    tall, lanes = mine.shape[-2:]
    thin = width // dp
    wide = 3 * thin
    parts = row_parts(tall, thin)
    x_dev = (y * 2 + 1 - x, place)
    y_dev = ((1 - y) * 2 + x, place)
    core_dev = (section, z * 2 + 1 - core)
    up_dev = (section, (z + 1) % depth * 2 + core)
    down_dev = (section, (z + depth - 1) % depth * 2 + core)
    used = {KIND_IN: (0, 1), KIND_HID: (2, 3), KIND_MIX: (4, 5, 6, 7)}
    slots = {KIND_HID: 0, KIND_MIX: 1}
    first, inner, active, branch, inputs, mix, heads, attn = held
    units = [step[1:3] for step in PLAN if step[0] == MUL and step[3] == 0]

    def loads(side, kind):
        layer = (1 - x) if side == 0 else x
        return [
            pltpu.make_async_copy(
                sources[number].at[2 * at + layer],
                held[number].at[pl.ds(at * rows, rows)],
                in_sems.at[number, at],
            )
            for number in used[kind]
            for at in range(segs_all)
        ]

    for side, kind in units:
        if side == 0:
            for copy in loads(0, kind):
                copy.start()
    barrier = pltpu.get_barrier_semaphore()
    for device in (x_dev, y_dev, core_dev):
        pl.semaphore_signal(barrier, inc=1, device_id=device, device_id_type=MESH)

    @pl.when(z < depth - 1)
    def _():
        pl.semaphore_signal(barrier, inc=1, device_id=up_dev, device_id_type=MESH)

    @pl.when(z > 0)
    def _():
        pl.semaphore_signal(barrier, inc=1, device_id=down_dev, device_id_type=MESH)

    build_extra(mem, sums_ref, memory_ref, extra)

    def remote(source, target, sems, index, device):
        return pltpu.make_async_remote_copy(
            src_ref=source, dst_ref=target, send_sem=sems.at[(0, *index)], recv_sem=sems.at[(1, *index)],
            device_id=device, device_id_type=MESH,
        )

    z_order = [at // 2 if at % 2 else depth - 1 - at // 2 for at in range(depth)]

    def core_parts(kind):
        return range({KIND_HID: 2, KIND_IN: depth, KIND_MIX: 1}[kind])

    def core_view(ref, kind, part):
        if kind == KIND_IN:
            return ref.at[pl.ds(z_order[part], 1)]
        return ref.at[:, :, pl.ds(*parts[kind][part])] if kind == KIND_HID else ref

    def core_copy(unit, part):
        kind = units[unit][1]
        return remote(
            core_view(theirs.at[unit % 2], kind, part), core_view(landed.at[unit % 2], kind, part), core_sems,
            (unit, part), core_dev,
        )

    def p_copy(kind, part):
        at = pl.ds(0, CUTS[kind])
        some = pl.ds(*parts[kind][part])
        return remote(
            mine.at[0, kind, at, :, some], xp.at[slots[kind], at, :, some], xp_sems, (slots[kind], part), x_dev
        )

    def q_copy(side, kind, part):
        some = pl.ds(*parts[kind][part])
        count = depth - CUTS[kind]
        return remote(
            mine.at[side, kind, pl.ds(CUTS[kind], count), 1 - y, some],
            (yqo, yqw)[side].at[slots[kind], pl.ds(0, count), some],
            (yqo_sems, yqw_sems)[side], (slots[kind], part), y_dev,
        )

    def xq_copy(kind, part):
        some = pl.ds(*parts[kind][part])
        count = depth - CUTS[kind]
        return remote(
            mine.at[0, kind, pl.ds(CUTS[kind], count), y, some],
            xq.at[slots[kind], pl.ds(0, count), some], xq_sems, (slots[kind], part), x_dev,
        )

    def yp_copy(kind, part):
        some = pl.ds(*parts[kind][part])
        at = pl.ds(0, CUTS[kind])
        return remote(
            mine.at[1, kind, at, 1 - y, some], yp.at[slots[kind], at, some], yp_sems, (slots[kind], part), y_dev
        )

    def xo_copy():
        return remote(mine.at[0, KIND_IN, z], xo, single_sems, (0,), x_dev)

    def yo_copy():
        return remote(xo.at[1 - y], yo, single_sems, (1,), y_dev)

    def ywall_copy(part):
        some = pl.ds(*parts[KIND_IN][part])
        return remote(
            mine.at[1, KIND_IN, :, 1 - y, some], ywall.at[:, some], single_sems, (2 + part,), y_dev
        )

    def line_rows(kind, part):
        return pl.ds(*parts[kind][part])

    def up_copy(name, kind, part, at):
        if name == FIRST_LINE:
            return remote(mine.at[0, kind, at], zo_low.at[at - 1], zo_up_sems, (at,), up_dev)
        some = line_rows(kind, part)
        return remote(
            mine.at[1, kind, at, y, some], z_low.at[kind, at - 1, some], up_sems, (kind, part, at), up_dev
        )

    def down_copy(name, kind, part, at):
        if name == FIRST_LINE:
            return remote(mine.at[0, kind, at], zo_high.at[at], zo_down_sems, (at,), down_dev)
        some = line_rows(kind, part)
        return remote(
            mine.at[1, kind, at, y, some], z_high.at[kind, at, some], down_sems, (kind, part, at), down_dev
        )

    def from_low(name, kind, part, at):
        up_copy(name, kind, part, at).wait_recv()
        if name == FIRST_LINE:
            for block in range(2):
                add_into(mine.at[0, kind, at, block], zo_low.at[at - 1, block])
        else:
            some = line_rows(kind, part)
            add_into(mine.at[1, kind, at, y, some], z_low.at[kind, at - 1, some])

    def from_high(name, kind, part, at):
        down_copy(name, kind, part, at).wait_recv()
        if name == FIRST_LINE:
            for block in range(2):
                add_into(mine.at[0, kind, at, block], zo_high.at[at, block])
        else:
            some = line_rows(kind, part)
            add_into(mine.at[1, kind, at, y, some], z_high.at[kind, at, some])

    def multiply(side, kind, part):
        unit = units.index((side, kind))
        slot = unit % 2

        def put(chunk_core, chunk_z, block, piece, start, stop):
            @pl.when(core == chunk_core)
            def _():
                mine[side, kind, chunk_z, block, start:stop, :] = piece

            @pl.when(core != chunk_core)
            def _():
                theirs[slot, chunk_z, block, start:stop, :] = piece

        if part == 0:
            for copy in loads(side, kind):
                copy.wait()
            if unit >= 2:
                for earlier in core_parts(units[unit - 2][1]):
                    core_copy(unit - 2, earlier).wait_send()
            layer = (1 - x) if side == 0 else x
            extra_rows = tall - half
            for block in range(2):
                added = extra[layer, block, kind * extra_rows : (kind + 1) * extra_rows, :].astype(BF16)
                for at in range(depth):
                    mine[side, kind, at, block, half:, :] = added
                    theirs[slot, at, block, half:, :] = added
        if kind == KIND_IN:
            tile = z_order[part]

            def in_tile(block, _):
                left = first[:, pl.ds(pl.multiple_of(block * half, half), half)]
                result = dot_tn(left, inner[:, tile * width : (tile + 1) * width]).astype(BF16)
                for at in range(2):
                    put(at, tile, block, result[:, at * lanes : (at + 1) * lanes], 0, half)
                return _

            lax.fori_loop(0, 2, in_tile, 0)
        elif kind == KIND_HID:

            def hid_tile(block, _):
                right = active[:, pl.ds(pl.multiple_of((block * 2 + part) * width, width), width)]
                for side_rows in range(2):
                    result = dot_tn(
                        branch[:, side_rows * half : (side_rows + 1) * half], right
                    ).astype(BF16)
                    for at in range(dp // 2):
                        chunk = side_rows * (dp // 2) + at
                        for piece in range(2):
                            row = (part * 2 + piece) * thin
                            put(
                                chunk % 2, chunk // 2, block,
                                result[at * thin : (at + 1) * thin, piece * half : (piece + 1) * half],
                                row, row + thin,
                            )
                return _

            lax.fori_loop(0, 2, hid_tile, 0)
        else:

            def mix_tile(block, _):
                columns = pl.ds(pl.multiple_of(block * half, half), half)
                for tile in range(2):
                    result = dot_tn(
                        mix[:, tile * 3 * half : (tile + 1) * 3 * half], inputs[:, columns]
                    ).astype(BF16)
                    for at in range(depth):
                        chunk = tile * depth + at
                        put(chunk % 2, chunk // 2, block, result[at * wide : (at + 1) * wide], 0, wide)
                result = dot_tn(attn[...], heads[:, columns]).astype(BF16)
                for chunk in range(dp):
                    put(chunk % 2, chunk // 2, block, result[chunk * thin : (chunk + 1) * thin], wide, half)
                return _

            lax.fori_loop(0, 2, mix_tile, 0)
        if unit == 0 and part == 0:
            pl.semaphore_wait(barrier, 3 + jnp.where(z > 0, 1, 0) + jnp.where(z < depth - 1, 1, 0))
        if unit >= 2 and part == 0:
            pl.semaphore_wait(free_sem, 1)
        core_copy(unit, part).start()
        if side == 0 and part == core_parts(kind)[-1]:
            for copy in loads(1, kind):
                copy.start()

    def add_core(side, kind, part):
        unit = units.index((side, kind))
        core_copy(unit, part).wait_recv()
        some = pl.ds(*parts[kind][part]) if kind == KIND_HID else pl.ds(0, tall)

        def add(at, _):
            for block in range(2):
                add_into(mine.at[side, kind, at, block, some], landed.at[unit % 2, at, block, some])
            return _

        if kind == KIND_IN:
            add(z_order[part], 0)
        else:
            lax.fori_loop(0, depth, add, 0)
        if unit + 2 < len(units) and part == core_parts(kind)[-1]:
            pl.semaphore_signal(free_sem, inc=1, device_id=core_dev, device_id_type=MESH)

    def forward_q(kind, part):
        q_copy(0, kind, part).wait_recv()
        some = pl.ds(*parts[kind][part])
        for at in range(depth - CUTS[kind]):
            add_into(mine.at[0, kind, CUTS[kind] + at, y, some], yqo.at[slots[kind], at, some])
        xq_copy(kind, part).start()

    def forward_p(kind, part):
        p_copy(kind, part).wait_recv()
        some = pl.ds(*parts[kind][part])
        for at in range(CUTS[kind]):
            for block in range(2):
                add_into(mine.at[1, kind, at, block, some], xp.at[slots[kind], at, block, some])
        yp_copy(kind, part).start()

    def finish_plane(kind, part):
        some = pl.ds(*parts[kind][part])
        if kind == KIND_IN:
            ywall_copy(part).wait_recv()
            for at in range(depth):
                add_into(mine.at[1, kind, at, y, some], ywall.at[at, some])
            return
        slot = slots[kind]
        q_copy(1, kind, part).wait_recv()
        xq_copy(kind, part).wait_recv()
        for at in range(depth - CUTS[kind]):
            ref = mine.at[1, kind, CUTS[kind] + at, y, some]
            total = ref[...].astype(F32) + yqw[slot, at, some].astype(F32) + xq[slot, at, some].astype(F32)
            ref[...] = total.astype(BF16)
        yp_copy(kind, part).wait_recv()
        for at in range(CUTS[kind]):
            add_into(mine.at[1, kind, at, y, some], yp.at[slot, at, some])

    def hop(name, kind, part, count):
        high = depth - 1 - count + z
        low = count - (depth - 1 - z)

        @pl.when(z <= count)
        def _():
            @pl.when(z > 0)
            def _():
                from_low(name, kind, part, high)

            up_copy(name, kind, part, high).start()

        @pl.when(low >= 0)
        def _():
            @pl.when(z < depth - 1)
            def _():
                from_high(name, kind, part, low)

            down_copy(name, kind, part, low).start()

    finished = []

    def finish(name, kind, part):
        @pl.when(z > 0)
        def _():
            from_low(name, kind, part, z)

        @pl.when(z < depth - 1)
        def _():
            from_high(name, kind, part, z)

        if name == FIRST_LINE:
            return
        some = line_rows(kind, part)
        if kind == KIND_IN:
            add_into(mine.at[1, kind, z, y, some], xo.at[y, some])
            if (name, kind, 1 - part) not in finished:
                yo_copy().wait_recv()
            add_into(mine.at[1, kind, z, y, some], yo.at[some])
        finished.append((name, kind, part))
        piece_out[kind, some, :] = mine[1, kind, z, y, some, :]

    def forward_o(kind):
        xo_copy().wait_recv()
        yo_copy().start()

    act = {
        MUL: multiply,
        CORE: add_core,
        SEND_P: lambda kind, part: p_copy(kind, part).start(),
        SEND_QO: lambda kind, part: q_copy(0, kind, part).start(),
        SEND_QW: lambda kind, part: q_copy(1, kind, part).start(),
        PASS_Q: forward_q,
        PASS_P: forward_p,
        PLANE: finish_plane,
        HOP: hop,
        FIN: finish,
        SEND_O: lambda kind: xo_copy().start(),
        PASS_O: forward_o,
        SEND_WALL: lambda kind, part: ywall_copy(part).start(),
    }
    for name, *numbers in PLAN:
        act[name](*numbers)

    for unit in (4, 5):
        for part in core_parts(units[unit][1]):
            core_copy(unit, part).wait_send()
    for copy in (xo_copy(), yo_copy(), ywall_copy(0), ywall_copy(1)):
        copy.wait_send()
    for kind in CUTS:
        for part in range(2):
            p_copy(kind, part).wait_send()
            xq_copy(kind, part).wait_send()
            yp_copy(kind, part).wait_send()
            for side in range(2):
                q_copy(side, kind, part).wait_send()
    lines = [(FIRST_LINE, KIND_IN, 0)]
    lines += [(LINE, kind, part) for kind in (KIND_IN, *CUTS) for part in range(2)]
    for line in lines:
        for at in range(depth):

            @pl.when(at > z)
            def _():
                up_copy(*line, at).wait_send()

            @pl.when(at < z)
            def _():
                down_copy(*line, at).wait_send()


def grad_reduce_shapes(dp, steps, rows, width):
    half = width // 2
    lanes = 4 * width // dp
    depth = dp // 2
    extra_rows = 16
    tall = half + extra_rows
    most, least = max(CUTS.values()), depth - min(CUTS.values())
    held = [width, 4 * width, 4 * width, width, width, 3 * width, width, width]
    return (
        [pltpu.VMEM((steps // 2 * rows, columns), BF16) for columns in held]
        + [
            pltpu.VMEM(shape + (tall, lanes), BF16)
            for shape in (
                (2, 3, depth, 2), (2, depth, 2), (2, depth, 2), (2, most, 2), (2, least), (2, least),
                (2, least), (2, most), (depth,), (2,), (), (3, depth - 1), (3, depth - 1),
                (depth - 1, 2), (depth - 1, 2),
            )
        ]
        + [pltpu.VMEM((2, 2, 3 * extra_rows, lanes), F32)]
    )


def unpack_body(mem, piece_ref, qkv_ref, out_ref, in_ref, hid_ref, memory_ref, bias_ref, gain_ref, vec_scr):
    wide, half = qkv_ref.shape[1:]
    thin, lanes = out_ref.shape[1], in_ref.shape[2]
    width = memory_ref.shape[1]
    qkv_ref[0] = piece_ref[0, 0:wide, :].astype(F32)
    out_ref[0] = piece_ref[0, wide:half, :].astype(F32)
    in_ref[0] = piece_ref[1, 0:half, :].astype(F32)
    for part in range(4):
        hid_ref[0, :, part * half : (part + 1) * half] = piece_ref[
            2, part * thin : (part + 1) * thin, :
        ].astype(F32)
    extra = jnp.concatenate([piece_ref[kind, half:, :].astype(F32) for kind in range(3)], axis=0)
    pieces = width // lanes
    for piece in range(pieces):
        memory_ref[:, piece * lanes : (piece + 1) * lanes] = extra[piece * mem : (piece + 1) * mem, :]
    for at in range(6 * pieces):
        row = mem * pieces + at
        vec_scr[0:1, at * lanes : (at + 1) * lanes] = extra[row : row + 1, :]
    place = lax.axis_index("dp")
    long = 5 * width
    for ref, first, last in ((bias_ref, 0, long), (gain_ref, long, long + width)):
        size = ref.shape[1]
        turned = pltpu.roll(vec_scr[:, first:last], (last - first - place * size) % (last - first), 1)
        ref[...] = turned[0:1, 0:size]


def grad_reduce(dp, mem, saved, sums, memory):
    sources = [saved[name] for name in GRAD_NAMES]
    steps, rows, width = sources[0].shape
    segs_all = steps // 2
    half = width // 2
    lanes = 4 * width // dp
    thin = width // dp
    depth = dp // 2
    any_spec = pl.BlockSpec(memory_space=pl.ANY)
    dma = pltpu.SemaphoreType.DMA
    shapes = grad_reduce_shapes(dp, steps, rows, width)
    piece = pl.pallas_call(
        functools.partial(grad_reduce_body, dp, mem, segs_all),
        in_specs=[any_spec] * 8 + [pl.BlockSpec(memory_space=pltpu.VMEM)] * 2,
        out_specs=pl.BlockSpec(memory_space=pltpu.VMEM),
        out_shape=jax.ShapeDtypeStruct((3,) + shapes[8].shape[-2:], BF16),
        scratch_shapes=shapes
        + [
            dma((8, segs_all)), dma((2, 6, depth)), pltpu.SemaphoreType.REGULAR, dma((2, 2, 2)), dma((2, 2, 2)),
            dma((2, 2, 2)), dma((2, 2, 2)), dma((2, 2, 2)), dma((2, 4)), dma((2, 3, 2, depth)),
            dma((2, 3, 2, depth)), dma((2, depth)), dma((2, depth)),
        ],
        compiler_params=pltpu.CompilerParams(
            vmem_limit_bytes=VMEM_BYTES, collective_id=0, has_side_effects=True
        ),
        name="grad_reduce",
    )(*sources, sums, memory)
    qkv, out, w_in, hid, memory, bias, gain = pl.pallas_call(
        functools.partial(unpack_body, mem),
        out_shape=[
            jax.ShapeDtypeStruct(shape, F32)
            for shape in (
                (1, 3 * thin, half), (1, thin, half), (1, half, lanes), (1, thin, 4 * half),
                (mem, width), (1, 5 * thin), (1, thin),
            )
        ],
        scratch_shapes=[pltpu.VMEM((8, 6 * width), F32)],
        name="unpack",
    )(piece)
    grads = (jnp.swapaxes(qkv, 1, 2), jnp.swapaxes(out, 1, 2), w_in, jnp.swapaxes(hid, 1, 2))
    return (memory, *grads, bias, gain)


def other_core(block, dp):
    return lax.ppermute(block, "dp", [(at, at ^ 1) for at in range(dp)])


def per_device(
    text_rows,
    memory_init,
    cotangent,
    w_qkv,
    w_out,
    w_in,
    w_hid,
    biases,
    norm_gains,
    boundaries,
    mem_resets,
    seg_counts,
):
    items, segs, text_len, width = text_rows.shape
    mem_rows = memory_init.shape[0]
    rows = text_len + 2 * mem_rows
    half = width // 2
    dp = lax.axis_size("dp")
    blocks = (w_qkv, w_out, w_in, w_hid)
    steps = 2 * items * segs
    text = jnp.swapaxes(text_rows, 1, 2)
    if dp == 8:
        saved, acts, masks, weights, vecs = gather_forward(
            text, mem_resets, seg_counts, memory_init, boundaries, blocks, biases, norm_gains
        )
    else:
        weights, vecs = gather_apart(blocks, biases, norm_gains)
        saved, acts, masks = forward_steps(
            text, mem_resets, seg_counts, memory_init, boundaries, weights, vecs
        )
    grads, sums, input_grads, memory_grad, acts = backward_steps(
        cotangent, mem_resets, seg_counts, masks, mem_rows, acts, weights, vecs, saved
    )
    saved.update(grads)
    reduce = grad_reduce if dp == 8 else grad_reduce_apart
    return (acts, input_grads, *reduce(dp, mem_rows, saved, sums, memory_grad))


def grad_reduce_apart(dp, mem_rows, saved, sums, memory_grad):
    steps, width = sums.shape[0], memory_grad.shape[1]
    half = width // 2
    vector_len = 5 * width
    lanes = 4 * width // dp
    memory_part = memory_grad[16 - mem_rows :].reshape(-1)
    memory_len = -(-memory_part.shape[0] // lanes) * lanes
    memory_part = jnp.pad(memory_part, (0, memory_len - memory_part.shape[0]))
    vector_part = vector_len // dp
    gain_part = width // dp
    used = memory_len + vector_part + gain_part
    extra_rows = -(-used // (3 * 16 * lanes)) * 16
    extras = []
    for layer in range(2):
        total = sums.reshape(steps // 2, 2, 12 * width)[:, layer].sum(axis=0)
        gain_two, shift_two, bias_hid, gain_one, shift_one, bias_o, bias_q, bias_v = [
            total[at * width : (at + 1) * width] for at in range(8)
        ]
        vector = jnp.concatenate(
            [bias_q, bias_v, bias_o, shift_one, total[8 * width :], bias_hid, shift_two]
        ).reshape(2, dp, vector_part)
        gain = jnp.stack([gain_one, gain_two]).reshape(2, dp, gain_part)
        extra = jnp.concatenate(
            [jnp.broadcast_to(memory_part, (2, dp, memory_len)), vector, gain], axis=-1
        )
        extra = jnp.pad(extra, ((0, 0), (0, 0), (0, 3 * extra_rows * lanes - used)))
        extra = extra.reshape(2, dp // 2, 2, 3, extra_rows, lanes).transpose(3, 2, 1, 0, 4, 5)
        extras.append(extra.astype(BF16))
    extras = jnp.stack(extras)
    wires = [weight_grads(layer, dp, saved, extras[layer]) for layer in range(2)]
    mine = jnp.stack([wires[0][0], wires[1][0]])
    theirs = other_core(jnp.stack([wires[0][1], wires[1][1]]), dp)
    both = mine.astype(F32) + theirs.astype(F32)
    both = both.transpose(3, 0, 2, 1, 4, 5).astype(BF16)
    tall, lanes = both.shape[-2:]
    both = both.reshape(4, dp // 2, 3, tall, lanes)
    own = lax.psum_scatter(both, "section", scatter_dimension=0, tiled=True)[0]
    groups = [[2 * at + side for at in range(dp // 2)] for side in range(2)]
    own = lax.psum_scatter(
        own, "dp", scatter_dimension=0, axis_index_groups=groups, tiled=True
    )[0].astype(F32)
    thin = lanes // 4
    body = own[:, :half]
    hid = body[2].reshape(half, 4, thin).transpose(1, 0, 2).reshape(4 * half, thin)
    flat = own[:, half:].reshape(-1)
    return (
        flat[: mem_rows * width].reshape(mem_rows, width),
        body[0, :, : 3 * thin][None],
        body[0, :, 3 * thin :][None],
        body[1][None],
        hid[None],
        flat[memory_len : memory_len + vector_part][None],
        flat[memory_len + vector_part : used][None],
    )


def solution(mesh):
    in_specs = (
        P(("section", "dp"), None, None, None),
        P(),
        P(("section", "dp"), None, None, None),
        P("section", None, None),
        P("section", None, None),
        P("section", None, None),
        P("section", None, None),
        P("section", None),
        P("section", None),
        P(("section", "dp"), None, None),
        P(("section", "dp"), None),
        P(("section", "dp")),
    )
    out_specs = (
        P(("section", "dp"), None, None, None),
        P(("section", "dp"), None, None, None),
        P(),
        P("section", None, "dp"),
        P("section", None, "dp"),
        P("section", None, "dp"),
        P("section", None, "dp"),
        P("section", "dp"),
        P("section", "dp"),
    )
    return jax.shard_map(
        per_device, mesh=mesh, in_specs=in_specs, out_specs=out_specs, check_vma=False
    )
```
